32 devices in a mesh: groups: 2 (over y), resi: 4 (over z), resj: 2 (over core), seq: 2 (over x).
Axes of the slice: x: 2, y: 2, z: 4, core: 2. Of those that a mesh axis runs over, the one named last changes fastest.
Arguments:
- homolog_matrix: bfloat16 [256, 128, 256], P(('groups', 'resj', 'seq'), 'resi'), parts along dimension 0, may hold values from -6 to 6
- sequence_pad_mask: int32 [256, 128], P(('groups', 'resj', 'seq'), 'resi'), parts along dimension 0, may hold values 0 or 1
- pair_features: bfloat16 [256, 128, 128], P(('groups', 'resi'), ('resj', 'seq')), parts along dimension 0, may hold values from -6 to 6
- residue_pad_mask: int32 [256], P('groups'), parts along dimension 0, may hold values 0 or 1
- residue_chain_index: int32 [256], P('groups'), parts along dimension 0, may hold values from 0 to 3, never falling along the last dimension, each value on 1 to 64 neighbouring positions
- homolog_standard_factor: float32 [256], replicated, may hold values from 0.5 to 1.5
- homolog_standard_offset: float32 [256], replicated, may hold values from -0.3 to 0.3
- factor_mapping_matrices: bfloat16 [256, 64], replicated, may hold values from -0.375 to 0.375
- outer_side_biases: float32 [64], replicated, may hold values from -0.3 to 0.3
- outer_pair_projection: bfloat16 [1024, 128], replicated, may hold values from -2.390625 to 2.390625
- relative_position_table: bfloat16 [66, 128], replicated, may hold values from -3 to 3
- pair_norm_gain: float32 [128], replicated, may hold values from 0.5 to 1.5
- pair_norm_bias: float32 [128], replicated, may hold values from -3 to 3
- triangle_projection_weights: bfloat16 [128, 640], replicated, may hold values from -0.5 to 0.5
- triangle_projection_biases: float32 [640], replicated, may hold values from -2 to 2
- triangle_sum_norm_gain: float32 [128], replicated, may hold values from 0.5 to 1.5
- triangle_sum_norm_bias: float32 [128], replicated, may hold values from -3 to 3
- triangle_output_weight: bfloat16 [128, 128], replicated, may hold values from -0.5 to 0.5
- outer_pair_bias: float32 [128], replicated, may hold values from -3 to 3
Outputs:
- new_pair: bfloat16 [256, 128, 128], P(('groups', 'resi'), ('resj', 'seq')), parts along dimension 0
The draws below stay inside these ranges and needn't reach their ends.
There are 2 independent parts, one for each index of `groups`. The reference program is written for one: setup_inputs(seed, part) draws one part's arguments, and reference() takes and returns one part's arrays. A program takes and returns all parts, laid end to end along the dimension named above; an argument that names none is the same for every part. Nothing has to cross between parts.
Inputs may be any that keep to these rules, and one draw needn't show every extreme that they name: residue_chain_index never falls along the residues; each chain holds 1 to 64 residues, one exactly 64.
All inputs are finite; a program needn't handle non-finite values. No bound on the sum of `sequence_pad_mask` on one device may be relied on, other than what follows from the above.
Results may differ from the reference program's by a relative error of at most 0.0085.
Values may be sent and summed in bfloat16 or wider, within the bound.
No kernel may reach another device: no remote copies, remote signals or barrier semaphores. Data moves between devices by JAX's collectives and lax.ppermute only.
A program may use at most 64 MiB of HBM per device.

```python
import math
import jax
import jax.numpy as jnp
import numpy as np
from jax import lax

COLUMN_FEAT_SIZE = 256
CZ = 128
HALF_WIDTH = 32
RELMAX = 32
RES_DEV = 32
AMINO_COUNT = 128
HOMOLOG_COUNT = 128
BINS = 66


def plant(entries, own_key, smallest, top_value):
    place = [jax.random.randint(jax.random.fold_in(own_key, axis), (), 0, length) for axis, length in enumerate(entries.shape)]
    widest = entries.shape.index(max(entries.shape))
    neighbour = place[:widest] + [(place[widest] + 1) % entries.shape[widest]] + place[widest + 1:]
    return entries.at[tuple(place)].set(smallest).at[tuple(neighbour)].set(top_value)


def block_levels(own_key, dims, split, low, high):
    factor_of, own = 1.0, jax.random.fold_in(own_key, 6)
    for axis_at, blocks in split:
        draws = jnp.exp(jax.random.uniform(jax.random.fold_in(own, axis_at), (blocks,), jnp.float32, low / len(split), high / len(split)))
        factor_of = factor_of * jnp.repeat(draws, dims[axis_at] // blocks).reshape([-1 if axis == axis_at else 1 for axis in range(len(dims))])
    return factor_of


def profile(amount, total, bound, slope):
    weights = [(1 << 20) // math.isqrt(rank ** slope) + 1 for rank in range(2, amount + 1)]
    surplus, given = total - bound - (amount - 1), [1] * (amount - 1)
    while surplus > 0:
        candidates = [i for i in range(amount - 1) if given[i] < bound]
        pool, budget = sum([weights[i] for i in candidates]), surplus
        for i in candidates:
            extra = min(bound - given[i], max(1, budget * weights[i] // pool), surplus)
            given[i] = given[i] + extra
            surplus = surplus - extra
    return np.array([bound] + given)


def uneven(rng, number_of, total, most, slope):
    if number_of == 2:
        one = jax.random.randint(rng, (), max(1, total - most), min(most, total - 1) + 1)
        return jnp.stack([one, total - one])
    tallies = jnp.asarray(profile(number_of, total, most, slope), jnp.int32)
    twos = (number_of - 1) // 2
    giver, sink = tallies[1:1 + 2 * twos:2], tallies[2:2 + 2 * twos:2]
    room = jnp.minimum(giver - 1, most - sink)
    shifted = jax.random.randint(jax.random.fold_in(rng, 1), (twos,), 0, 1 << 20) % (room + 1)
    tallies = tallies.at[1:1 + 2 * twos:2].set(giver - shifted).at[2:2 + 2 * twos:2].set(sink + shifted)
    return tallies[jax.random.permutation(jax.random.fold_in(rng, 2), number_of)]


def noise(stream_key, dims, deviation, limit, cuts=(), kind=jnp.bfloat16):
    entries = deviation * jax.random.normal(stream_key, dims, jnp.float32)
    if cuts:
        entries = entries * block_levels(stream_key, dims, cuts, -0.22, 0.18)
    return jnp.clip(entries, -limit, limit).astype(kind)


def setup_inputs(seed: int = 0, part: int = 0) -> dict:
    arg_keys = jax.random.split(jax.random.key(seed), 20)
    part_splits = jax.random.split(jax.random.fold_in(arg_keys[19], part), 20)
    return {
        "homolog_matrix": noise(part_splits[0], (HOMOLOG_COUNT, AMINO_COUNT, COLUMN_FEAT_SIZE), 1.0, 6.0, ((0, 4), (1, 4))),
        "sequence_pad_mask": plant((jax.random.randint(part_splits[1], (HOMOLOG_COUNT, AMINO_COUNT), 0, 4) < 3).astype(jnp.int32), jax.random.fold_in(part_splits[1], 1), 0, 1),
        "pair_features": noise(part_splits[2], (AMINO_COUNT, AMINO_COUNT, CZ), 1.0, 6.0, ((0, 4), (1, 4))),
        "residue_pad_mask": plant((jax.random.randint(part_splits[3], (AMINO_COUNT,), 0, 8) < 7).astype(jnp.int32), jax.random.fold_in(part_splits[3], 1), 0, 1),
        "residue_chain_index": jnp.searchsorted(jnp.cumsum(uneven(part_splits[4], 4, AMINO_COUNT, AMINO_COUNT // 2, 0)), jnp.arange(AMINO_COUNT), side="right").astype(jnp.int32),
        "homolog_standard_factor": jnp.clip(1.0 + 0.1 * jax.random.normal(arg_keys[5], (COLUMN_FEAT_SIZE,), jnp.float32), 0.5, 1.5),
        "homolog_standard_offset": noise(arg_keys[6], (COLUMN_FEAT_SIZE,), 0.05, 0.3, (), jnp.float32),
        "factor_mapping_matrices": noise(arg_keys[7], (COLUMN_FEAT_SIZE, 2 * HALF_WIDTH), COLUMN_FEAT_SIZE ** -0.5, 0.375),
        "outer_side_biases": noise(arg_keys[8], (2 * HALF_WIDTH,), 0.05, 0.3, (), jnp.float32),
        "outer_pair_projection": noise(arg_keys[9], (HALF_WIDTH * HALF_WIDTH, CZ), 0.4, 2.390625),
        "relative_position_table": noise(arg_keys[10], (BINS, CZ), 0.5, 3.0),
        "pair_norm_gain": jnp.clip(1.0 + 0.1 * jax.random.normal(arg_keys[11], (CZ,), jnp.float32), 0.5, 1.5),
        "pair_norm_bias": noise(arg_keys[12], (CZ,), 0.5, 3.0, (), jnp.float32),
        "triangle_projection_weights": noise(arg_keys[13], (CZ, 5 * CZ), CZ ** -0.5, 0.5),
        "triangle_projection_biases": noise(arg_keys[14], (5 * CZ,), 0.5, 2.0, (), jnp.float32),
        "triangle_sum_norm_gain": jnp.clip(1.0 + 0.1 * jax.random.normal(arg_keys[15], (CZ,), jnp.float32), 0.5, 1.5),
        "triangle_sum_norm_bias": noise(arg_keys[16], (CZ,), 0.5, 3.0, (), jnp.float32),
        "triangle_output_weight": noise(arg_keys[17], (CZ, CZ), CZ ** -0.5, 0.5),
        "outer_pair_bias": noise(arg_keys[18], (CZ,), 0.5, 3.0, (), jnp.float32),
    }


def apply_layer_norm(values, gain_vec, shift_vec):
    average = lax.optimization_barrier(jnp.mean(values, axis=-1, keepdims=True))
    centred = values - average
    variance = lax.optimization_barrier(jnp.mean(centred * centred, axis=-1, keepdims=True))
    return centred * lax.rsqrt(variance + 1e-05) * gain_vec + shift_vec

def reference(homolog_matrix, sequence_pad_mask, pair_features, residue_pad_mask, residue_chain_index, homolog_standard_factor, homolog_standard_offset, factor_mapping_matrices, outer_side_biases, outer_pair_projection, relative_position_table, pair_norm_gain, pair_norm_bias, triangle_projection_weights, triangle_projection_biases, triangle_sum_norm_gain, triangle_sum_norm_bias, triangle_output_weight, outer_pair_bias):
    residue_live = residue_pad_mask.astype(jnp.float32)
    seq_live = sequence_pad_mask.astype(jnp.float32) * residue_live[None, :]
    standardized_homologs = apply_layer_norm(homolog_matrix.astype(jnp.float32), homolog_standard_factor, homolog_standard_offset).astype(jnp.bfloat16)
    mapped_factors = jnp.dot(standardized_homologs.reshape(HOMOLOG_COUNT * AMINO_COUNT, COLUMN_FEAT_SIZE), factor_mapping_matrices, preferred_element_type=jnp.float32)
    mapped_factors = (mapped_factors.reshape(HOMOLOG_COUNT, AMINO_COUNT, 2 * HALF_WIDTH) + outer_side_biases) * seq_live[:, :, None]
    mapped_factors = mapped_factors.astype(jnp.bfloat16)
    left_feat = mapped_factors[:, :, :HALF_WIDTH].astype(jnp.float32)
    right_feat = mapped_factors[:, :, HALF_WIDTH:].astype(jnp.float32)
    counts = jnp.dot(seq_live.T, seq_live, precision=lax.Precision.HIGHEST)

    def outer_block(block_index):
        left_block = lax.dynamic_slice_in_dim(left_feat, block_index * RES_DEV, RES_DEV, 1)
        products = jnp.einsum('sic,sjd->ijcd', left_block, right_feat).astype(jnp.bfloat16)
        flattened = products.reshape(RES_DEV * AMINO_COUNT, HALF_WIDTH * HALF_WIDTH)
        return jnp.dot(flattened, outer_pair_projection, preferred_element_type=jnp.float32).reshape(RES_DEV, AMINO_COUNT, CZ)
    outer_sum = lax.map(outer_block, jnp.arange(AMINO_COUNT // RES_DEV, dtype=jnp.int32)).reshape(AMINO_COUNT, AMINO_COUNT, CZ)
    outer_mean = outer_sum / jnp.maximum(counts, 1.0)[:, :, None]
    positions = jnp.arange(AMINO_COUNT, dtype=jnp.int32)
    offsets = jnp.clip(positions[None, :] - positions[:, None] + RELMAX, 0, 2 * RELMAX)
    same_chain = residue_chain_index[:, None] == residue_chain_index[None, :]
    bin_index = jnp.where(same_chain, offsets, 2 * RELMAX + 1)
    embedded = relative_position_table.astype(jnp.float32)[bin_index]
    updated = (pair_features.astype(jnp.float32) + embedded + outer_mean).astype(jnp.bfloat16)
    normed_pair = apply_layer_norm(updated.astype(jnp.float32), pair_norm_gain, pair_norm_bias).astype(jnp.bfloat16)
    mixture = jnp.dot(normed_pair.reshape(AMINO_COUNT * AMINO_COUNT, CZ), triangle_projection_weights, preferred_element_type=jnp.float32)
    mixture = mixture.reshape(AMINO_COUNT, AMINO_COUNT, 5 * CZ) + triangle_projection_biases
    pair_live = (residue_live[:, None] * residue_live[None, :])[:, :, None]
    left_edge = (jax.nn.sigmoid(mixture[:, :, :CZ]) * mixture[:, :, CZ:2 * CZ] * pair_live).astype(jnp.bfloat16)
    right_edge = (jax.nn.sigmoid(mixture[:, :, 2 * CZ:3 * CZ]) * mixture[:, :, 3 * CZ:4 * CZ] * pair_live).astype(jnp.bfloat16)
    gating = jax.nn.sigmoid(mixture[:, :, 4 * CZ:])
    triangle = jnp.einsum('ikc,jkc->ijc', left_edge.astype(jnp.float32), right_edge.astype(jnp.float32))
    normed_tri = apply_layer_norm(triangle, triangle_sum_norm_gain, triangle_sum_norm_bias).astype(jnp.bfloat16)
    result = jnp.dot(normed_tri.reshape(AMINO_COUNT * AMINO_COUNT, CZ), triangle_output_weight, preferred_element_type=jnp.float32)
    result = result.reshape(AMINO_COUNT, AMINO_COUNT, CZ) + outer_pair_bias
    return (updated.astype(jnp.float32) + gating * result).astype(jnp.bfloat16)
```

```python
import jax
import jax.numpy as jnp
from jax import lax
from jax.sharding import PartitionSpec as P

RELMAX = 32


PLANE = ("resj", "seq")
GROUP = ("resi", "resj", "seq")


def gather_plane(block, count):
    me = lax.axis_index(PLANE)
    parts = [block]
    for step in range(1, count):
        parts.append(lax.ppermute(block, PLANE, [(p, p ^ step) for p in range(count)]))
    stacked = jnp.stack(parts)
    return jnp.stack([lax.dynamic_index_in_dim(stacked, b ^ me, 0, False) for b in range(count)])


def gather_turned(block, count):
    me = lax.axis_index("resi")
    parts = []
    for step in range(count):
        pairs = [
            (z * count + p, (p ^ step) * count + z) for z in range(count) for p in range(count)
        ]
        parts.append(lax.ppermute(block, GROUP, pairs))
    stacked = jnp.stack(parts)
    return jnp.stack([lax.dynamic_index_in_dim(stacked, b ^ me, 0, False) for b in range(count)])


def apply_layer_norm(values, gain_vec, shift_vec):
    average = jnp.mean(values, axis=-1, keepdims=True)
    centred = values - average
    variance = jnp.mean(centred * centred, axis=-1, keepdims=True)
    return centred * lax.rsqrt(variance + 1e-05) * gain_vec + shift_vec


def body(
    homolog_matrix,
    sequence_pad_mask,
    pair_features,
    residue_pad_mask,
    residue_chain_index,
    homolog_standard_factor,
    homolog_standard_offset,
    factor_mapping_matrices,
    outer_side_biases,
    outer_pair_projection,
    relative_position_table,
    pair_norm_gain,
    pair_norm_bias,
    triangle_projection_weights,
    triangle_projection_biases,
    triangle_sum_norm_gain,
    triangle_sum_norm_bias,
    triangle_output_weight,
    outer_pair_bias,
):
    row_count = pair_features.shape[0]
    col_count = pair_features.shape[1]
    channels = pair_features.shape[2]
    seq_local = homolog_matrix.shape[0]
    narrow = factor_mapping_matrices.shape[1] // 2
    row_start = lax.axis_index("resi") * row_count
    col_index = lax.axis_index(("resj", "seq"))
    col_start = col_index * col_count
    residue_live = residue_pad_mask.astype(jnp.float32)
    row_live = lax.dynamic_slice_in_dim(residue_live, row_start, row_count)
    col_live = lax.dynamic_slice_in_dim(residue_live, col_start, col_count)
    seq_live = sequence_pad_mask.astype(jnp.float32) * row_live[None, :]
    standardized_homologs = apply_layer_norm(
        homolog_matrix.astype(jnp.float32), homolog_standard_factor, homolog_standard_offset
    ).astype(jnp.bfloat16)
    mapped_factors = jnp.dot(
        standardized_homologs.reshape(seq_local * row_count, -1),
        factor_mapping_matrices,
        preferred_element_type=jnp.float32,
    )
    mapped_factors = (
        mapped_factors.reshape(seq_local, row_count, 2 * narrow) + outer_side_biases
    ) * seq_live[:, :, None]
    mapped_factors = mapped_factors.astype(jnp.bfloat16)
    live_bf = seq_live.astype(jnp.bfloat16)
    count = lax.axis_size(PLANE)
    left_pack = jnp.concatenate(
        [mapped_factors[:, :, :narrow].reshape(seq_local, row_count * narrow), live_bf], axis=1
    )
    right_pack = jnp.concatenate(
        [mapped_factors[:, :, narrow:].reshape(seq_local, row_count * narrow), live_bf], axis=1
    )
    left_all = gather_plane(left_pack, count).reshape(count * seq_local, -1)
    right_all = gather_turned(right_pack, count).reshape(count * seq_local, -1)
    wide = row_count * narrow
    live_all, live_cols = left_all[:, wide:], right_all[:, wide:]
    total_seqs = count * seq_local
    products = jnp.einsum(
        "sic,sjd->ijcd",
        left_all[:, :wide].reshape(total_seqs, row_count, narrow),
        right_all[:, :wide].reshape(total_seqs, col_count, narrow),
        preferred_element_type=jnp.float32,
    )
    counts = jnp.dot(live_all.T, live_cols, preferred_element_type=jnp.float32)
    flattened = products.astype(jnp.bfloat16).reshape(row_count * col_count, narrow * narrow)
    outer_sum = jnp.dot(
        flattened, outer_pair_projection, preferred_element_type=jnp.float32
    ).reshape(row_count, col_count, channels)
    outer_mean = outer_sum / jnp.maximum(counts, 1.0)[:, :, None]
    row_pos = row_start + jnp.arange(row_count, dtype=jnp.int32)
    col_pos = col_start + jnp.arange(col_count, dtype=jnp.int32)
    offsets = jnp.clip(col_pos[None, :] - row_pos[:, None] + RELMAX, 0, 2 * RELMAX)
    chain_rows = lax.dynamic_slice_in_dim(residue_chain_index, row_start, row_count)
    chain_cols = lax.dynamic_slice_in_dim(residue_chain_index, col_start, col_count)
    same_chain = chain_rows[:, None] == chain_cols[None, :]
    bin_index = jnp.where(same_chain, offsets, 2 * RELMAX + 1)
    one_hot = (
        bin_index[:, :, None] == jnp.arange(relative_position_table.shape[0], dtype=jnp.int32)
    ).astype(jnp.bfloat16)
    embedded = jnp.einsum(
        "ijb,bc->ijc", one_hot, relative_position_table, preferred_element_type=jnp.float32
    )
    updated = (pair_features.astype(jnp.float32) + embedded + outer_mean).astype(jnp.bfloat16)
    normed_pair = apply_layer_norm(
        updated.astype(jnp.float32), pair_norm_gain, pair_norm_bias
    ).astype(jnp.bfloat16)
    mixture = jnp.dot(
        normed_pair.reshape(row_count * col_count, channels),
        triangle_projection_weights,
        preferred_element_type=jnp.float32,
    )
    mixture = mixture.reshape(row_count, col_count, 5 * channels) + triangle_projection_biases
    pair_live = (row_live[:, None] * col_live[None, :])[:, :, None]
    left_edge = (
        jax.nn.sigmoid(mixture[:, :, :channels])
        * mixture[:, :, channels : 2 * channels]
        * pair_live
    ).astype(jnp.bfloat16)
    right_edge = (
        jax.nn.sigmoid(mixture[:, :, 2 * channels : 3 * channels])
        * mixture[:, :, 3 * channels : 4 * channels]
        * pair_live
    ).astype(jnp.bfloat16)
    gating = jax.nn.sigmoid(mixture[:, :, 4 * channels :])
    left_panel = gather_plane(left_edge, count)
    right_match = gather_turned(right_edge, count)
    triangle = jnp.einsum(
        "bikc,bjkc->ijc", left_panel, right_match, preferred_element_type=jnp.float32
    )
    normed_tri = apply_layer_norm(triangle, triangle_sum_norm_gain, triangle_sum_norm_bias).astype(
        jnp.bfloat16
    )
    result = jnp.dot(
        normed_tri.reshape(row_count * col_count, channels),
        triangle_output_weight,
        preferred_element_type=jnp.float32,
    )
    result = result.reshape(row_count, col_count, channels) + outer_pair_bias
    return (updated.astype(jnp.float32) + gating * result).astype(jnp.bfloat16)


def solution(mesh):
    placed = (
        P(("groups", "resj", "seq"), "resi", None),
        P(("groups", "resj", "seq"), "resi"),
        P(("groups", "resi"), ("resj", "seq"), None),
        P("groups"),
        P("groups"),
        P(),
        P(),
        P(),
        P(),
        P(),
        P(),
        P(),
        P(),
        P(),
        P(),
        P(),
        P(),
        P(),
        P(),
    )
    return jax.shard_map(
        body,
        mesh=mesh,
        in_specs=placed,
        out_specs=P(("groups", "resi"), ("resj", "seq"), None),
        check_vma=False,
    )
```

```python
import jax
import jax.numpy as jnp
from jax import lax
from jax.sharding import PartitionSpec as P

RELMAX = 32


PLANE = ("resj", "seq")
GROUP = ("resi", "resj", "seq")


def gather_plane(block, count):
    me = lax.axis_index(PLANE)
    parts = [block]
    for step in range(1, count):
        parts.append(lax.ppermute(block, PLANE, [(p, p ^ step) for p in range(count)]))
    stacked = jnp.stack(parts)
    return jnp.stack([lax.dynamic_index_in_dim(stacked, b ^ me, 0, False) for b in range(count)])


def gather_turned(block, count):
    me = lax.axis_index("resi")
    parts = []
    for step in range(count):
        pairs = [
            (z * count + p, (p ^ step) * count + z) for z in range(count) for p in range(count)
        ]
        parts.append(lax.ppermute(block, GROUP, pairs))
    stacked = jnp.stack(parts)
    return jnp.stack([lax.dynamic_index_in_dim(stacked, b ^ me, 0, False) for b in range(count)])


def apply_layer_norm(values, gain_vec, shift_vec):
    average = jnp.mean(values, axis=-1, keepdims=True)
    centred = values - average
    variance = jnp.mean(centred * centred, axis=-1, keepdims=True)
    return centred * lax.rsqrt(variance + 1e-05) * gain_vec + shift_vec


def body(
    homolog_matrix,
    sequence_pad_mask,
    pair_features,
    residue_pad_mask,
    residue_chain_index,
    homolog_standard_factor,
    homolog_standard_offset,
    factor_mapping_matrices,
    outer_side_biases,
    outer_pair_projection,
    relative_position_table,
    pair_norm_gain,
    pair_norm_bias,
    triangle_projection_weights,
    triangle_projection_biases,
    triangle_sum_norm_gain,
    triangle_sum_norm_bias,
    triangle_output_weight,
    outer_pair_bias,
):
    row_count = pair_features.shape[0]
    col_count = pair_features.shape[1]
    channels = pair_features.shape[2]
    seq_local = homolog_matrix.shape[0]
    narrow = factor_mapping_matrices.shape[1] // 2
    row_start = lax.axis_index("resi") * row_count
    col_index = lax.axis_index(("resj", "seq"))
    col_start = col_index * col_count
    residue_live = residue_pad_mask.astype(jnp.float32)
    row_live = lax.dynamic_slice_in_dim(residue_live, row_start, row_count)
    col_live = lax.dynamic_slice_in_dim(residue_live, col_start, col_count)
    seq_live = sequence_pad_mask.astype(jnp.float32) * row_live[None, :]
    standardized_homologs = apply_layer_norm(
        homolog_matrix.astype(jnp.float32), homolog_standard_factor, homolog_standard_offset
    ).astype(jnp.bfloat16)
    mapped_factors = jnp.dot(
        standardized_homologs.reshape(seq_local * row_count, -1),
        factor_mapping_matrices,
        preferred_element_type=jnp.float32,
    )
    mapped_factors = (
        mapped_factors.reshape(seq_local, row_count, 2 * narrow) + outer_side_biases
    ) * seq_live[:, :, None]
    mapped_factors = mapped_factors.astype(jnp.bfloat16)
    live_bf = seq_live.astype(jnp.bfloat16)
    count = lax.axis_size(PLANE)
    left_pack = jnp.concatenate(
        [mapped_factors[:, :, :narrow].reshape(seq_local, row_count * narrow), live_bf], axis=1
    )
    right_pack = jnp.concatenate(
        [mapped_factors[:, :, narrow:].reshape(seq_local, row_count * narrow), live_bf], axis=1
    )
    left_all = gather_plane(left_pack, count).reshape(count * seq_local, -1)
    right_all = gather_turned(right_pack, count).reshape(count * seq_local, -1)
    wide = row_count * narrow
    live_all, live_cols = left_all[:, wide:], right_all[:, wide:]
    total_seqs = count * seq_local
    products = jnp.einsum(
        "sic,sjd->ijcd",
        left_all[:, :wide].reshape(total_seqs, row_count, narrow),
        right_all[:, :wide].reshape(total_seqs, col_count, narrow),
        preferred_element_type=jnp.float32,
    )
    counts = jnp.dot(live_all.T, live_cols, preferred_element_type=jnp.float32)
    flattened = products.astype(jnp.bfloat16).reshape(row_count * col_count, narrow * narrow)
    outer_sum = jnp.dot(
        flattened, outer_pair_projection, preferred_element_type=jnp.float32
    ).reshape(row_count, col_count, channels)
    outer_mean = outer_sum / jnp.maximum(counts, 1.0)[:, :, None]
    row_pos = row_start + jnp.arange(row_count, dtype=jnp.int32)
    col_pos = col_start + jnp.arange(col_count, dtype=jnp.int32)
    offsets = jnp.clip(col_pos[None, :] - row_pos[:, None] + RELMAX, 0, 2 * RELMAX)
    chain_rows = lax.dynamic_slice_in_dim(residue_chain_index, row_start, row_count)
    chain_cols = lax.dynamic_slice_in_dim(residue_chain_index, col_start, col_count)
    same_chain = chain_rows[:, None] == chain_cols[None, :]
    bin_index = jnp.where(same_chain, offsets, 2 * RELMAX + 1)
    one_hot = (
        bin_index[:, :, None] == jnp.arange(relative_position_table.shape[0], dtype=jnp.int32)
    ).astype(jnp.bfloat16)
    embedded = jnp.einsum(
        "ijb,bc->ijc", one_hot, relative_position_table, preferred_element_type=jnp.float32
    )
    updated = (pair_features.astype(jnp.float32) + embedded + outer_mean).astype(jnp.bfloat16)
    normed_pair = apply_layer_norm(
        updated.astype(jnp.float32), pair_norm_gain, pair_norm_bias
    ).astype(jnp.bfloat16)
    mixture = jnp.dot(
        normed_pair.reshape(row_count * col_count, channels),
        triangle_projection_weights,
        preferred_element_type=jnp.float32,
    )
    mixture = mixture.reshape(row_count, col_count, 5 * channels) + triangle_projection_biases
    pair_live = (row_live[:, None] * col_live[None, :])[:, :, None]
    left_edge = (
        jax.nn.sigmoid(mixture[:, :, :channels])
        * mixture[:, :, channels : 2 * channels]
        * pair_live
    ).astype(jnp.bfloat16)
    right_edge = (
        jax.nn.sigmoid(mixture[:, :, 2 * channels : 3 * channels])
        * mixture[:, :, 3 * channels : 4 * channels]
        * pair_live
    ).astype(jnp.bfloat16)
    gating = jax.nn.sigmoid(mixture[:, :, 4 * channels :])
    devices = lax.axis_size(GROUP)
    if channels % (8 * devices) == 0:
        share = channels // devices
        edges = jnp.stack([left_edge, right_edge]).reshape(
            2, row_count * col_count, devices, share
        ).transpose(2, 0, 3, 1)
        edges = lax.all_to_all(edges, GROUP, 0, 0, tiled=True)
        edges = edges.reshape(count, count, 2, share, row_count, col_count)
        edges = edges.transpose(2, 3, 0, 4, 1, 5).reshape(
            2, share, count * row_count, count * col_count
        )
        sums = jnp.einsum("cik,cjk->cij", edges[0], edges[1], preferred_element_type=jnp.float32)
        sums = sums.astype(jnp.bfloat16).reshape(share, count, row_count, count, col_count)
        sums = sums.transpose(1, 3, 0, 2, 4).reshape(devices, share, row_count * col_count)
        sums = lax.all_to_all(sums, GROUP, 0, 0, tiled=True)
        triangle = sums.reshape(channels, row_count, col_count).transpose(1, 2, 0).astype(jnp.float32)
    else:
        left_panel = gather_plane(left_edge, count)
        right_match = gather_turned(right_edge, count)
        triangle = jnp.einsum(
            "bikc,bjkc->ijc", left_panel, right_match, preferred_element_type=jnp.float32
        )
    normed_tri = apply_layer_norm(triangle, triangle_sum_norm_gain, triangle_sum_norm_bias).astype(
        jnp.bfloat16
    )
    result = jnp.dot(
        normed_tri.reshape(row_count * col_count, channels),
        triangle_output_weight,
        preferred_element_type=jnp.float32,
    )
    result = result.reshape(row_count, col_count, channels) + outer_pair_bias
    return (updated.astype(jnp.float32) + gating * result).astype(jnp.bfloat16)


def solution(mesh):
    placed = (
        P(("groups", "resj", "seq"), "resi", None),
        P(("groups", "resj", "seq"), "resi"),
        P(("groups", "resi"), ("resj", "seq"), None),
        P("groups"),
        P("groups"),
        P(),
        P(),
        P(),
        P(),
        P(),
        P(),
        P(),
        P(),
        P(),
        P(),
        P(),
        P(),
        P(),
        P(),
    )
    return jax.shard_map(
        body,
        mesh=mesh,
        in_specs=placed,
        out_specs=P(("groups", "resi"), ("resj", "seq"), None),
        check_vma=False,
    )
```

```python
import functools

import jax
import jax.numpy as jnp
from jax import lax
from jax.experimental import pallas as pl
from jax.experimental.pallas import tpu as pltpu
from jax.sharding import PartitionSpec as P

RELMAX = 32
LANES = 128
PLANE = ("resj", "seq")
GROUP = ("resi", "resj", "seq")
F32 = jnp.float32
BF16 = jnp.bfloat16
MIB = 1 << 20


def iota(shape, axis):
    return lax.broadcasted_iota(jnp.int32, shape, axis)


def dot(a, b):
    return jnp.dot(a, b, preferred_element_type=F32)


def sigmoid(v):
    return 0.5 * jnp.tanh(0.5 * v) + 0.5


def layer_norm(values, gain, shift):
    average = jnp.mean(values, axis=-1, keepdims=True)
    centred = values - average
    variance = jnp.mean(centred * centred, axis=-1, keepdims=True)
    return centred * lax.rsqrt(variance + 1e-05) * gain + shift


def pack_kernel(x_ref, mask_ref, res_ref, gain_ref, shift_ref, w_ref, bias_ref,
                left_ref, right_ref, lscr, rscr):
    seqs, rows, depth = x_ref.shape
    half = w_ref.shape[1] // 2
    per = LANES // half
    row_start = lax.axis_index("resi") * rows
    x = x_ref[...].reshape(seqs * rows, depth).astype(F32)
    normed = layer_norm(x, gain_ref[...], shift_ref[...]).astype(BF16)
    lane = iota((2 * half, 2 * LANES), 1)
    spread = lane % half + jnp.where(lane >= LANES, half, 0) == iota((2 * half, 2 * LANES), 0)
    spread = spread.astype(F32)
    wide = dot(w_ref[...], spread.astype(BF16)).astype(BF16)
    bias = jnp.dot(jnp.broadcast_to(bias_ref[...], (8, 2 * half)), spread,
                   precision=lax.Precision.HIGHEST, preferred_element_type=F32)[0:1]
    mapped = dot(normed, wide)
    lscr[...] = mapped[:, :LANES]
    rscr[...] = mapped[:, LANES:]
    total = res_ref.shape[1]
    pick = (iota((total, rows), 0) == iota((total, rows), 1) + row_start).astype(BF16)
    row_live = dot(jnp.broadcast_to(res_ref[...].astype(F32), (8, total)).astype(BF16), pick)[0:1]
    live = (mask_ref[...].astype(F32) * row_live).astype(BF16)
    width = rows * half
    spread_live = (iota((rows, width), 1) // half == iota((rows, width), 0)).astype(BF16)
    live_wide = dot(live, spread_live)
    sub = iota((seqs, LANES), 1) // half
    for tile in range(width // LANES):
        at = slice(tile * LANES, (tile + 1) * LANES)
        for scr, ref, first in ((lscr, left_ref, 0), (rscr, right_ref, LANES)):
            value = scr[pl.ds(tile * per, seqs, stride=rows), :]
            for k in range(1, per):
                value = jnp.where(sub == k, scr[pl.ds(tile * per + k, seqs, stride=rows), :], value)
            value = (value + bias[:, first:first + LANES]) * live_wide[:, at]
            ref[:, at] = value.astype(BF16)
    live_tile = dot(live, (iota((rows, LANES), 0) == iota((rows, LANES), 1)).astype(BF16))
    left_ref[:, width:] = live_tile.astype(BF16)
    right_ref[:, width:] = live_tile.astype(BF16)


def base_kernel(pair_ref, table_ref, chain_ref, chain_smem, w_ref, base_ref, block_ref, tscr, wscr):
    rows, cols, channels = pair_ref.shape
    total = chain_ref.shape[1]
    row_start = lax.axis_index("resi") * rows
    col_start = lax.axis_index(PLANE) * cols
    tscr[...] = jnp.zeros_like(tscr)
    tscr[0:table_ref.shape[0], :] = table_ref[...].astype(F32)
    table = tscr[...].astype(BF16)
    own = iota((cols, total), 1) == iota((cols, total), 0) + col_start
    chain_cols = jnp.sum(
        jnp.where(own, jnp.broadcast_to(chain_ref[...], (cols, total)).astype(F32), 0.0),
        axis=1, keepdims=True)
    col_pos = iota((cols, 1), 0) + col_start
    for i in range(rows):
        offset = jnp.clip(col_pos - (row_start + i) + RELMAX, 0, 2 * RELMAX)
        same = chain_cols == chain_smem[row_start + i].astype(F32)
        bins = jnp.where(same, offset, 2 * RELMAX + 1)
        one_hot = (iota((cols, LANES), 1) == bins).astype(F32).astype(BF16)
        base_ref[i] = pair_ref[i].astype(F32) + dot(one_hot, table)
    wscr[...] = w_ref[...].astype(F32)
    half = int(round(w_ref.shape[0] ** 0.5))
    per = LANES // half
    block_ref[...] = jnp.zeros_like(block_ref)
    for d in range(half):
        value = wscr[pl.ds(d, half, stride=half), :].astype(BF16)
        for k in range(per):
            block_ref[pl.ds(d * LANES + k * half, half), k * channels:(k + 1) * channels] = value


def edges_kernel(count, *refs):
    lefts, rights = refs[:count], refs[count:2 * count]
    (base_ref, block_ref, res_ref, res_smem, gain_ref, shift_ref, w_ref, bias_ref,
     updated_ref, left_ref, right_ref, gate_ref,
     lall, rall, tscr, rscr, oscr, nscr, escr) = refs[2 * count:]
    rows, cols, channels = base_ref.shape
    seqs = lefts[0].shape[0]
    half = block_ref.shape[0] // LANES
    per = LANES // half
    width = rows * half
    total_seqs = count * seqs
    z = lax.axis_index("resi")
    q = lax.axis_index(PLANE)
    row_start, col_start = z * rows, q * cols
    for step in range(count):
        lall[q ^ step] = lefts[step][...]
        rall[z ^ step] = rights[step][...]
    right = rall[...].reshape(total_seqs, -1)
    left = lall[...].reshape(total_seqs, -1)
    for at in range(0, width, LANES):
        for s in range(0, total_seqs, LANES):
            tscr[s // LANES, at:at + LANES, :] = right[s:s + LANES, at:at + LANES].astype(F32).T
    for d in range(half):
        for s in range(0, total_seqs, LANES):
            turned = tscr[s // LANES, pl.ds(d, cols, stride=half), :]
            rscr[d * cols:(d + 1) * cols, s:s + LANES] = turned.astype(BF16)
    live_cols = right[:, width:].astype(F32).T[0:cols].astype(BF16)
    counts = dot(live_cols, left[:, width:])
    inverse = 1.0 / jnp.maximum(counts, 1.0)
    wide = 2 * LANES
    tall = 8
    for first in range(0, width, wide):
        for d0 in range(0, half, tall):
            product = dot(rscr[d0 * cols:(d0 + tall) * cols, :], left[:, first:first + wide])
            product = product.astype(BF16)
            for dd in range(tall):
                for t in range(wide // LANES):
                    g = first // LANES + t
                    oscr[g * cols:(g + 1) * cols, (d0 + dd) * LANES:(d0 + dd + 1) * LANES] = (
                        product[dd * cols:(dd + 1) * cols, t * LANES:(t + 1) * LANES])
    outer = dot(oscr[...], block_ref[...])
    for i in range(rows):
        g, k = i // per, i % per
        part = outer[g * cols:(g + 1) * cols, k * channels:(k + 1) * channels]
        updated = (base_ref[i] + part * inverse[:, i:i + 1]).astype(BF16)
        updated_ref[i] = updated
        normed = layer_norm(updated.astype(F32), gain_ref[...], shift_ref[...])
        nscr[i * cols:(i + 1) * cols, :] = normed.astype(BF16)
    total = res_ref.shape[1]
    own = iota((cols, total), 1) == iota((cols, total), 0) + col_start
    col_live = jnp.sum(
        jnp.where(own, jnp.broadcast_to(res_ref[...], (cols, total)).astype(F32), 0.0),
        axis=1, keepdims=True)
    col_live = jnp.broadcast_to(col_live, (cols, channels))
    chunk = 8
    for i0 in range(0, rows, chunk):
        mixture = dot(nscr[i0 * cols:(i0 + chunk) * cols, :], w_ref[...]) + bias_ref[...]
        part = [mixture[:, n * channels:(n + 1) * channels] for n in range(5)]
        left_edge = sigmoid(part[0]) * part[1]
        right_edge = sigmoid(part[2]) * part[3]
        gate_ref[i0 * cols:(i0 + chunk) * cols, :] = sigmoid(part[4])
        for ii in range(chunk):
            live = col_live * res_smem[row_start + i0 + ii].astype(F32)
            at = slice(ii * cols, (ii + 1) * cols)
            left_ref[i0 + ii] = (left_edge[at] * live).astype(BF16)
            escr[(i0 + ii) * cols:(i0 + ii + 1) * cols, :] = right_edge[at] * live
    for k in range(cols):
        right_ref[k] = escr[pl.ds(k, rows, stride=cols), :].astype(BF16)


def triangle_kernel(count, *refs):
    lefts, rights = refs[:count], refs[count:2 * count]
    (updated_ref, gate_ref, gain_ref, shift_ref, w_ref, bias_ref,
     out_ref, lscr, rscr, acc) = refs[2 * count:]
    rows, depth, channels = lefts[0].shape
    cols = rights[0].shape[1]
    turn = lax.axis_index("resi") ^ lax.axis_index(PLANE)
    for step in range(count):
        lscr[step] = lefts[step][...].astype(F32).reshape(rows * depth, channels)
        rscr[step] = rights[step][...].astype(F32).reshape(depth * cols, channels)
    block = 4
    tiles = cols // 8

    def rows_body(at, carry):
        sums = [[jnp.zeros((8, channels), F32) for _ in range(tiles)] for _ in range(block)]

        def step_body(step, sums):
            own = step ^ turn
            for k in range(depth):
                column = [rscr[step, k * cols + t * 8:k * cols + t * 8 + 8, :] for t in range(tiles)]
                for b in range(block):
                    row = lscr[own, pl.ds((at * block + b) * depth + k, 1), :]
                    for t in range(tiles):
                        sums[b][t] = sums[b][t] + row * column[t]
            return sums

        sums = lax.fori_loop(0, count, step_body, sums)
        for b in range(block):
            for t in range(tiles):
                acc[pl.ds(pl.multiple_of((at * block + b) * cols + t * 8, 8), 8), :] = sums[b][t]
        return carry

    lax.fori_loop(0, rows // block, rows_body, 0)
    chunk = 8
    for i0 in range(0, rows, chunk):
        at = slice(i0 * cols, (i0 + chunk) * cols)
        normed = layer_norm(acc[at, :], gain_ref[...], shift_ref[...]).astype(BF16)
        result = dot(normed, w_ref[...]) + bias_ref[...]
        updated = updated_ref[i0:i0 + chunk].reshape(chunk * cols, channels).astype(F32)
        value = updated + gate_ref[at, :] * result
        out_ref[i0:i0 + chunk] = value.astype(BF16).reshape(chunk, cols, channels)


def send_plane(block, count):
    return [block] + [
        lax.ppermute(block, PLANE, [(p, p ^ m) for p in range(count)]) for m in range(1, count)
    ]


def send_turned(block, count):
    return [
        lax.ppermute(
            block, GROUP,
            [(z * count + p, (p ^ m) * count + z) for z in range(count) for p in range(count)])
        for m in range(count)
    ]


def call(kernel, outs, scratch, args, smem=(), flops=0, name=None):
    vmem = pl.BlockSpec(memory_space=pltpu.VMEM)
    specs = [pl.BlockSpec(memory_space=pltpu.SMEM) if n in smem else vmem for n in range(len(args))]
    size = sum(a.size * a.dtype.itemsize for a in args)
    return pl.pallas_call(
        kernel,
        out_shape=outs,
        in_specs=specs,
        out_specs=[vmem] * len(outs) if isinstance(outs, list) else vmem,
        scratch_shapes=scratch,
        compiler_params=pltpu.CompilerParams(vmem_limit_bytes=40 * MIB),
        cost_estimate=pl.CostEstimate(flops=flops, bytes_accessed=size, transcendentals=0),
        name=name,
    )(*args)


def body(
    homolog_matrix,
    sequence_pad_mask,
    pair_features,
    residue_pad_mask,
    residue_chain_index,
    homolog_standard_factor,
    homolog_standard_offset,
    factor_mapping_matrices,
    outer_side_biases,
    outer_pair_projection,
    relative_position_table,
    pair_norm_gain,
    pair_norm_bias,
    triangle_projection_weights,
    triangle_projection_biases,
    triangle_sum_norm_gain,
    triangle_sum_norm_bias,
    triangle_output_weight,
    outer_pair_bias,
):
    rows, cols, channels = pair_features.shape
    seqs, _, depth = homolog_matrix.shape
    half = factor_mapping_matrices.shape[1] // 2
    per = LANES // half
    count = lax.axis_size(PLANE)
    width = rows * half
    flat = lambda v: v.reshape(1, -1)
    shape = jax.ShapeDtypeStruct
    residue = flat(residue_pad_mask)
    chain = flat(residue_chain_index)
    pack = shape((seqs, width + LANES), BF16)
    left, right = call(
        pack_kernel, [pack, pack],
        [pltpu.VMEM((seqs * rows, LANES), F32)] * 2,
        [homolog_matrix, sequence_pad_mask, residue, flat(homolog_standard_factor),
         flat(homolog_standard_offset), factor_mapping_matrices, flat(outer_side_biases)],
        name="pack")
    rights = send_turned(right, count)
    lefts = send_plane(left, count)
    base, block = call(
        base_kernel,
        [shape((rows, cols, channels), F32), shape((half * LANES, per * channels), BF16)],
        [pltpu.VMEM((LANES, channels), F32), pltpu.VMEM((half * half, channels), F32)],
        [pair_features, relative_position_table, chain, residue_chain_index, outer_pair_projection],
        smem=(3,), flops=1 << 30, name="base")
    updated, left_edge, right_edge, gate = call(
        functools.partial(edges_kernel, count),
        [shape((rows, cols, channels), BF16), shape((rows, cols, channels), BF16),
         shape((cols, rows, channels), BF16), shape((rows * cols, channels), F32)],
        [pltpu.VMEM((count, seqs, width + LANES), BF16), pltpu.VMEM((count, seqs, width + LANES), BF16),
         pltpu.VMEM((count * seqs // LANES, width, LANES), F32),
         pltpu.VMEM((width, count * seqs), BF16),
         pltpu.VMEM((rows // per * cols, half * LANES), BF16),
         pltpu.VMEM((rows * cols, channels), BF16), pltpu.VMEM((rows * cols, channels), F32)],
        lefts + rights + [base, block, residue, residue_pad_mask, flat(pair_norm_gain),
                          flat(pair_norm_bias), triangle_projection_weights,
                          flat(triangle_projection_biases)],
        smem=(2 * count + 3,), name="edges")
    right_edges = send_turned(right_edge, count)
    left_edges = send_plane(left_edge, count)
    return call(
        functools.partial(triangle_kernel, count),
        shape((rows, cols, channels), BF16),
        [pltpu.VMEM((count, rows * cols, channels), F32), pltpu.VMEM((count, rows * cols, channels), F32),
         pltpu.VMEM((rows * cols, channels), F32)],
        left_edges + right_edges + [updated, gate, flat(triangle_sum_norm_gain),
                                    flat(triangle_sum_norm_bias), triangle_output_weight,
                                    flat(outer_pair_bias)],
        name="triangle")


def solution(mesh):
    pair = P(("groups", "resi"), ("resj", "seq"), None)
    placed = (
        P(("groups", "resj", "seq"), "resi", None),
        P(("groups", "resj", "seq"), "resi"),
        pair,
        P("groups"),
        P("groups"),
    ) + (P(),) * 14
    return jax.shard_map(body, mesh=mesh, in_specs=placed, out_specs=pair, check_vma=False)
```

```python
import functools

import jax
import jax.numpy as jnp
from jax import lax
from jax.experimental import pallas as pl
from jax.experimental.pallas import tpu as pltpu
from jax.sharding import PartitionSpec as P

RELMAX = 32
LANES = 128
PLANE = ("resj", "seq")
GROUP = ("resi", "resj", "seq")
F32 = jnp.float32
BF16 = jnp.bfloat16
MIB = 1 << 20


def iota(shape, axis):
    return lax.broadcasted_iota(jnp.int32, shape, axis)


def dot(a, b):
    return jnp.dot(a, b, preferred_element_type=F32)


def sigmoid(v):
    return 0.5 * jnp.tanh(0.5 * v) + 0.5


def layer_norm(values, gain, shift):
    average = jnp.mean(values, axis=-1, keepdims=True)
    centred = values - average
    variance = jnp.mean(centred * centred, axis=-1, keepdims=True)
    return centred * lax.rsqrt(variance + 1e-05) * gain + shift


def norm_kernel(x_ref, out_ref):
    x = x_ref[...].reshape(out_ref.shape).astype(F32)
    out_ref[...] = layer_norm(x, 1.0, 0.0)


def pack_kernel(x_ref, mask_ref, res_ref, gain_ref, shift_ref, w_ref, bias_ref,
                left_ref, right_ref, lscr, rscr):
    seqs, rows = mask_ref.shape
    half = w_ref.shape[0] // 2
    per = LANES // half
    row_start = lax.axis_index("resi") * rows
    normed = (x_ref[...] * gain_ref[...] + shift_ref[...]).astype(BF16)
    lane = iota((2 * half, 2 * LANES), 1)
    spread = lane % half + jnp.where(lane >= LANES, half, 0) == iota((2 * half, 2 * LANES), 0)
    spread = spread.astype(F32)
    wide = lax.dot_general(
        w_ref[...], spread.astype(BF16), (((0,), (0,)), ((), ())), preferred_element_type=F32)
    wide = wide.astype(BF16)
    bias = jnp.dot(jnp.broadcast_to(bias_ref[...], (8, 2 * half)), spread,
                   precision=lax.Precision.HIGHEST, preferred_element_type=F32)[0:1]
    mapped = dot(normed, wide)
    lscr[...] = mapped[:, :LANES]
    rscr[...] = mapped[:, LANES:]
    row_live = pick_rows(res_ref[...], row_start, rows)
    live = (mask_ref[...].astype(F32) * row_live).astype(BF16)
    width = rows * half
    spread_live = (iota((rows, width), 1) // half == iota((rows, width), 0)).astype(BF16)
    live_wide = dot(live, spread_live)
    sub = iota((seqs, LANES), 1) // half
    for tile in range(width // LANES):
        at = slice(tile * LANES, (tile + 1) * LANES)
        for scr, ref, first in ((lscr, left_ref, 0), (rscr, right_ref, LANES)):
            value = scr[pl.ds(tile * per, seqs, stride=rows), :]
            for k in range(1, per):
                value = jnp.where(sub == k, scr[pl.ds(tile * per + k, seqs, stride=rows), :], value)
            value = (value + bias[:, first:first + LANES]) * live_wide[:, at]
            ref[:, at] = value.astype(BF16)
    live_tile = dot(live, (iota((rows, LANES), 0) == iota((rows, LANES), 1)).astype(BF16))
    left_ref[:, width:] = live_tile.astype(BF16)
    right_ref[:, width:] = live_tile.astype(BF16)


def pick_columns(values, start, size):
    total = values.shape[1]
    own = iota((size, total), 1) == iota((size, total), 0) + start
    spread = jnp.broadcast_to(values, (size, total)).astype(F32)
    return jnp.sum(jnp.where(own, spread, 0.0), axis=1, keepdims=True)


def pick_rows(values, start, size):
    total = values.shape[1]
    pick = (iota((total, size), 0) == iota((total, size), 1) + start).astype(BF16)
    return dot(jnp.broadcast_to(values.astype(F32), (8, total)).astype(BF16), pick)[0:1]


def base_kernel(pair_ref, table_ref, chain_ref, w_ref, base_ref, block_ref, tscr, wscr):
    rows, cols, channels = pair_ref.shape
    row_start = lax.axis_index("resi") * rows
    col_start = lax.axis_index(PLANE) * cols
    tscr[...] = jnp.zeros_like(tscr)
    tscr[0:table_ref.shape[0], :] = table_ref[...].astype(F32)
    table = tscr[...].astype(BF16)
    chain = chain_ref[...]
    same = pick_columns(chain, col_start, cols) == pick_rows(chain, row_start, rows)
    offset = iota((cols, rows), 0) + col_start - iota((cols, rows), 1) - row_start + RELMAX
    bins = jnp.where(same, jnp.clip(offset, 0, 2 * RELMAX), 2 * RELMAX + 1)
    lane = iota((cols, LANES), 1)
    for i in range(rows):
        one_hot = (lane == bins[:, i:i + 1]).astype(F32).astype(BF16)
        base_ref[i] = pair_ref[i].astype(F32) + dot(one_hot, table)
    wscr[...] = w_ref[...].astype(F32)
    half = int(round(w_ref.shape[0] ** 0.5))
    per = LANES // half
    block_ref[...] = jnp.zeros_like(block_ref)
    for d in range(half):
        value = wscr[pl.ds(d, half, stride=half), :].astype(BF16)
        for k in range(per):
            block_ref[pl.ds(d * LANES + k * half, half), k * channels:(k + 1) * channels] = value


def edges_kernel(count, *refs):
    lefts, rights = refs[:count], refs[count:2 * count]
    (base_ref, block_ref, res_ref, gain_ref, shift_ref, w_ref, bias_ref,
     updated_ref, left_ref, right_ref, gate_ref,
     lall, rall, tscr, rscr, oscr, nscr, escr) = refs[2 * count:]
    rows, cols, channels = base_ref.shape
    seqs = lefts[0].shape[0]
    half = block_ref.shape[0] // LANES
    per = LANES // half
    width = rows * half
    total_seqs = count * seqs
    z = lax.axis_index("resi")
    q = lax.axis_index(PLANE)
    row_start, col_start = z * rows, q * cols
    for step in range(count):
        lall[q ^ step] = lefts[step][...]
        rall[z ^ step] = rights[step][...]
    right = rall[...].reshape(total_seqs, -1)
    left = lall[...].reshape(total_seqs, -1)
    for at in range(0, width, LANES):
        for s in range(0, total_seqs, LANES):
            tscr[s // LANES, at:at + LANES, :] = right[s:s + LANES, at:at + LANES].astype(F32).T
    for d in range(half):
        for s in range(0, total_seqs, LANES):
            turned = tscr[s // LANES, pl.ds(d, cols, stride=half), :]
            rscr[d * cols:(d + 1) * cols, s:s + LANES] = turned.astype(BF16)
    live_cols = right[:, width:].astype(F32).T[0:cols].astype(BF16)
    counts = dot(live_cols, left[:, width:])
    inverse = 1.0 / jnp.maximum(counts, 1.0)
    wide = 2 * LANES
    tall = 8
    for first in range(0, width, wide):
        for d0 in range(0, half, tall):
            product = dot(rscr[d0 * cols:(d0 + tall) * cols, :], left[:, first:first + wide])
            product = product.astype(BF16)
            for dd in range(tall):
                for t in range(wide // LANES):
                    g = first // LANES + t
                    oscr[g * cols:(g + 1) * cols, (d0 + dd) * LANES:(d0 + dd + 1) * LANES] = (
                        product[dd * cols:(dd + 1) * cols, t * LANES:(t + 1) * LANES])
    outer = dot(oscr[...], block_ref[...])
    for i in range(rows):
        g, k = i // per, i % per
        part = outer[g * cols:(g + 1) * cols, k * channels:(k + 1) * channels]
        updated = (base_ref[i] + part * inverse[:, i:i + 1]).astype(BF16)
        updated_ref[i] = updated
        normed = layer_norm(updated.astype(F32), gain_ref[...], shift_ref[...])
        nscr[i * cols:(i + 1) * cols, :] = normed.astype(BF16)
    live = pick_columns(res_ref[...], col_start, cols) * pick_rows(res_ref[...], row_start, rows)
    chunk = 8
    for i0 in range(0, rows, chunk):
        mixture = dot(nscr[i0 * cols:(i0 + chunk) * cols, :], w_ref[...]) + bias_ref[...]
        part = [mixture[:, n * channels:(n + 1) * channels] for n in range(5)]
        left_edge = sigmoid(part[0]) * part[1]
        right_edge = sigmoid(part[2]) * part[3]
        gate_ref[i0 * cols:(i0 + chunk) * cols, :] = sigmoid(part[4])
        for ii in range(chunk):
            here = live[:, i0 + ii:i0 + ii + 1]
            at = slice(ii * cols, (ii + 1) * cols)
            left_ref[i0 + ii] = (left_edge[at] * here).astype(BF16)
            escr[(i0 + ii) * cols:(i0 + ii + 1) * cols, :] = right_edge[at] * here
    for k in range(cols):
        right_ref[k] = escr[pl.ds(k, rows, stride=cols), :].astype(BF16)


def panel_kernel(count, *refs):
    lefts, panel_ref = refs[:count], refs[count]
    q = lax.axis_index(PLANE)
    for step in range(count):
        panel_ref[q ^ step] = lefts[step][...].astype(F32).reshape(panel_ref.shape[1:])


def add_block(step, panel_ref, right_ref, rscr, before, store):
    depth, cols, channels = right_ref.shape
    rows = panel_ref.shape[1] // depth
    own = lax.axis_index("resi") ^ step
    rscr[...] = right_ref[...].astype(F32).reshape(rscr.shape)
    block = 4
    tiles = cols // 8

    def rows_body(at, carry):
        place = [[pl.ds(pl.multiple_of((at * block + b) * cols + t * 8, 8), 8) for t in range(tiles)]
                 for b in range(block)]
        if before is None:
            sums = [[jnp.zeros((8, channels), F32) for _ in range(tiles)] for _ in range(block)]
        else:
            sums = [[before[place[b][t], :] for t in range(tiles)] for b in range(block)]
        for k in range(depth):
            column = [rscr[k * cols + t * 8:k * cols + t * 8 + 8, :] for t in range(tiles)]
            for b in range(block):
                row = panel_ref[own, pl.ds((at * block + b) * depth + k, 1), :]
                for t in range(tiles):
                    sums[b][t] = sums[b][t] + row * column[t]
        for b in range(block):
            for t in range(tiles):
                store[place[b][t], :] = sums[b][t]
        return carry

    lax.fori_loop(0, rows // block, rows_body, 0)


def step_kernel(step, panel_ref, right_ref, *refs):
    before = refs[0] if len(refs) == 3 else None
    add_block(step, panel_ref, right_ref, refs[-1], before, refs[-2])


def final_kernel(step, panel_ref, right_ref, before, updated_ref, gate_ref, gain_ref, shift_ref,
                 w_ref, bias_ref, out_ref, acc, rscr):
    add_block(step, panel_ref, right_ref, rscr, before, acc)
    rows, cols, channels = out_ref.shape
    chunk = 8
    for i0 in range(0, rows, chunk):
        at = slice(i0 * cols, (i0 + chunk) * cols)
        normed = layer_norm(acc[at, :], gain_ref[...], shift_ref[...]).astype(BF16)
        result = dot(normed, w_ref[...]) + bias_ref[...]
        updated = updated_ref[i0:i0 + chunk].reshape(chunk * cols, channels).astype(F32)
        value = updated + gate_ref[at, :] * result
        out_ref[i0:i0 + chunk] = value.astype(BF16).reshape(chunk, cols, channels)


def send_plane(block, count):
    parts, bit = [block], 1
    while bit < count:
        pairs = [(p, p ^ bit) for p in range(count)]
        parts += [lax.ppermute(part, PLANE, pairs) for part in parts]
        bit *= 2
    return parts


def send_turned(block, count):
    return [
        lax.ppermute(
            block, GROUP,
            [(z * count + p, (p ^ m) * count + z) for z in range(count) for p in range(count)])
        for m in range(count)
    ]


def call(kernel, outs, scratch, args, flops=0, name=None):
    vmem = pl.BlockSpec(memory_space=pltpu.VMEM)
    size = sum(a.size * a.dtype.itemsize for a in args)
    return pl.pallas_call(
        kernel,
        out_shape=outs,
        in_specs=[vmem] * len(args),
        out_specs=[vmem] * len(outs) if isinstance(outs, list) else vmem,
        scratch_shapes=scratch,
        compiler_params=pltpu.CompilerParams(vmem_limit_bytes=40 * MIB),
        cost_estimate=pl.CostEstimate(flops=flops, bytes_accessed=size, transcendentals=0),
        name=name,
    )(*args)


def body(
    homolog_matrix,
    sequence_pad_mask,
    pair_features,
    residue_pad_mask,
    residue_chain_index,
    homolog_standard_factor,
    homolog_standard_offset,
    factor_mapping_matrices,
    outer_side_biases,
    outer_pair_projection,
    relative_position_table,
    pair_norm_gain,
    pair_norm_bias,
    triangle_projection_weights,
    triangle_projection_biases,
    triangle_sum_norm_gain,
    triangle_sum_norm_bias,
    triangle_output_weight,
    outer_pair_bias,
):
    rows, cols, channels = pair_features.shape
    seqs, _, depth = homolog_matrix.shape
    half = factor_mapping_matrices.shape[1] // 2
    per = LANES // half
    count = lax.axis_size(PLANE)
    width = rows * half
    flat = lambda v: v.reshape(1, -1)
    shape = jax.ShapeDtypeStruct
    residue = flat(residue_pad_mask)
    chain = flat(residue_chain_index)
    pack = shape((seqs, width + LANES), BF16)
    normed = call(norm_kernel, shape((seqs * rows, depth), F32), [], [homolog_matrix],
                  flops=1 << 36, name="norm")
    left, right = call(
        pack_kernel, [pack, pack],
        [pltpu.VMEM((seqs * rows, LANES), F32)] * 2,
        [normed, sequence_pad_mask, residue, flat(homolog_standard_factor),
         flat(homolog_standard_offset), factor_mapping_matrices.T, flat(outer_side_biases)],
        flops=1 << 30, name="pack")
    rights = send_turned(right, count)
    lefts = send_plane(left, count)
    base, block = call(
        base_kernel,
        [shape((rows, cols, channels), F32), shape((half * LANES, per * channels), BF16)],
        [pltpu.VMEM((LANES, channels), F32), pltpu.VMEM((half * half, channels), F32)],
        [pair_features, relative_position_table, chain, outer_pair_projection],
        flops=1 << 30, name="base")
    updated, left_edge, right_edge, gate = call(
        functools.partial(edges_kernel, count),
        [shape((rows, cols, channels), BF16), shape((rows, cols, channels), BF16),
         shape((cols, rows, channels), BF16), shape((rows * cols, channels), F32)],
        [pltpu.VMEM((count, seqs, width + LANES), BF16), pltpu.VMEM((count, seqs, width + LANES), BF16),
         pltpu.VMEM((count * seqs // LANES, width, LANES), F32),
         pltpu.VMEM((width, count * seqs), BF16),
         pltpu.VMEM((rows // per * cols, half * LANES), BF16),
         pltpu.VMEM((rows * cols, channels), BF16), pltpu.VMEM((rows * cols, channels), F32)],
        lefts + rights + [base, block, residue, flat(pair_norm_gain), flat(pair_norm_bias),
                          triangle_projection_weights, flat(triangle_projection_biases)],
        name="edges")
    right_edges = send_turned(right_edge, count)
    left_edges = send_plane(left_edge, count)
    sums = shape((rows * cols, channels), F32)
    turned = pltpu.VMEM((rows * cols, channels), F32)
    panel = call(
        functools.partial(panel_kernel, count), shape((count, rows * cols, channels), F32), [],
        left_edges, name="panel")
    args = []
    for step in range(count - 1):
        args = [call(functools.partial(step_kernel, step), sums, [turned],
                     [panel, right_edges[step]] + args, name="triangle")]
    return call(
        functools.partial(final_kernel, count - 1), shape((rows, cols, channels), BF16),
        [turned, turned],
        [panel, right_edges[-1]] + args + [
            updated, gate, flat(triangle_sum_norm_gain), flat(triangle_sum_norm_bias),
            triangle_output_weight, flat(outer_pair_bias)],
        name="final")


def solution(mesh):
    pair = P(("groups", "resi"), ("resj", "seq"), None)
    placed = (
        P(("groups", "resj", "seq"), "resi", None),
        P(("groups", "resj", "seq"), "resi"),
        pair,
        P("groups"),
        P("groups"),
    ) + (P(),) * 14
    return jax.shard_map(body, mesh=mesh, in_specs=placed, out_specs=pair, check_vma=False)
```

```python
import functools

import jax
import jax.numpy as jnp
from jax import lax
from jax.experimental import pallas as pl
from jax.experimental.pallas import tpu as pltpu
from jax.sharding import PartitionSpec as P

RELMAX = 32
LANES = 128
PLANE = ("resj", "seq")
GROUP = ("resi", "resj", "seq")
F32 = jnp.float32
BF16 = jnp.bfloat16
MIB = 1 << 20


def iota(shape, axis):
    return lax.broadcasted_iota(jnp.int32, shape, axis)


def dot(a, b):
    return jnp.dot(a, b, preferred_element_type=F32)


def sigmoid(v):
    return 0.5 * jnp.tanh(0.5 * v) + 0.5


def layer_norm(values, gain, shift):
    average = jnp.mean(values, axis=-1, keepdims=True)
    centred = values - average
    variance = jnp.mean(centred * centred, axis=-1, keepdims=True)
    return centred * lax.rsqrt(variance + 1e-05) * gain + shift


def norm_kernel(x_ref, out_ref):
    x = x_ref[...].reshape(out_ref.shape).astype(F32)
    out_ref[...] = layer_norm(x, 1.0, 0.0)


def pack_kernel(x_ref, mask_ref, res_ref, gain_ref, shift_ref, w_ref, bias_ref,
                left_ref, right_ref, lscr, rscr):
    seqs, rows = mask_ref.shape
    half = w_ref.shape[0] // 2
    per = LANES // half
    row_start = lax.axis_index("resi") * rows
    normed = (x_ref[...] * gain_ref[...] + shift_ref[...]).astype(BF16)
    lane = iota((2 * half, 2 * LANES), 1)
    spread = lane % half + jnp.where(lane >= LANES, half, 0) == iota((2 * half, 2 * LANES), 0)
    spread = spread.astype(F32)
    wide = lax.dot_general(
        w_ref[...], spread.astype(BF16), (((0,), (0,)), ((), ())), preferred_element_type=F32)
    wide = wide.astype(BF16)
    bias = jnp.dot(jnp.broadcast_to(bias_ref[...], (8, 2 * half)), spread,
                   precision=lax.Precision.HIGHEST, preferred_element_type=F32)[0:1]
    mapped = dot(normed, wide)
    lscr[...] = mapped[:, :LANES]
    rscr[...] = mapped[:, LANES:]
    row_live = pick_rows(res_ref[...], row_start, rows)
    live = (mask_ref[...].astype(F32) * row_live).astype(BF16)
    width = rows * half
    spread_live = (iota((rows, width), 1) // half == iota((rows, width), 0)).astype(BF16)
    live_wide = dot(live, spread_live)
    sub = iota((seqs, LANES), 1) // half
    for tile in range(width // LANES):
        at = slice(tile * LANES, (tile + 1) * LANES)
        for scr, ref, first in ((lscr, left_ref, 0), (rscr, right_ref, LANES)):
            value = scr[pl.ds(tile * per, seqs, stride=rows), :]
            for k in range(1, per):
                value = jnp.where(sub == k, scr[pl.ds(tile * per + k, seqs, stride=rows), :], value)
            value = (value + bias[:, first:first + LANES]) * live_wide[:, at]
            ref[:, at] = value.astype(BF16)
    live_tile = dot(live, (iota((rows, LANES), 0) == iota((rows, LANES), 1)).astype(BF16))
    left_ref[:, width:] = live_tile.astype(BF16)
    right_ref[:, width:] = live_tile.astype(BF16)


def pick_columns(values, start, size):
    total = values.shape[1]
    own = iota((size, total), 1) == iota((size, total), 0) + start
    spread = jnp.broadcast_to(values, (size, total)).astype(F32)
    return jnp.sum(jnp.where(own, spread, 0.0), axis=1, keepdims=True)


def pick_rows(values, start, size):
    total = values.shape[1]
    pick = (iota((total, size), 0) == iota((total, size), 1) + start).astype(BF16)
    return dot(jnp.broadcast_to(values.astype(F32), (8, total)).astype(BF16), pick)[0:1]


def base_kernel(pair_ref, table_ref, chain_ref, w_ref, base_ref, block_ref, tscr, wscr):
    rows, cols, channels = pair_ref.shape
    row_start = lax.axis_index("resi") * rows
    col_start = lax.axis_index(PLANE) * cols
    tscr[...] = jnp.zeros_like(tscr)
    tscr[0:table_ref.shape[0], :] = table_ref[...].astype(F32)
    table = tscr[...].astype(BF16)
    chain = chain_ref[...]
    same = pick_columns(chain, col_start, cols) == pick_rows(chain, row_start, rows)
    offset = iota((cols, rows), 0) + col_start - iota((cols, rows), 1) - row_start + RELMAX
    bins = jnp.where(same, jnp.clip(offset, 0, 2 * RELMAX), 2 * RELMAX + 1)
    lane = iota((cols, LANES), 1)
    for i in range(rows):
        one_hot = (lane == bins[:, i:i + 1]).astype(F32).astype(BF16)
        base_ref[i] = pair_ref[i].astype(F32) + dot(one_hot, table)
    wscr[...] = w_ref[...].astype(F32)
    half = int(round(w_ref.shape[0] ** 0.5))
    per = LANES // half
    block_ref[...] = jnp.zeros_like(block_ref)
    for d in range(half):
        value = wscr[pl.ds(d, half, stride=half), :].astype(BF16)
        for k in range(per):
            block_ref[pl.ds(d * LANES + k * half, half), k * channels:(k + 1) * channels] = value


def edges_kernel(count, *refs):
    rights, lefts = refs[:count], refs[count:2 * count]
    (base_ref, block_ref, res_ref, gain_ref, shift_ref, w_ref, bias_ref,
     updated_ref, left_ref, right_ref, gate_ref,
     lall, rall, tscr, rscr, oscr, nscr, escr) = refs[2 * count:]
    rows, cols, channels = base_ref.shape
    seqs = lefts[0].shape[0]
    half = block_ref.shape[0] // LANES
    per = LANES // half
    width = rows * half
    total_seqs = count * seqs
    z = lax.axis_index("resi")
    q = lax.axis_index(PLANE)
    row_start, col_start = z * rows, q * cols
    for step in range(count):
        lall[q ^ step] = lefts[step][...]
        rall[z ^ step] = rights[step][...]
    right = rall[...].reshape(total_seqs, -1)
    left = lall[...].reshape(total_seqs, -1)
    for at in range(0, width, LANES):
        for s in range(0, total_seqs, LANES):
            tscr[s // LANES, at:at + LANES, :] = right[s:s + LANES, at:at + LANES].astype(F32).T
    for d in range(half):
        for s in range(0, total_seqs, LANES):
            turned = tscr[s // LANES, pl.ds(d, cols, stride=half), :]
            rscr[d * cols:(d + 1) * cols, s:s + LANES] = turned.astype(BF16)
    live_cols = right[:, width:].astype(F32).T[0:cols].astype(BF16)
    counts = dot(live_cols, left[:, width:])
    inverse = 1.0 / jnp.maximum(counts, 1.0)
    wide = 2 * LANES
    tall = 8
    for first in range(0, width, wide):
        for d0 in range(0, half, tall):
            product = dot(rscr[d0 * cols:(d0 + tall) * cols, :], left[:, first:first + wide])
            product = product.astype(BF16)
            for dd in range(tall):
                for t in range(wide // LANES):
                    g = first // LANES + t
                    oscr[g * cols:(g + 1) * cols, (d0 + dd) * LANES:(d0 + dd + 1) * LANES] = (
                        product[dd * cols:(dd + 1) * cols, t * LANES:(t + 1) * LANES])
    outer = dot(oscr[...], block_ref[...])
    for i in range(rows):
        g, k = i // per, i % per
        part = outer[g * cols:(g + 1) * cols, k * channels:(k + 1) * channels]
        updated = (base_ref[i] + part * inverse[:, i:i + 1]).astype(BF16)
        updated_ref[i] = updated
        normed = layer_norm(updated.astype(F32), gain_ref[...], shift_ref[...])
        nscr[i * cols:(i + 1) * cols, :] = normed.astype(BF16)
    live = pick_columns(res_ref[...], col_start, cols) * pick_rows(res_ref[...], row_start, rows)
    chunk = 8
    for i0 in range(0, rows, chunk):
        mixture = dot(nscr[i0 * cols:(i0 + chunk) * cols, :], w_ref[...]) + bias_ref[...]
        part = [mixture[:, n * channels:(n + 1) * channels] for n in range(5)]
        left_edge = sigmoid(part[0]) * part[1]
        right_edge = sigmoid(part[2]) * part[3]
        gate_ref[i0 * cols:(i0 + chunk) * cols, :] = sigmoid(part[4])
        for ii in range(chunk):
            here = live[:, i0 + ii:i0 + ii + 1]
            at = slice(ii * cols, (ii + 1) * cols)
            left_ref[i0 + ii] = (left_edge[at] * here).astype(BF16)
            escr[(i0 + ii) * cols:(i0 + ii + 1) * cols, :] = right_edge[at] * here
    for k in range(cols):
        right_ref[k] = escr[pl.ds(k, rows, stride=cols), :].astype(BF16)


def panel_kernel(left_ref, panel_ref):
    for step in range(left_ref.shape[0]):
        panel_ref[step] = left_ref[step].astype(F32).reshape(panel_ref.shape[1:])


def add_block(step, panel_ref, right_ref, rscr, before, store):
    depth, cols, channels = right_ref.shape
    rows = panel_ref.shape[1] // depth
    own = lax.axis_index("resi") ^ step
    rscr[...] = right_ref[...].astype(F32).reshape(rscr.shape)
    block = 4
    tiles = cols // 8

    def rows_body(at, carry):
        place = [[pl.ds(pl.multiple_of((at * block + b) * cols + t * 8, 8), 8) for t in range(tiles)]
                 for b in range(block)]
        if before is None:
            sums = [[jnp.zeros((8, channels), F32) for _ in range(tiles)] for _ in range(block)]
        else:
            sums = [[before[place[b][t], :] for t in range(tiles)] for b in range(block)]
        for k in range(depth):
            column = [rscr[k * cols + t * 8:k * cols + t * 8 + 8, :] for t in range(tiles)]
            for b in range(block):
                row = panel_ref[own, pl.ds((at * block + b) * depth + k, 1), :]
                for t in range(tiles):
                    sums[b][t] = sums[b][t] + row * column[t]
        for b in range(block):
            for t in range(tiles):
                store[place[b][t], :] = sums[b][t]
        return carry

    lax.fori_loop(0, rows // block, rows_body, 0)


def step_kernel(step, right_ref, panel_ref, *refs):
    before = refs[0] if len(refs) == 3 else None
    add_block(step, panel_ref, right_ref, refs[-1], before, refs[-2])


def final_kernel(step, right_ref, panel_ref, before, updated_ref, gate_ref, gain_ref, shift_ref,
                 w_ref, bias_ref, out_ref, acc, rscr):
    add_block(step, panel_ref, right_ref, rscr, before, acc)
    rows, cols, channels = out_ref.shape
    chunk = 8
    for i0 in range(0, rows, chunk):
        at = slice(i0 * cols, (i0 + chunk) * cols)
        normed = layer_norm(acc[at, :], gain_ref[...], shift_ref[...]).astype(BF16)
        result = dot(normed, w_ref[...]) + bias_ref[...]
        updated = updated_ref[i0:i0 + chunk].reshape(chunk * cols, channels).astype(F32)
        value = updated + gate_ref[at, :] * result
        out_ref[i0:i0 + chunk] = value.astype(BF16).reshape(chunk, cols, channels)


def send_plane(block, count):
    return [block] + [
        lax.ppermute(block, PLANE, [(p, p ^ m) for p in range(count)]) for m in range(1, count)
    ]


def send_turned(block, count):
    return [
        lax.ppermute(
            block, GROUP,
            [(z * count + p, (p ^ m) * count + z) for z in range(count) for p in range(count)])
        for m in range(count)
    ]


def call(kernel, outs, scratch, args, flops=0, name=None):
    vmem = pl.BlockSpec(memory_space=pltpu.VMEM)
    size = sum(a.size * a.dtype.itemsize for a in args)
    return pl.pallas_call(
        kernel,
        out_shape=outs,
        in_specs=[vmem] * len(args),
        out_specs=[vmem] * len(outs) if isinstance(outs, list) else vmem,
        scratch_shapes=scratch,
        compiler_params=pltpu.CompilerParams(vmem_limit_bytes=40 * MIB),
        cost_estimate=pl.CostEstimate(flops=flops, bytes_accessed=size, transcendentals=0),
        name=name,
    )(*args)


def body(
    homolog_matrix,
    sequence_pad_mask,
    pair_features,
    residue_pad_mask,
    residue_chain_index,
    homolog_standard_factor,
    homolog_standard_offset,
    factor_mapping_matrices,
    outer_side_biases,
    outer_pair_projection,
    relative_position_table,
    pair_norm_gain,
    pair_norm_bias,
    triangle_projection_weights,
    triangle_projection_biases,
    triangle_sum_norm_gain,
    triangle_sum_norm_bias,
    triangle_output_weight,
    outer_pair_bias,
):
    rows, cols, channels = pair_features.shape
    seqs, _, depth = homolog_matrix.shape
    half = factor_mapping_matrices.shape[1] // 2
    per = LANES // half
    count = lax.axis_size(PLANE)
    width = rows * half
    flat = lambda v: v.reshape(1, -1)
    shape = jax.ShapeDtypeStruct
    residue = flat(residue_pad_mask)
    chain = flat(residue_chain_index)
    pack = shape((seqs, width + LANES), BF16)
    normed = call(norm_kernel, shape((seqs * rows, depth), F32), [], [homolog_matrix],
                  flops=1 << 36, name="norm")
    left, right = call(
        pack_kernel, [pack, pack],
        [pltpu.VMEM((seqs * rows, LANES), F32)] * 2,
        [normed, sequence_pad_mask, residue, flat(homolog_standard_factor),
         flat(homolog_standard_offset), factor_mapping_matrices.T, flat(outer_side_biases)],
        flops=1 << 30, name="pack")
    rights = send_turned(right, count)
    lefts = send_plane(left, count)
    base, block = call(
        base_kernel,
        [shape((rows, cols, channels), F32), shape((half * LANES, per * channels), BF16)],
        [pltpu.VMEM((LANES, channels), F32), pltpu.VMEM((half * half, channels), F32)],
        [pair_features, relative_position_table, chain, outer_pair_projection],
        flops=1 << 30, name="base")
    updated, left_edge, right_edge, gate = call(
        functools.partial(edges_kernel, count),
        [shape((rows, cols, channels), BF16), shape((rows, cols, channels), BF16),
         shape((cols, rows, channels), BF16), shape((rows * cols, channels), F32)],
        [pltpu.VMEM((count, seqs, width + LANES), BF16), pltpu.VMEM((count, seqs, width + LANES), BF16),
         pltpu.VMEM((count * seqs // LANES, width, LANES), F32),
         pltpu.VMEM((width, count * seqs), BF16),
         pltpu.VMEM((rows // per * cols, half * LANES), BF16),
         pltpu.VMEM((rows * cols, channels), BF16), pltpu.VMEM((rows * cols, channels), F32)],
        rights + lefts + [base, block, residue, flat(pair_norm_gain), flat(pair_norm_bias),
                          triangle_projection_weights, flat(triangle_projection_biases)],
        name="edges")
    right_edges = send_turned(right_edge, count)
    left_edges = lax.all_gather(left_edge, PLANE)
    sums = shape((rows * cols, channels), F32)
    turned = pltpu.VMEM((rows * cols, channels), F32)
    panel = call(
        panel_kernel, shape((count, rows * cols, channels), F32), [], [left_edges], name="panel")
    args = []
    for step in range(count - 1):
        args = [call(functools.partial(step_kernel, step), sums, [turned],
                     [right_edges[step], panel] + args, name="triangle")]
    return call(
        functools.partial(final_kernel, count - 1), shape((rows, cols, channels), BF16),
        [turned, turned],
        [right_edges[-1], panel] + args + [
            updated, gate, flat(triangle_sum_norm_gain), flat(triangle_sum_norm_bias),
            triangle_output_weight, flat(outer_pair_bias)],
        name="final")


def solution(mesh):
    pair = P(("groups", "resi"), ("resj", "seq"), None)
    placed = (
        P(("groups", "resj", "seq"), "resi", None),
        P(("groups", "resj", "seq"), "resi"),
        pair,
        P("groups"),
        P("groups"),
    ) + (P(),) * 14
    return jax.shard_map(body, mesh=mesh, in_specs=placed, out_specs=pair, check_vma=False)
```

```python
import functools

import jax
import jax.numpy as jnp
from jax import lax
from jax.experimental import pallas as pl
from jax.experimental.pallas import tpu as pltpu
from jax.sharding import PartitionSpec as P

RELMAX = 32
LANES = 128
PLANE = ("resj", "seq")
GROUP = ("resi", "resj", "seq")
F32 = jnp.float32
BF16 = jnp.bfloat16
MIB = 1 << 20


def iota(shape, axis):
    return lax.broadcasted_iota(jnp.int32, shape, axis)


def dot(a, b):
    return jnp.dot(a, b, preferred_element_type=F32)


def sigmoid(v):
    return 0.5 * jnp.tanh(0.5 * v) + 0.5


def layer_norm(values, gain, shift):
    average = jnp.mean(values, axis=-1, keepdims=True)
    centred = values - average
    variance = jnp.mean(centred * centred, axis=-1, keepdims=True)
    return centred * lax.rsqrt(variance + 1e-05) * gain + shift


def norm_kernel(x_ref, out_ref):
    x = x_ref[...].reshape(out_ref.shape).astype(F32)
    out_ref[...] = layer_norm(x, 1.0, 0.0)


def pack_kernel(x_ref, mask_ref, res_ref, gain_ref, shift_ref, w_ref, bias_ref,
                out_ref, lscr, rscr):
    seqs, rows = mask_ref.shape
    half = w_ref.shape[0] // 2
    per = LANES // half
    row_start = lax.axis_index("resi") * rows
    normed = (x_ref[...] * gain_ref[...] + shift_ref[...]).astype(BF16)
    lane = iota((2 * half, 2 * LANES), 1)
    spread = lane % half + jnp.where(lane >= LANES, half, 0) == iota((2 * half, 2 * LANES), 0)
    spread = spread.astype(F32)
    wide = lax.dot_general(
        w_ref[...], spread.astype(BF16), (((0,), (0,)), ((), ())), preferred_element_type=F32)
    wide = wide.astype(BF16)
    bias = jnp.dot(jnp.broadcast_to(bias_ref[...], (8, 2 * half)), spread,
                   precision=lax.Precision.HIGHEST, preferred_element_type=F32)[0:1]
    mapped = dot(normed, wide)
    lscr[...] = mapped[:, :LANES]
    rscr[...] = mapped[:, LANES:]
    row_live = pick_rows(res_ref[...], row_start, rows)
    live = (mask_ref[...].astype(F32) * row_live).astype(BF16)
    width = rows * half
    spread_live = (iota((rows, width), 1) // half == iota((rows, width), 0)).astype(BF16)
    live_wide = dot(live, spread_live)
    sub = iota((seqs, LANES), 1) // half
    for tile in range(width // LANES):
        at = slice(tile * LANES, (tile + 1) * LANES)
        for side, scr, first in ((0, lscr, 0), (1, rscr, LANES)):
            value = scr[pl.ds(tile * per, seqs, stride=rows), :]
            for k in range(1, per):
                value = jnp.where(sub == k, scr[pl.ds(tile * per + k, seqs, stride=rows), :], value)
            value = (value + bias[:, first:first + LANES]) * live_wide[:, at]
            out_ref[side, :, at] = value.astype(BF16)
    live_tile = dot(live, (iota((rows, LANES), 0) == iota((rows, LANES), 1)).astype(BF16))
    for side in range(2):
        out_ref[side, :, width:] = live_tile.astype(BF16)


def join_kernel(own_ref, other_ref, base_ref, left_ref, right_ref):
    for n, ref in enumerate((own_ref, other_ref)):
        left_ref[n] = ref[0]
        right_ref[n] = ref[1]


def pair_kernel(own_ref, other_ref, pair_ref):
    pair_ref[0] = own_ref[...]
    pair_ref[1] = other_ref[...]


def pick_columns(values, start, size):
    total = values.shape[1]
    own = iota((size, total), 1) == iota((size, total), 0) + start
    spread = jnp.broadcast_to(values, (size, total)).astype(F32)
    return jnp.sum(jnp.where(own, spread, 0.0), axis=1, keepdims=True)


def pick_rows(values, start, size):
    total = values.shape[1]
    pick = (iota((total, size), 0) == iota((total, size), 1) + start).astype(BF16)
    return dot(jnp.broadcast_to(values.astype(F32), (8, total)).astype(BF16), pick)[0:1]


def base_kernel(pair_ref, table_ref, chain_ref, w_ref, base_ref, block_ref, tscr, wscr):
    rows, cols, channels = pair_ref.shape
    row_start = lax.axis_index("resi") * rows
    col_start = lax.axis_index(PLANE) * cols
    tscr[...] = jnp.zeros_like(tscr)
    tscr[0:table_ref.shape[0], :] = table_ref[...].astype(F32)
    table = tscr[...].astype(BF16)
    chain = chain_ref[...]
    same = pick_columns(chain, col_start, cols) == pick_rows(chain, row_start, rows)
    offset = iota((cols, rows), 0) + col_start - iota((cols, rows), 1) - row_start + RELMAX
    bins = jnp.where(same, jnp.clip(offset, 0, 2 * RELMAX), 2 * RELMAX + 1)
    lane = iota((cols, LANES), 1)
    for i in range(rows):
        one_hot = (lane == bins[:, i:i + 1]).astype(F32).astype(BF16)
        base_ref[i] = pair_ref[i].astype(F32) + dot(one_hot, table)
    wscr[...] = w_ref[...].astype(F32)
    half = int(round(w_ref.shape[0] ** 0.5))
    per = LANES // half
    block_ref[...] = jnp.zeros_like(block_ref)
    for d in range(half):
        value = wscr[pl.ds(d, half, stride=half), :].astype(BF16)
        for k in range(per):
            block_ref[pl.ds(d * LANES + k * half, half), k * channels:(k + 1) * channels] = value


def edges_kernel(count, *refs):
    pairs = count // 2
    rights, lefts = refs[:pairs], refs[pairs:2 * pairs]
    (base_ref, block_ref, res_ref, gain_ref, shift_ref, w_ref, bias_ref,
     updated_ref, left_ref, right_ref, gate_ref,
     lall, rall, tscr, rscr, oscr, nscr, escr) = refs[2 * pairs:]
    rows, cols, channels = base_ref.shape
    seqs = lefts[0].shape[1]
    half = block_ref.shape[0] // LANES
    per = LANES // half
    width = rows * half
    total_seqs = count * seqs
    z = lax.axis_index("resi")
    q = lax.axis_index(PLANE)
    row_start, col_start = z * rows, q * cols
    for step in range(pairs):
        for n in range(2):
            lall[q ^ (step + n * pairs)] = lefts[step][n]
            rall[z ^ (step + n * pairs)] = rights[step][n]
    right = rall[...].reshape(total_seqs, -1)
    left = lall[...].reshape(total_seqs, -1)
    for at in range(0, width, LANES):
        for s in range(0, total_seqs, LANES):
            tscr[s // LANES, at:at + LANES, :] = right[s:s + LANES, at:at + LANES].astype(F32).T
    for d in range(half):
        for s in range(0, total_seqs, LANES):
            turned = tscr[s // LANES, pl.ds(d, cols, stride=half), :]
            rscr[d * cols:(d + 1) * cols, s:s + LANES] = turned.astype(BF16)
    live_cols = right[:, width:].astype(F32).T[0:cols].astype(BF16)
    counts = dot(live_cols, left[:, width:])
    inverse = 1.0 / jnp.maximum(counts, 1.0)
    wide = 2 * LANES
    tall = 8
    for first in range(0, width, wide):
        for d0 in range(0, half, tall):
            product = dot(rscr[d0 * cols:(d0 + tall) * cols, :], left[:, first:first + wide])
            product = product.astype(BF16)
            for dd in range(tall):
                for t in range(wide // LANES):
                    g = first // LANES + t
                    oscr[g * cols:(g + 1) * cols, (d0 + dd) * LANES:(d0 + dd + 1) * LANES] = (
                        product[dd * cols:(dd + 1) * cols, t * LANES:(t + 1) * LANES])
    outer = dot(oscr[...], block_ref[...])
    for i in range(rows):
        g, k = i // per, i % per
        part = outer[g * cols:(g + 1) * cols, k * channels:(k + 1) * channels]
        updated = (base_ref[i] + part * inverse[:, i:i + 1]).astype(BF16)
        updated_ref[i] = updated
        normed = layer_norm(updated.astype(F32), gain_ref[...], shift_ref[...])
        nscr[i * cols:(i + 1) * cols, :] = normed.astype(BF16)
    live = pick_columns(res_ref[...], col_start, cols) * pick_rows(res_ref[...], row_start, rows)
    chunk = 8
    for i0 in range(0, rows, chunk):
        mixture = dot(nscr[i0 * cols:(i0 + chunk) * cols, :], w_ref[...]) + bias_ref[...]
        part = [mixture[:, n * channels:(n + 1) * channels] for n in range(5)]
        left_edge = sigmoid(part[0]) * part[1]
        right_edge = sigmoid(part[2]) * part[3]
        gate_ref[i0 * cols:(i0 + chunk) * cols, :] = sigmoid(part[4])
        for ii in range(chunk):
            here = live[:, i0 + ii:i0 + ii + 1]
            at = slice(ii * cols, (ii + 1) * cols)
            left_ref[i0 + ii] = (left_edge[at] * here).astype(BF16)
            escr[(i0 + ii) * cols:(i0 + ii + 1) * cols, :] = right_edge[at] * here
    for k in range(cols):
        right_ref[k] = escr[pl.ds(k, rows, stride=cols), :].astype(BF16)


def panel_kernel(count, *refs):
    pairs = count // 2
    lefts, panel_ref = refs[:pairs], refs[pairs]
    q = lax.axis_index(PLANE)
    for step in range(pairs):
        for n in range(2):
            panel_ref[q ^ (step + n * pairs)] = (
                lefts[step][n].astype(F32).reshape(panel_ref.shape[1:]))


def add_block(step, panel_ref, right_ref, rscr, before, store):
    depth, cols, channels = right_ref.shape
    rows = panel_ref.shape[1] // depth
    own = lax.axis_index("resi") ^ step
    rscr[...] = right_ref[...].astype(F32).reshape(rscr.shape)
    block = 4
    tiles = cols // 8

    def rows_body(at, carry):
        place = [[pl.ds(pl.multiple_of((at * block + b) * cols + t * 8, 8), 8) for t in range(tiles)]
                 for b in range(block)]
        if before is None:
            sums = [[jnp.zeros((8, channels), F32) for _ in range(tiles)] for _ in range(block)]
        else:
            sums = [[before[place[b][t], :] for t in range(tiles)] for b in range(block)]
        for k in range(depth):
            column = [rscr[k * cols + t * 8:k * cols + t * 8 + 8, :] for t in range(tiles)]
            for b in range(block):
                row = panel_ref[own, pl.ds((at * block + b) * depth + k, 1), :]
                for t in range(tiles):
                    sums[b][t] = sums[b][t] + row * column[t]
        for b in range(block):
            for t in range(tiles):
                store[place[b][t], :] = sums[b][t]
        return carry

    lax.fori_loop(0, rows // block, rows_body, 0)


def step_kernel(step, right_ref, panel_ref, *refs):
    before = refs[0] if len(refs) == 3 else None
    add_block(step, panel_ref, right_ref, refs[-1], before, refs[-2])


def final_kernel(step, right_ref, panel_ref, before, updated_ref, gate_ref, gain_ref, shift_ref,
                 w_ref, bias_ref, out_ref, acc, rscr):
    add_block(step, panel_ref, right_ref, rscr, before, acc)
    rows, cols, channels = out_ref.shape
    chunk = 8
    for i0 in range(0, rows, chunk):
        at = slice(i0 * cols, (i0 + chunk) * cols)
        normed = layer_norm(acc[at, :], gain_ref[...], shift_ref[...]).astype(BF16)
        result = dot(normed, w_ref[...]) + bias_ref[...]
        updated = updated_ref[i0:i0 + chunk].reshape(chunk * cols, channels).astype(F32)
        value = updated + gate_ref[at, :] * result
        out_ref[i0:i0 + chunk] = value.astype(BF16).reshape(chunk, cols, channels)


def swap_cores(block, count):
    return lax.ppermute(block, PLANE, [(p, p ^ (count // 2)) for p in range(count)])


def send_plane(pair, count):
    return [pair] + [
        lax.ppermute(pair, PLANE, [(p, p ^ m) for p in range(count)]) for m in range(1, count // 2)
    ]


def send_turned(block, count, steps):
    return [
        lax.ppermute(
            block, GROUP,
            [(z * count + p, (p ^ m) * count + z) for z in range(count) for p in range(count)])
        for m in range(steps)
    ]


def call(kernel, outs, scratch, args, flops=0, name=None):
    vmem = pl.BlockSpec(memory_space=pltpu.VMEM)
    size = sum(a.size * a.dtype.itemsize for a in args)
    return pl.pallas_call(
        kernel,
        out_shape=outs,
        in_specs=[vmem] * len(args),
        out_specs=[vmem] * len(outs) if isinstance(outs, list) else vmem,
        scratch_shapes=scratch,
        compiler_params=pltpu.CompilerParams(vmem_limit_bytes=40 * MIB),
        cost_estimate=pl.CostEstimate(flops=flops, bytes_accessed=size, transcendentals=0),
        name=name,
    )(*args)


def body(
    homolog_matrix,
    sequence_pad_mask,
    pair_features,
    residue_pad_mask,
    residue_chain_index,
    homolog_standard_factor,
    homolog_standard_offset,
    factor_mapping_matrices,
    outer_side_biases,
    outer_pair_projection,
    relative_position_table,
    pair_norm_gain,
    pair_norm_bias,
    triangle_projection_weights,
    triangle_projection_biases,
    triangle_sum_norm_gain,
    triangle_sum_norm_bias,
    triangle_output_weight,
    outer_pair_bias,
):
    rows, cols, channels = pair_features.shape
    seqs, _, depth = homolog_matrix.shape
    half = factor_mapping_matrices.shape[1] // 2
    per = LANES // half
    count = lax.axis_size(PLANE)
    width = rows * half
    flat = lambda v: v.reshape(1, -1)
    shape = jax.ShapeDtypeStruct
    residue = flat(residue_pad_mask)
    chain = flat(residue_chain_index)
    pack = shape((2, seqs, width + LANES), BF16)
    normed = call(norm_kernel, shape((seqs * rows, depth), F32), [], [homolog_matrix],
                  flops=1 << 36, name="norm")
    factors = call(
        pack_kernel, pack,
        [pltpu.VMEM((seqs * rows, LANES), F32)] * 2,
        [normed, sequence_pad_mask, residue, flat(homolog_standard_factor),
         flat(homolog_standard_offset), factor_mapping_matrices.T, flat(outer_side_biases)],
        flops=1 << 30, name="pack")
    other = swap_cores(factors, count)
    base, block = call(
        base_kernel,
        [shape((rows, cols, channels), F32), shape((half * LANES, per * channels), BF16)],
        [pltpu.VMEM((LANES, channels), F32), pltpu.VMEM((half * half, channels), F32)],
        [pair_features, relative_position_table, chain, outer_pair_projection],
        flops=1 << 30, name="base")
    left, right = call(join_kernel, [pack, pack], [], [factors, other, base], name="join")
    rights = send_turned(right, count, count // 2)
    lefts = send_plane(left, count)
    updated, left_edge, right_edge, gate = call(
        functools.partial(edges_kernel, count),
        [shape((rows, cols, channels), BF16), shape((rows, cols, channels), BF16),
         shape((cols, rows, channels), BF16), shape((rows * cols, channels), F32)],
        [pltpu.VMEM((count, seqs, width + LANES), BF16), pltpu.VMEM((count, seqs, width + LANES), BF16),
         pltpu.VMEM((count * seqs // LANES, width, LANES), F32),
         pltpu.VMEM((width, count * seqs), BF16),
         pltpu.VMEM((rows // per * cols, half * LANES), BF16),
         pltpu.VMEM((rows * cols, channels), BF16), pltpu.VMEM((rows * cols, channels), F32)],
        rights + lefts + [base, block, residue, flat(pair_norm_gain), flat(pair_norm_bias),
                          triangle_projection_weights, flat(triangle_projection_biases)],
        name="edges")
    right_edges = send_turned(right_edge, count, count)
    left_pair = call(pair_kernel, shape((2,) + left_edge.shape, BF16), [],
                     [left_edge, swap_cores(left_edge, count)], name="pair")
    left_edges = send_plane(left_pair, count)
    sums = shape((rows * cols, channels), F32)
    turned = pltpu.VMEM((rows * cols, channels), F32)
    panel = call(
        functools.partial(panel_kernel, count), shape((count, rows * cols, channels), F32), [],
        left_edges, name="panel")
    args = []
    for step in range(count - 1):
        args = [call(functools.partial(step_kernel, step), sums, [turned],
                     [right_edges[step], panel] + args, name="triangle")]
    return call(
        functools.partial(final_kernel, count - 1), shape((rows, cols, channels), BF16),
        [turned, turned],
        [right_edges[-1], panel] + args + [
            updated, gate, flat(triangle_sum_norm_gain), flat(triangle_sum_norm_bias),
            triangle_output_weight, flat(outer_pair_bias)],
        name="final")


def solution(mesh):
    pair = P(("groups", "resi"), ("resj", "seq"), None)
    placed = (
        P(("groups", "resj", "seq"), "resi", None),
        P(("groups", "resj", "seq"), "resi"),
        pair,
        P("groups"),
        P("groups"),
    ) + (P(),) * 14
    return jax.shard_map(body, mesh=mesh, in_specs=placed, out_specs=pair, check_vma=False)
```

```python
import functools

import jax
import jax.numpy as jnp
from jax import lax
from jax.experimental import pallas as pl
from jax.experimental.pallas import tpu as pltpu
from jax.sharding import PartitionSpec as P

RELMAX = 32
LANES = 128
PLANE = ("resj", "seq")
GROUP = ("resi", "resj", "seq")
F32 = jnp.float32
BF16 = jnp.bfloat16
MIB = 1 << 20


def iota(shape, axis):
    return lax.broadcasted_iota(jnp.int32, shape, axis)


def dot(a, b):
    return jnp.dot(a, b, preferred_element_type=F32)


def sigmoid(v):
    return 0.5 * jnp.tanh(0.5 * v) + 0.5


def layer_norm(values, gain, shift):
    average = jnp.mean(values, axis=-1, keepdims=True)
    centred = values - average
    variance = jnp.mean(centred * centred, axis=-1, keepdims=True)
    return centred * lax.rsqrt(variance + 1e-05) * gain + shift


def norm_kernel(x_ref, out_ref):
    x = x_ref[...].reshape(out_ref.shape).astype(F32)
    out_ref[...] = layer_norm(x, 1.0, 0.0)


def pack_kernel(x_ref, mask_ref, res_ref, gain_ref, shift_ref, w_ref, bias_ref,
                out_ref, lscr, rscr):
    seqs, rows = mask_ref.shape
    half = w_ref.shape[0] // 2
    per = LANES // half
    row_start = lax.axis_index("resi") * rows
    normed = (x_ref[...] * gain_ref[...] + shift_ref[...]).astype(BF16)
    lane = iota((2 * half, 2 * LANES), 1)
    spread = lane % half + jnp.where(lane >= LANES, half, 0) == iota((2 * half, 2 * LANES), 0)
    spread = spread.astype(F32)
    wide = lax.dot_general(
        w_ref[...], spread.astype(BF16), (((0,), (0,)), ((), ())), preferred_element_type=F32)
    wide = wide.astype(BF16)
    bias = jnp.dot(jnp.broadcast_to(bias_ref[...], (8, 2 * half)), spread,
                   precision=lax.Precision.HIGHEST, preferred_element_type=F32)[0:1]
    mapped = dot(normed, wide)
    lscr[...] = mapped[:, :LANES]
    rscr[...] = mapped[:, LANES:]
    row_live = pick_rows(res_ref[...], row_start, rows)
    live = (mask_ref[...].astype(F32) * row_live).astype(BF16)
    width = rows * half
    spread_live = (iota((rows, width), 1) // half == iota((rows, width), 0)).astype(BF16)
    live_wide = dot(live, spread_live)
    sub = iota((seqs, LANES), 1) // half
    for tile in range(width // LANES):
        at = slice(tile * LANES, (tile + 1) * LANES)
        for side, scr, first in ((0, lscr, 0), (1, rscr, LANES)):
            value = scr[pl.ds(tile * per, seqs, stride=rows), :]
            for k in range(1, per):
                value = jnp.where(sub == k, scr[pl.ds(tile * per + k, seqs, stride=rows), :], value)
            value = (value + bias[:, first:first + LANES]) * live_wide[:, at]
            out_ref[side, :, at] = value.astype(BF16)
    live_tile = dot(live, (iota((rows, LANES), 0) == iota((rows, LANES), 1)).astype(BF16))
    for side in range(2):
        out_ref[side, :, width:] = live_tile.astype(BF16)


def join_kernel(own_ref, other_ref, base_ref, left_ref, right_ref):
    for n, ref in enumerate((own_ref, other_ref)):
        left_ref[n] = ref[0]
        right_ref[n] = ref[1]


def pick_columns(values, start, size):
    total = values.shape[1]
    own = iota((size, total), 1) == iota((size, total), 0) + start
    spread = jnp.broadcast_to(values, (size, total)).astype(F32)
    return jnp.sum(jnp.where(own, spread, 0.0), axis=1, keepdims=True)


def pick_rows(values, start, size):
    total = values.shape[1]
    pick = (iota((total, size), 0) == iota((total, size), 1) + start).astype(BF16)
    return dot(jnp.broadcast_to(values.astype(F32), (8, total)).astype(BF16), pick)[0:1]


def base_kernel(pair_ref, table_ref, chain_ref, w_ref, base_ref, block_ref, tscr, wscr):
    rows, cols, channels = pair_ref.shape
    row_start = lax.axis_index("resi") * rows
    col_start = lax.axis_index(PLANE) * cols
    tscr[...] = jnp.zeros_like(tscr)
    tscr[0:table_ref.shape[0], :] = table_ref[...].astype(F32)
    table = tscr[...].astype(BF16)
    chain = chain_ref[...]
    same = pick_columns(chain, col_start, cols) == pick_rows(chain, row_start, rows)
    offset = iota((cols, rows), 0) + col_start - iota((cols, rows), 1) - row_start + RELMAX
    bins = jnp.where(same, jnp.clip(offset, 0, 2 * RELMAX), 2 * RELMAX + 1)
    lane = iota((cols, LANES), 1)
    for i in range(rows):
        one_hot = (lane == bins[:, i:i + 1]).astype(F32).astype(BF16)
        base_ref[i] = pair_ref[i].astype(F32) + dot(one_hot, table)
    wscr[...] = w_ref[...].astype(F32)
    half = int(round(w_ref.shape[0] ** 0.5))
    per = LANES // half
    block_ref[...] = jnp.zeros_like(block_ref)
    for d in range(half):
        value = wscr[pl.ds(d, half, stride=half), :].astype(BF16)
        for k in range(per):
            block_ref[pl.ds(d * LANES + k * half, half), k * channels:(k + 1) * channels] = value


def edges_kernel(count, *refs):
    pairs = count // 2
    rights, lefts = refs[:pairs], refs[pairs:2 * pairs]
    (base_ref, block_ref, res_ref, gain_ref, shift_ref, w_ref, bias_ref,
     updated_ref, left_ref, right_ref, gate_ref,
     lall, rall, tscr, rscr, oscr, nscr, escr) = refs[2 * pairs:]
    rows, cols, channels = base_ref.shape
    seqs = lefts[0].shape[1]
    half = block_ref.shape[0] // LANES
    per = LANES // half
    width = rows * half
    total_seqs = count * seqs
    z = lax.axis_index("resi")
    q = lax.axis_index(PLANE)
    row_start, col_start = z * rows, q * cols
    for step in range(pairs):
        for n in range(2):
            lall[q ^ (step + n * pairs)] = lefts[step][n]
            rall[z ^ (step + n * pairs)] = rights[step][n]
    right = rall[...].reshape(total_seqs, -1)
    left = lall[...].reshape(total_seqs, -1)
    for at in range(0, width, LANES):
        for s in range(0, total_seqs, LANES):
            tscr[s // LANES, at:at + LANES, :] = right[s:s + LANES, at:at + LANES].astype(F32).T
    for d in range(half):
        for s in range(0, total_seqs, LANES):
            turned = tscr[s // LANES, pl.ds(d, cols, stride=half), :]
            rscr[d * cols:(d + 1) * cols, s:s + LANES] = turned.astype(BF16)
    live_cols = right[:, width:].astype(F32).T[0:cols].astype(BF16)
    counts = dot(live_cols, left[:, width:])
    inverse = 1.0 / jnp.maximum(counts, 1.0)
    wide = 2 * LANES
    tall = 8
    for first in range(0, width, wide):
        for d0 in range(0, half, tall):
            product = dot(rscr[d0 * cols:(d0 + tall) * cols, :], left[:, first:first + wide])
            product = product.astype(BF16)
            for dd in range(tall):
                for t in range(wide // LANES):
                    g = first // LANES + t
                    oscr[g * cols:(g + 1) * cols, (d0 + dd) * LANES:(d0 + dd + 1) * LANES] = (
                        product[dd * cols:(dd + 1) * cols, t * LANES:(t + 1) * LANES])
    outer = dot(oscr[...], block_ref[...])
    for i in range(rows):
        g, k = i // per, i % per
        part = outer[g * cols:(g + 1) * cols, k * channels:(k + 1) * channels]
        updated = (base_ref[i] + part * inverse[:, i:i + 1]).astype(BF16)
        updated_ref[i] = updated
        normed = layer_norm(updated.astype(F32), gain_ref[...], shift_ref[...])
        nscr[i * cols:(i + 1) * cols, :] = normed.astype(BF16)
    live = pick_columns(res_ref[...], col_start, cols) * pick_rows(res_ref[...], row_start, rows)
    chunk = 8
    for i0 in range(0, rows, chunk):
        mixture = dot(nscr[i0 * cols:(i0 + chunk) * cols, :], w_ref[...]) + bias_ref[...]
        part = [mixture[:, n * channels:(n + 1) * channels] for n in range(5)]
        left_edge = sigmoid(part[0]) * part[1]
        right_edge = sigmoid(part[2]) * part[3]
        gate_ref[i0 * cols:(i0 + chunk) * cols, :] = sigmoid(part[4])
        for ii in range(chunk):
            here = live[:, i0 + ii:i0 + ii + 1]
            at = slice(ii * cols, (ii + 1) * cols)
            left_ref[i0 + ii] = (left_edge[at] * here).astype(BF16)
            escr[(i0 + ii) * cols:(i0 + ii + 1) * cols, :] = right_edge[at] * here
    for k in range(cols):
        right_ref[k] = escr[pl.ds(k, rows, stride=cols), :].astype(BF16)


def panel_kernel(*refs):
    *lefts, panel_ref = refs
    x = lax.axis_index("seq")
    for step, left in enumerate(lefts):
        panel_ref[x ^ step] = left[...].astype(F32).reshape(panel_ref.shape[1:])


def origin(step, chips):
    source = lax.axis_index("resi") ^ step
    return (source // chips) ^ lax.axis_index("resj"), source % chips


def add_block(panel_ref, chip, rscr, rows, before, store):
    cols = store.shape[0] // rows
    depth, channels = rscr.shape[0] // cols, rscr.shape[1]
    block = 4
    tiles = cols // 8

    def rows_body(at, carry):
        place = [[pl.ds(pl.multiple_of((at * block + b) * cols + t * 8, 8), 8) for t in range(tiles)]
                 for b in range(block)]
        if before is None:
            sums = [[jnp.zeros((8, channels), F32) for _ in range(tiles)] for _ in range(block)]
        else:
            sums = [[before[place[b][t], :] for t in range(tiles)] for b in range(block)]
        for k in range(depth):
            column = [rscr[k * cols + t * 8:k * cols + t * 8 + 8, :] for t in range(tiles)]
            for b in range(block):
                row = panel_ref[chip, pl.ds((at * block + b) * depth + k, 1), :]
                for t in range(tiles):
                    sums[b][t] = sums[b][t] + row * column[t]
        for b in range(block):
            for t in range(tiles):
                store[place[b][t], :] = sums[b][t].astype(store.dtype)
        return carry

    lax.fori_loop(0, rows // block, rows_body, 0)


def step_kernel(step, chips, fresh, right_ref, panel_ref, *refs):
    out_ref, rscr = refs[-2:]
    side, chip = origin(step, chips)
    rscr[...] = right_ref[...].astype(F32).reshape(rscr.shape)
    before = None if fresh else refs[0].at[side]
    add_block(panel_ref, chip, rscr, right_ref.shape[1], before, out_ref.at[side])


def last_kernel(side, steps, chips, first_ref, second_ref, panel_ref, sums_ref, out_ref, rscr):
    first_side, first_chip = origin(steps[0], chips)
    second_chip = origin(steps[1], chips)[1]
    mine = first_side == side

    @pl.when(mine)
    def _():
        rscr[...] = first_ref[...].astype(F32).reshape(rscr.shape)

    @pl.when(jnp.logical_not(mine))
    def _():
        rscr[...] = second_ref[...].astype(F32).reshape(rscr.shape)

    chip = jnp.where(mine, first_chip, second_chip)
    add_block(panel_ref, chip, rscr, first_ref.shape[1], sums_ref.at[side], out_ref)


def final_kernel(own_ref, other_ref, updated_ref, gate_ref, gain_ref, shift_ref, w_ref, bias_ref, out_ref):
    rows, cols, channels = out_ref.shape
    chunk = 8
    for i0 in range(0, rows, chunk):
        at = slice(i0 * cols, (i0 + chunk) * cols)
        sums = own_ref[at, :] + other_ref[at, :].astype(F32)
        normed = layer_norm(sums, gain_ref[...], shift_ref[...]).astype(BF16)
        result = dot(normed, w_ref[...]) + bias_ref[...]
        updated = updated_ref[i0:i0 + chunk].reshape(chunk * cols, channels).astype(F32)
        value = updated + gate_ref[at, :] * result
        out_ref[i0:i0 + chunk] = value.astype(BF16).reshape(chunk, cols, channels)


def swap_cores(block, count):
    return lax.ppermute(block, PLANE, [(p, p ^ (count // 2)) for p in range(count)])


def send_plane(pair, count):
    return [pair] + [
        lax.ppermute(pair, PLANE, [(p, p ^ m) for p in range(count)]) for m in range(1, count // 2)
    ]


def send_turned(block, count, steps):
    return [
        lax.ppermute(
            block, GROUP,
            [(z * count + p, (p ^ m) * count + z) for z in range(count) for p in range(count)])
        for m in range(steps)
    ]


def send_same_core(block, count, chips, steps):
    def target(z, p, m):
        core, x = p // chips, p % chips
        return ((z // chips * chips + x) ^ m) * count + core * chips + z % chips

    return [
        lax.ppermute(
            block, GROUP,
            [(z * count + p, target(z, p, m)) for z in range(count) for p in range(count)])
        for m in steps
    ]


def call(kernel, outs, scratch, args, flops=0, aliases=None, name=None):
    vmem = pl.BlockSpec(memory_space=pltpu.VMEM)
    size = sum(a.size * a.dtype.itemsize for a in args)
    return pl.pallas_call(
        kernel,
        out_shape=outs,
        in_specs=[vmem] * len(args),
        out_specs=[vmem] * len(outs) if isinstance(outs, list) else vmem,
        scratch_shapes=scratch,
        input_output_aliases=aliases or {},
        compiler_params=pltpu.CompilerParams(vmem_limit_bytes=40 * MIB),
        cost_estimate=pl.CostEstimate(flops=flops, bytes_accessed=size, transcendentals=0),
        name=name,
    )(*args)


def body(
    homolog_matrix,
    sequence_pad_mask,
    pair_features,
    residue_pad_mask,
    residue_chain_index,
    homolog_standard_factor,
    homolog_standard_offset,
    factor_mapping_matrices,
    outer_side_biases,
    outer_pair_projection,
    relative_position_table,
    pair_norm_gain,
    pair_norm_bias,
    triangle_projection_weights,
    triangle_projection_biases,
    triangle_sum_norm_gain,
    triangle_sum_norm_bias,
    triangle_output_weight,
    outer_pair_bias,
):
    rows, cols, channels = pair_features.shape
    seqs, _, depth = homolog_matrix.shape
    half = factor_mapping_matrices.shape[1] // 2
    per = LANES // half
    count = lax.axis_size(PLANE)
    width = rows * half
    flat = lambda v: v.reshape(1, -1)
    shape = jax.ShapeDtypeStruct
    residue = flat(residue_pad_mask)
    chain = flat(residue_chain_index)
    pack = shape((2, seqs, width + LANES), BF16)
    normed = call(norm_kernel, shape((seqs * rows, depth), F32), [], [homolog_matrix],
                  flops=1 << 36, name="norm")
    factors = call(
        pack_kernel, pack,
        [pltpu.VMEM((seqs * rows, LANES), F32)] * 2,
        [normed, sequence_pad_mask, residue, flat(homolog_standard_factor),
         flat(homolog_standard_offset), factor_mapping_matrices.T, flat(outer_side_biases)],
        flops=1 << 30, name="pack")
    other = swap_cores(factors, count)
    base, block = call(
        base_kernel,
        [shape((rows, cols, channels), F32), shape((half * LANES, per * channels), BF16)],
        [pltpu.VMEM((LANES, channels), F32), pltpu.VMEM((half * half, channels), F32)],
        [pair_features, relative_position_table, chain, outer_pair_projection],
        flops=1 << 30, name="base")
    left, right = call(join_kernel, [pack, pack], [], [factors, other, base], name="join")
    rights = send_turned(right, count, count // 2)
    lefts = send_plane(left, count)
    updated, left_edge, right_edge, gate = call(
        functools.partial(edges_kernel, count),
        [shape((rows, cols, channels), BF16), shape((rows, cols, channels), BF16),
         shape((cols, rows, channels), BF16), shape((rows * cols, channels), F32)],
        [pltpu.VMEM((count, seqs, width + LANES), BF16), pltpu.VMEM((count, seqs, width + LANES), BF16),
         pltpu.VMEM((count * seqs // LANES, width, LANES), F32),
         pltpu.VMEM((width, count * seqs), BF16),
         pltpu.VMEM((rows // per * cols, half * LANES), BF16),
         pltpu.VMEM((rows * cols, channels), BF16), pltpu.VMEM((rows * cols, channels), F32)],
        rights + lefts + [base, block, residue, flat(pair_norm_gain), flat(pair_norm_bias),
                          triangle_projection_weights, flat(triangle_projection_biases)],
        name="edges")
    chips = lax.axis_size("seq")
    steps = [m + n * chips for m in range(chips) for n in range(2)]
    right_edges = send_same_core(right_edge, count, chips, steps)
    left_edges = [left_edge] + [
        lax.ppermute(left_edge, "seq", [(x, x ^ m) for x in range(chips)]) for m in range(1, chips)
    ]
    block_sums = shape((rows * cols, channels), F32)
    turned = pltpu.VMEM((rows * cols, channels), F32)
    panel = call(panel_kernel, shape((chips, rows * cols, channels), F32), [], left_edges, name="panel")
    sums = []
    for n, step in enumerate(steps[:-2]):
        sums = [call(
            functools.partial(step_kernel, step, chips, n < 2), shape((2, rows * cols, channels), F32),
            [turned], [right_edges[n], panel] + sums, aliases={2: 0} if n else None, name="triangle")]
    last = right_edges[-2:] + [panel] + sums
    half_sums = call(
        functools.partial(last_kernel, 1, steps[-2:], chips), shape((rows * cols, channels), BF16),
        [turned], last, name="others")
    other_sums = swap_cores(half_sums, count)
    own_sums = call(
        functools.partial(last_kernel, 0, steps[-2:], chips), block_sums, [turned], last,
        flops=1 << 32, name="own")
    return call(
        final_kernel, shape((rows, cols, channels), BF16), [],
        [own_sums, other_sums, updated, gate, flat(triangle_sum_norm_gain),
         flat(triangle_sum_norm_bias), triangle_output_weight, flat(outer_pair_bias)],
        name="final")


def solution(mesh):
    pair = P(("groups", "resi"), ("resj", "seq"), None)
    placed = (
        P(("groups", "resj", "seq"), "resi", None),
        P(("groups", "resj", "seq"), "resi"),
        pair,
        P("groups"),
        P("groups"),
    ) + (P(),) * 14
    return jax.shard_map(body, mesh=mesh, in_specs=placed, out_specs=pair, check_vma=False)
```

```python
import functools

import jax
import jax.numpy as jnp
from jax import lax
from jax.experimental import pallas as pl
from jax.experimental.pallas import tpu as pltpu
from jax.sharding import PartitionSpec as P

RELMAX = 32
LANES = 128
PLANE = ("resj", "seq")
GROUP = ("resi", "resj", "seq")
F32 = jnp.float32
BF16 = jnp.bfloat16
MIB = 1 << 20


def iota(shape, axis):
    return lax.broadcasted_iota(jnp.int32, shape, axis)


def dot(a, b):
    return jnp.dot(a, b, preferred_element_type=F32)


def sigmoid(v):
    return 0.5 * jnp.tanh(0.5 * v) + 0.5


def layer_norm(values, gain, shift):
    average = jnp.mean(values, axis=-1, keepdims=True)
    centred = values - average
    variance = jnp.mean(centred * centred, axis=-1, keepdims=True)
    return centred * lax.rsqrt(variance + 1e-05) * gain + shift


def norm_kernel(x_ref, out_ref):
    x = x_ref[...].reshape(out_ref.shape).astype(F32)
    out_ref[...] = layer_norm(x, 1.0, 0.0)


def pack_kernel(x_ref, mask_ref, res_ref, gain_ref, shift_ref, w_ref, bias_ref,
                left_ref, right_ref, lscr, rscr):
    seqs, rows = mask_ref.shape
    half = w_ref.shape[0] // 2
    per = LANES // half
    row_start = lax.axis_index("resi") * rows
    normed = (x_ref[...] * gain_ref[...] + shift_ref[...]).astype(BF16)
    lane = iota((2 * half, 2 * LANES), 1)
    spread = lane % half + jnp.where(lane >= LANES, half, 0) == iota((2 * half, 2 * LANES), 0)
    spread = spread.astype(F32)
    wide = lax.dot_general(
        w_ref[...], spread.astype(BF16), (((0,), (0,)), ((), ())), preferred_element_type=F32)
    wide = wide.astype(BF16)
    bias = jnp.dot(jnp.broadcast_to(bias_ref[...], (8, 2 * half)), spread,
                   precision=lax.Precision.HIGHEST, preferred_element_type=F32)[0:1]
    mapped = dot(normed, wide)
    lscr[...] = mapped[:, :LANES]
    rscr[...] = mapped[:, LANES:]
    row_live = pick_rows(res_ref[...], row_start, rows)
    live = (mask_ref[...].astype(F32) * row_live).astype(BF16)
    width = rows * half
    spread_live = (iota((rows, width), 1) // half == iota((rows, width), 0)).astype(BF16)
    live_wide = dot(live, spread_live)
    sub = iota((seqs, LANES), 1) // half
    for tile in range(width // LANES):
        at = slice(tile * LANES, (tile + 1) * LANES)
        for ref, scr, first in ((left_ref, lscr, 0), (right_ref, rscr, LANES)):
            value = scr[pl.ds(tile * per, seqs, stride=rows), :]
            for k in range(1, per):
                value = jnp.where(sub == k, scr[pl.ds(tile * per + k, seqs, stride=rows), :], value)
            value = (value + bias[:, first:first + LANES]) * live_wide[:, at]
            ref[:, at] = value.astype(BF16)
    live_tile = dot(live, (iota((rows, LANES), 0) == iota((rows, LANES), 1)).astype(BF16))
    for ref in (left_ref, right_ref):
        ref[:, width:] = live_tile.astype(BF16)


def join_kernel(count, *refs):
    for n in range(count):
        refs[-1][n] = refs[n][...]


def pick_columns(values, start, size):
    total = values.shape[1]
    own = iota((size, total), 1) == iota((size, total), 0) + start
    spread = jnp.broadcast_to(values, (size, total)).astype(F32)
    return jnp.sum(jnp.where(own, spread, 0.0), axis=1, keepdims=True)


def pick_rows(values, start, size):
    total = values.shape[1]
    pick = (iota((total, size), 0) == iota((total, size), 1) + start).astype(BF16)
    return dot(jnp.broadcast_to(values.astype(F32), (8, total)).astype(BF16), pick)[0:1]


def base_kernel(pair_ref, table_ref, chain_ref, w_ref, base_ref, block_ref, tscr, wscr):
    rows, cols, channels = pair_ref.shape
    row_start = lax.axis_index("resi") * rows
    col_start = lax.axis_index(PLANE) * cols
    tscr[...] = jnp.zeros_like(tscr)
    tscr[0:table_ref.shape[0], :] = table_ref[...].astype(F32)
    table = tscr[...].astype(BF16)
    chain = chain_ref[...]
    same = pick_columns(chain, col_start, cols) == pick_rows(chain, row_start, rows)
    offset = iota((cols, rows), 0) + col_start - iota((cols, rows), 1) - row_start + RELMAX
    bins = jnp.where(same, jnp.clip(offset, 0, 2 * RELMAX), 2 * RELMAX + 1)
    lane = iota((cols, LANES), 1)
    for i in range(rows):
        one_hot = (lane == bins[:, i:i + 1]).astype(F32).astype(BF16)
        base_ref[i] = pair_ref[i].astype(F32) + dot(one_hot, table)
    wscr[...] = w_ref[...].astype(F32)
    half = int(round(w_ref.shape[0] ** 0.5))
    per = LANES // half
    block_ref[...] = jnp.zeros_like(block_ref)
    for d in range(half):
        value = wscr[pl.ds(d, half, stride=half), :].astype(BF16)
        for k in range(per):
            block_ref[pl.ds(d * LANES + k * half, half), k * channels:(k + 1) * channels] = value


def edges_kernel(count, *refs):
    pairs = count // 2
    rights, lefts = refs[:pairs], refs[pairs:pairs + 2]
    (base_ref, block_ref, res_ref, gain_ref, shift_ref, w_ref, bias_ref,
     updated_ref, left_ref, right_ref, nscr,
     lall, rall, tscr, rscr, oscr, escr) = refs[pairs + 2:]
    rows, cols, channels = base_ref.shape
    seqs = lefts[0].shape[1]
    half = block_ref.shape[0] // LANES
    per = LANES // half
    width = rows * half
    total_seqs = count * seqs
    z = lax.axis_index("resi")
    q = lax.axis_index(PLANE)
    row_start, col_start = z * rows, q * cols
    for step in range(pairs):
        for n in range(2):
            lall[q ^ (step + n * pairs)] = lefts[n][step]
            rall[z ^ (step + n * pairs)] = rights[step][n]
    right = rall[...].reshape(total_seqs, -1)
    left = lall[...].reshape(total_seqs, -1)
    for at in range(0, width, LANES):
        for s in range(0, total_seqs, LANES):
            tscr[s // LANES, at:at + LANES, :] = right[s:s + LANES, at:at + LANES].astype(F32).T
    for d in range(half):
        for s in range(0, total_seqs, LANES):
            turned = tscr[s // LANES, pl.ds(d, cols, stride=half), :]
            rscr[d * cols:(d + 1) * cols, s:s + LANES] = turned.astype(BF16)
    live_cols = right[:, width:].astype(F32).T[0:cols].astype(BF16)
    counts = dot(live_cols, left[:, width:])
    inverse = 1.0 / jnp.maximum(counts, 1.0)
    wide = 2 * LANES
    tall = 8
    for first in range(0, width, wide):
        for d0 in range(0, half, tall):
            product = dot(rscr[d0 * cols:(d0 + tall) * cols, :], left[:, first:first + wide])
            product = product.astype(BF16)
            for dd in range(tall):
                for t in range(wide // LANES):
                    g = first // LANES + t
                    oscr[g * cols:(g + 1) * cols, (d0 + dd) * LANES:(d0 + dd + 1) * LANES] = (
                        product[dd * cols:(dd + 1) * cols, t * LANES:(t + 1) * LANES])
    outer = dot(oscr[...], block_ref[...])
    for i in range(rows):
        g, k = i // per, i % per
        part = outer[g * cols:(g + 1) * cols, k * channels:(k + 1) * channels]
        updated = (base_ref[i] + part * inverse[:, i:i + 1]).astype(BF16)
        updated_ref[i] = updated
        normed = layer_norm(updated.astype(F32), gain_ref[...], shift_ref[...])
        nscr[i * cols:(i + 1) * cols, :] = normed.astype(BF16)
    live = pick_columns(res_ref[...], col_start, cols) * pick_rows(res_ref[...], row_start, rows)
    chunk = 8
    for i0 in range(0, rows, chunk):
        mixture = dot(nscr[i0 * cols:(i0 + chunk) * cols, :], w_ref[:, :4 * channels])
        mixture = mixture + bias_ref[:, :4 * channels]
        part = [mixture[:, n * channels:(n + 1) * channels] for n in range(4)]
        left_edge = sigmoid(part[0]) * part[1]
        right_edge = sigmoid(part[2]) * part[3]
        for ii in range(chunk):
            here = live[:, i0 + ii:i0 + ii + 1]
            at = slice(ii * cols, (ii + 1) * cols)
            left_ref[i0 + ii] = (left_edge[at] * here).astype(BF16)
            escr[(i0 + ii) * cols:(i0 + ii + 1) * cols, :] = right_edge[at] * here
    for k in range(cols):
        right_ref[k] = escr[pl.ds(k, rows, stride=cols), :].astype(BF16)


def gate_kernel(normed_ref, w_ref, bias_ref, gate_ref):
    first = w_ref.shape[1] - gate_ref.shape[1]
    gate_ref[...] = sigmoid(dot(normed_ref[...], w_ref[:, first:]) + bias_ref[:, first:])


def panel_kernel(*refs):
    *lefts, _, panel_ref = refs
    x = lax.axis_index("seq")
    for step, left in enumerate(lefts):
        panel_ref[x ^ step] = left[...].astype(F32).reshape(panel_ref.shape[1:])


def origin(step, chips):
    source = lax.axis_index("resi") ^ step
    return (source // chips) ^ lax.axis_index("resj"), source % chips


def add_block(panel_ref, chip, rscr, rows, before, store):
    cols = store.shape[0] // rows
    depth, channels = rscr.shape[0] // cols, rscr.shape[1]
    block = 8
    tiles = cols // 8

    def rows_body(at, carry):
        place = [[pl.ds(pl.multiple_of((at * block + b) * cols + t * 8, 8), 8) for t in range(tiles)]
                 for b in range(block)]
        if before is None:
            sums = [[jnp.zeros((8, channels), F32) for _ in range(tiles)] for _ in range(block)]
        else:
            sums = [[before[place[b][t], :] for t in range(tiles)] for b in range(block)]
        for k in range(depth):
            column = [rscr[k * cols + t * 8:k * cols + t * 8 + 8, :] for t in range(tiles)]
            for b in range(block):
                row = panel_ref[chip, pl.ds((at * block + b) * depth + k, 1), :]
                for t in range(tiles):
                    sums[b][t] = sums[b][t] + row * column[t]
        for b in range(block):
            for t in range(tiles):
                store[place[b][t], :] = sums[b][t].astype(store.dtype)
        return carry

    lax.fori_loop(0, rows // block, rows_body, 0)


def step_kernel(step, chips, fresh, right_ref, panel_ref, *refs):
    out_ref, rscr = refs[-2:]
    side, chip = origin(step, chips)
    rscr[...] = right_ref[...].astype(F32).reshape(rscr.shape)
    before = None if fresh else refs[0].at[side]
    add_block(panel_ref, chip, rscr, right_ref.shape[1], before, out_ref.at[side])


def last_kernel(side, steps, chips, first_ref, second_ref, panel_ref, sums_ref, out_ref, rscr):
    first_side, first_chip = origin(steps[0], chips)
    second_chip = origin(steps[1], chips)[1]
    mine = first_side == side

    @pl.when(mine)
    def _():
        rscr[...] = first_ref[...].astype(F32).reshape(rscr.shape)

    @pl.when(jnp.logical_not(mine))
    def _():
        rscr[...] = second_ref[...].astype(F32).reshape(rscr.shape)

    chip = jnp.where(mine, first_chip, second_chip)
    add_block(panel_ref, chip, rscr, first_ref.shape[1], sums_ref.at[side], out_ref)


def final_kernel(own_ref, other_ref, updated_ref, gate_ref, gain_ref, shift_ref, w_ref, bias_ref, out_ref):
    rows, cols, channels = out_ref.shape
    chunk = 8
    for i0 in range(0, rows, chunk):
        at = slice(i0 * cols, (i0 + chunk) * cols)
        sums = own_ref[at, :] + other_ref[at, :].astype(F32)
        normed = layer_norm(sums, gain_ref[...], shift_ref[...]).astype(BF16)
        result = dot(normed, w_ref[...]) + bias_ref[...]
        updated = updated_ref[i0:i0 + chunk].reshape(chunk * cols, channels).astype(F32)
        value = updated + gate_ref[at, :] * result
        out_ref[i0:i0 + chunk] = value.astype(BF16).reshape(chunk, cols, channels)


def swap_cores(block, count):
    return lax.ppermute(block, PLANE, [(p, p ^ (count // 2)) for p in range(count)])


def send_chips(block, chips):
    return [
        lax.ppermute(block, "seq", [(x, x ^ m) for x in range(chips)]) for m in range(1, chips)
    ]


def send_turned(block, count, steps):
    return [
        lax.ppermute(
            block, GROUP,
            [(z * count + p, (p ^ m) * count + z) for z in range(count) for p in range(count)])
        for m in range(steps)
    ]


def send_same_core(block, count, chips, steps):
    def target(z, p, m):
        core, x = p // chips, p % chips
        return ((z // chips * chips + x) ^ m) * count + core * chips + z % chips

    return [
        lax.ppermute(
            block, GROUP,
            [(z * count + p, target(z, p, m)) for z in range(count) for p in range(count)])
        for m in steps
    ]


def call(kernel, outs, scratch, args, flops=0, aliases=None, name=None):
    vmem = pl.BlockSpec(memory_space=pltpu.VMEM)
    size = sum(a.size * a.dtype.itemsize for a in args)
    return pl.pallas_call(
        kernel,
        out_shape=outs,
        in_specs=[vmem] * len(args),
        out_specs=[vmem] * len(outs) if isinstance(outs, list) else vmem,
        scratch_shapes=scratch,
        input_output_aliases=aliases or {},
        compiler_params=pltpu.CompilerParams(vmem_limit_bytes=40 * MIB),
        cost_estimate=pl.CostEstimate(flops=flops, bytes_accessed=size, transcendentals=0),
        name=name,
    )(*args)


def body(
    homolog_matrix,
    sequence_pad_mask,
    pair_features,
    residue_pad_mask,
    residue_chain_index,
    homolog_standard_factor,
    homolog_standard_offset,
    factor_mapping_matrices,
    outer_side_biases,
    outer_pair_projection,
    relative_position_table,
    pair_norm_gain,
    pair_norm_bias,
    triangle_projection_weights,
    triangle_projection_biases,
    triangle_sum_norm_gain,
    triangle_sum_norm_bias,
    triangle_output_weight,
    outer_pair_bias,
):
    rows, cols, channels = pair_features.shape
    seqs, _, depth = homolog_matrix.shape
    half = factor_mapping_matrices.shape[1] // 2
    per = LANES // half
    count = lax.axis_size(PLANE)
    width = rows * half
    flat = lambda v: v.reshape(1, -1)
    shape = jax.ShapeDtypeStruct
    residue = flat(residue_pad_mask)
    chain = flat(residue_chain_index)
    pack = shape((seqs, width + LANES), BF16)
    chips = lax.axis_size("seq")
    normed = call(norm_kernel, shape((seqs * rows, depth), F32), [], [homolog_matrix],
                  flops=1 << 36, name="norm")
    left, right = call(
        pack_kernel, [pack, pack],
        [pltpu.VMEM((seqs * rows, LANES), F32)] * 2,
        [normed, sequence_pad_mask, residue, flat(homolog_standard_factor),
         flat(homolog_standard_offset), factor_mapping_matrices.T, flat(outer_side_biases)],
        flops=1 << 30, name="pack")
    right_swap = swap_cores(right, count)
    left_blocks = [left] + send_chips(left, chips)
    base, block = call(
        base_kernel,
        [shape((rows, cols, channels), F32), shape((half * LANES, per * channels), BF16)],
        [pltpu.VMEM((LANES, channels), F32), pltpu.VMEM((half * half, channels), F32)],
        [pair_features, relative_position_table, chain, outer_pair_projection],
        flops=1 << 30, name="base")
    pair = call(functools.partial(join_kernel, 2), shape((2,) + pack.shape, BF16), [],
                [right, right_swap, base], name="join")
    rights = send_turned(pair, count, count // 2)
    own_lefts = call(functools.partial(join_kernel, chips), shape((chips,) + pack.shape, BF16), [],
                     left_blocks, name="join")
    lefts = [own_lefts, swap_cores(own_lefts, count)]
    updated, left_edge, right_edge, normed_pair = call(
        functools.partial(edges_kernel, count),
        [shape((rows, cols, channels), BF16), shape((rows, cols, channels), BF16),
         shape((cols, rows, channels), BF16), shape((rows * cols, channels), BF16)],
        [pltpu.VMEM((count, seqs, width + LANES), BF16), pltpu.VMEM((count, seqs, width + LANES), BF16),
         pltpu.VMEM((count * seqs // LANES, width, LANES), F32),
         pltpu.VMEM((width, count * seqs), BF16),
         pltpu.VMEM((rows // per * cols, half * LANES), BF16),
         pltpu.VMEM((rows * cols, channels), F32)],
        rights + lefts + [base, block, residue, flat(pair_norm_gain), flat(pair_norm_bias),
                          triangle_projection_weights, flat(triangle_projection_biases)],
        name="edges")
    steps = [m + n * chips for m in range(chips) for n in range(2)]
    right_edges = send_same_core(right_edge, count, chips, steps)
    left_edges = [left_edge] + send_chips(left_edge, chips)
    gate = call(gate_kernel, shape((rows * cols, channels), F32), [],
                [normed_pair, triangle_projection_weights, flat(triangle_projection_biases)],
                flops=1 << 30, name="gate")
    block_sums = shape((rows * cols, channels), F32)
    turned = pltpu.VMEM((rows * cols, channels), F32)
    panel = call(panel_kernel, shape((chips, rows * cols, channels), F32), [],
                 left_edges + [gate], name="panel")
    sums = []
    for n, step in enumerate(steps[:-2]):
        sums = [call(
            functools.partial(step_kernel, step, chips, n < 2), shape((2, rows * cols, channels), F32),
            [turned], [right_edges[n], panel] + sums, aliases={2: 0} if n else None, name="triangle")]
    last = right_edges[-2:] + [panel] + sums
    half_sums = call(
        functools.partial(last_kernel, 1, steps[-2:], chips), shape((rows * cols, channels), BF16),
        [turned], last, name="others")
    other_sums = swap_cores(half_sums, count)
    own_sums = call(
        functools.partial(last_kernel, 0, steps[-2:], chips), block_sums, [turned], last,
        flops=1 << 32, name="own")
    return call(
        final_kernel, shape((rows, cols, channels), BF16), [],
        [own_sums, other_sums, updated, gate, flat(triangle_sum_norm_gain),
         flat(triangle_sum_norm_bias), triangle_output_weight, flat(outer_pair_bias)],
        name="final")


def solution(mesh):
    pair = P(("groups", "resi"), ("resj", "seq"), None)
    placed = (
        P(("groups", "resj", "seq"), "resi", None),
        P(("groups", "resj", "seq"), "resi"),
        pair,
        P("groups"),
        P("groups"),
    ) + (P(),) * 14
    return jax.shard_map(body, mesh=mesh, in_specs=placed, out_specs=pair, check_vma=False)
```

```python
import functools

import jax
import jax.numpy as jnp
from jax import lax
from jax.experimental import pallas as pl
from jax.experimental.pallas import tpu as pltpu
from jax.sharding import PartitionSpec as P

RELMAX = 32
LANES = 128
PLANE = ("resj", "seq")
GROUP = ("resi", "resj", "seq")
F32 = jnp.float32
BF16 = jnp.bfloat16
MIB = 1 << 20


def iota(shape, axis):
    return lax.broadcasted_iota(jnp.int32, shape, axis)


def dot(a, b):
    return jnp.dot(a, b, preferred_element_type=F32)


def sigmoid(v):
    return 0.5 * jnp.tanh(0.5 * v) + 0.5


def layer_norm(values, gain, shift):
    average = jnp.mean(values, axis=-1, keepdims=True)
    centred = values - average
    variance = jnp.mean(centred * centred, axis=-1, keepdims=True)
    return centred * lax.rsqrt(variance + 1e-05) * gain + shift


def norm_kernel(x_ref, out_ref):
    x = x_ref[...].reshape(out_ref.shape).astype(F32)
    out_ref[...] = layer_norm(x, 1.0, 0.0)


def pack_kernel(x_ref, mask_ref, res_ref, gain_ref, shift_ref, w_ref, bias_ref,
                left_ref, right_ref, lscr, rscr):
    seqs, rows = mask_ref.shape
    half = w_ref.shape[0] // 2
    per = LANES // half
    row_start = lax.axis_index("resi") * rows
    normed = (x_ref[...] * gain_ref[...] + shift_ref[...]).astype(BF16)
    lane = iota((2 * half, 2 * LANES), 1)
    spread = lane % half + jnp.where(lane >= LANES, half, 0) == iota((2 * half, 2 * LANES), 0)
    spread = spread.astype(F32)
    wide = lax.dot_general(
        w_ref[...], spread.astype(BF16), (((0,), (0,)), ((), ())), preferred_element_type=F32)
    wide = wide.astype(BF16)
    bias = jnp.dot(jnp.broadcast_to(bias_ref[...], (8, 2 * half)), spread,
                   precision=lax.Precision.HIGHEST, preferred_element_type=F32)[0:1]
    mapped = dot(normed, wide)
    lscr[...] = mapped[:, :LANES]
    rscr[...] = mapped[:, LANES:]
    row_live = pick_rows(res_ref[...], row_start, rows)
    live = (mask_ref[...].astype(F32) * row_live).astype(BF16)
    width = rows * half
    spread_live = (iota((rows, width), 1) // half == iota((rows, width), 0)).astype(BF16)
    live_wide = dot(live, spread_live)
    sub = iota((seqs, LANES), 1) // half
    for tile in range(width // LANES):
        at = slice(tile * LANES, (tile + 1) * LANES)
        for ref, scr, first in ((left_ref, lscr, 0), (right_ref, rscr, LANES)):
            value = scr[pl.ds(tile * per, seqs, stride=rows), :]
            for k in range(1, per):
                value = jnp.where(sub == k, scr[pl.ds(tile * per + k, seqs, stride=rows), :], value)
            value = (value + bias[:, first:first + LANES]) * live_wide[:, at]
            ref[:, at] = value.astype(BF16)
    live_tile = dot(live, (iota((rows, LANES), 0) == iota((rows, LANES), 1)).astype(BF16))
    for ref in (left_ref, right_ref):
        ref[:, width:] = live_tile.astype(BF16)


def join_kernel(count, *refs):
    for n in range(count):
        refs[-1][n] = refs[n][...]


def pick_columns(values, start, size):
    total = values.shape[1]
    own = iota((size, total), 1) == iota((size, total), 0) + start
    spread = jnp.broadcast_to(values, (size, total)).astype(F32)
    return jnp.sum(jnp.where(own, spread, 0.0), axis=1, keepdims=True)


def pick_rows(values, start, size):
    total = values.shape[1]
    pick = (iota((total, size), 0) == iota((total, size), 1) + start).astype(BF16)
    return dot(jnp.broadcast_to(values.astype(F32), (8, total)).astype(BF16), pick)[0:1]


def base_kernel(pair_ref, table_ref, chain_ref, w_ref, base_ref, block_ref, tscr, wscr):
    rows, cols, channels = pair_ref.shape
    row_start = lax.axis_index("resi") * rows
    col_start = lax.axis_index(PLANE) * cols
    tscr[...] = jnp.zeros_like(tscr)
    tscr[0:table_ref.shape[0], :] = table_ref[...].astype(F32)
    table = tscr[...].astype(BF16)
    chain = chain_ref[...]
    same = pick_columns(chain, col_start, cols) == pick_rows(chain, row_start, rows)
    offset = iota((cols, rows), 0) + col_start - iota((cols, rows), 1) - row_start + RELMAX
    bins = jnp.where(same, jnp.clip(offset, 0, 2 * RELMAX), 2 * RELMAX + 1)
    lane = iota((cols, LANES), 1)
    for i in range(rows):
        one_hot = (lane == bins[:, i:i + 1]).astype(F32).astype(BF16)
        base_ref[i] = pair_ref[i].astype(F32) + dot(one_hot, table)
    wscr[...] = w_ref[...].astype(F32)
    half = int(round(w_ref.shape[0] ** 0.5))
    per = LANES // half
    block_ref[...] = jnp.zeros_like(block_ref)
    for d in range(half):
        value = wscr[pl.ds(d, half, stride=half), :].astype(BF16)
        for k in range(per):
            block_ref[pl.ds(d * LANES + k * half, half), k * channels:(k + 1) * channels] = value


def turn_kernel(count, *refs):
    pairs = count // 2
    rights, (turned_ref, live_ref, rall, tscr) = refs[:pairs], refs[pairs:]
    z = lax.axis_index("resi")
    width, total_seqs = turned_ref.shape
    cols = live_ref.shape[0]
    half = width // cols
    for step in range(pairs):
        for n in range(2):
            rall[z ^ (step + n * pairs)] = rights[step][n]
    right = rall[...].reshape(total_seqs, -1)
    for at in range(0, width, LANES):
        for s in range(0, total_seqs, LANES):
            tscr[s // LANES, at:at + LANES, :] = right[s:s + LANES, at:at + LANES].astype(F32).T
    for d in range(half):
        for s in range(0, total_seqs, LANES):
            turned = tscr[s // LANES, pl.ds(d, cols, stride=half), :]
            turned_ref[d * cols:(d + 1) * cols, s:s + LANES] = turned.astype(BF16)
    live_ref[...] = right[:, width:].astype(F32).T[0:cols].astype(BF16)


def edges_kernel(turned_ref, live_ref, own_ref, swapped_ref, base_ref, block_ref, res_ref,
                 gain_ref, shift_ref, w_ref, bias_ref,
                 updated_ref, left_ref, right_ref, nscr, lall, oscr, escr):
    rows, cols, channels = base_ref.shape
    chips, seqs = own_ref.shape[:2]
    half = block_ref.shape[0] // LANES
    per = LANES // half
    width = rows * half
    q = lax.axis_index(PLANE)
    row_start, col_start = lax.axis_index("resi") * rows, q * cols
    for step in range(chips):
        lall[q ^ step] = own_ref[step]
        lall[q ^ (chips + step)] = swapped_ref[step]
    left = lall[...].reshape(2 * chips * seqs, -1)
    counts = dot(live_ref[...], left[:, width:])
    inverse = 1.0 / jnp.maximum(counts, 1.0)
    wide = 2 * LANES
    tall = 8
    for first in range(0, width, wide):
        for d0 in range(0, half, tall):
            product = dot(turned_ref[d0 * cols:(d0 + tall) * cols, :], left[:, first:first + wide])
            product = product.astype(BF16)
            for dd in range(tall):
                for t in range(wide // LANES):
                    g = first // LANES + t
                    oscr[g * cols:(g + 1) * cols, (d0 + dd) * LANES:(d0 + dd + 1) * LANES] = (
                        product[dd * cols:(dd + 1) * cols, t * LANES:(t + 1) * LANES])
    outer = dot(oscr[...], block_ref[...])
    for i in range(rows):
        g, k = i // per, i % per
        part = outer[g * cols:(g + 1) * cols, k * channels:(k + 1) * channels]
        updated = (base_ref[i] + part * inverse[:, i:i + 1]).astype(BF16)
        updated_ref[i] = updated
        normed = layer_norm(updated.astype(F32), gain_ref[...], shift_ref[...])
        nscr[i * cols:(i + 1) * cols, :] = normed.astype(BF16)
    live = pick_columns(res_ref[...], col_start, cols) * pick_rows(res_ref[...], row_start, rows)
    chunk = 8
    for i0 in range(0, rows, chunk):
        mixture = dot(nscr[i0 * cols:(i0 + chunk) * cols, :], w_ref[:, :4 * channels])
        mixture = mixture + bias_ref[:, :4 * channels]
        part = [mixture[:, n * channels:(n + 1) * channels] for n in range(4)]
        left_edge = sigmoid(part[0]) * part[1]
        right_edge = sigmoid(part[2]) * part[3]
        for ii in range(chunk):
            here = live[:, i0 + ii:i0 + ii + 1]
            at = slice(ii * cols, (ii + 1) * cols)
            left_ref[i0 + ii] = (left_edge[at] * here).astype(BF16)
            escr[(i0 + ii) * cols:(i0 + ii + 1) * cols, :] = right_edge[at] * here
    for k in range(cols):
        right_ref[k] = escr[pl.ds(k, rows, stride=cols), :].astype(BF16)


def gate_kernel(normed_ref, w_ref, bias_ref, gate_ref):
    first = w_ref.shape[1] - gate_ref.shape[1]
    gate_ref[...] = sigmoid(dot(normed_ref[...], w_ref[:, first:]) + bias_ref[:, first:])


def panel_kernel(*refs):
    *lefts, _, panel_ref = refs
    x = lax.axis_index("seq")
    for step, left in enumerate(lefts):
        panel_ref[x ^ step] = left[...].astype(F32).reshape(panel_ref.shape[1:])


def source_of(z, x, step, chips):
    block = z ^ step ^ (x % 2 if step >= chips else 0)
    return block // chips, block % chips


def add_block(panel_ref, chip, rscr, rows, before, store):
    cols = store.shape[0] // rows
    depth, channels = rscr.shape[0] // cols, rscr.shape[1]
    block = 8
    tiles = cols // 8

    def rows_body(at, carry):
        place = [[pl.ds(pl.multiple_of((at * block + b) * cols + t * 8, 8), 8) for t in range(tiles)]
                 for b in range(block)]
        if before is None:
            sums = [[jnp.zeros((8, channels), F32) for _ in range(tiles)] for _ in range(block)]
        else:
            sums = [[before[place[b][t], :] for t in range(tiles)] for b in range(block)]
        for k in range(depth):
            column = [rscr[k * cols + t * 8:k * cols + t * 8 + 8, :] for t in range(tiles)]
            for b in range(block):
                row = panel_ref[chip, pl.ds((at * block + b) * depth + k, 1), :]
                for t in range(tiles):
                    sums[b][t] = sums[b][t] + row * column[t]
        for b in range(block):
            for t in range(tiles):
                store[place[b][t], :] = sums[b][t].astype(store.dtype)
        return carry

    lax.fori_loop(0, rows // block, rows_body, 0)


def step_kernel(step, chips, fresh, right_ref, panel_ref, *refs):
    out_ref, rscr = refs[-2:]
    chip = source_of(lax.axis_index("resi"), lax.axis_index("seq"), step, chips)[1]
    rscr[...] = right_ref[...].astype(F32).reshape(rscr.shape)
    add_block(panel_ref, chip, rscr, right_ref.shape[1], None if fresh else refs[0], out_ref)


def last_kernel(step, chips, right_ref, panel_ref, far_ref, near_ref, own_ref, other_ref, rscr, acc):
    step_kernel(step, chips, False, right_ref, panel_ref, far_ref, acc, rscr)
    mine = lax.axis_index("resi") // chips == lax.axis_index("resj")

    @pl.when(mine)
    def _():
        own_ref[...] = near_ref[...]
        other_ref[...] = acc[...].astype(BF16)

    @pl.when(jnp.logical_not(mine))
    def _():
        own_ref[...] = acc[...]
        other_ref[...] = near_ref[...].astype(BF16)


def final_kernel(own_ref, other_ref, updated_ref, gate_ref, gain_ref, shift_ref, w_ref, bias_ref, out_ref):
    rows, cols, channels = out_ref.shape
    chunk = 8
    for i0 in range(0, rows, chunk):
        at = slice(i0 * cols, (i0 + chunk) * cols)
        sums = own_ref[at, :] + other_ref[at, :].astype(F32)
        normed = layer_norm(sums, gain_ref[...], shift_ref[...]).astype(BF16)
        result = dot(normed, w_ref[...]) + bias_ref[...]
        updated = updated_ref[i0:i0 + chunk].reshape(chunk * cols, channels).astype(F32)
        value = updated + gate_ref[at, :] * result
        out_ref[i0:i0 + chunk] = value.astype(BF16).reshape(chunk, cols, channels)


def swap_cores(block, count):
    return lax.ppermute(block, PLANE, [(p, p ^ (count // 2)) for p in range(count)])


def send_chips(block, chips):
    return [
        lax.ppermute(block, "seq", [(x, x ^ m) for x in range(chips)]) for m in range(1, chips)
    ]


def send_turned(block, count, steps):
    return [
        lax.ppermute(
            block, GROUP,
            [(z * count + p, (p ^ m) * count + z) for z in range(count) for p in range(count)])
        for m in range(steps)
    ]


def send_same_core(block, count, chips, step):
    pairs = []
    for z in range(count):
        for p in range(count):
            core, x = p // chips, p % chips
            far, chip = source_of(z, x, step, chips)
            pairs.append(((far * chips + x) * count + core * chips + chip, z * count + p))
    return lax.ppermute(block, GROUP, pairs)


def pass_on(block, count):
    return lax.ppermute(block, "resi", [(z, z ^ 1) for z in range(count)])


def call(kernel, outs, scratch, args, flops=0, aliases=None, name=None):
    vmem = pl.BlockSpec(memory_space=pltpu.VMEM)
    size = sum(a.size * a.dtype.itemsize for a in args)
    return pl.pallas_call(
        kernel,
        out_shape=outs,
        in_specs=[vmem] * len(args),
        out_specs=[vmem] * len(outs) if isinstance(outs, list) else vmem,
        scratch_shapes=scratch,
        input_output_aliases=aliases or {},
        compiler_params=pltpu.CompilerParams(vmem_limit_bytes=40 * MIB),
        cost_estimate=pl.CostEstimate(flops=flops, bytes_accessed=size, transcendentals=0),
        name=name,
    )(*args)


def body(
    homolog_matrix,
    sequence_pad_mask,
    pair_features,
    residue_pad_mask,
    residue_chain_index,
    homolog_standard_factor,
    homolog_standard_offset,
    factor_mapping_matrices,
    outer_side_biases,
    outer_pair_projection,
    relative_position_table,
    pair_norm_gain,
    pair_norm_bias,
    triangle_projection_weights,
    triangle_projection_biases,
    triangle_sum_norm_gain,
    triangle_sum_norm_bias,
    triangle_output_weight,
    outer_pair_bias,
):
    rows, cols, channels = pair_features.shape
    seqs, _, depth = homolog_matrix.shape
    half = factor_mapping_matrices.shape[1] // 2
    per = LANES // half
    count = lax.axis_size(PLANE)
    width = rows * half
    flat = lambda v: v.reshape(1, -1)
    shape = jax.ShapeDtypeStruct
    residue = flat(residue_pad_mask)
    chain = flat(residue_chain_index)
    pack = shape((seqs, width + LANES), BF16)
    chips = lax.axis_size("seq")
    normed = call(norm_kernel, shape((seqs * rows, depth), F32), [], [homolog_matrix],
                  flops=1 << 36, name="norm")
    left, right = call(
        pack_kernel, [pack, pack],
        [pltpu.VMEM((seqs * rows, LANES), F32)] * 2,
        [normed, sequence_pad_mask, residue, flat(homolog_standard_factor),
         flat(homolog_standard_offset), factor_mapping_matrices.T, flat(outer_side_biases)],
        flops=1 << 30, name="pack")
    right_swap = swap_cores(right, count)
    left_blocks = [left] + send_chips(left, chips)
    base, block = call(
        base_kernel,
        [shape((rows, cols, channels), F32), shape((half * LANES, per * channels), BF16)],
        [pltpu.VMEM((LANES, channels), F32), pltpu.VMEM((half * half, channels), F32)],
        [pair_features, relative_position_table, chain, outer_pair_projection],
        flops=1 << 30, name="base")
    pair = call(functools.partial(join_kernel, 2), shape((2,) + pack.shape, BF16), [],
                [right, right_swap, base], name="join")
    rights = send_turned(pair, count, count // 2)
    own_lefts = call(functools.partial(join_kernel, chips), shape((chips,) + pack.shape, BF16), [],
                     left_blocks, name="join")
    lefts = [own_lefts, swap_cores(own_lefts, count)]
    turned, live = call(
        functools.partial(turn_kernel, count),
        [shape((width, count * seqs), BF16), shape((cols, count * seqs), BF16)],
        [pltpu.VMEM((count,) + pack.shape, BF16),
         pltpu.VMEM((count * seqs // LANES, width, LANES), F32)],
        rights, flops=1 << 36, name="turn")
    updated, left_edge, right_edge, normed_pair = call(
        edges_kernel,
        [shape((rows, cols, channels), BF16), shape((rows, cols, channels), BF16),
         shape((cols, rows, channels), BF16), shape((rows * cols, channels), BF16)],
        [pltpu.VMEM((count,) + pack.shape, BF16),
         pltpu.VMEM((rows // per * cols, half * LANES), BF16),
         pltpu.VMEM((rows * cols, channels), F32)],
        [turned, live] + lefts + [
            base, block, residue, flat(pair_norm_gain), flat(pair_norm_bias),
            triangle_projection_weights, flat(triangle_projection_biases)],
        name="edges")
    right_edges = [send_same_core(right_edge, count, chips, step) for step in range(chips)]
    for step in range(chips, count, 2):
        block_far = send_same_core(right_edge, count, chips, step)
        right_edges += [block_far, pass_on(block_far, count)]
    left_edges = [left_edge] + send_chips(left_edge, chips)
    gate = call(gate_kernel, shape((rows * cols, channels), F32), [],
                [normed_pair, triangle_projection_weights, flat(triangle_projection_biases)],
                flops=1 << 30, name="gate")
    block_sums = shape((rows * cols, channels), F32)
    scratch = pltpu.VMEM((rows * cols, channels), F32)
    panel = call(panel_kernel, shape((chips, rows * cols, channels), F32), [],
                 left_edges + [gate], name="panel")
    near, far = [], []
    for step in range(count - 1):
        sums = near if step < chips else far
        sums[:] = [call(
            functools.partial(step_kernel, step, chips, not sums), block_sums, [scratch],
            [right_edges[step], panel] + sums, name="triangle")]
    own_sums, half_sums = call(
        functools.partial(last_kernel, count - 1, chips),
        [block_sums, shape((rows * cols, channels), BF16)], [scratch, scratch],
        [right_edges[-1], panel] + far + near, name="last")
    other_sums = swap_cores(half_sums, count)
    return call(
        final_kernel, shape((rows, cols, channels), BF16), [],
        [own_sums, other_sums, updated, gate, flat(triangle_sum_norm_gain),
         flat(triangle_sum_norm_bias), triangle_output_weight, flat(outer_pair_bias)],
        name="final")


def solution(mesh):
    pair = P(("groups", "resi"), ("resj", "seq"), None)
    placed = (
        P(("groups", "resj", "seq"), "resi", None),
        P(("groups", "resj", "seq"), "resi"),
        pair,
        P("groups"),
        P("groups"),
    ) + (P(),) * 14
    return jax.shard_map(body, mesh=mesh, in_specs=placed, out_specs=pair, check_vma=False)
```

```python
import functools

import jax
import jax.numpy as jnp
from jax import lax
from jax.experimental import pallas as pl
from jax.experimental.pallas import tpu as pltpu
from jax.sharding import PartitionSpec as P

RELMAX = 32
LANES = 128
PLANE = ("resj", "seq")
GROUP = ("resi", "resj", "seq")
F32 = jnp.float32
BF16 = jnp.bfloat16
MIB = 1 << 20


def iota(shape, axis):
    return lax.broadcasted_iota(jnp.int32, shape, axis)


def dot(a, b):
    return jnp.dot(a, b, preferred_element_type=F32)


def sigmoid(v):
    return 0.5 * jnp.tanh(0.5 * v) + 0.5


def layer_norm(values, gain, shift):
    average = jnp.mean(values, axis=-1, keepdims=True)
    centred = values - average
    variance = jnp.mean(centred * centred, axis=-1, keepdims=True)
    return centred * lax.rsqrt(variance + 1e-05) * gain + shift


def norm_kernel(x_ref, out_ref):
    x = x_ref[...].reshape(out_ref.shape).astype(F32)
    out_ref[...] = layer_norm(x, 1.0, 0.0)


def pack_kernel(x_ref, mask_ref, res_ref, gain_ref, shift_ref, w_ref, bias_ref,
                left_ref, right_ref, lscr, rscr):
    seqs, rows = mask_ref.shape
    half = w_ref.shape[0] // 2
    per = LANES // half
    row_start = lax.axis_index("resi") * rows
    normed = (x_ref[...] * gain_ref[...] + shift_ref[...]).astype(BF16)
    lane = iota((2 * half, 2 * LANES), 1)
    spread = lane % half + jnp.where(lane >= LANES, half, 0) == iota((2 * half, 2 * LANES), 0)
    spread = spread.astype(F32)
    wide = lax.dot_general(
        w_ref[...], spread.astype(BF16), (((0,), (0,)), ((), ())), preferred_element_type=F32)
    wide = wide.astype(BF16)
    bias = jnp.dot(jnp.broadcast_to(bias_ref[...], (8, 2 * half)), spread,
                   precision=lax.Precision.HIGHEST, preferred_element_type=F32)[0:1]
    mapped = dot(normed, wide)
    lscr[...] = mapped[:, :LANES]
    rscr[...] = mapped[:, LANES:]
    row_live = pick_rows(res_ref[...], row_start, rows)
    live = (mask_ref[...].astype(F32) * row_live).astype(BF16)
    width = rows * half
    spread_live = (iota((rows, width), 1) // half == iota((rows, width), 0)).astype(BF16)
    live_wide = dot(live, spread_live)
    sub = iota((seqs, LANES), 1) // half
    for tile in range(width // LANES):
        at = slice(tile * LANES, (tile + 1) * LANES)
        for ref, scr, first in ((left_ref, lscr, 0), (right_ref, rscr, LANES)):
            value = scr[pl.ds(tile * per, seqs, stride=rows), :]
            for k in range(1, per):
                value = jnp.where(sub == k, scr[pl.ds(tile * per + k, seqs, stride=rows), :], value)
            value = (value + bias[:, first:first + LANES]) * live_wide[:, at]
            ref[:, at] = value.astype(BF16)
    live_tile = dot(live, (iota((rows, LANES), 0) == iota((rows, LANES), 1)).astype(BF16))
    for ref in (left_ref, right_ref):
        ref[:, width:] = live_tile.astype(BF16)


def join_kernel(count, *refs):
    for n in range(count):
        refs[-1][n] = refs[n][...]


def pick_columns(values, start, size):
    total = values.shape[1]
    own = iota((size, total), 1) == iota((size, total), 0) + start
    spread = jnp.broadcast_to(values, (size, total)).astype(F32)
    return jnp.sum(jnp.where(own, spread, 0.0), axis=1, keepdims=True)


def pick_rows(values, start, size):
    total = values.shape[1]
    pick = (iota((total, size), 0) == iota((total, size), 1) + start).astype(BF16)
    return dot(jnp.broadcast_to(values.astype(F32), (8, total)).astype(BF16), pick)[0:1]


def base_kernel(pair_ref, table_ref, chain_ref, w_ref, base_ref, block_ref, tscr, wscr):
    rows, cols, channels = pair_ref.shape
    row_start = lax.axis_index("resi") * rows
    col_start = lax.axis_index(PLANE) * cols
    tscr[...] = jnp.zeros_like(tscr)
    tscr[0:table_ref.shape[0], :] = table_ref[...].astype(F32)
    table = tscr[...].astype(BF16)
    chain = chain_ref[...]
    same = pick_columns(chain, col_start, cols) == pick_rows(chain, row_start, rows)
    offset = iota((cols, rows), 0) + col_start - iota((cols, rows), 1) - row_start + RELMAX
    bins = jnp.where(same, jnp.clip(offset, 0, 2 * RELMAX), 2 * RELMAX + 1)
    lane = iota((cols, LANES), 1)
    for i in range(rows):
        one_hot = (lane == bins[:, i:i + 1]).astype(F32).astype(BF16)
        base_ref[i] = pair_ref[i].astype(F32) + dot(one_hot, table)
    wscr[...] = w_ref[...].astype(F32)
    half = int(round(w_ref.shape[0] ** 0.5))
    per = LANES // half
    block_ref[...] = jnp.zeros_like(block_ref)
    for d in range(half):
        value = wscr[pl.ds(d, half, stride=half), :].astype(BF16)
        for k in range(per):
            block_ref[pl.ds(d * LANES + k * half, half), k * channels:(k + 1) * channels] = value


def turn_kernel(count, *refs):
    pairs = count // 2
    rights, (turned_ref, live_ref, rall, tscr) = refs[:pairs], refs[pairs:]
    z = lax.axis_index("resi")
    width, total_seqs = turned_ref.shape
    cols = live_ref.shape[0]
    half = width // cols
    for step in range(pairs):
        for n in range(2):
            rall[z ^ (step + n * pairs)] = rights[step][n]
    right = rall[...].reshape(total_seqs, -1)
    for at in range(0, width, LANES):
        for s in range(0, total_seqs, LANES):
            tscr[s // LANES, at:at + LANES, :] = right[s:s + LANES, at:at + LANES].astype(F32).T
    for d in range(half):
        for s in range(0, total_seqs, LANES):
            turned = tscr[s // LANES, pl.ds(d, cols, stride=half), :]
            turned_ref[d * cols:(d + 1) * cols, s:s + LANES] = turned.astype(BF16)
    live_ref[...] = right[:, width:].astype(F32).T[0:cols].astype(BF16)


def edges_kernel(turned_ref, live_ref, own_ref, swapped_ref, base_ref, block_ref, res_ref,
                 gain_ref, shift_ref, w_ref, bias_ref,
                 updated_ref, left_ref, right_ref, nscr, lall, oscr, escr):
    rows, cols, channels = base_ref.shape
    chips, seqs = own_ref.shape[:2]
    half = block_ref.shape[0] // LANES
    per = LANES // half
    width = rows * half
    q = lax.axis_index(PLANE)
    row_start, col_start = lax.axis_index("resi") * rows, q * cols
    for step in range(chips):
        lall[q ^ step] = own_ref[step]
        lall[q ^ (chips + step)] = swapped_ref[step]
    left = lall[...].reshape(2 * chips * seqs, -1)
    counts = dot(live_ref[...], left[:, width:])
    inverse = 1.0 / jnp.maximum(counts, 1.0)
    wide = 2 * LANES
    tall = 8
    for first in range(0, width, wide):
        for d0 in range(0, half, tall):
            product = dot(turned_ref[d0 * cols:(d0 + tall) * cols, :], left[:, first:first + wide])
            product = product.astype(BF16)
            for dd in range(tall):
                for t in range(wide // LANES):
                    g = first // LANES + t
                    oscr[g * cols:(g + 1) * cols, (d0 + dd) * LANES:(d0 + dd + 1) * LANES] = (
                        product[dd * cols:(dd + 1) * cols, t * LANES:(t + 1) * LANES])
    outer = dot(oscr[...], block_ref[...])
    for i in range(rows):
        g, k = i // per, i % per
        part = outer[g * cols:(g + 1) * cols, k * channels:(k + 1) * channels]
        updated = (base_ref[i] + part * inverse[:, i:i + 1]).astype(BF16)
        updated_ref[i] = updated
        normed = layer_norm(updated.astype(F32), gain_ref[...], shift_ref[...])
        nscr[i * cols:(i + 1) * cols, :] = normed.astype(BF16)
    live = pick_columns(res_ref[...], col_start, cols) * pick_rows(res_ref[...], row_start, rows)
    chunk = 8
    for i0 in range(0, rows, chunk):
        mixture = dot(nscr[i0 * cols:(i0 + chunk) * cols, :], w_ref[:, :4 * channels])
        mixture = mixture + bias_ref[:, :4 * channels]
        part = [mixture[:, n * channels:(n + 1) * channels] for n in range(4)]
        left_edge = sigmoid(part[0]) * part[1]
        right_edge = sigmoid(part[2]) * part[3]
        for ii in range(chunk):
            here = live[:, i0 + ii:i0 + ii + 1]
            at = slice(ii * cols, (ii + 1) * cols)
            left_ref[i0 + ii] = (left_edge[at] * here).astype(BF16)
            escr[(i0 + ii) * cols:(i0 + ii + 1) * cols, :] = right_edge[at] * here
    for k in range(cols):
        right_ref[k] = escr[pl.ds(k, rows, stride=cols), :].astype(BF16)


def gate_kernel(normed_ref, w_ref, bias_ref, gate_ref):
    first = w_ref.shape[1] - gate_ref.shape[1]
    gate_ref[...] = sigmoid(dot(normed_ref[...], w_ref[:, first:]) + bias_ref[:, first:])


def panel_kernel(*refs):
    *lefts, _, panel_ref = refs
    x = lax.axis_index("seq")
    for step, left in enumerate(lefts):
        panel_ref[x ^ step] = left[...].astype(F32).reshape(panel_ref.shape[1:])


def source_of(z, core, x, step, chips):
    block = z ^ step ^ ((x + core) % 2 if step >= chips else 0)
    return block // chips, block % chips


def add_block(panel_ref, chip, rscr, rows, before, store):
    cols = store.shape[0] // rows
    depth, channels = rscr.shape[0] // cols, rscr.shape[1]
    block = 8
    tiles = cols // 8

    def rows_body(at, carry):
        place = [[pl.ds(pl.multiple_of((at * block + b) * cols + t * 8, 8), 8) for t in range(tiles)]
                 for b in range(block)]
        if before is None:
            sums = [[jnp.zeros((8, channels), F32) for _ in range(tiles)] for _ in range(block)]
        else:
            sums = [[before[place[b][t], :] for t in range(tiles)] for b in range(block)]
        for k in range(depth):
            column = [rscr[k * cols + t * 8:k * cols + t * 8 + 8, :] for t in range(tiles)]
            for b in range(block):
                row = panel_ref[chip, pl.ds((at * block + b) * depth + k, 1), :]
                for t in range(tiles):
                    sums[b][t] = sums[b][t] + row * column[t]
        for b in range(block):
            for t in range(tiles):
                store[place[b][t], :] = sums[b][t].astype(store.dtype)
        return carry

    lax.fori_loop(0, rows // block, rows_body, 0)


def step_kernel(step, chips, fresh, right_ref, panel_ref, *refs):
    out_ref, rscr = refs[-2:]
    z, core, x = [lax.axis_index(axis) for axis in GROUP]
    chip = source_of(z, core, x, step, chips)[1]
    rscr[...] = right_ref[...].astype(F32).reshape(rscr.shape)
    add_block(panel_ref, chip, rscr, right_ref.shape[1], None if fresh else refs[0], out_ref)


def last_kernel(step, chips, right_ref, panel_ref, far_ref, near_ref, own_ref, other_ref, rscr, acc):
    step_kernel(step, chips, False, right_ref, panel_ref, far_ref, acc, rscr)
    mine = lax.axis_index("resi") // chips == lax.axis_index("resj")

    @pl.when(mine)
    def _():
        own_ref[...] = near_ref[...]
        other_ref[...] = acc[...].astype(BF16)

    @pl.when(jnp.logical_not(mine))
    def _():
        own_ref[...] = acc[...]
        other_ref[...] = near_ref[...].astype(BF16)


def final_kernel(own_ref, other_ref, updated_ref, gate_ref, gain_ref, shift_ref, w_ref, bias_ref, out_ref):
    rows, cols, channels = out_ref.shape
    chunk = 8
    for i0 in range(0, rows, chunk):
        at = slice(i0 * cols, (i0 + chunk) * cols)
        sums = own_ref[at, :] + other_ref[at, :].astype(F32)
        normed = layer_norm(sums, gain_ref[...], shift_ref[...]).astype(BF16)
        result = dot(normed, w_ref[...]) + bias_ref[...]
        updated = updated_ref[i0:i0 + chunk].reshape(chunk * cols, channels).astype(F32)
        value = updated + gate_ref[at, :] * result
        out_ref[i0:i0 + chunk] = value.astype(BF16).reshape(chunk, cols, channels)


def swap_cores(block, count):
    return lax.ppermute(block, PLANE, [(p, p ^ (count // 2)) for p in range(count)])


def send_chips(block, chips):
    return [
        lax.ppermute(block, "seq", [(x, x ^ m) for x in range(chips)]) for m in range(1, chips)
    ]


def send_turned(block, count, steps):
    return [
        lax.ppermute(
            block, GROUP,
            [(z * count + p, (p ^ m) * count + z) for z in range(count) for p in range(count)])
        for m in range(steps)
    ]


def send_same_core(block, count, chips, step):
    pairs = []
    for z in range(count):
        for p in range(count):
            core, x = p // chips, p % chips
            far, chip = source_of(z, core, x, step, chips)
            pairs.append(((far * chips + x) * count + core * chips + chip, z * count + p))
    return lax.ppermute(block, GROUP, pairs)


def pass_on(block, count):
    return lax.ppermute(block, "resi", [(z, z ^ 1) for z in range(count)])


def call(kernel, outs, scratch, args, flops=0, aliases=None, name=None):
    vmem = pl.BlockSpec(memory_space=pltpu.VMEM)
    size = sum(a.size * a.dtype.itemsize for a in args)
    return pl.pallas_call(
        kernel,
        out_shape=outs,
        in_specs=[vmem] * len(args),
        out_specs=[vmem] * len(outs) if isinstance(outs, list) else vmem,
        scratch_shapes=scratch,
        input_output_aliases=aliases or {},
        compiler_params=pltpu.CompilerParams(vmem_limit_bytes=40 * MIB),
        cost_estimate=pl.CostEstimate(flops=flops, bytes_accessed=size, transcendentals=0),
        name=name,
    )(*args)


def body(
    homolog_matrix,
    sequence_pad_mask,
    pair_features,
    residue_pad_mask,
    residue_chain_index,
    homolog_standard_factor,
    homolog_standard_offset,
    factor_mapping_matrices,
    outer_side_biases,
    outer_pair_projection,
    relative_position_table,
    pair_norm_gain,
    pair_norm_bias,
    triangle_projection_weights,
    triangle_projection_biases,
    triangle_sum_norm_gain,
    triangle_sum_norm_bias,
    triangle_output_weight,
    outer_pair_bias,
):
    rows, cols, channels = pair_features.shape
    seqs, _, depth = homolog_matrix.shape
    half = factor_mapping_matrices.shape[1] // 2
    per = LANES // half
    count = lax.axis_size(PLANE)
    width = rows * half
    flat = lambda v: v.reshape(1, -1)
    shape = jax.ShapeDtypeStruct
    residue = flat(residue_pad_mask)
    chain = flat(residue_chain_index)
    pack = shape((seqs, width + LANES), BF16)
    chips = lax.axis_size("seq")
    normed = call(norm_kernel, shape((seqs * rows, depth), F32), [], [homolog_matrix],
                  flops=1 << 36, name="norm")
    left, right = call(
        pack_kernel, [pack, pack],
        [pltpu.VMEM((seqs * rows, LANES), F32)] * 2,
        [normed, sequence_pad_mask, residue, flat(homolog_standard_factor),
         flat(homolog_standard_offset), factor_mapping_matrices.T, flat(outer_side_biases)],
        flops=1 << 30, name="pack")
    right_swap = swap_cores(right, count)
    left_blocks = [left] + send_chips(left, chips)
    base, block = call(
        base_kernel,
        [shape((rows, cols, channels), F32), shape((half * LANES, per * channels), BF16)],
        [pltpu.VMEM((LANES, channels), F32), pltpu.VMEM((half * half, channels), F32)],
        [pair_features, relative_position_table, chain, outer_pair_projection],
        flops=1 << 30, name="base")
    pair = call(functools.partial(join_kernel, 2), shape((2,) + pack.shape, BF16), [],
                [right, right_swap, base], name="join")
    rights = send_turned(pair, count, count // 2)
    own_lefts = call(functools.partial(join_kernel, chips), shape((chips,) + pack.shape, BF16), [],
                     left_blocks, flops=1 << 36, name="join")
    lefts = [own_lefts, swap_cores(own_lefts, count)]
    turned, live = call(
        functools.partial(turn_kernel, count),
        [shape((width, count * seqs), BF16), shape((cols, count * seqs), BF16)],
        [pltpu.VMEM((count,) + pack.shape, BF16),
         pltpu.VMEM((count * seqs // LANES, width, LANES), F32)],
        rights, flops=1 << 36, name="turn")
    updated, left_edge, right_edge, normed_pair = call(
        edges_kernel,
        [shape((rows, cols, channels), BF16), shape((rows, cols, channels), BF16),
         shape((cols, rows, channels), BF16), shape((rows * cols, channels), BF16)],
        [pltpu.VMEM((count,) + pack.shape, BF16),
         pltpu.VMEM((rows // per * cols, half * LANES), BF16),
         pltpu.VMEM((rows * cols, channels), F32)],
        [turned, live] + lefts + [
            base, block, residue, flat(pair_norm_gain), flat(pair_norm_bias),
            triangle_projection_weights, flat(triangle_projection_biases)],
        name="edges")
    right_edges = [send_same_core(right_edge, count, chips, step) for step in range(chips)]
    for step in range(chips, count, 2):
        block_far = send_same_core(right_edge, count, chips, step)
        right_edges += [block_far, pass_on(block_far, count)]
    left_edges = [left_edge] + send_chips(left_edge, chips)
    gate = call(gate_kernel, shape((rows * cols, channels), F32), [],
                [normed_pair, triangle_projection_weights, flat(triangle_projection_biases)],
                flops=1 << 30, name="gate")
    block_sums = shape((rows * cols, channels), F32)
    scratch = pltpu.VMEM((rows * cols, channels), F32)
    panel = call(panel_kernel, shape((chips, rows * cols, channels), F32), [],
                 left_edges + [gate], name="panel")
    near, far = [], []
    for step in range(count - 1):
        sums = near if step < chips else far
        sums[:] = [call(
            functools.partial(step_kernel, step, chips, not sums), block_sums, [scratch],
            [right_edges[step], panel] + sums, name="triangle")]
    own_sums, half_sums = call(
        functools.partial(last_kernel, count - 1, chips),
        [block_sums, shape((rows * cols, channels), BF16)], [scratch, scratch],
        [right_edges[-1], panel] + far + near, name="last")
    other_sums = swap_cores(half_sums, count)
    return call(
        final_kernel, shape((rows, cols, channels), BF16), [],
        [own_sums, other_sums, updated, gate, flat(triangle_sum_norm_gain),
         flat(triangle_sum_norm_bias), triangle_output_weight, flat(outer_pair_bias)],
        name="final")


def solution(mesh):
    pair = P(("groups", "resi"), ("resj", "seq"), None)
    placed = (
        P(("groups", "resj", "seq"), "resi", None),
        P(("groups", "resj", "seq"), "resi"),
        pair,
        P("groups"),
        P("groups"),
    ) + (P(),) * 14
    return jax.shard_map(body, mesh=mesh, in_specs=placed, out_specs=pair, check_vma=False)
```

```python
import functools

import jax
import jax.numpy as jnp
from jax import lax
from jax.experimental import pallas as pl
from jax.experimental.pallas import tpu as pltpu
from jax.sharding import PartitionSpec as P

RELMAX = 32
LANES = 128
PLANE = ("resj", "seq")
GROUP = ("resi", "resj", "seq")
F32 = jnp.float32
BF16 = jnp.bfloat16
MIB = 1 << 20


def iota(shape, axis):
    return lax.broadcasted_iota(jnp.int32, shape, axis)


def dot(a, b):
    return jnp.dot(a, b, preferred_element_type=F32)


def sigmoid(v):
    return 0.5 * jnp.tanh(0.5 * v) + 0.5


def layer_norm(values, gain, shift):
    average = jnp.mean(values, axis=-1, keepdims=True)
    centred = values - average
    variance = jnp.mean(centred * centred, axis=-1, keepdims=True)
    return centred * lax.rsqrt(variance + 1e-05) * gain + shift


def norm_kernel(x_ref, out_ref):
    x = x_ref[...].reshape(out_ref.shape).astype(F32)
    out_ref[...] = layer_norm(x, 1.0, 0.0)


def pack_kernel(x_ref, mask_ref, res_ref, gain_ref, shift_ref, w_ref, bias_ref,
                left_ref, right_ref, lscr, rscr):
    seqs, rows = mask_ref.shape
    half = w_ref.shape[0] // 2
    per = LANES // half
    row_start = lax.axis_index("resi") * rows
    normed = (x_ref[...] * gain_ref[...] + shift_ref[...]).astype(BF16)
    lane = iota((2 * half, 2 * LANES), 1)
    spread = lane % half + jnp.where(lane >= LANES, half, 0) == iota((2 * half, 2 * LANES), 0)
    spread = spread.astype(F32)
    wide = lax.dot_general(
        w_ref[...], spread.astype(BF16), (((0,), (0,)), ((), ())), preferred_element_type=F32)
    wide = wide.astype(BF16)
    bias = jnp.dot(jnp.broadcast_to(bias_ref[...], (8, 2 * half)), spread,
                   precision=lax.Precision.HIGHEST, preferred_element_type=F32)[0:1]
    mapped = dot(normed, wide)
    lscr[...] = mapped[:, :LANES]
    rscr[...] = mapped[:, LANES:]
    row_live = pick_rows(res_ref[...], row_start, rows)
    live = (mask_ref[...].astype(F32) * row_live).astype(BF16)
    width = rows * half
    spread_live = (iota((rows, width), 1) // half == iota((rows, width), 0)).astype(BF16)
    live_wide = dot(live, spread_live)
    sub = iota((seqs, LANES), 1) // half
    for tile in range(width // LANES):
        at = slice(tile * LANES, (tile + 1) * LANES)
        for ref, scr, first in ((left_ref, lscr, 0), (right_ref, rscr, LANES)):
            value = scr[pl.ds(tile * per, seqs, stride=rows), :]
            for k in range(1, per):
                value = jnp.where(sub == k, scr[pl.ds(tile * per + k, seqs, stride=rows), :], value)
            value = (value + bias[:, first:first + LANES]) * live_wide[:, at]
            ref[:, at] = value.astype(BF16)
    live_tile = dot(live, (iota((rows, LANES), 0) == iota((rows, LANES), 1)).astype(BF16))
    for ref in (left_ref, right_ref):
        ref[:, width:] = live_tile.astype(BF16)


def join_kernel(count, *refs):
    for n in range(count):
        refs[-1][n] = refs[n][...]


def pick_columns(values, start, size):
    total = values.shape[1]
    own = iota((size, total), 1) == iota((size, total), 0) + start
    spread = jnp.broadcast_to(values, (size, total)).astype(F32)
    return jnp.sum(jnp.where(own, spread, 0.0), axis=1, keepdims=True)


def pick_rows(values, start, size):
    total = values.shape[1]
    pick = (iota((total, size), 0) == iota((total, size), 1) + start).astype(BF16)
    return dot(jnp.broadcast_to(values.astype(F32), (8, total)).astype(BF16), pick)[0:1]


def base_kernel(pair_ref, table_ref, chain_ref, w_ref, _, base_ref, block_ref, tscr, wscr):
    rows, cols, channels = pair_ref.shape
    row_start = lax.axis_index("resi") * rows
    col_start = lax.axis_index(PLANE) * cols
    tscr[...] = jnp.zeros_like(tscr)
    tscr[0:table_ref.shape[0], :] = table_ref[...].astype(F32)
    table = tscr[...].astype(BF16)
    chain = chain_ref[...]
    same = pick_columns(chain, col_start, cols) == pick_rows(chain, row_start, rows)
    offset = iota((cols, rows), 0) + col_start - iota((cols, rows), 1) - row_start + RELMAX
    bins = jnp.where(same, jnp.clip(offset, 0, 2 * RELMAX), 2 * RELMAX + 1)
    lane = iota((cols, LANES), 1)
    for i in range(rows):
        one_hot = (lane == bins[:, i:i + 1]).astype(F32).astype(BF16)
        base_ref[i] = pair_ref[i].astype(F32) + dot(one_hot, table)
    wscr[...] = w_ref[...].astype(F32)
    half = int(round(w_ref.shape[0] ** 0.5))
    per = LANES // half
    block_ref[...] = jnp.zeros_like(block_ref)
    for d in range(half):
        value = wscr[pl.ds(d, half, stride=half), :].astype(BF16)
        for k in range(per):
            block_ref[pl.ds(d * LANES + k * half, half), k * channels:(k + 1) * channels] = value


def turn_kernel(count, *refs):
    pairs = count // 2
    rights, (turned_ref, live_ref, rall, tscr) = refs[:pairs], refs[pairs:]
    z, shift = lax.axis_index("resi"), lax.axis_index("resj")
    width, total_seqs = turned_ref.shape
    cols = live_ref.shape[0]
    half = width // cols
    for step in range(pairs):
        for n in range(2):
            rall[z ^ shift ^ (step + n * pairs)] = rights[step][n]
    right = rall[...].reshape(total_seqs, -1)
    for at in range(0, width, LANES):
        for s in range(0, total_seqs, LANES):
            tscr[s // LANES, at:at + LANES, :] = right[s:s + LANES, at:at + LANES].astype(F32).T
    for d in range(half):
        for s in range(0, total_seqs, LANES):
            turned = tscr[s // LANES, pl.ds(d, cols, stride=half), :]
            turned_ref[d * cols:(d + 1) * cols, s:s + LANES] = turned.astype(BF16)
    live_ref[...] = right[:, width:].astype(F32).T[0:cols].astype(BF16)


def edges_kernel(turned_ref, live_ref, own_ref, swapped_ref, base_ref, block_ref, res_ref,
                 gain_ref, shift_ref, w_ref, bias_ref,
                 updated_ref, left_ref, right_ref, nscr, lall, oscr, escr):
    rows, cols, channels = base_ref.shape
    chips, seqs = own_ref.shape[:2]
    half = block_ref.shape[0] // LANES
    per = LANES // half
    width = rows * half
    q = lax.axis_index(PLANE)
    row_start, col_start = lax.axis_index("resi") * rows, q * cols
    for step in range(chips):
        lall[q ^ step] = own_ref[step]
        lall[q ^ (chips + step)] = swapped_ref[step]
    left = lall[...].reshape(2 * chips * seqs, -1)
    counts = dot(live_ref[...], left[:, width:])
    inverse = 1.0 / jnp.maximum(counts, 1.0)
    wide = 2 * LANES
    tall = 8
    for first in range(0, width, wide):
        for d0 in range(0, half, tall):
            product = dot(turned_ref[d0 * cols:(d0 + tall) * cols, :], left[:, first:first + wide])
            product = product.astype(BF16)
            for dd in range(tall):
                for t in range(wide // LANES):
                    g = first // LANES + t
                    oscr[g * cols:(g + 1) * cols, (d0 + dd) * LANES:(d0 + dd + 1) * LANES] = (
                        product[dd * cols:(dd + 1) * cols, t * LANES:(t + 1) * LANES])
    outer = dot(oscr[...], block_ref[...])
    for i in range(rows):
        g, k = i // per, i % per
        part = outer[g * cols:(g + 1) * cols, k * channels:(k + 1) * channels]
        updated = (base_ref[i] + part * inverse[:, i:i + 1]).astype(BF16)
        updated_ref[i] = updated
        normed = layer_norm(updated.astype(F32), gain_ref[...], shift_ref[...])
        nscr[i * cols:(i + 1) * cols, :] = normed.astype(BF16)
    live = pick_columns(res_ref[...], col_start, cols) * pick_rows(res_ref[...], row_start, rows)
    chunk = 8
    for i0 in range(0, rows, chunk):
        mixture = dot(nscr[i0 * cols:(i0 + chunk) * cols, :], w_ref[:, :4 * channels])
        mixture = mixture + bias_ref[:, :4 * channels]
        part = [mixture[:, n * channels:(n + 1) * channels] for n in range(4)]
        left_edge = sigmoid(part[0]) * part[1]
        right_edge = sigmoid(part[2]) * part[3]
        for ii in range(chunk):
            here = live[:, i0 + ii:i0 + ii + 1]
            at = slice(ii * cols, (ii + 1) * cols)
            left_ref[i0 + ii] = (left_edge[at] * here).astype(BF16)
            escr[(i0 + ii) * cols:(i0 + ii + 1) * cols, :] = right_edge[at] * here
    for k in range(cols):
        right_ref[k] = escr[pl.ds(k, rows, stride=cols), :].astype(BF16)


def gate_kernel(normed_ref, w_ref, bias_ref, gate_ref):
    first = w_ref.shape[1] - gate_ref.shape[1]
    gate_ref[...] = sigmoid(dot(normed_ref[...], w_ref[:, first:]) + bias_ref[:, first:])


def panel_kernel(*refs):
    *lefts, _, panel_ref = refs
    x = lax.axis_index("seq")
    for step, left in enumerate(lefts):
        panel_ref[x ^ step] = left[...].astype(F32).reshape(panel_ref.shape[1:])


def source_of(z, core, x, step, chips):
    block = z ^ step ^ ((x + core) % 2 if step >= chips else core % 2)
    return block // chips, block % chips


def add_block(panel_ref, chip, rscr, rows, before, store):
    cols = store.shape[0] // rows
    depth, channels = rscr.shape[0] // cols, rscr.shape[1]
    block = 8
    tiles = cols // 8

    def rows_body(at, carry):
        place = [[pl.ds(pl.multiple_of((at * block + b) * cols + t * 8, 8), 8) for t in range(tiles)]
                 for b in range(block)]
        if before is None:
            sums = [[jnp.zeros((8, channels), F32) for _ in range(tiles)] for _ in range(block)]
        else:
            sums = [[before[place[b][t], :] for t in range(tiles)] for b in range(block)]
        for k in range(depth):
            column = [rscr[k * cols + t * 8:k * cols + t * 8 + 8, :] for t in range(tiles)]
            for b in range(block):
                row = panel_ref[chip, pl.ds((at * block + b) * depth + k, 1), :]
                for t in range(tiles):
                    sums[b][t] = sums[b][t] + row * column[t]
        for b in range(block):
            for t in range(tiles):
                store[place[b][t], :] = sums[b][t].astype(store.dtype)
        return carry

    lax.fori_loop(0, rows // block, rows_body, 0)


def step_kernel(step, chips, fresh, right_ref, panel_ref, *refs):
    out_ref, rscr = refs[-2:]
    z, core, x = [lax.axis_index(axis) for axis in GROUP]
    chip = source_of(z, core, x, step, chips)[1]
    rscr[...] = right_ref[...].astype(F32).reshape(rscr.shape)
    add_block(panel_ref, chip, rscr, right_ref.shape[1], None if fresh else refs[0], out_ref)


def last_kernel(step, chips, right_ref, panel_ref, far_ref, near_ref, own_ref, other_ref, rscr, acc):
    step_kernel(step, chips, False, right_ref, panel_ref, far_ref, acc, rscr)
    mine = lax.axis_index("resi") // chips == lax.axis_index("resj")

    @pl.when(mine)
    def _():
        own_ref[...] = near_ref[...]
        other_ref[...] = acc[...].astype(BF16)

    @pl.when(jnp.logical_not(mine))
    def _():
        own_ref[...] = acc[...]
        other_ref[...] = near_ref[...].astype(BF16)


def final_kernel(own_ref, other_ref, updated_ref, gate_ref, gain_ref, shift_ref, w_ref, bias_ref, out_ref):
    rows, cols, channels = out_ref.shape
    chunk = 8
    for i0 in range(0, rows, chunk):
        at = slice(i0 * cols, (i0 + chunk) * cols)
        sums = own_ref[at, :] + other_ref[at, :].astype(F32)
        normed = layer_norm(sums, gain_ref[...], shift_ref[...]).astype(BF16)
        result = dot(normed, w_ref[...]) + bias_ref[...]
        updated = updated_ref[i0:i0 + chunk].reshape(chunk * cols, channels).astype(F32)
        value = updated + gate_ref[at, :] * result
        out_ref[i0:i0 + chunk] = value.astype(BF16).reshape(chunk, cols, channels)


def swap_cores(block, count):
    return lax.ppermute(block, PLANE, [(p, p ^ (count // 2)) for p in range(count)])


def send_chips(block, chips):
    return [
        lax.ppermute(block, "seq", [(x, x ^ m) for x in range(chips)]) for m in range(1, chips)
    ]


def send_turned(block, count, chips, steps):
    return [
        lax.ppermute(
            block, GROUP,
            [(z * count + p, (p ^ m ^ (z // chips)) * count + z)
             for z in range(count) for p in range(count)])
        for m in range(steps)
    ]


def send_same_core(block, count, chips, step):
    pairs = []
    for z in range(count):
        for p in range(count):
            core, x = p // chips, p % chips
            far, chip = source_of(z, core, x, step, chips)
            pairs.append(((far * chips + x) * count + core * chips + chip, z * count + p))
    return lax.ppermute(block, GROUP, pairs)


def pass_on(block, count):
    return lax.ppermute(block, "resi", [(z, z ^ 1) for z in range(count)])


def call(kernel, outs, scratch, args, flops=0, aliases=None, name=None):
    vmem = pl.BlockSpec(memory_space=pltpu.VMEM)
    size = sum(a.size * a.dtype.itemsize for a in args)
    return pl.pallas_call(
        kernel,
        out_shape=outs,
        in_specs=[vmem] * len(args),
        out_specs=[vmem] * len(outs) if isinstance(outs, list) else vmem,
        scratch_shapes=scratch,
        input_output_aliases=aliases or {},
        compiler_params=pltpu.CompilerParams(vmem_limit_bytes=40 * MIB),
        cost_estimate=pl.CostEstimate(flops=flops, bytes_accessed=size, transcendentals=0),
        name=name,
    )(*args)


def body(
    homolog_matrix,
    sequence_pad_mask,
    pair_features,
    residue_pad_mask,
    residue_chain_index,
    homolog_standard_factor,
    homolog_standard_offset,
    factor_mapping_matrices,
    outer_side_biases,
    outer_pair_projection,
    relative_position_table,
    pair_norm_gain,
    pair_norm_bias,
    triangle_projection_weights,
    triangle_projection_biases,
    triangle_sum_norm_gain,
    triangle_sum_norm_bias,
    triangle_output_weight,
    outer_pair_bias,
):
    rows, cols, channels = pair_features.shape
    seqs, _, depth = homolog_matrix.shape
    half = factor_mapping_matrices.shape[1] // 2
    per = LANES // half
    count = lax.axis_size(PLANE)
    width = rows * half
    flat = lambda v: v.reshape(1, -1)
    shape = jax.ShapeDtypeStruct
    residue = flat(residue_pad_mask)
    chain = flat(residue_chain_index)
    pack = shape((seqs, width + LANES), BF16)
    chips = lax.axis_size("seq")
    normed = call(norm_kernel, shape((seqs * rows, depth), F32), [], [homolog_matrix],
                  flops=1 << 36, name="norm")
    left, right = call(
        pack_kernel, [pack, pack],
        [pltpu.VMEM((seqs * rows, LANES), F32)] * 2,
        [normed, sequence_pad_mask, residue, flat(homolog_standard_factor),
         flat(homolog_standard_offset), factor_mapping_matrices.T, flat(outer_side_biases)],
        flops=1 << 30, name="pack")
    right_swap = swap_cores(right, count)
    left_blocks = [left] + send_chips(left, chips)
    pair = call(functools.partial(join_kernel, 2), shape((2,) + pack.shape, BF16), [],
                [right, right_swap], name="join")
    base, block = call(
        base_kernel,
        [shape((rows, cols, channels), F32), shape((half * LANES, per * channels), BF16)],
        [pltpu.VMEM((LANES, channels), F32), pltpu.VMEM((half * half, channels), F32)],
        [pair_features, relative_position_table, chain, outer_pair_projection, pair],
        flops=1 << 30, name="base")
    rights = send_turned(pair, count, chips, count // 2)
    own_lefts = call(functools.partial(join_kernel, chips), shape((chips,) + pack.shape, BF16), [],
                     left_blocks, flops=1 << 36, name="join")
    lefts = [own_lefts, swap_cores(own_lefts, count)]
    turned, live = call(
        functools.partial(turn_kernel, count),
        [shape((width, count * seqs), BF16), shape((cols, count * seqs), BF16)],
        [pltpu.VMEM((count,) + pack.shape, BF16),
         pltpu.VMEM((count * seqs // LANES, width, LANES), F32)],
        rights, flops=1 << 36, name="turn")
    updated, left_edge, right_edge, normed_pair = call(
        edges_kernel,
        [shape((rows, cols, channels), BF16), shape((rows, cols, channels), BF16),
         shape((cols, rows, channels), BF16), shape((rows * cols, channels), BF16)],
        [pltpu.VMEM((count,) + pack.shape, BF16),
         pltpu.VMEM((rows // per * cols, half * LANES), BF16),
         pltpu.VMEM((rows * cols, channels), F32)],
        [turned, live] + lefts + [
            base, block, residue, flat(pair_norm_gain), flat(pair_norm_bias),
            triangle_projection_weights, flat(triangle_projection_biases)],
        name="edges")
    right_edges = [send_same_core(right_edge, count, chips, step) for step in range(chips)]
    for step in range(chips, count, 2):
        block_far = send_same_core(right_edge, count, chips, step)
        right_edges += [block_far, pass_on(block_far, count)]
    left_edges = [left_edge] + send_chips(left_edge, chips)
    gate = call(gate_kernel, shape((rows * cols, channels), F32), [],
                [normed_pair, triangle_projection_weights, flat(triangle_projection_biases)],
                flops=1 << 30, name="gate")
    block_sums = shape((rows * cols, channels), F32)
    scratch = pltpu.VMEM((rows * cols, channels), F32)
    panel = call(panel_kernel, shape((chips, rows * cols, channels), F32), [],
                 left_edges + [gate], name="panel")
    near, far = [], []
    for step in range(count - 1):
        sums = near if step < chips else far
        sums[:] = [call(
            functools.partial(step_kernel, step, chips, not sums), block_sums, [scratch],
            [right_edges[step], panel] + sums, name="triangle")]
    own_sums, half_sums = call(
        functools.partial(last_kernel, count - 1, chips),
        [block_sums, shape((rows * cols, channels), BF16)], [scratch, scratch],
        [right_edges[-1], panel] + far + near, name="last")
    other_sums = swap_cores(half_sums, count)
    return call(
        final_kernel, shape((rows, cols, channels), BF16), [],
        [own_sums, other_sums, updated, gate, flat(triangle_sum_norm_gain),
         flat(triangle_sum_norm_bias), triangle_output_weight, flat(outer_pair_bias)],
        name="final")


def solution(mesh):
    pair = P(("groups", "resi"), ("resj", "seq"), None)
    placed = (
        P(("groups", "resj", "seq"), "resi", None),
        P(("groups", "resj", "seq"), "resi"),
        pair,
        P("groups"),
        P("groups"),
    ) + (P(),) * 14
    return jax.shard_map(body, mesh=mesh, in_specs=placed, out_specs=pair, check_vma=False)
```

```python
import functools

import jax
import jax.numpy as jnp
from jax import lax
from jax.experimental import pallas as pl
from jax.experimental.pallas import tpu as pltpu
from jax.sharding import PartitionSpec as P

RELMAX = 32
LANES = 128
PLANE = ("resj", "seq")
GROUP = ("resi", "resj", "seq")
F32 = jnp.float32
BF16 = jnp.bfloat16
MIB = 1 << 20


def iota(shape, axis):
    return lax.broadcasted_iota(jnp.int32, shape, axis)


def dot(a, b):
    return jnp.dot(a, b, preferred_element_type=F32)


def sigmoid(v):
    return 0.5 * jnp.tanh(0.5 * v) + 0.5


def layer_norm(values, gain, shift):
    average = jnp.mean(values, axis=-1, keepdims=True)
    centred = values - average
    variance = jnp.mean(centred * centred, axis=-1, keepdims=True)
    return centred * lax.rsqrt(variance + 1e-05) * gain + shift


def norm_kernel(x_ref, out_ref):
    x = x_ref[...].reshape(out_ref.shape).astype(F32)
    out_ref[...] = layer_norm(x, 1.0, 0.0)


def pack_kernel(x_ref, mask_ref, res_ref, gain_ref, shift_ref, w_ref, bias_ref,
                left_ref, right_ref, lscr, rscr):
    seqs, rows = mask_ref.shape
    half = w_ref.shape[0] // 2
    per = LANES // half
    row_start = lax.axis_index("resi") * rows
    normed = (x_ref[...] * gain_ref[...] + shift_ref[...]).astype(BF16)
    lane = iota((2 * half, 2 * LANES), 1)
    spread = lane % half + jnp.where(lane >= LANES, half, 0) == iota((2 * half, 2 * LANES), 0)
    spread = spread.astype(F32)
    wide = lax.dot_general(
        w_ref[...], spread.astype(BF16), (((0,), (0,)), ((), ())), preferred_element_type=F32)
    wide = wide.astype(BF16)
    bias = jnp.dot(jnp.broadcast_to(bias_ref[...], (8, 2 * half)), spread,
                   precision=lax.Precision.HIGHEST, preferred_element_type=F32)[0:1]
    mapped = dot(normed, wide)
    lscr[...] = mapped[:, :LANES]
    rscr[...] = mapped[:, LANES:]
    row_live = pick_rows(res_ref[...], row_start, rows)
    live = (mask_ref[...].astype(F32) * row_live).astype(BF16)
    width = rows * half
    spread_live = (iota((rows, width), 1) // half == iota((rows, width), 0)).astype(BF16)
    live_wide = dot(live, spread_live)
    sub = iota((seqs, LANES), 1) // half
    for tile in range(width // LANES):
        at = slice(tile * LANES, (tile + 1) * LANES)
        for ref, scr, first in ((left_ref, lscr, 0), (right_ref, rscr, LANES)):
            value = scr[pl.ds(tile * per, seqs, stride=rows), :]
            for k in range(1, per):
                value = jnp.where(sub == k, scr[pl.ds(tile * per + k, seqs, stride=rows), :], value)
            value = (value + bias[:, first:first + LANES]) * live_wide[:, at]
            ref[:, at] = value.astype(BF16)
    live_tile = dot(live, (iota((rows, LANES), 0) == iota((rows, LANES), 1)).astype(BF16))
    for ref in (left_ref, right_ref):
        ref[:, width:] = live_tile.astype(BF16)


def join_kernel(count, *refs):
    for n in range(count):
        refs[-1][n] = refs[n][...]


def pick_columns(values, start, size):
    total = values.shape[1]
    own = iota((size, total), 1) == iota((size, total), 0) + start
    spread = jnp.broadcast_to(values, (size, total)).astype(F32)
    return jnp.sum(jnp.where(own, spread, 0.0), axis=1, keepdims=True)


def pick_rows(values, start, size):
    total = values.shape[1]
    pick = (iota((total, size), 0) == iota((total, size), 1) + start).astype(BF16)
    return dot(jnp.broadcast_to(values.astype(F32), (8, total)).astype(BF16), pick)[0:1]


def base_kernel(pair_ref, table_ref, chain_ref, w_ref, base_ref, block_ref, tscr, wscr):
    rows, cols, channels = pair_ref.shape
    row_start = lax.axis_index("resi") * rows
    col_start = lax.axis_index(PLANE) * cols
    tscr[...] = jnp.zeros_like(tscr)
    tscr[0:table_ref.shape[0], :] = table_ref[...].astype(F32)
    table = tscr[...].astype(BF16)
    chain = chain_ref[...]
    same = pick_columns(chain, col_start, cols) == pick_rows(chain, row_start, rows)
    offset = iota((cols, rows), 0) + col_start - iota((cols, rows), 1) - row_start + RELMAX
    bins = jnp.where(same, jnp.clip(offset, 0, 2 * RELMAX), 2 * RELMAX + 1)
    lane = iota((cols, LANES), 1)
    for i in range(rows):
        one_hot = (lane == bins[:, i:i + 1]).astype(F32).astype(BF16)
        base_ref[i] = pair_ref[i].astype(F32) + dot(one_hot, table)
    wscr[...] = w_ref[...].astype(F32)
    half = int(round(w_ref.shape[0] ** 0.5))
    per = LANES // half
    block_ref[...] = jnp.zeros_like(block_ref)
    for d in range(half):
        value = wscr[pl.ds(d, half, stride=half), :].astype(BF16)
        for k in range(per):
            block_ref[pl.ds(d * LANES + k * half, half), k * channels:(k + 1) * channels] = value


def turn_kernel(count, *refs):
    pairs = count // 2
    rights, (turned_ref, live_ref, rall, tscr) = refs[:pairs], refs[pairs:]
    z, shift = lax.axis_index("resi"), lax.axis_index("resj")
    width, total_seqs = turned_ref.shape
    cols = live_ref.shape[0]
    half = width // cols
    for step in range(pairs):
        for n in range(2):
            rall[z ^ shift ^ (step + n * pairs)] = rights[step][n]
    right = rall[...].reshape(total_seqs, -1)
    for at in range(0, width, LANES):
        for s in range(0, total_seqs, LANES):
            tscr[s // LANES, at:at + LANES, :] = right[s:s + LANES, at:at + LANES].astype(F32).T
    for d in range(half):
        for s in range(0, total_seqs, LANES):
            turned = tscr[s // LANES, pl.ds(d, cols, stride=half), :]
            turned_ref[d * cols:(d + 1) * cols, s:s + LANES] = turned.astype(BF16)
    live_ref[...] = right[:, width:].astype(F32).T[0:cols].astype(BF16)


def edges_kernel(turned_ref, live_ref, own_ref, swapped_ref, base_ref, block_ref, res_ref,
                 gain_ref, shift_ref, w_ref, bias_ref,
                 updated_ref, left_ref, right_ref, nscr, lall, oscr, escr):
    rows, cols, channels = base_ref.shape
    chips, seqs = own_ref.shape[:2]
    half = block_ref.shape[0] // LANES
    per = LANES // half
    width = rows * half
    q = lax.axis_index(PLANE)
    row_start, col_start = lax.axis_index("resi") * rows, q * cols
    for step in range(chips):
        lall[q ^ step] = own_ref[step]
        lall[q ^ (chips + step)] = swapped_ref[step]
    left = lall[...].reshape(2 * chips * seqs, -1)
    counts = dot(live_ref[...], left[:, width:])
    inverse = 1.0 / jnp.maximum(counts, 1.0)
    wide = 2 * LANES
    tall = 8
    for first in range(0, width, wide):
        for d0 in range(0, half, tall):
            product = dot(turned_ref[d0 * cols:(d0 + tall) * cols, :], left[:, first:first + wide])
            product = product.astype(BF16)
            for dd in range(tall):
                for t in range(wide // LANES):
                    g = first // LANES + t
                    oscr[g * cols:(g + 1) * cols, (d0 + dd) * LANES:(d0 + dd + 1) * LANES] = (
                        product[dd * cols:(dd + 1) * cols, t * LANES:(t + 1) * LANES])
    outer = dot(oscr[...], block_ref[...])
    for i in range(rows):
        g, k = i // per, i % per
        part = outer[g * cols:(g + 1) * cols, k * channels:(k + 1) * channels]
        updated = (base_ref[i] + part * inverse[:, i:i + 1]).astype(BF16)
        updated_ref[i] = updated
        normed = layer_norm(updated.astype(F32), gain_ref[...], shift_ref[...])
        nscr[i * cols:(i + 1) * cols, :] = normed.astype(BF16)
    live = pick_columns(res_ref[...], col_start, cols) * pick_rows(res_ref[...], row_start, rows)
    chunk = 8
    for i0 in range(0, rows, chunk):
        mixture = dot(nscr[i0 * cols:(i0 + chunk) * cols, :], w_ref[:, :4 * channels])
        mixture = mixture + bias_ref[:, :4 * channels]
        part = [mixture[:, n * channels:(n + 1) * channels] for n in range(4)]
        left_edge = sigmoid(part[0]) * part[1]
        right_edge = sigmoid(part[2]) * part[3]
        for ii in range(chunk):
            here = live[:, i0 + ii:i0 + ii + 1]
            at = slice(ii * cols, (ii + 1) * cols)
            left_ref[i0 + ii] = (left_edge[at] * here).astype(BF16)
            escr[(i0 + ii) * cols:(i0 + ii + 1) * cols, :] = right_edge[at] * here
    for k in range(cols):
        right_ref[k] = escr[pl.ds(k, rows, stride=cols), :].astype(BF16)


def gate_kernel(normed_ref, w_ref, bias_ref, gate_ref):
    first = w_ref.shape[1] - gate_ref.shape[1]
    gate_ref[...] = sigmoid(dot(normed_ref[...], w_ref[:, first:]) + bias_ref[:, first:])


def panel_kernel(*refs):
    *lefts, _, panel_ref = refs
    x = lax.axis_index("seq")
    for step, left in enumerate(lefts):
        panel_ref[x ^ step] = left[...].astype(F32).reshape(panel_ref.shape[1:])


def source_of(z, core, x, step, chips):
    block = z ^ step ^ ((x + core) % 2 if step >= chips else core % 2)
    return block // chips, block % chips


def add_block(panel_ref, chip, rscr, cols, first, before, store):
    rows, depth, channels = store.shape[0] // cols, rscr.shape[0] // cols, rscr.shape[1]
    block = 8
    tiles = cols // 8

    def rows_body(at, carry):
        def place(b, t, start=0):
            return pl.ds(pl.multiple_of((start + at * block + b) * cols + t * 8, 8), 8)

        if before is None:
            sums = [[jnp.zeros((8, channels), F32) for _ in range(tiles)] for _ in range(block)]
        else:
            sums = [[before[place(b, t, first), :] for t in range(tiles)] for b in range(block)]
        for k in range(depth):
            column = [rscr[k * cols + t * 8:k * cols + t * 8 + 8, :] for t in range(tiles)]
            for b in range(block):
                row = panel_ref[chip, pl.ds((first + at * block + b) * depth + k, 1), :]
                for t in range(tiles):
                    sums[b][t] = sums[b][t] + row * column[t]
        for b in range(block):
            for t in range(tiles):
                store[place(b, t), :] = sums[b][t].astype(store.dtype)
        return carry

    lax.fori_loop(0, rows // block, rows_body, 0)


def step_kernel(step, chips, first, fresh, right_ref, panel_ref, *refs):
    out_ref, rscr = refs[-2:]
    z, core, x = [lax.axis_index(axis) for axis in GROUP]
    chip = source_of(z, core, x, step, chips)[1]
    rscr[...] = right_ref[...].astype(F32).reshape(rscr.shape)
    add_block(panel_ref, chip, rscr, right_ref.shape[1], first, None if fresh else refs[0], out_ref)


def last_kernel(step, chips, first, right_ref, panel_ref, far_ref, near_ref, own_ref, other_ref,
                rscr, acc):
    step_kernel(step, chips, first, False, right_ref, panel_ref, far_ref, acc, rscr)
    mine = lax.axis_index("resi") // chips == lax.axis_index("resj")
    at = pl.ds(first * right_ref.shape[1], acc.shape[0])

    @pl.when(mine)
    def _():
        own_ref[...] = near_ref[at, :]
        other_ref[...] = acc[...].astype(BF16)

    @pl.when(jnp.logical_not(mine))
    def _():
        own_ref[...] = acc[...]
        other_ref[...] = near_ref[at, :].astype(BF16)


def final_kernel(first, own_ref, other_ref, updated_ref, gate_ref, gain_ref, shift_ref, w_ref, bias_ref,
                 *refs):
    out_ref = refs[-1]
    cols, channels = out_ref.shape[1:]
    rows = own_ref.shape[0] // cols
    start = 0
    if first:
        out_ref[:first] = refs[0][...]
        start = first
    chunk = 8
    for i0 in range(0, rows, chunk):
        at = slice(i0 * cols, (i0 + chunk) * cols)
        here = slice((first + i0) * cols, (first + i0 + chunk) * cols)
        sums = own_ref[at, :] + other_ref[at, :].astype(F32)
        normed = layer_norm(sums, gain_ref[...], shift_ref[...]).astype(BF16)
        result = dot(normed, w_ref[...]) + bias_ref[...]
        updated = updated_ref[first + i0:first + i0 + chunk].reshape(chunk * cols, channels).astype(F32)
        value = updated + gate_ref[here, :] * result
        out_ref[start + i0:start + i0 + chunk] = value.astype(BF16).reshape(chunk, cols, channels)


def swap_cores(block, count):
    return lax.ppermute(block, PLANE, [(p, p ^ (count // 2)) for p in range(count)])


def send_chips(block, chips):
    return [
        lax.ppermute(block, "seq", [(x, x ^ m) for x in range(chips)]) for m in range(1, chips)
    ]


def send_turned(block, count, chips, steps):
    return [
        lax.ppermute(
            block, GROUP,
            [(z * count + p, (p ^ m ^ (z // chips)) * count + z)
             for z in range(count) for p in range(count)])
        for m in range(steps)
    ]


def send_same_core(block, count, chips, step):
    pairs = []
    for z in range(count):
        for p in range(count):
            core, x = p // chips, p % chips
            far, chip = source_of(z, core, x, step, chips)
            pairs.append(((far * chips + x) * count + core * chips + chip, z * count + p))
    return lax.ppermute(block, GROUP, pairs)


def pass_on(block, count):
    return lax.ppermute(block, "resi", [(z, z ^ 1) for z in range(count)])


def call(kernel, outs, scratch, args, flops=0, aliases=None, name=None):
    vmem = pl.BlockSpec(memory_space=pltpu.VMEM)
    size = sum(a.size * a.dtype.itemsize for a in args)
    return pl.pallas_call(
        kernel,
        out_shape=outs,
        in_specs=[vmem] * len(args),
        out_specs=[vmem] * len(outs) if isinstance(outs, list) else vmem,
        scratch_shapes=scratch,
        input_output_aliases=aliases or {},
        compiler_params=pltpu.CompilerParams(vmem_limit_bytes=40 * MIB),
        cost_estimate=pl.CostEstimate(flops=flops, bytes_accessed=size, transcendentals=0),
        name=name,
    )(*args)


def body(
    homolog_matrix,
    sequence_pad_mask,
    pair_features,
    residue_pad_mask,
    residue_chain_index,
    homolog_standard_factor,
    homolog_standard_offset,
    factor_mapping_matrices,
    outer_side_biases,
    outer_pair_projection,
    relative_position_table,
    pair_norm_gain,
    pair_norm_bias,
    triangle_projection_weights,
    triangle_projection_biases,
    triangle_sum_norm_gain,
    triangle_sum_norm_bias,
    triangle_output_weight,
    outer_pair_bias,
):
    rows, cols, channels = pair_features.shape
    seqs, _, depth = homolog_matrix.shape
    half = factor_mapping_matrices.shape[1] // 2
    per = LANES // half
    count = lax.axis_size(PLANE)
    width = rows * half
    flat = lambda v: v.reshape(1, -1)
    shape = jax.ShapeDtypeStruct
    residue = flat(residue_pad_mask)
    chain = flat(residue_chain_index)
    pack = shape((seqs, width + LANES), BF16)
    chips = lax.axis_size("seq")
    normed = call(norm_kernel, shape((seqs * rows, depth), F32), [], [homolog_matrix],
                  flops=1 << 36, name="norm")
    left, right = call(
        pack_kernel, [pack, pack],
        [pltpu.VMEM((seqs * rows, LANES), F32)] * 2,
        [normed, sequence_pad_mask, residue, flat(homolog_standard_factor),
         flat(homolog_standard_offset), factor_mapping_matrices.T, flat(outer_side_biases)],
        flops=1 << 30, name="pack")
    right_swap = swap_cores(right, count)
    left_blocks = [left] + send_chips(left, chips)
    base, block = call(
        base_kernel,
        [shape((rows, cols, channels), F32), shape((half * LANES, per * channels), BF16)],
        [pltpu.VMEM((LANES, channels), F32), pltpu.VMEM((half * half, channels), F32)],
        [pair_features, relative_position_table, chain, outer_pair_projection],
        flops=1 << 30, name="base")
    pair = call(functools.partial(join_kernel, 2), shape((2,) + pack.shape, BF16), [],
                [right, right_swap, base], name="join")
    rights = send_turned(pair, count, chips, count // 2)
    own_lefts = call(functools.partial(join_kernel, chips), shape((chips,) + pack.shape, BF16), [],
                     left_blocks, flops=1 << 36, name="join")
    lefts = [own_lefts, swap_cores(own_lefts, count)]
    turned, live = call(
        functools.partial(turn_kernel, count),
        [shape((width, count * seqs), BF16), shape((cols, count * seqs), BF16)],
        [pltpu.VMEM((count,) + pack.shape, BF16),
         pltpu.VMEM((count * seqs // LANES, width, LANES), F32)],
        rights, flops=1 << 36, name="turn")
    updated, left_edge, right_edge, normed_pair = call(
        edges_kernel,
        [shape((rows, cols, channels), BF16), shape((rows, cols, channels), BF16),
         shape((cols, rows, channels), BF16), shape((rows * cols, channels), BF16)],
        [pltpu.VMEM((count,) + pack.shape, BF16),
         pltpu.VMEM((rows // per * cols, half * LANES), BF16),
         pltpu.VMEM((rows * cols, channels), F32)],
        [turned, live] + lefts + [
            base, block, residue, flat(pair_norm_gain), flat(pair_norm_bias),
            triangle_projection_weights, flat(triangle_projection_biases)],
        name="edges")
    right_edges = [send_same_core(right_edge, count, chips, step) for step in range(chips)]
    for step in range(chips, count, 2):
        block_far = send_same_core(right_edge, count, chips, step)
        right_edges += [block_far, pass_on(block_far, count)]
    left_edges = [left_edge] + send_chips(left_edge, chips)
    gate = call(gate_kernel, shape((rows * cols, channels), F32), [],
                [normed_pair, triangle_projection_weights, flat(triangle_projection_biases)],
                flops=1 << 30, name="gate")
    block_sums = shape((rows * cols, channels), F32)
    scratch = pltpu.VMEM((rows * cols, channels), F32)
    panel = call(panel_kernel, shape((chips, rows * cols, channels), F32), [],
                 left_edges + [gate], name="panel")
    near, far = [], []
    for step in range(count - 1):
        sums = near if step < chips else far
        sums[:] = [call(
            functools.partial(step_kernel, step, chips, 0, not sums), block_sums, [scratch],
            [right_edges[step], panel] + sums, name="triangle")]
    part = rows // 2
    own_sums, other_sums, result = [], [], []
    for first in (0, part):
        own, half_sums = call(
            functools.partial(last_kernel, count - 1, chips, first),
            [shape((part * cols, channels), F32), shape((part * cols, channels), BF16)],
            [scratch, pltpu.VMEM((part * cols, channels), F32)],
            [right_edges[-1], panel] + far + near, flops=1 << 28, name="last")
        own_sums.append(own)
        other_sums.append(swap_cores(half_sums, count))
    for n, first in enumerate((0, part)):
        result = [call(
            functools.partial(final_kernel, first), shape((first + part, cols, channels), BF16), [],
            [own_sums[n], other_sums[n], updated, gate, flat(triangle_sum_norm_gain),
             flat(triangle_sum_norm_bias), triangle_output_weight, flat(outer_pair_bias)] + result,
            flops=1 << 28, name="final")]
    return result[0]


def solution(mesh):
    pair = P(("groups", "resi"), ("resj", "seq"), None)
    placed = (
        P(("groups", "resj", "seq"), "resi", None),
        P(("groups", "resj", "seq"), "resi"),
        pair,
        P("groups"),
        P("groups"),
    ) + (P(),) * 14
    return jax.shard_map(body, mesh=mesh, in_specs=placed, out_specs=pair, check_vma=False)
```

```python
import functools

import jax
import jax.numpy as jnp
from jax import lax
from jax.experimental import pallas as pl
from jax.experimental.pallas import tpu as pltpu
from jax.sharding import PartitionSpec as P

RELMAX = 32
LANES = 128
PLANE = ("resj", "seq")
GROUP = ("resi", "resj", "seq")
F32 = jnp.float32
BF16 = jnp.bfloat16
MIB = 1 << 20


def iota(shape, axis):
    return lax.broadcasted_iota(jnp.int32, shape, axis)


def dot(a, b):
    return jnp.dot(a, b, preferred_element_type=F32)


def sigmoid(v):
    return 0.5 * jnp.tanh(0.5 * v) + 0.5


def layer_norm(values, gain, shift):
    average = jnp.mean(values, axis=-1, keepdims=True)
    centred = values - average
    variance = jnp.mean(centred * centred, axis=-1, keepdims=True)
    return centred * lax.rsqrt(variance + 1e-05) * gain + shift


def norm_kernel(x_ref, out_ref):
    x = x_ref[...].reshape(out_ref.shape).astype(F32)
    out_ref[...] = layer_norm(x, 1.0, 0.0)


def pack_kernel(x_ref, mask_ref, res_ref, gain_ref, shift_ref, w_ref, bias_ref,
                left_ref, right_ref, lscr, rscr):
    seqs, rows = mask_ref.shape
    half = w_ref.shape[0] // 2
    per = LANES // half
    row_start = lax.axis_index("resi") * rows
    normed = (x_ref[...] * gain_ref[...] + shift_ref[...]).astype(BF16)
    lane = iota((2 * half, 2 * LANES), 1)
    spread = lane % half + jnp.where(lane >= LANES, half, 0) == iota((2 * half, 2 * LANES), 0)
    spread = spread.astype(F32)
    wide = lax.dot_general(
        w_ref[...], spread.astype(BF16), (((0,), (0,)), ((), ())), preferred_element_type=F32)
    wide = wide.astype(BF16)
    bias = jnp.dot(jnp.broadcast_to(bias_ref[...], (8, 2 * half)), spread,
                   precision=lax.Precision.HIGHEST, preferred_element_type=F32)[0:1]
    mapped = dot(normed, wide)
    lscr[...] = mapped[:, :LANES]
    rscr[...] = mapped[:, LANES:]
    row_live = pick_rows(res_ref[...], row_start, rows)
    live = (mask_ref[...].astype(F32) * row_live).astype(BF16)
    width = rows * half
    spread_live = (iota((rows, width), 1) // half == iota((rows, width), 0)).astype(BF16)
    live_wide = dot(live, spread_live)
    sub = iota((seqs, LANES), 1) // half
    for tile in range(width // LANES):
        at = slice(tile * LANES, (tile + 1) * LANES)
        for ref, scr, first in ((left_ref, lscr, 0), (right_ref, rscr, LANES)):
            value = scr[pl.ds(tile * per, seqs, stride=rows), :]
            for k in range(1, per):
                value = jnp.where(sub == k, scr[pl.ds(tile * per + k, seqs, stride=rows), :], value)
            value = (value + bias[:, first:first + LANES]) * live_wide[:, at]
            ref[:, at] = value.astype(BF16)
    live_tile = dot(live, (iota((rows, LANES), 0) == iota((rows, LANES), 1)).astype(BF16))
    for ref in (left_ref, right_ref):
        ref[:, width:] = live_tile.astype(BF16)


def join_kernel(count, *refs):
    for n in range(count):
        refs[-1][n] = refs[n][...]


def pick_columns(values, start, size):
    total = values.shape[1]
    own = iota((size, total), 1) == iota((size, total), 0) + start
    spread = jnp.broadcast_to(values, (size, total)).astype(F32)
    return jnp.sum(jnp.where(own, spread, 0.0), axis=1, keepdims=True)


def pick_rows(values, start, size):
    total = values.shape[1]
    pick = (iota((total, size), 0) == iota((total, size), 1) + start).astype(BF16)
    return dot(jnp.broadcast_to(values.astype(F32), (8, total)).astype(BF16), pick)[0:1]


def base_kernel(pair_ref, table_ref, chain_ref, w_ref, _, base_ref, block_ref, tscr, wscr):
    rows, cols, channels = pair_ref.shape
    row_start = lax.axis_index("resi") * rows
    col_start = lax.axis_index(PLANE) * cols
    tscr[...] = jnp.zeros_like(tscr)
    tscr[0:table_ref.shape[0], :] = table_ref[...].astype(F32)
    table = tscr[...].astype(BF16)
    chain = chain_ref[...]
    same = pick_columns(chain, col_start, cols) == pick_rows(chain, row_start, rows)
    offset = iota((cols, rows), 0) + col_start - iota((cols, rows), 1) - row_start + RELMAX
    bins = jnp.where(same, jnp.clip(offset, 0, 2 * RELMAX), 2 * RELMAX + 1)
    lane = iota((cols, LANES), 1)
    for i in range(rows):
        one_hot = (lane == bins[:, i:i + 1]).astype(F32).astype(BF16)
        base_ref[i] = pair_ref[i].astype(F32) + dot(one_hot, table)
    wscr[...] = w_ref[...].astype(F32)
    half = int(round(w_ref.shape[0] ** 0.5))
    per = LANES // half
    block_ref[...] = jnp.zeros_like(block_ref)
    for d in range(half):
        value = wscr[pl.ds(d, half, stride=half), :].astype(BF16)
        for k in range(per):
            block_ref[pl.ds(d * LANES + k * half, half), k * channels:(k + 1) * channels] = value


def turn_kernel(count, *refs):
    pairs = count // 2
    rights, (turned_ref, live_ref, rall, tscr) = refs[:pairs], refs[pairs:]
    z = lax.axis_index("resi")
    width, total_seqs = turned_ref.shape
    cols = live_ref.shape[0]
    half = width // cols
    for step in range(pairs):
        for n in range(2):
            rall[z ^ (step + n * pairs)] = rights[step][n]
    right = rall[...].reshape(total_seqs, -1)
    for at in range(0, width, LANES):
        for s in range(0, total_seqs, LANES):
            tscr[s // LANES, at:at + LANES, :] = right[s:s + LANES, at:at + LANES].astype(F32).T
    for d in range(half):
        for s in range(0, total_seqs, LANES):
            turned = tscr[s // LANES, pl.ds(d, cols, stride=half), :]
            turned_ref[d * cols:(d + 1) * cols, s:s + LANES] = turned.astype(BF16)
    live_ref[...] = right[:, width:].astype(F32).T[0:cols].astype(BF16)


def edges_kernel(turned_ref, live_ref, own_ref, swapped_ref, base_ref, block_ref, res_ref,
                 gain_ref, shift_ref, w_ref, bias_ref,
                 updated_ref, left_ref, right_ref, nscr, lall, oscr, escr):
    rows, cols, channels = base_ref.shape
    chips, seqs = own_ref.shape[:2]
    half = block_ref.shape[0] // LANES
    per = LANES // half
    width = rows * half
    q = lax.axis_index(PLANE)
    row_start, col_start = lax.axis_index("resi") * rows, q * cols
    for step in range(chips):
        lall[q ^ step] = own_ref[step]
        lall[q ^ (chips + step)] = swapped_ref[step]
    left = lall[...].reshape(2 * chips * seqs, -1)
    counts = dot(live_ref[...], left[:, width:])
    inverse = 1.0 / jnp.maximum(counts, 1.0)
    wide = 2 * LANES
    tall = 8
    for first in range(0, width, wide):
        for d0 in range(0, half, tall):
            product = dot(turned_ref[d0 * cols:(d0 + tall) * cols, :], left[:, first:first + wide])
            product = product.astype(BF16)
            for dd in range(tall):
                for t in range(wide // LANES):
                    g = first // LANES + t
                    oscr[g * cols:(g + 1) * cols, (d0 + dd) * LANES:(d0 + dd + 1) * LANES] = (
                        product[dd * cols:(dd + 1) * cols, t * LANES:(t + 1) * LANES])
    outer = dot(oscr[...], block_ref[...])
    for i in range(rows):
        g, k = i // per, i % per
        part = outer[g * cols:(g + 1) * cols, k * channels:(k + 1) * channels]
        updated = (base_ref[i] + part * inverse[:, i:i + 1]).astype(BF16)
        updated_ref[i] = updated
        normed = layer_norm(updated.astype(F32), gain_ref[...], shift_ref[...])
        nscr[i * cols:(i + 1) * cols, :] = normed.astype(BF16)
    live = pick_columns(res_ref[...], col_start, cols) * pick_rows(res_ref[...], row_start, rows)
    chunk = 8
    for i0 in range(0, rows, chunk):
        mixture = dot(nscr[i0 * cols:(i0 + chunk) * cols, :], w_ref[:, :4 * channels])
        mixture = mixture + bias_ref[:, :4 * channels]
        part = [mixture[:, n * channels:(n + 1) * channels] for n in range(4)]
        left_edge = sigmoid(part[0]) * part[1]
        right_edge = sigmoid(part[2]) * part[3]
        for ii in range(chunk):
            here = live[:, i0 + ii:i0 + ii + 1]
            at = slice(ii * cols, (ii + 1) * cols)
            left_ref[i0 + ii] = (left_edge[at] * here).astype(BF16)
            escr[(i0 + ii) * cols:(i0 + ii + 1) * cols, :] = right_edge[at] * here
    for k in range(cols):
        right_ref[k] = escr[pl.ds(k, rows, stride=cols), :].astype(BF16)


def gate_kernel(normed_ref, w_ref, bias_ref, gate_ref):
    first = w_ref.shape[1] - gate_ref.shape[1]
    gate_ref[...] = sigmoid(dot(normed_ref[...], w_ref[:, first:]) + bias_ref[:, first:])


def panel_kernel(*refs):
    *lefts, _, panel_ref = refs
    x = lax.axis_index("seq")
    for step, left in enumerate(lefts):
        panel_ref[x ^ step] = left[...].astype(F32).reshape(panel_ref.shape[1:])


def source_of(z, core, x, step, chips):
    block = z ^ step ^ ((x + core) % 2 if step >= chips else core % 2)
    return block // chips, block % chips


def add_block(panel_ref, chip, rscr, cols, first, before, store):
    rows, depth, channels = store.shape[0] // cols, rscr.shape[0] // cols, rscr.shape[1]
    block = 8
    tiles = cols // 8

    def rows_body(at, carry):
        def place(b, t, start=0):
            return pl.ds(pl.multiple_of((start + at * block + b) * cols + t * 8, 8), 8)

        if before is None:
            sums = [[jnp.zeros((8, channels), F32) for _ in range(tiles)] for _ in range(block)]
        else:
            sums = [[before[place(b, t, first), :] for t in range(tiles)] for b in range(block)]
        for k in range(depth):
            column = [rscr[k * cols + t * 8:k * cols + t * 8 + 8, :] for t in range(tiles)]
            for b in range(block):
                row = panel_ref[chip, pl.ds((first + at * block + b) * depth + k, 1), :]
                for t in range(tiles):
                    sums[b][t] = sums[b][t] + row * column[t]
        for b in range(block):
            for t in range(tiles):
                store[place(b, t), :] = sums[b][t].astype(store.dtype)
        return carry

    lax.fori_loop(0, rows // block, rows_body, 0)


def step_kernel(step, chips, first, fresh, right_ref, panel_ref, *refs):
    out_ref, rscr = refs[-2:]
    z, core, x = [lax.axis_index(axis) for axis in GROUP]
    chip = source_of(z, core, x, step, chips)[1]
    rscr[...] = right_ref[...].astype(F32).reshape(rscr.shape)
    add_block(panel_ref, chip, rscr, right_ref.shape[1], first, None if fresh else refs[0], out_ref)


def last_kernel(step, chips, first, right_ref, panel_ref, far_ref, near_ref, own_ref, other_ref,
                rscr, acc):
    step_kernel(step, chips, first, False, right_ref, panel_ref, far_ref, acc, rscr)
    mine = lax.axis_index("resi") // chips == lax.axis_index("resj")
    at = pl.ds(first * right_ref.shape[1], acc.shape[0])

    @pl.when(mine)
    def _():
        own_ref[...] = near_ref[at, :]
        other_ref[...] = acc[...].astype(BF16)

    @pl.when(jnp.logical_not(mine))
    def _():
        own_ref[...] = acc[...]
        other_ref[...] = near_ref[at, :].astype(BF16)


def final_kernel(first, own_ref, other_ref, updated_ref, gate_ref, gain_ref, shift_ref, w_ref, bias_ref,
                 *refs):
    out_hbm, vscr, sems = refs[-3:]
    rows, cols, channels = vscr.shape
    chunk = 8
    moves = []
    for i0 in range(0, rows, chunk):
        at = slice(i0 * cols, (i0 + chunk) * cols)
        here = slice((first + i0) * cols, (first + i0 + chunk) * cols)
        sums = own_ref[at, :] + other_ref[at, :].astype(F32)
        normed = layer_norm(sums, gain_ref[...], shift_ref[...]).astype(BF16)
        result = dot(normed, w_ref[...]) + bias_ref[...]
        updated = updated_ref[first + i0:first + i0 + chunk].reshape(chunk * cols, channels).astype(F32)
        value = updated + gate_ref[here, :] * result
        vscr[i0:i0 + chunk] = value.astype(BF16).reshape(chunk, cols, channels)
        moves.append(pltpu.make_async_copy(
            vscr.at[i0:i0 + chunk], out_hbm.at[first + i0:first + i0 + chunk], sems.at[i0 // chunk]))
        moves[-1].start()
    for move in moves:
        move.wait()


def swap_cores(block, count):
    return lax.ppermute(block, PLANE, [(p, p ^ (count // 2)) for p in range(count)])


def send_chips(block, chips):
    return [
        lax.ppermute(block, "seq", [(x, x ^ m) for x in range(chips)]) for m in range(1, chips)
    ]


def send_turned(block, count, steps):
    return [
        lax.ppermute(
            block, GROUP,
            [(z * count + p, (p ^ m) * count + z) for z in range(count) for p in range(count)])
        for m in range(steps)
    ]


def send_same_core(block, count, chips, step):
    pairs = []
    for z in range(count):
        for p in range(count):
            core, x = p // chips, p % chips
            far, chip = source_of(z, core, x, step, chips)
            pairs.append(((far * chips + x) * count + core * chips + chip, z * count + p))
    return lax.ppermute(block, GROUP, pairs)


def pass_on(block, count):
    return lax.ppermute(block, "resi", [(z, z ^ 1) for z in range(count)])


def call(kernel, outs, scratch, args, flops=0, aliases=None, hbm=False, name=None):
    vmem = pl.BlockSpec(memory_space=pltpu.VMEM)
    result = pl.BlockSpec(memory_space=pl.ANY) if hbm else vmem
    size = sum(a.size * a.dtype.itemsize for a in args)
    return pl.pallas_call(
        kernel,
        out_shape=outs,
        in_specs=[result if n in (aliases or {}) else vmem for n in range(len(args))],
        out_specs=[vmem] * len(outs) if isinstance(outs, list) else result,
        scratch_shapes=scratch,
        input_output_aliases=aliases or {},
        compiler_params=pltpu.CompilerParams(vmem_limit_bytes=40 * MIB),
        cost_estimate=pl.CostEstimate(flops=flops, bytes_accessed=size, transcendentals=0),
        name=name,
    )(*args)


def body(
    homolog_matrix,
    sequence_pad_mask,
    pair_features,
    residue_pad_mask,
    residue_chain_index,
    homolog_standard_factor,
    homolog_standard_offset,
    factor_mapping_matrices,
    outer_side_biases,
    outer_pair_projection,
    relative_position_table,
    pair_norm_gain,
    pair_norm_bias,
    triangle_projection_weights,
    triangle_projection_biases,
    triangle_sum_norm_gain,
    triangle_sum_norm_bias,
    triangle_output_weight,
    outer_pair_bias,
):
    rows, cols, channels = pair_features.shape
    seqs, _, depth = homolog_matrix.shape
    half = factor_mapping_matrices.shape[1] // 2
    per = LANES // half
    count = lax.axis_size(PLANE)
    width = rows * half
    flat = lambda v: v.reshape(1, -1)
    shape = jax.ShapeDtypeStruct
    residue = flat(residue_pad_mask)
    chain = flat(residue_chain_index)
    pack = shape((seqs, width + LANES), BF16)
    chips = lax.axis_size("seq")
    normed = call(norm_kernel, shape((seqs * rows, depth), F32), [], [homolog_matrix],
                  flops=1 << 36, name="norm")
    left, right = call(
        pack_kernel, [pack, pack],
        [pltpu.VMEM((seqs * rows, LANES), F32)] * 2,
        [normed, sequence_pad_mask, residue, flat(homolog_standard_factor),
         flat(homolog_standard_offset), factor_mapping_matrices.T, flat(outer_side_biases)],
        flops=1 << 30, name="pack")
    right_swap = swap_cores(right, count)
    left_blocks = [left] + send_chips(left, chips)
    pair = call(functools.partial(join_kernel, 2), shape((2,) + pack.shape, BF16), [],
                [right, right_swap], name="join")
    base, block = call(
        base_kernel,
        [shape((rows, cols, channels), F32), shape((half * LANES, per * channels), BF16)],
        [pltpu.VMEM((LANES, channels), F32), pltpu.VMEM((half * half, channels), F32)],
        [pair_features, relative_position_table, chain, outer_pair_projection, pair],
        flops=1 << 30, name="base")
    rights = send_turned(pair, count, count // 2)
    own_lefts = call(functools.partial(join_kernel, chips), shape((chips,) + pack.shape, BF16), [],
                     left_blocks, flops=1 << 36, name="join")
    lefts = [own_lefts, swap_cores(own_lefts, count)]
    turned, live = call(
        functools.partial(turn_kernel, count),
        [shape((width, count * seqs), BF16), shape((cols, count * seqs), BF16)],
        [pltpu.VMEM((count,) + pack.shape, BF16),
         pltpu.VMEM((count * seqs // LANES, width, LANES), F32)],
        rights, flops=1 << 36, name="turn")
    updated, left_edge, right_edge, normed_pair = call(
        edges_kernel,
        [shape((rows, cols, channels), BF16), shape((rows, cols, channels), BF16),
         shape((cols, rows, channels), BF16), shape((rows * cols, channels), BF16)],
        [pltpu.VMEM((count,) + pack.shape, BF16),
         pltpu.VMEM((rows // per * cols, half * LANES), BF16),
         pltpu.VMEM((rows * cols, channels), F32)],
        [turned, live] + lefts + [
            base, block, residue, flat(pair_norm_gain), flat(pair_norm_bias),
            triangle_projection_weights, flat(triangle_projection_biases)],
        name="edges")
    right_edges = [send_same_core(right_edge, count, chips, step) for step in range(chips)]
    for step in range(chips, count, 2):
        block_far = send_same_core(right_edge, count, chips, step)
        right_edges += [block_far, pass_on(block_far, count)]
    left_edges = [left_edge] + send_chips(left_edge, chips)
    gate = call(gate_kernel, shape((rows * cols, channels), F32), [],
                [normed_pair, triangle_projection_weights, flat(triangle_projection_biases)],
                flops=1 << 30, name="gate")
    block_sums = shape((rows * cols, channels), F32)
    scratch = pltpu.VMEM((rows * cols, channels), F32)
    panel = call(panel_kernel, shape((chips, rows * cols, channels), F32), [],
                 left_edges + [gate], name="panel")
    near, far = [], []
    for step in range(count - 1):
        sums = near if step < chips else far
        sums[:] = [call(
            functools.partial(step_kernel, step, chips, 0, not sums), block_sums, [scratch],
            [right_edges[step], panel] + sums, name="triangle")]
    part = rows // 2
    own_sums, other_sums, result = [], [], []
    for first in (0, part):
        own, half_sums = call(
            functools.partial(last_kernel, count - 1, chips, first),
            [shape((part * cols, channels), F32), shape((part * cols, channels), BF16)],
            [scratch, pltpu.VMEM((part * cols, channels), F32)],
            [right_edges[-1], panel] + far + near, flops=1 << 28, name="last")
        own_sums.append(own)
        other_sums.append(swap_cores(half_sums, count))
    for n, first in enumerate((0, part)):
        args = [own_sums[n], other_sums[n], updated, gate, flat(triangle_sum_norm_gain),
                flat(triangle_sum_norm_bias), triangle_output_weight, flat(outer_pair_bias)]
        result = [call(
            functools.partial(final_kernel, first), shape((rows, cols, channels), BF16),
            [pltpu.VMEM((part, cols, channels), BF16), pltpu.SemaphoreType.DMA((part // 8,))],
            args + result, flops=1 << 28, aliases={len(args): 0} if n else None, hbm=True,
            name="final")]
    return result[0]


def solution(mesh):
    pair = P(("groups", "resi"), ("resj", "seq"), None)
    placed = (
        P(("groups", "resj", "seq"), "resi", None),
        P(("groups", "resj", "seq"), "resi"),
        pair,
        P("groups"),
        P("groups"),
    ) + (P(),) * 14
    return jax.shard_map(body, mesh=mesh, in_specs=placed, out_specs=pair, check_vma=False)
```

```python
import functools

import jax
import jax.numpy as jnp
from jax import lax
from jax.experimental import pallas as pl
from jax.experimental.pallas import tpu as pltpu
from jax.sharding import PartitionSpec as P

RELMAX = 32
LANES = 128
PLANE = ("resj", "seq")
GROUP = ("resi", "resj", "seq")
F32 = jnp.float32
BF16 = jnp.bfloat16
MIB = 1 << 20


def iota(shape, axis):
    return lax.broadcasted_iota(jnp.int32, shape, axis)


def dot(a, b):
    return jnp.dot(a, b, preferred_element_type=F32)


def sigmoid(v):
    return 0.5 * jnp.tanh(0.5 * v) + 0.5


def layer_norm(values, gain, shift):
    average = jnp.mean(values, axis=-1, keepdims=True)
    centred = values - average
    variance = jnp.mean(centred * centred, axis=-1, keepdims=True)
    return centred * lax.rsqrt(variance + 1e-05) * gain + shift


def norm_kernel(x_ref, out_ref):
    x = x_ref[...].reshape(out_ref.shape).astype(F32)
    out_ref[...] = layer_norm(x, 1.0, 0.0)


def pack_kernel(x_ref, mask_ref, res_ref, gain_ref, shift_ref, w_ref, bias_ref,
                left_ref, right_ref, lscr, rscr):
    seqs, rows = mask_ref.shape
    half = w_ref.shape[0] // 2
    per = LANES // half
    row_start = lax.axis_index("resi") * rows
    normed = (x_ref[...] * gain_ref[...] + shift_ref[...]).astype(BF16)
    lane = iota((2 * half, 2 * LANES), 1)
    spread = lane % half + jnp.where(lane >= LANES, half, 0) == iota((2 * half, 2 * LANES), 0)
    spread = spread.astype(F32)
    wide = lax.dot_general(
        w_ref[...], spread.astype(BF16), (((0,), (0,)), ((), ())), preferred_element_type=F32)
    wide = wide.astype(BF16)
    bias = jnp.dot(jnp.broadcast_to(bias_ref[...], (8, 2 * half)), spread,
                   precision=lax.Precision.HIGHEST, preferred_element_type=F32)[0:1]
    mapped = dot(normed, wide)
    lscr[...] = mapped[:, :LANES]
    rscr[...] = mapped[:, LANES:]
    row_live = pick_rows(res_ref[...], row_start, rows)
    live = (mask_ref[...].astype(F32) * row_live).astype(BF16)
    width = rows * half
    spread_live = (iota((rows, width), 1) // half == iota((rows, width), 0)).astype(BF16)
    live_wide = dot(live, spread_live)
    sub = iota((seqs, LANES), 1) // half
    for tile in range(width // LANES):
        at = slice(tile * LANES, (tile + 1) * LANES)
        for ref, scr, first in ((left_ref, lscr, 0), (right_ref, rscr, LANES)):
            value = scr[pl.ds(tile * per, seqs, stride=rows), :]
            for k in range(1, per):
                value = jnp.where(sub == k, scr[pl.ds(tile * per + k, seqs, stride=rows), :], value)
            value = (value + bias[:, first:first + LANES]) * live_wide[:, at]
            ref[:, at] = value.astype(BF16)
    live_tile = dot(live, (iota((rows, LANES), 0) == iota((rows, LANES), 1)).astype(BF16))
    for ref in (left_ref, right_ref):
        ref[:, width:] = live_tile.astype(BF16)


def carry_kernel(in_ref, out_ref):
    out_ref[...] = in_ref[...]


def join_kernel(count, *refs):
    for n in range(count):
        refs[-1][n] = refs[n][...]


def pick_columns(values, start, size):
    total = values.shape[1]
    own = iota((size, total), 1) == iota((size, total), 0) + start
    spread = jnp.broadcast_to(values, (size, total)).astype(F32)
    return jnp.sum(jnp.where(own, spread, 0.0), axis=1, keepdims=True)


def pick_rows(values, start, size):
    total = values.shape[1]
    pick = (iota((total, size), 0) == iota((total, size), 1) + start).astype(BF16)
    return dot(jnp.broadcast_to(values.astype(F32), (8, total)).astype(BF16), pick)[0:1]


def base_kernel(pair_ref, table_ref, chain_ref, w_ref, _, base_ref, block_ref, tscr, wscr):
    rows, cols, channels = pair_ref.shape
    row_start = lax.axis_index("resi") * rows
    col_start = lax.axis_index(PLANE) * cols
    tscr[...] = jnp.zeros_like(tscr)
    tscr[0:table_ref.shape[0], :] = table_ref[...].astype(F32)
    table = tscr[...].astype(BF16)
    chain = chain_ref[...]
    same = pick_columns(chain, col_start, cols) == pick_rows(chain, row_start, rows)
    offset = iota((cols, rows), 0) + col_start - iota((cols, rows), 1) - row_start + RELMAX
    bins = jnp.where(same, jnp.clip(offset, 0, 2 * RELMAX), 2 * RELMAX + 1)
    lane = iota((cols, LANES), 1)
    for i in range(rows):
        one_hot = (lane == bins[:, i:i + 1]).astype(F32).astype(BF16)
        base_ref[i] = pair_ref[i].astype(F32) + dot(one_hot, table)
    wscr[...] = w_ref[...].astype(F32)
    half = int(round(w_ref.shape[0] ** 0.5))
    per = LANES // half
    block_ref[...] = jnp.zeros_like(block_ref)
    for d in range(half):
        value = wscr[pl.ds(d, half, stride=half), :].astype(BF16)
        for k in range(per):
            block_ref[pl.ds(d * LANES + k * half, half), k * channels:(k + 1) * channels] = value


def turn_kernel(count, *refs):
    pairs = count // 2
    rights, (turned_ref, live_ref, rall, tscr) = refs[:pairs], refs[pairs:]
    z = lax.axis_index("resi")
    width, total_seqs = turned_ref.shape
    cols = live_ref.shape[0]
    half = width // cols
    for step in range(pairs):
        for n in range(2):
            rall[z ^ (step + n * pairs)] = rights[step][n]
    right = rall[...].reshape(total_seqs, -1)
    for at in range(0, width, LANES):
        for s in range(0, total_seqs, LANES):
            tscr[s // LANES, at:at + LANES, :] = right[s:s + LANES, at:at + LANES].astype(F32).T
    for d in range(half):
        for s in range(0, total_seqs, LANES):
            turned = tscr[s // LANES, pl.ds(d, cols, stride=half), :]
            turned_ref[d * cols:(d + 1) * cols, s:s + LANES] = turned.astype(BF16)
    live_ref[...] = right[:, width:].astype(F32).T[0:cols].astype(BF16)


def edges_kernel(turned_ref, live_ref, own_ref, swapped_ref, base_ref, block_ref, res_ref,
                 gain_ref, shift_ref, w_ref, bias_ref,
                 updated_ref, left_ref, right_ref, low_ref, high_ref, nscr, lall, oscr, escr):
    rows, cols, channels = base_ref.shape
    chips, seqs = own_ref.shape[:2]
    half = block_ref.shape[0] // LANES
    per = LANES // half
    width = rows * half
    q = lax.axis_index(PLANE)
    row_start, col_start = lax.axis_index("resi") * rows, q * cols
    for step in range(chips):
        lall[q ^ step] = own_ref[step]
        lall[q ^ (chips + step)] = swapped_ref[step]
    left = lall[...].reshape(2 * chips * seqs, -1)
    counts = dot(live_ref[...], left[:, width:])
    inverse = 1.0 / jnp.maximum(counts, 1.0)
    wide = 2 * LANES
    tall = 8
    for first in range(0, width, wide):
        for d0 in range(0, half, tall):
            product = dot(turned_ref[d0 * cols:(d0 + tall) * cols, :], left[:, first:first + wide])
            product = product.astype(BF16)
            for dd in range(tall):
                for t in range(wide // LANES):
                    g = first // LANES + t
                    oscr[g * cols:(g + 1) * cols, (d0 + dd) * LANES:(d0 + dd + 1) * LANES] = (
                        product[dd * cols:(dd + 1) * cols, t * LANES:(t + 1) * LANES])
    outer = dot(oscr[...], block_ref[...])
    for i in range(rows):
        g, k = i // per, i % per
        part = outer[g * cols:(g + 1) * cols, k * channels:(k + 1) * channels]
        updated = (base_ref[i] + part * inverse[:, i:i + 1]).astype(BF16)
        updated_ref[i] = updated
        normed = layer_norm(updated.astype(F32), gain_ref[...], shift_ref[...])
        nscr[i * cols:(i + 1) * cols, :] = normed.astype(BF16)
    live = pick_columns(res_ref[...], col_start, cols) * pick_rows(res_ref[...], row_start, rows)
    chunk = 8
    for i0 in range(0, rows, chunk):
        mixture = dot(nscr[i0 * cols:(i0 + chunk) * cols, :], w_ref[:, :4 * channels])
        mixture = mixture + bias_ref[:, :4 * channels]
        part = [mixture[:, n * channels:(n + 1) * channels] for n in range(4)]
        left_edge = sigmoid(part[0]) * part[1]
        right_edge = sigmoid(part[2]) * part[3]
        for ii in range(chunk):
            here = live[:, i0 + ii:i0 + ii + 1]
            at = slice(ii * cols, (ii + 1) * cols)
            left_ref[i0 + ii] = (left_edge[at] * here).astype(BF16)
            escr[(i0 + ii) * cols:(i0 + ii + 1) * cols, :] = right_edge[at] * here
    part = cols // 2
    for k in range(cols):
        value = escr[pl.ds(k, rows, stride=cols), :].astype(BF16)
        right_ref[k] = value
        (low_ref if k < part else high_ref)[k % part] = value


def gate_kernel(normed_ref, w_ref, bias_ref, gate_ref):
    first = w_ref.shape[1] - gate_ref.shape[1]
    gate_ref[...] = sigmoid(dot(normed_ref[...], w_ref[:, first:]) + bias_ref[:, first:])


def panel_kernel(*refs):
    *lefts, _, panel_ref = refs
    x = lax.axis_index("seq")
    for step, left in enumerate(lefts):
        panel_ref[x ^ step] = left[...].astype(F32).reshape(panel_ref.shape[1:])


def source_of(z, core, x, step, chips):
    block = z ^ step ^ ((x + core) % 2 if step >= chips else core % 2)
    return block // chips, block % chips


def add_block(panel_ref, chip, rscr, cols, skip, first, before, store):
    rows, depth, channels = store.shape[0] // cols, rscr.shape[0] // cols, rscr.shape[1]
    whole = panel_ref.shape[1] // cols
    block = 8
    tiles = cols // 8

    def rows_body(at, carry):
        def place(b, t, start=0):
            return pl.ds(pl.multiple_of((start + at * block + b) * cols + t * 8, 8), 8)

        if before is None:
            sums = [[jnp.zeros((8, channels), F32) for _ in range(tiles)] for _ in range(block)]
        else:
            sums = [[before[place(b, t, first), :] for t in range(tiles)] for b in range(block)]
        for k in range(depth):
            column = [rscr[k * cols + t * 8:k * cols + t * 8 + 8, :] for t in range(tiles)]
            for b in range(block):
                row = panel_ref[chip, pl.ds((first + at * block + b) * whole + skip + k, 1), :]
                for t in range(tiles):
                    sums[b][t] = sums[b][t] + row * column[t]
        for b in range(block):
            for t in range(tiles):
                store[place(b, t), :] = sums[b][t].astype(store.dtype)
        return carry

    lax.fori_loop(0, rows // block, rows_body, 0)


def step_kernel(step, chips, skip, first, fresh, right_ref, panel_ref, *refs):
    out_ref, rscr = refs[-2:]
    z, core, x = [lax.axis_index(axis) for axis in GROUP]
    chip = source_of(z, core, x, step, chips)[1]
    rscr[...] = right_ref[...].astype(F32).reshape(rscr.shape)
    add_block(
        panel_ref, chip, rscr, right_ref.shape[1], skip, first, None if fresh else refs[0], out_ref)


def last_kernel(step, chips, skip, first, right_ref, panel_ref, far_ref, near_ref, own_ref, other_ref,
                rscr, acc):
    step_kernel(step, chips, skip, first, False, right_ref, panel_ref, far_ref, acc, rscr)
    mine = lax.axis_index("resi") // chips == lax.axis_index("resj")
    at = pl.ds(first * right_ref.shape[1], acc.shape[0])

    @pl.when(mine)
    def _():
        own_ref[...] = near_ref[at, :]
        other_ref[...] = acc[...].astype(BF16)

    @pl.when(jnp.logical_not(mine))
    def _():
        own_ref[...] = acc[...]
        other_ref[...] = near_ref[at, :].astype(BF16)


def final_kernel(first, own_ref, other_ref, updated_ref, gate_ref, gain_ref, shift_ref, w_ref, bias_ref,
                 *refs):
    if first:
        before_ref, out_hbm, value_ref, sems = refs
        moves = [pltpu.make_async_copy(before_ref, out_hbm.at[:first], sems.at[0])]
        moves[0].start()
    else:
        value_ref, = refs
    rows, cols, channels = value_ref.shape
    chunk = 8
    for i0 in range(0, rows, chunk):
        at = slice(i0 * cols, (i0 + chunk) * cols)
        here = slice((first + i0) * cols, (first + i0 + chunk) * cols)
        sums = own_ref[at, :] + other_ref[at, :].astype(F32)
        normed = layer_norm(sums, gain_ref[...], shift_ref[...]).astype(BF16)
        result = dot(normed, w_ref[...]) + bias_ref[...]
        updated = updated_ref[first + i0:first + i0 + chunk].reshape(chunk * cols, channels).astype(F32)
        value = updated + gate_ref[here, :] * result
        value_ref[i0:i0 + chunk] = value.astype(BF16).reshape(chunk, cols, channels)
        if first:
            moves.append(pltpu.make_async_copy(
                value_ref.at[i0:i0 + chunk], out_hbm.at[first + i0:first + i0 + chunk],
                sems.at[1 + i0 // chunk]))
            moves[-1].start()
    if first:
        for move in moves:
            move.wait()


def swap_cores(block, count):
    return lax.ppermute(block, PLANE, [(p, p ^ (count // 2)) for p in range(count)])


def send_chips(block, chips):
    return [
        lax.ppermute(block, "seq", [(x, x ^ m) for x in range(chips)]) for m in range(1, chips)
    ]


def send_turned(block, count, steps):
    return [
        lax.ppermute(
            block, GROUP,
            [(z * count + p, (p ^ m) * count + z) for z in range(count) for p in range(count)])
        for m in range(steps)
    ]


def send_same_core(block, count, chips, step):
    pairs = []
    for z in range(count):
        for p in range(count):
            core, x = p // chips, p % chips
            far, chip = source_of(z, core, x, step, chips)
            pairs.append(((far * chips + x) * count + core * chips + chip, z * count + p))
    return lax.ppermute(block, GROUP, pairs)


def pass_on(block, count):
    return lax.ppermute(block, "resi", [(z, z ^ 1) for z in range(count)])


def call(kernel, outs, scratch, args, flops=0, hbm=False, name=None):
    vmem = pl.BlockSpec(memory_space=pltpu.VMEM)
    size = sum(a.size * a.dtype.itemsize for a in args)
    return pl.pallas_call(
        kernel,
        out_shape=outs,
        in_specs=[vmem] * len(args),
        out_specs=[vmem] * len(outs) if isinstance(outs, list) else (
            pl.BlockSpec(memory_space=pl.ANY) if hbm else vmem),
        scratch_shapes=scratch,
        compiler_params=pltpu.CompilerParams(vmem_limit_bytes=40 * MIB),
        cost_estimate=pl.CostEstimate(flops=flops, bytes_accessed=size, transcendentals=0),
        name=name,
    )(*args)


def body(
    homolog_matrix,
    sequence_pad_mask,
    pair_features,
    residue_pad_mask,
    residue_chain_index,
    homolog_standard_factor,
    homolog_standard_offset,
    factor_mapping_matrices,
    outer_side_biases,
    outer_pair_projection,
    relative_position_table,
    pair_norm_gain,
    pair_norm_bias,
    triangle_projection_weights,
    triangle_projection_biases,
    triangle_sum_norm_gain,
    triangle_sum_norm_bias,
    triangle_output_weight,
    outer_pair_bias,
):
    rows, cols, channels = pair_features.shape
    seqs, _, depth = homolog_matrix.shape
    half = factor_mapping_matrices.shape[1] // 2
    per = LANES // half
    count = lax.axis_size(PLANE)
    width = rows * half
    flat = lambda v: v.reshape(1, -1)
    shape = jax.ShapeDtypeStruct
    residue = flat(residue_pad_mask)
    chain = flat(residue_chain_index)
    pack = shape((seqs, width + LANES), BF16)
    chips = lax.axis_size("seq")
    normed = call(norm_kernel, shape((seqs * rows, depth), F32), [], [homolog_matrix],
                  flops=1 << 36, name="norm")
    left, right = call(
        pack_kernel, [pack, pack],
        [pltpu.VMEM((seqs * rows, LANES), F32)] * 2,
        [normed, sequence_pad_mask, residue, flat(homolog_standard_factor),
         flat(homolog_standard_offset), factor_mapping_matrices.T, flat(outer_side_biases)],
        flops=1 << 30, name="pack")
    right_swap = swap_cores(right, count)
    left_blocks = [left] + send_chips(left, chips)
    pair = call(functools.partial(join_kernel, 2), shape((2,) + pack.shape, BF16), [],
                [right, right_swap], name="join")
    base, block = call(
        base_kernel,
        [shape((rows, cols, channels), F32), shape((half * LANES, per * channels), BF16)],
        [pltpu.VMEM((LANES, channels), F32), pltpu.VMEM((half * half, channels), F32)],
        [pair_features, relative_position_table, chain, outer_pair_projection, pair],
        flops=1 << 30, name="base")
    rights = send_turned(pair, count, count // 2)
    own_lefts = call(functools.partial(join_kernel, chips), shape((chips,) + pack.shape, BF16), [],
                     left_blocks, flops=1 << 36, name="join")
    lefts = [own_lefts, swap_cores(own_lefts, count)]
    turned, live = call(
        functools.partial(turn_kernel, count),
        [shape((width, count * seqs), BF16), shape((cols, count * seqs), BF16)],
        [pltpu.VMEM((count,) + pack.shape, BF16),
         pltpu.VMEM((count * seqs // LANES, width, LANES), F32)],
        rights, flops=1 << 36, name="turn")
    updated, left_edge, right_edge, low_edge, high_edge, normed_pair = call(
        edges_kernel,
        [shape((rows, cols, channels), BF16), shape((rows, cols, channels), BF16),
         shape((cols, rows, channels), BF16), shape((cols // 2, rows, channels), BF16),
         shape((cols // 2, rows, channels), BF16), shape((rows * cols, channels), BF16)],
        [pltpu.VMEM((count,) + pack.shape, BF16),
         pltpu.VMEM((rows // per * cols, half * LANES), BF16),
         pltpu.VMEM((rows * cols, channels), F32)],
        [turned, live] + lefts + [
            base, block, residue, flat(pair_norm_gain), flat(pair_norm_bias),
            triangle_projection_weights, flat(triangle_projection_biases)],
        name="edges")
    near_parts = [
        (step, 0, send_same_core(right_edge, count, chips, step)) for step in range(chips)]
    far_parts = [
        (step, skip, send_same_core(half_edge, count, chips, step))
        for step in range(chips, count, 2) for skip, half_edge in ((0, low_edge), (cols // 2, high_edge))]
    for step, skip, block_far in far_parts[:]:
        carried = call(carry_kernel, shape(block_far.shape, BF16), [], [block_far], flops=1 << 29,
                       name="carry")
        far_parts.append((step + 1, skip, pass_on(carried, count)))
    left_edges = [left_edge] + send_chips(left_edge, chips)
    gate = call(gate_kernel, shape((rows * cols, channels), F32), [],
                [normed_pair, triangle_projection_weights, flat(triangle_projection_biases)],
                flops=1 << 30, name="gate")
    block_sums = shape((rows * cols, channels), F32)
    panel = call(panel_kernel, shape((chips, rows * cols, channels), F32), [],
                 left_edges + [gate], flops=1 << 28, name="panel")
    near, far = [], []
    for sums, parts in ((far, far_parts[:-1]), (near, near_parts)):
        for step, skip, right_block in parts:
            sums[:] = [call(
                functools.partial(step_kernel, step, chips, skip, 0, not sums), block_sums,
                [pltpu.VMEM((right_block.shape[0] * rows, channels), F32)],
                [right_block, panel] + sums, name="triangle")]
    step, skip, right_block = far_parts[-1]
    part = rows // 2
    own_sums, other_sums, result = [], [], []
    for first in (0, part):
        own, half_sums = call(
            functools.partial(last_kernel, step, chips, skip, first),
            [shape((part * cols, channels), F32), shape((part * cols, channels), BF16)],
            [pltpu.VMEM((right_block.shape[0] * rows, channels), F32),
             pltpu.VMEM((part * cols, channels), F32)],
            [right_block, panel] + far + near, flops=1 << 28, name="last")
        own_sums.append(own)
        other_sums.append(swap_cores(half_sums, count))
    for n, first in enumerate((0, part)):
        args = [own_sums[n], other_sums[n], updated, gate, flat(triangle_sum_norm_gain),
                flat(triangle_sum_norm_bias), triangle_output_weight, flat(outer_pair_bias)]
        half_shape = (part, cols, channels)
        result = [call(
            functools.partial(final_kernel, first),
            shape((rows, cols, channels) if n else half_shape, BF16),
            [pltpu.VMEM(half_shape, BF16), pltpu.SemaphoreType.DMA((1 + part // 8,))] if n else [],
            args + result, flops=1 << 28, hbm=n == 1, name="final")]
    return result[0]


def solution(mesh):
    pair = P(("groups", "resi"), ("resj", "seq"), None)
    placed = (
        P(("groups", "resj", "seq"), "resi", None),
        P(("groups", "resj", "seq"), "resi"),
        pair,
        P("groups"),
        P("groups"),
    ) + (P(),) * 14
    return jax.shard_map(body, mesh=mesh, in_specs=placed, out_specs=pair, check_vma=False)
```

```python
import functools

import jax
import jax.numpy as jnp
from jax import lax
from jax.experimental import pallas as pl
from jax.experimental.pallas import tpu as pltpu
from jax.sharding import PartitionSpec as P

RELMAX = 32
LANES = 128
PLANE = ("resj", "seq")
GROUP = ("resi", "resj", "seq")
F32 = jnp.float32
BF16 = jnp.bfloat16
MIB = 1 << 20


def iota(shape, axis):
    return lax.broadcasted_iota(jnp.int32, shape, axis)


def dot(a, b):
    return jnp.dot(a, b, preferred_element_type=F32)


def sigmoid(v):
    return 0.5 * jnp.tanh(0.5 * v) + 0.5


def layer_norm(values, gain, shift):
    average = jnp.mean(values, axis=-1, keepdims=True)
    centred = values - average
    variance = jnp.mean(centred * centred, axis=-1, keepdims=True)
    return centred * lax.rsqrt(variance + 1e-05) * gain + shift


def norm_kernel(x_ref, out_ref):
    x = x_ref[...].reshape(out_ref.shape).astype(F32)
    out_ref[...] = layer_norm(x, 1.0, 0.0)


def pack_kernel(x_ref, mask_ref, res_ref, gain_ref, shift_ref, w_ref, bias_ref,
                left_ref, right_ref, lscr, rscr):
    seqs, rows = mask_ref.shape
    half = w_ref.shape[0] // 2
    per = LANES // half
    row_start = lax.axis_index("resi") * rows
    normed = (x_ref[...] * gain_ref[...] + shift_ref[...]).astype(BF16)
    lane = iota((2 * half, 2 * LANES), 1)
    spread = lane % half + jnp.where(lane >= LANES, half, 0) == iota((2 * half, 2 * LANES), 0)
    spread = spread.astype(F32)
    wide = lax.dot_general(
        w_ref[...], spread.astype(BF16), (((0,), (0,)), ((), ())), preferred_element_type=F32)
    wide = wide.astype(BF16)
    bias = jnp.dot(jnp.broadcast_to(bias_ref[...], (8, 2 * half)), spread,
                   precision=lax.Precision.HIGHEST, preferred_element_type=F32)[0:1]
    mapped = dot(normed, wide)
    lscr[...] = mapped[:, :LANES]
    rscr[...] = mapped[:, LANES:]
    row_live = pick_rows(res_ref[...], row_start, rows)
    live = (mask_ref[...].astype(F32) * row_live).astype(BF16)
    width = rows * half
    spread_live = (iota((rows, width), 1) // half == iota((rows, width), 0)).astype(BF16)
    live_wide = dot(live, spread_live)
    sub = iota((seqs, LANES), 1) // half
    for tile in range(width // LANES):
        at = slice(tile * LANES, (tile + 1) * LANES)
        for ref, scr, first in ((left_ref, lscr, 0), (right_ref, rscr, LANES)):
            value = scr[pl.ds(tile * per, seqs, stride=rows), :]
            for k in range(1, per):
                value = jnp.where(sub == k, scr[pl.ds(tile * per + k, seqs, stride=rows), :], value)
            value = (value + bias[:, first:first + LANES]) * live_wide[:, at]
            ref[:, at] = value.astype(BF16)
    live_tile = dot(live, (iota((rows, LANES), 0) == iota((rows, LANES), 1)).astype(BF16))
    for ref in (left_ref, right_ref):
        ref[:, width:] = live_tile.astype(BF16)


def carry_kernel(in_ref, out_ref):
    out_ref[...] = in_ref[...]


def join_kernel(count, *refs):
    for n in range(count):
        refs[-1][n] = refs[n][...]


def pick_columns(values, start, size):
    total = values.shape[1]
    own = iota((size, total), 1) == iota((size, total), 0) + start
    spread = jnp.broadcast_to(values, (size, total)).astype(F32)
    return jnp.sum(jnp.where(own, spread, 0.0), axis=1, keepdims=True)


def pick_rows(values, start, size):
    total = values.shape[1]
    pick = (iota((total, size), 0) == iota((total, size), 1) + start).astype(BF16)
    return dot(jnp.broadcast_to(values.astype(F32), (8, total)).astype(BF16), pick)[0:1]


def base_kernel(pair_ref, table_ref, chain_ref, w_ref, _, base_ref, block_ref, tscr, wscr):
    rows, cols, channels = pair_ref.shape
    row_start = lax.axis_index("resi") * rows
    col_start = lax.axis_index(PLANE) * cols
    tscr[...] = jnp.zeros_like(tscr)
    tscr[0:table_ref.shape[0], :] = table_ref[...].astype(F32)
    table = tscr[...].astype(BF16)
    chain = chain_ref[...]
    same = pick_columns(chain, col_start, cols) == pick_rows(chain, row_start, rows)
    offset = iota((cols, rows), 0) + col_start - iota((cols, rows), 1) - row_start + RELMAX
    bins = jnp.where(same, jnp.clip(offset, 0, 2 * RELMAX), 2 * RELMAX + 1)
    lane = iota((cols, LANES), 1)
    for i in range(rows):
        one_hot = (lane == bins[:, i:i + 1]).astype(F32).astype(BF16)
        base_ref[i] = pair_ref[i].astype(F32) + dot(one_hot, table)
    wscr[...] = w_ref[...].astype(F32)
    half = int(round(w_ref.shape[0] ** 0.5))
    per = LANES // half
    block_ref[...] = jnp.zeros_like(block_ref)
    for d in range(half):
        value = wscr[pl.ds(d, half, stride=half), :].astype(BF16)
        for k in range(per):
            block_ref[pl.ds(d * LANES + k * half, half), k * channels:(k + 1) * channels] = value


def turn_kernel(count, *refs):
    pairs = count // 2
    rights, (turned_ref, live_ref, rall, tscr) = refs[:pairs], refs[pairs:]
    z = lax.axis_index("resi")
    width, total_seqs = turned_ref.shape
    cols = live_ref.shape[0]
    half = width // cols
    for step in range(pairs):
        for n in range(2):
            rall[z ^ (step + n * pairs)] = rights[step][n]
    right = rall[...].reshape(total_seqs, -1)
    for at in range(0, width, LANES):
        for s in range(0, total_seqs, LANES):
            tscr[s // LANES, at:at + LANES, :] = right[s:s + LANES, at:at + LANES].astype(F32).T
    for d in range(half):
        for s in range(0, total_seqs, LANES):
            turned = tscr[s // LANES, pl.ds(d, cols, stride=half), :]
            turned_ref[d * cols:(d + 1) * cols, s:s + LANES] = turned.astype(BF16)
    live_ref[...] = right[:, width:].astype(F32).T[0:cols].astype(BF16)


def edges_kernel(turned_ref, live_ref, own_ref, swapped_ref, base_ref, block_ref, res_ref,
                 gain_ref, shift_ref, w_ref, bias_ref,
                 updated_ref, left_ref, right_ref, low_ref, high_ref, nscr, lall, oscr, escr):
    rows, cols, channels = base_ref.shape
    chips, seqs = own_ref.shape[:2]
    half = block_ref.shape[0] // LANES
    per = LANES // half
    width = rows * half
    q = lax.axis_index(PLANE)
    row_start, col_start = lax.axis_index("resi") * rows, q * cols
    for step in range(chips):
        lall[q ^ step] = own_ref[step]
        lall[q ^ (chips + step)] = swapped_ref[step]
    left = lall[...].reshape(2 * chips * seqs, -1)
    counts = dot(live_ref[...], left[:, width:])
    inverse = 1.0 / jnp.maximum(counts, 1.0)
    wide = 2 * LANES
    tall = 8
    for first in range(0, width, wide):
        for d0 in range(0, half, tall):
            product = dot(turned_ref[d0 * cols:(d0 + tall) * cols, :], left[:, first:first + wide])
            product = product.astype(BF16)
            for dd in range(tall):
                for t in range(wide // LANES):
                    g = first // LANES + t
                    oscr[g * cols:(g + 1) * cols, (d0 + dd) * LANES:(d0 + dd + 1) * LANES] = (
                        product[dd * cols:(dd + 1) * cols, t * LANES:(t + 1) * LANES])
    outer = dot(oscr[...], block_ref[...])
    for i in range(rows):
        g, k = i // per, i % per
        part = outer[g * cols:(g + 1) * cols, k * channels:(k + 1) * channels]
        updated = (base_ref[i] + part * inverse[:, i:i + 1]).astype(BF16)
        updated_ref[i] = updated
        normed = layer_norm(updated.astype(F32), gain_ref[...], shift_ref[...])
        nscr[i * cols:(i + 1) * cols, :] = normed.astype(BF16)
    live = pick_columns(res_ref[...], col_start, cols) * pick_rows(res_ref[...], row_start, rows)
    chunk = 8
    for i0 in range(0, rows, chunk):
        mixture = dot(nscr[i0 * cols:(i0 + chunk) * cols, :], w_ref[:, :4 * channels])
        mixture = mixture + bias_ref[:, :4 * channels]
        part = [mixture[:, n * channels:(n + 1) * channels] for n in range(4)]
        left_edge = sigmoid(part[0]) * part[1]
        right_edge = sigmoid(part[2]) * part[3]
        for ii in range(chunk):
            here = live[:, i0 + ii:i0 + ii + 1]
            at = slice(ii * cols, (ii + 1) * cols)
            left_ref[i0 + ii] = (left_edge[at] * here).astype(BF16)
            escr[(i0 + ii) * cols:(i0 + ii + 1) * cols, :] = right_edge[at] * here
    part = cols // 2
    for k in range(cols):
        value = escr[pl.ds(k, rows, stride=cols), :].astype(BF16)
        right_ref[k] = value
        (low_ref if k < part else high_ref)[k % part] = value


def gate_kernel(normed_ref, w_ref, bias_ref, gate_ref):
    first = w_ref.shape[1] - gate_ref.shape[1]
    gate_ref[...] = sigmoid(dot(normed_ref[...], w_ref[:, first:]) + bias_ref[:, first:])


def panel_kernel(*refs):
    *lefts, _, panel_ref = refs
    x = lax.axis_index("seq")
    for step, left in enumerate(lefts):
        panel_ref[x ^ step] = left[...].astype(F32).reshape(panel_ref.shape[1:])


def source_of(z, core, x, step, chips):
    block = z ^ step ^ ((x + core) % 2 if step >= chips else core % 2)
    return block // chips, block % chips


def add_block(panel_ref, chip, rscr, cols, skip, first, before, store):
    rows, depth, channels = store.shape[0] // cols, rscr.shape[0] // cols, rscr.shape[1]
    whole = panel_ref.shape[1] // cols
    block = 8
    tiles = cols // 8

    def rows_body(at, carry):
        def place(b, t, start=0):
            return pl.ds(pl.multiple_of((start + at * block + b) * cols + t * 8, 8), 8)

        if before is None:
            sums = [[jnp.zeros((8, channels), F32) for _ in range(tiles)] for _ in range(block)]
        else:
            sums = [[before[place(b, t, first), :] for t in range(tiles)] for b in range(block)]
        for k in range(depth):
            column = [rscr[k * cols + t * 8:k * cols + t * 8 + 8, :] for t in range(tiles)]
            for b in range(block):
                row = panel_ref[chip, pl.ds((first + at * block + b) * whole + skip + k, 1), :]
                for t in range(tiles):
                    sums[b][t] = sums[b][t] + row * column[t]
        for b in range(block):
            for t in range(tiles):
                store[place(b, t), :] = sums[b][t].astype(store.dtype)
        return carry

    lax.fori_loop(0, rows // block, rows_body, 0)


def step_kernel(step, chips, skip, first, fresh, right_ref, panel_ref, *refs):
    out_ref, rscr = refs[-2:]
    z, core, x = [lax.axis_index(axis) for axis in GROUP]
    chip = source_of(z, core, x, step, chips)[1]
    rscr[...] = right_ref[...].astype(F32).reshape(rscr.shape)
    add_block(
        panel_ref, chip, rscr, right_ref.shape[1], skip, first, None if fresh else refs[0], out_ref)


def last_kernel(step, chips, skip, first, right_ref, panel_ref, far_ref, near_ref, own_ref, other_ref,
                rscr, acc):
    step_kernel(step, chips, skip, first, False, right_ref, panel_ref, far_ref, acc, rscr)
    mine = lax.axis_index("resi") // chips == lax.axis_index("resj")
    at = pl.ds(first * right_ref.shape[1], acc.shape[0])

    @pl.when(mine)
    def _():
        own_ref[...] = near_ref[at, :]
        other_ref[...] = acc[...].astype(BF16)

    @pl.when(jnp.logical_not(mine))
    def _():
        own_ref[...] = acc[...]
        other_ref[...] = near_ref[at, :].astype(BF16)


def final_kernel(first, own_ref, other_ref, updated_ref, gate_ref, gain_ref, shift_ref, w_ref, bias_ref,
                 *refs):
    if first:
        before_ref, out_hbm, value_ref, sems = refs
        moves = [pltpu.make_async_copy(before_ref, out_hbm.at[:first], sems.at[0])]
        moves[0].start()
    else:
        value_ref, = refs
    rows, cols, channels = value_ref.shape
    chunk = 8
    for i0 in range(0, rows, chunk):
        at = slice(i0 * cols, (i0 + chunk) * cols)
        here = slice((first + i0) * cols, (first + i0 + chunk) * cols)
        sums = own_ref[at, :] + other_ref[at, :].astype(F32)
        normed = layer_norm(sums, gain_ref[...], shift_ref[...]).astype(BF16)
        result = dot(normed, w_ref[...]) + bias_ref[...]
        updated = updated_ref[first + i0:first + i0 + chunk].reshape(chunk * cols, channels).astype(F32)
        value = updated + gate_ref[here, :] * result
        value_ref[i0:i0 + chunk] = value.astype(BF16).reshape(chunk, cols, channels)
        if first:
            moves.append(pltpu.make_async_copy(
                value_ref.at[i0:i0 + chunk], out_hbm.at[first + i0:first + i0 + chunk],
                sems.at[1 + i0 // chunk]))
            moves[-1].start()
    if first:
        for move in moves:
            move.wait()


def swap_cores(block, count):
    return lax.ppermute(block, PLANE, [(p, p ^ (count // 2)) for p in range(count)])


def send_chips(block, chips):
    return [
        lax.ppermute(block, "seq", [(x, x ^ m) for x in range(chips)]) for m in range(1, chips)
    ]


def send_turned(block, count, steps):
    return [
        lax.ppermute(
            block, GROUP,
            [(z * count + p, (p ^ m) * count + z) for z in range(count) for p in range(count)])
        for m in range(steps)
    ]


def send_same_core(block, count, chips, step):
    pairs = []
    for z in range(count):
        for p in range(count):
            core, x = p // chips, p % chips
            far, chip = source_of(z, core, x, step, chips)
            pairs.append(((far * chips + x) * count + core * chips + chip, z * count + p))
    return lax.ppermute(block, GROUP, pairs)


def pass_on(block, count):
    return lax.ppermute(block, "resi", [(z, z ^ 1) for z in range(count)])


def call(kernel, outs, scratch, args, flops=0, hbm=False, name=None):
    vmem = pl.BlockSpec(memory_space=pltpu.VMEM)
    size = sum(a.size * a.dtype.itemsize for a in args)
    return pl.pallas_call(
        kernel,
        out_shape=outs,
        in_specs=[vmem] * len(args),
        out_specs=[vmem] * len(outs) if isinstance(outs, list) else (
            pl.BlockSpec(memory_space=pl.ANY) if hbm else vmem),
        scratch_shapes=scratch,
        compiler_params=pltpu.CompilerParams(vmem_limit_bytes=40 * MIB),
        cost_estimate=pl.CostEstimate(flops=flops, bytes_accessed=size, transcendentals=0),
        name=name,
    )(*args)


def body(
    homolog_matrix,
    sequence_pad_mask,
    pair_features,
    residue_pad_mask,
    residue_chain_index,
    homolog_standard_factor,
    homolog_standard_offset,
    factor_mapping_matrices,
    outer_side_biases,
    outer_pair_projection,
    relative_position_table,
    pair_norm_gain,
    pair_norm_bias,
    triangle_projection_weights,
    triangle_projection_biases,
    triangle_sum_norm_gain,
    triangle_sum_norm_bias,
    triangle_output_weight,
    outer_pair_bias,
):
    rows, cols, channels = pair_features.shape
    seqs, _, depth = homolog_matrix.shape
    half = factor_mapping_matrices.shape[1] // 2
    per = LANES // half
    count = lax.axis_size(PLANE)
    width = rows * half
    flat = lambda v: v.reshape(1, -1)
    shape = jax.ShapeDtypeStruct
    residue = flat(residue_pad_mask)
    chain = flat(residue_chain_index)
    pack = shape((seqs, width + LANES), BF16)
    chips = lax.axis_size("seq")
    normed = call(norm_kernel, shape((seqs * rows, depth), F32), [], [homolog_matrix],
                  flops=1 << 36, name="norm")
    left, right = call(
        pack_kernel, [pack, pack],
        [pltpu.VMEM((seqs * rows, LANES), F32)] * 2,
        [normed, sequence_pad_mask, residue, flat(homolog_standard_factor),
         flat(homolog_standard_offset), factor_mapping_matrices.T, flat(outer_side_biases)],
        flops=1 << 30, name="pack")
    right_swap = swap_cores(right, count)
    left_blocks = [left] + send_chips(left, chips)
    pair = call(functools.partial(join_kernel, 2), shape((2,) + pack.shape, BF16), [],
                [right, right_swap], name="join")
    base, block = call(
        base_kernel,
        [shape((rows, cols, channels), F32), shape((half * LANES, per * channels), BF16)],
        [pltpu.VMEM((LANES, channels), F32), pltpu.VMEM((half * half, channels), F32)],
        [pair_features, relative_position_table, chain, outer_pair_projection, pair],
        flops=1 << 30, name="base")
    rights = send_turned(pair, count, count // 2)
    own_lefts = call(functools.partial(join_kernel, chips), shape((chips,) + pack.shape, BF16), [],
                     left_blocks, flops=1 << 36, name="join")
    lefts = [own_lefts, swap_cores(own_lefts, count)]
    turned, live = call(
        functools.partial(turn_kernel, count),
        [shape((width, count * seqs), BF16), shape((cols, count * seqs), BF16)],
        [pltpu.VMEM((count,) + pack.shape, BF16),
         pltpu.VMEM((count * seqs // LANES, width, LANES), F32)],
        rights, flops=1 << 36, name="turn")
    updated, left_edge, right_edge, low_edge, high_edge, normed_pair = call(
        edges_kernel,
        [shape((rows, cols, channels), BF16), shape((rows, cols, channels), BF16),
         shape((cols, rows, channels), BF16), shape((cols // 2, rows, channels), BF16),
         shape((cols // 2, rows, channels), BF16), shape((rows * cols, channels), BF16)],
        [pltpu.VMEM((count,) + pack.shape, BF16),
         pltpu.VMEM((rows // per * cols, half * LANES), BF16),
         pltpu.VMEM((rows * cols, channels), F32)],
        [turned, live] + lefts + [
            base, block, residue, flat(pair_norm_gain), flat(pair_norm_bias),
            triangle_projection_weights, flat(triangle_projection_biases)],
        name="edges")
    near_parts = [
        (step, 0, send_same_core(right_edge, count, chips, step)) for step in range(chips)]
    far_parts = [
        (step, skip, send_same_core(half_edge, count, chips, step))
        for step in range(chips, count, 2) for skip, half_edge in ((0, low_edge), (cols // 2, high_edge))]
    for step, skip, block_far in far_parts[::-1]:
        carried = call(carry_kernel, shape(block_far.shape, BF16), [], [block_far], flops=1 << 27,
                       name="carry")
        far_parts.append((step + 1, skip, pass_on(carried, count)))
    left_edges = [left_edge] + send_chips(left_edge, chips)
    gate = call(gate_kernel, shape((rows * cols, channels), F32), [],
                [normed_pair, triangle_projection_weights, flat(triangle_projection_biases)],
                flops=1 << 30, name="gate")
    block_sums = shape((rows * cols, channels), F32)
    panel = call(panel_kernel, shape((chips, rows * cols, channels), F32), [],
                 left_edges + [gate], flops=1 << 28, name="panel")
    near, far = [], []
    for sums, parts in ((far, far_parts[:-1]), (near, near_parts)):
        for step, skip, right_block in parts:
            sums[:] = [call(
                functools.partial(step_kernel, step, chips, skip, 0, not sums), block_sums,
                [pltpu.VMEM((right_block.shape[0] * rows, channels), F32)],
                [right_block, panel] + sums, name="triangle")]
    step, skip, right_block = far_parts[-1]
    part = rows // 2
    own_sums, other_sums, result = [], [], []
    for first in (0, part):
        own, half_sums = call(
            functools.partial(last_kernel, step, chips, skip, first),
            [shape((part * cols, channels), F32), shape((part * cols, channels), BF16)],
            [pltpu.VMEM((right_block.shape[0] * rows, channels), F32),
             pltpu.VMEM((part * cols, channels), F32)],
            [right_block, panel] + far + near, flops=1 << 28, name="last")
        own_sums.append(own)
        other_sums.append(swap_cores(half_sums, count))
    for n, first in enumerate((0, part)):
        args = [own_sums[n], other_sums[n], updated, gate, flat(triangle_sum_norm_gain),
                flat(triangle_sum_norm_bias), triangle_output_weight, flat(outer_pair_bias)]
        half_shape = (part, cols, channels)
        result = [call(
            functools.partial(final_kernel, first),
            shape((rows, cols, channels) if n else half_shape, BF16),
            [pltpu.VMEM(half_shape, BF16), pltpu.SemaphoreType.DMA((1 + part // 8,))] if n else [],
            args + result, flops=1 << 28, hbm=n == 1, name="final")]
    return result[0]


def solution(mesh):
    pair = P(("groups", "resi"), ("resj", "seq"), None)
    placed = (
        P(("groups", "resj", "seq"), "resi", None),
        P(("groups", "resj", "seq"), "resi"),
        pair,
        P("groups"),
        P("groups"),
    ) + (P(),) * 14
    return jax.shard_map(body, mesh=mesh, in_specs=placed, out_specs=pair, check_vma=False)
```

```python
import functools

import jax
import jax.numpy as jnp
from jax import lax
from jax.experimental import pallas as pl
from jax.experimental.pallas import tpu as pltpu
from jax.sharding import PartitionSpec as P

RELMAX = 32
LANES = 128
PLANE = ("resj", "seq")
GROUP = ("resi", "resj", "seq")
F32 = jnp.float32
BF16 = jnp.bfloat16
MIB = 1 << 20


def iota(shape, axis):
    return lax.broadcasted_iota(jnp.int32, shape, axis)


def dot(a, b):
    return jnp.dot(a, b, preferred_element_type=F32)


def sigmoid(v):
    return 0.5 * jnp.tanh(0.5 * v) + 0.5


def layer_norm(values, gain, shift):
    average = jnp.mean(values, axis=-1, keepdims=True)
    centred = values - average
    variance = jnp.mean(centred * centred, axis=-1, keepdims=True)
    return centred * lax.rsqrt(variance + 1e-05) * gain + shift


def norm_kernel(x_ref, out_ref):
    x = x_ref[...].reshape(out_ref.shape).astype(F32)
    out_ref[...] = layer_norm(x, 1.0, 0.0)


def pack_kernel(x_ref, mask_ref, res_ref, gain_ref, shift_ref, w_ref, bias_ref,
                left_ref, right_ref, lscr, rscr):
    seqs, rows = mask_ref.shape
    half = w_ref.shape[0] // 2
    per = LANES // half
    row_start = lax.axis_index("resi") * rows
    normed = (x_ref[...] * gain_ref[...] + shift_ref[...]).astype(BF16)
    lane = iota((2 * half, 2 * LANES), 1)
    spread = lane % half + jnp.where(lane >= LANES, half, 0) == iota((2 * half, 2 * LANES), 0)
    spread = spread.astype(F32)
    wide = lax.dot_general(
        w_ref[...], spread.astype(BF16), (((0,), (0,)), ((), ())), preferred_element_type=F32)
    wide = wide.astype(BF16)
    bias = jnp.dot(jnp.broadcast_to(bias_ref[...], (8, 2 * half)), spread,
                   precision=lax.Precision.HIGHEST, preferred_element_type=F32)[0:1]
    mapped = dot(normed, wide)
    lscr[...] = mapped[:, :LANES]
    rscr[...] = mapped[:, LANES:]
    row_live = pick_rows(res_ref[...], row_start, rows)
    live = (mask_ref[...].astype(F32) * row_live).astype(BF16)
    width = rows * half
    spread_live = (iota((rows, width), 1) // half == iota((rows, width), 0)).astype(BF16)
    live_wide = dot(live, spread_live)
    sub = iota((seqs, LANES), 1) // half
    for tile in range(width // LANES):
        at = slice(tile * LANES, (tile + 1) * LANES)
        for ref, scr, first in ((left_ref, lscr, 0), (right_ref, rscr, LANES)):
            value = scr[pl.ds(tile * per, seqs, stride=rows), :]
            for k in range(1, per):
                value = jnp.where(sub == k, scr[pl.ds(tile * per + k, seqs, stride=rows), :], value)
            value = (value + bias[:, first:first + LANES]) * live_wide[:, at]
            ref[:, at] = value.astype(BF16)
    live_tile = dot(live, (iota((rows, LANES), 0) == iota((rows, LANES), 1)).astype(BF16))
    for ref in (left_ref, right_ref):
        ref[:, width:] = live_tile.astype(BF16)


def join_kernel(count, *refs):
    for n in range(count):
        refs[-1][n] = refs[n][...]


def pick_columns(values, start, size):
    total = values.shape[1]
    own = iota((size, total), 1) == iota((size, total), 0) + start
    spread = jnp.broadcast_to(values, (size, total)).astype(F32)
    return jnp.sum(jnp.where(own, spread, 0.0), axis=1, keepdims=True)


def pick_rows(values, start, size):
    total = values.shape[1]
    pick = (iota((total, size), 0) == iota((total, size), 1) + start).astype(BF16)
    return dot(jnp.broadcast_to(values.astype(F32), (8, total)).astype(BF16), pick)[0:1]


def base_kernel(pair_ref, table_ref, chain_ref, w_ref, _, base_ref, block_ref, tscr, wscr):
    rows, cols, channels = pair_ref.shape
    row_start = lax.axis_index("resi") * rows
    col_start = lax.axis_index(PLANE) * cols
    tscr[...] = jnp.zeros_like(tscr)
    tscr[0:table_ref.shape[0], :] = table_ref[...].astype(F32)
    table = tscr[...].astype(BF16)
    chain = chain_ref[...]
    same = pick_columns(chain, col_start, cols) == pick_rows(chain, row_start, rows)
    offset = iota((cols, rows), 0) + col_start - iota((cols, rows), 1) - row_start + RELMAX
    bins = jnp.where(same, jnp.clip(offset, 0, 2 * RELMAX), 2 * RELMAX + 1)
    lane = iota((cols, LANES), 1)
    for i in range(rows):
        one_hot = (lane == bins[:, i:i + 1]).astype(F32).astype(BF16)
        base_ref[i] = pair_ref[i].astype(F32) + dot(one_hot, table)
    wscr[...] = w_ref[...].astype(F32)
    half = int(round(w_ref.shape[0] ** 0.5))
    per = LANES // half
    block_ref[...] = jnp.zeros_like(block_ref)
    for d in range(half):
        value = wscr[pl.ds(d, half, stride=half), :].astype(BF16)
        for k in range(per):
            block_ref[pl.ds(d * LANES + k * half, half), k * channels:(k + 1) * channels] = value


def turn_kernel(count, *refs):
    pairs = count // 2
    rights, (turned_ref, live_ref, rall, tscr) = refs[:pairs], refs[pairs:]
    z = lax.axis_index("resi")
    width, total_seqs = turned_ref.shape
    cols = live_ref.shape[0]
    half = width // cols
    for step in range(pairs):
        for n in range(2):
            rall[z ^ (step + n * pairs)] = rights[step][n]
    right = rall[...].reshape(total_seqs, -1)
    for at in range(0, width, LANES):
        for s in range(0, total_seqs, LANES):
            tscr[s // LANES, at:at + LANES, :] = right[s:s + LANES, at:at + LANES].astype(F32).T
    for d in range(half):
        for s in range(0, total_seqs, LANES):
            turned = tscr[s // LANES, pl.ds(d, cols, stride=half), :]
            turned_ref[d * cols:(d + 1) * cols, s:s + LANES] = turned.astype(BF16)
    live_ref[...] = right[:, width:].astype(F32).T[0:cols].astype(BF16)


def edges_kernel(turned_ref, live_ref, own_ref, swapped_ref, base_ref, block_ref, res_ref,
                 gain_ref, shift_ref, w_ref, bias_ref,
                 updated_ref, left_ref, right_ref, nscr, lall, oscr, escr):
    rows, cols, channels = base_ref.shape
    chips, seqs = own_ref.shape[:2]
    half = block_ref.shape[0] // LANES
    per = LANES // half
    width = rows * half
    q = lax.axis_index(PLANE)
    row_start, col_start = lax.axis_index("resi") * rows, q * cols
    for step in range(chips):
        lall[q ^ step] = own_ref[step]
        lall[q ^ (chips + step)] = swapped_ref[step]
    left = lall[...].reshape(2 * chips * seqs, -1)
    counts = dot(live_ref[...], left[:, width:])
    inverse = 1.0 / jnp.maximum(counts, 1.0)
    wide = 2 * LANES
    tall = 8
    for first in range(0, width, wide):
        for d0 in range(0, half, tall):
            product = dot(turned_ref[d0 * cols:(d0 + tall) * cols, :], left[:, first:first + wide])
            product = product.astype(BF16)
            for dd in range(tall):
                for t in range(wide // LANES):
                    g = first // LANES + t
                    oscr[g * cols:(g + 1) * cols, (d0 + dd) * LANES:(d0 + dd + 1) * LANES] = (
                        product[dd * cols:(dd + 1) * cols, t * LANES:(t + 1) * LANES])
    outer = dot(oscr[...], block_ref[...])
    for i in range(rows):
        g, k = i // per, i % per
        part = outer[g * cols:(g + 1) * cols, k * channels:(k + 1) * channels]
        updated = (base_ref[i] + part * inverse[:, i:i + 1]).astype(BF16)
        updated_ref[i] = updated
        normed = layer_norm(updated.astype(F32), gain_ref[...], shift_ref[...])
        nscr[i * cols:(i + 1) * cols, :] = normed.astype(BF16)
    live = pick_columns(res_ref[...], col_start, cols) * pick_rows(res_ref[...], row_start, rows)
    chunk = 8
    for i0 in range(0, rows, chunk):
        mixture = dot(nscr[i0 * cols:(i0 + chunk) * cols, :], w_ref[:, :4 * channels])
        mixture = mixture + bias_ref[:, :4 * channels]
        part = [mixture[:, n * channels:(n + 1) * channels] for n in range(4)]
        left_edge = sigmoid(part[0]) * part[1]
        right_edge = sigmoid(part[2]) * part[3]
        for ii in range(chunk):
            here = live[:, i0 + ii:i0 + ii + 1]
            at = slice(ii * cols, (ii + 1) * cols)
            left_ref[i0 + ii] = (left_edge[at] * here).astype(BF16)
            escr[(i0 + ii) * cols:(i0 + ii + 1) * cols, :] = right_edge[at] * here
    for k in range(cols):
        right_ref[k] = escr[pl.ds(k, rows, stride=cols), :].astype(BF16)


def gate_kernel(normed_ref, w_ref, bias_ref, gate_ref):
    first = w_ref.shape[1] - gate_ref.shape[1]
    gate_ref[...] = sigmoid(dot(normed_ref[...], w_ref[:, first:]) + bias_ref[:, first:])


def panel_kernel(*refs):
    *lefts, _, panel_ref = refs
    x = lax.axis_index("seq")
    for step, left in enumerate(lefts):
        panel_ref[x ^ step] = left[...].astype(F32).reshape(panel_ref.shape[1:])


def source_of(z, core, x, step, chips):
    block = z ^ step ^ ((x + core) % 2 if step >= chips else core % 2)
    return block // chips, block % chips


def add_block(panel_ref, chip, rscr, cols, first, before, store):
    rows, depth, channels = store.shape[0] // cols, rscr.shape[0] // cols, rscr.shape[1]
    block = 8
    tiles = cols // 8

    def rows_body(at, carry):
        def place(b, t, start=0):
            return pl.ds(pl.multiple_of((start + at * block + b) * cols + t * 8, 8), 8)

        if before is None:
            sums = [[jnp.zeros((8, channels), F32) for _ in range(tiles)] for _ in range(block)]
        else:
            sums = [[before[place(b, t, first), :] for t in range(tiles)] for b in range(block)]
        for k in range(depth):
            column = [rscr[k * cols + t * 8:k * cols + t * 8 + 8, :] for t in range(tiles)]
            for b in range(block):
                row = panel_ref[chip, pl.ds((first + at * block + b) * depth + k, 1), :]
                for t in range(tiles):
                    sums[b][t] = sums[b][t] + row * column[t]
        for b in range(block):
            for t in range(tiles):
                store[place(b, t), :] = sums[b][t].astype(store.dtype)
        return carry

    lax.fori_loop(0, rows // block, rows_body, 0)


def step_kernel(step, chips, first, fresh, right_ref, panel_ref, *refs):
    out_ref, rscr = refs[-2:]
    z, core, x = [lax.axis_index(axis) for axis in GROUP]
    chip = source_of(z, core, x, step, chips)[1]
    rscr[...] = right_ref[...].astype(F32).reshape(rscr.shape)
    add_block(panel_ref, chip, rscr, right_ref.shape[1], first, None if fresh else refs[0], out_ref)


def last_kernel(step, chips, first, right_ref, panel_ref, far_ref, near_ref, own_ref, other_ref,
                rscr, acc):
    step_kernel(step, chips, first, False, right_ref, panel_ref, far_ref, acc, rscr)
    mine = lax.axis_index("resi") // chips == lax.axis_index("resj")
    at = pl.ds(first * right_ref.shape[1], acc.shape[0])

    @pl.when(mine)
    def _():
        own_ref[...] = near_ref[at, :]
        other_ref[...] = acc[...].astype(BF16)

    @pl.when(jnp.logical_not(mine))
    def _():
        own_ref[...] = acc[...]
        other_ref[...] = near_ref[at, :].astype(BF16)


def final_kernel(first, own_ref, other_ref, updated_ref, gate_ref, gain_ref, shift_ref, w_ref, bias_ref,
                 *refs):
    if first:
        before_ref, out_hbm, value_ref, sems = refs
        moves = [pltpu.make_async_copy(before_ref, out_hbm.at[:first], sems.at[0])]
        moves[0].start()
    else:
        value_ref, = refs
    rows, cols, channels = value_ref.shape
    chunk = 8
    for i0 in range(0, rows, chunk):
        at = slice(i0 * cols, (i0 + chunk) * cols)
        here = slice((first + i0) * cols, (first + i0 + chunk) * cols)
        sums = own_ref[at, :] + other_ref[at, :].astype(F32)
        normed = layer_norm(sums, gain_ref[...], shift_ref[...]).astype(BF16)
        result = dot(normed, w_ref[...]) + bias_ref[...]
        updated = updated_ref[first + i0:first + i0 + chunk].reshape(chunk * cols, channels).astype(F32)
        value = updated + gate_ref[here, :] * result
        value_ref[i0:i0 + chunk] = value.astype(BF16).reshape(chunk, cols, channels)
        if first:
            moves.append(pltpu.make_async_copy(
                value_ref.at[i0:i0 + chunk], out_hbm.at[first + i0:first + i0 + chunk],
                sems.at[1 + i0 // chunk]))
            moves[-1].start()
    if first:
        for move in moves:
            move.wait()


def swap_cores(block, count):
    return lax.ppermute(block, PLANE, [(p, p ^ (count // 2)) for p in range(count)])


def send_chips(block, chips):
    return [
        lax.ppermute(block, "seq", [(x, x ^ m) for x in range(chips)]) for m in range(1, chips)
    ]


def send_turned(block, count, steps):
    return [
        lax.ppermute(
            block, GROUP,
            [(z * count + p, (p ^ m) * count + z) for z in range(count) for p in range(count)])
        for m in range(steps)
    ]


def send_same_core(block, count, chips, step):
    pairs = []
    for z in range(count):
        for p in range(count):
            core, x = p // chips, p % chips
            far, chip = source_of(z, core, x, step, chips)
            pairs.append(((far * chips + x) * count + core * chips + chip, z * count + p))
    return lax.ppermute(block, GROUP, pairs)


def pass_on(block, count):
    return lax.ppermute(block, "resi", [(z, z ^ 1) for z in range(count)])


def call(kernel, outs, scratch, args, flops=0, hbm=False, name=None):
    vmem = pl.BlockSpec(memory_space=pltpu.VMEM)
    size = sum(a.size * a.dtype.itemsize for a in args)
    return pl.pallas_call(
        kernel,
        out_shape=outs,
        in_specs=[vmem] * len(args),
        out_specs=[vmem] * len(outs) if isinstance(outs, list) else (
            pl.BlockSpec(memory_space=pl.ANY) if hbm else vmem),
        scratch_shapes=scratch,
        compiler_params=pltpu.CompilerParams(vmem_limit_bytes=40 * MIB),
        cost_estimate=pl.CostEstimate(flops=flops, bytes_accessed=size, transcendentals=0),
        name=name,
    )(*args)


def body(
    homolog_matrix,
    sequence_pad_mask,
    pair_features,
    residue_pad_mask,
    residue_chain_index,
    homolog_standard_factor,
    homolog_standard_offset,
    factor_mapping_matrices,
    outer_side_biases,
    outer_pair_projection,
    relative_position_table,
    pair_norm_gain,
    pair_norm_bias,
    triangle_projection_weights,
    triangle_projection_biases,
    triangle_sum_norm_gain,
    triangle_sum_norm_bias,
    triangle_output_weight,
    outer_pair_bias,
):
    rows, cols, channels = pair_features.shape
    seqs, _, depth = homolog_matrix.shape
    half = factor_mapping_matrices.shape[1] // 2
    per = LANES // half
    count = lax.axis_size(PLANE)
    width = rows * half
    flat = lambda v: v.reshape(1, -1)
    shape = jax.ShapeDtypeStruct
    residue = flat(residue_pad_mask)
    chain = flat(residue_chain_index)
    pack = shape((seqs, width + LANES), BF16)
    chips = lax.axis_size("seq")
    normed = call(norm_kernel, shape((seqs * rows, depth), F32), [], [homolog_matrix],
                  flops=1 << 36, name="norm")
    left, right = call(
        pack_kernel, [pack, pack],
        [pltpu.VMEM((seqs * rows, LANES), F32)] * 2,
        [normed, sequence_pad_mask, residue, flat(homolog_standard_factor),
         flat(homolog_standard_offset), factor_mapping_matrices.T, flat(outer_side_biases)],
        flops=1 << 30, name="pack")
    right_swap = swap_cores(right, count)
    left_blocks = [left] + send_chips(left, chips)
    pair = call(functools.partial(join_kernel, 2), shape((2,) + pack.shape, BF16), [],
                [right, right_swap], name="join")
    base, block = call(
        base_kernel,
        [shape((rows, cols, channels), F32), shape((half * LANES, per * channels), BF16)],
        [pltpu.VMEM((LANES, channels), F32), pltpu.VMEM((half * half, channels), F32)],
        [pair_features, relative_position_table, chain, outer_pair_projection, pair],
        flops=1 << 30, name="base")
    rights = send_turned(pair, count, count // 2)
    own_lefts = call(functools.partial(join_kernel, chips), shape((chips,) + pack.shape, BF16), [],
                     left_blocks, flops=1 << 36, name="join")
    lefts = [own_lefts, swap_cores(own_lefts, count)]
    turned, live = call(
        functools.partial(turn_kernel, count),
        [shape((width, count * seqs), BF16), shape((cols, count * seqs), BF16)],
        [pltpu.VMEM((count,) + pack.shape, BF16),
         pltpu.VMEM((count * seqs // LANES, width, LANES), F32)],
        rights, flops=1 << 36, name="turn")
    updated, left_edge, right_edge, normed_pair = call(
        edges_kernel,
        [shape((rows, cols, channels), BF16), shape((rows, cols, channels), BF16),
         shape((cols, rows, channels), BF16), shape((rows * cols, channels), BF16)],
        [pltpu.VMEM((count,) + pack.shape, BF16),
         pltpu.VMEM((rows // per * cols, half * LANES), BF16),
         pltpu.VMEM((rows * cols, channels), F32)],
        [turned, live] + lefts + [
            base, block, residue, flat(pair_norm_gain), flat(pair_norm_bias),
            triangle_projection_weights, flat(triangle_projection_biases)],
        name="edges")
    right_edges = [send_same_core(right_edge, count, chips, step) for step in range(chips)]
    for step in range(chips, count, 2):
        block_far = send_same_core(right_edge, count, chips, step)
        right_edges += [block_far, pass_on(block_far, count)]
    left_edges = [left_edge] + send_chips(left_edge, chips)
    gate = call(gate_kernel, shape((rows * cols, channels), F32), [],
                [normed_pair, triangle_projection_weights, flat(triangle_projection_biases)],
                flops=1 << 30, name="gate")
    block_sums = shape((rows * cols, channels), F32)
    scratch = pltpu.VMEM((rows * cols, channels), F32)
    panel = call(panel_kernel, shape((chips, rows * cols, channels), F32), [],
                 left_edges + [gate], name="panel")
    near, far = [], []
    for step in range(count - 1):
        sums = near if step < chips else far
        sums[:] = [call(
            functools.partial(step_kernel, step, chips, 0, not sums), block_sums, [scratch],
            [right_edges[step], panel] + sums, name="triangle")]
    part = rows // 2
    own_sums, other_sums, result = [], [], []
    for first in (0, part):
        own, half_sums = call(
            functools.partial(last_kernel, count - 1, chips, first),
            [shape((part * cols, channels), F32), shape((part * cols, channels), BF16)],
            [scratch, pltpu.VMEM((part * cols, channels), F32)],
            [right_edges[-1], panel] + far + near, flops=1 << 28, name="last")
        own_sums.append(own)
        other_sums.append(swap_cores(half_sums, count))
    for n, first in enumerate((0, part)):
        args = [own_sums[n], other_sums[n], updated, gate, flat(triangle_sum_norm_gain),
                flat(triangle_sum_norm_bias), triangle_output_weight, flat(outer_pair_bias)]
        half_shape = (part, cols, channels)
        result = [call(
            functools.partial(final_kernel, first),
            shape((rows, cols, channels) if n else half_shape, BF16),
            [pltpu.VMEM(half_shape, BF16), pltpu.SemaphoreType.DMA((1 + part // 8,))] if n else [],
            args + result, flops=1 << 28, hbm=n == 1, name="final")]
    return result[0]


def solution(mesh):
    pair = P(("groups", "resi"), ("resj", "seq"), None)
    placed = (
        P(("groups", "resj", "seq"), "resi", None),
        P(("groups", "resj", "seq"), "resi"),
        pair,
        P("groups"),
        P("groups"),
    ) + (P(),) * 14
    return jax.shard_map(body, mesh=mesh, in_specs=placed, out_specs=pair, check_vma=False)
```

```python
import functools

import jax
import jax.numpy as jnp
from jax import lax
from jax.experimental import pallas as pl
from jax.experimental.pallas import tpu as pltpu
from jax.sharding import PartitionSpec as P

RELMAX = 32
LANES = 128
PLANE = ("resj", "seq")
GROUP = ("resi", "resj", "seq")
F32 = jnp.float32
BF16 = jnp.bfloat16
MIB = 1 << 20


def iota(shape, axis):
    return lax.broadcasted_iota(jnp.int32, shape, axis)


def dot(a, b):
    return jnp.dot(a, b, preferred_element_type=F32)


def sigmoid(v):
    return 0.5 * jnp.tanh(0.5 * v) + 0.5


def layer_norm(values, gain, shift):
    average = jnp.mean(values, axis=-1, keepdims=True)
    centred = values - average
    variance = jnp.mean(centred * centred, axis=-1, keepdims=True)
    return centred * lax.rsqrt(variance + 1e-05) * gain + shift


def norm_kernel(x_ref, out_ref):
    x = x_ref[...].reshape(out_ref.shape).astype(F32)
    out_ref[...] = layer_norm(x, 1.0, 0.0)


def pack_kernel(x_ref, mask_ref, res_ref, gain_ref, shift_ref, w_ref, bias_ref,
                left_ref, right_ref, lscr, rscr):
    seqs, rows = mask_ref.shape
    half = w_ref.shape[0] // 2
    per = LANES // half
    row_start = lax.axis_index("resi") * rows
    normed = (x_ref[...] * gain_ref[...] + shift_ref[...]).astype(BF16)
    lane = iota((2 * half, 2 * LANES), 1)
    spread = lane % half + jnp.where(lane >= LANES, half, 0) == iota((2 * half, 2 * LANES), 0)
    spread = spread.astype(F32)
    wide = lax.dot_general(
        w_ref[...], spread.astype(BF16), (((0,), (0,)), ((), ())), preferred_element_type=F32)
    wide = wide.astype(BF16)
    bias = jnp.dot(jnp.broadcast_to(bias_ref[...], (8, 2 * half)), spread,
                   precision=lax.Precision.HIGHEST, preferred_element_type=F32)[0:1]
    mapped = dot(normed, wide)
    lscr[...] = mapped[:, :LANES]
    rscr[...] = mapped[:, LANES:]
    row_live = pick_rows(res_ref[...], row_start, rows)
    live = (mask_ref[...].astype(F32) * row_live).astype(BF16)
    width = rows * half
    spread_live = (iota((rows, width), 1) // half == iota((rows, width), 0)).astype(BF16)
    live_wide = dot(live, spread_live)
    sub = iota((seqs, LANES), 1) // half
    for tile in range(width // LANES):
        at = slice(tile * LANES, (tile + 1) * LANES)
        for ref, scr, first in ((left_ref, lscr, 0), (right_ref, rscr, LANES)):
            value = scr[pl.ds(tile * per, seqs, stride=rows), :]
            for k in range(1, per):
                value = jnp.where(sub == k, scr[pl.ds(tile * per + k, seqs, stride=rows), :], value)
            value = (value + bias[:, first:first + LANES]) * live_wide[:, at]
            ref[:, at] = value.astype(BF16)
    live_tile = dot(live, (iota((rows, LANES), 0) == iota((rows, LANES), 1)).astype(BF16))
    for ref in (left_ref, right_ref):
        ref[:, width:] = live_tile.astype(BF16)


def join_kernel(count, *refs):
    for n in range(count):
        refs[-1][n] = refs[n][...]


def pick_columns(values, start, size):
    total = values.shape[1]
    own = iota((size, total), 1) == iota((size, total), 0) + start
    spread = jnp.broadcast_to(values, (size, total)).astype(F32)
    return jnp.sum(jnp.where(own, spread, 0.0), axis=1, keepdims=True)


def pick_rows(values, start, size):
    total = values.shape[1]
    pick = (iota((total, size), 0) == iota((total, size), 1) + start).astype(BF16)
    return dot(jnp.broadcast_to(values.astype(F32), (8, total)).astype(BF16), pick)[0:1]


def base_kernel(pair_ref, table_ref, chain_ref, w_ref, _, base_ref, block_ref, tscr, wscr):
    rows, cols, channels = pair_ref.shape
    row_start = lax.axis_index("resi") * rows
    col_start = lax.axis_index(PLANE) * cols
    tscr[...] = jnp.zeros_like(tscr)
    tscr[0:table_ref.shape[0], :] = table_ref[...].astype(F32)
    table = tscr[...].astype(BF16)
    chain = chain_ref[...]
    same = pick_columns(chain, col_start, cols) == pick_rows(chain, row_start, rows)
    offset = iota((cols, rows), 0) + col_start - iota((cols, rows), 1) - row_start + RELMAX
    bins = jnp.where(same, jnp.clip(offset, 0, 2 * RELMAX), 2 * RELMAX + 1)
    lane = iota((cols, LANES), 1)
    for i in range(rows):
        one_hot = (lane == bins[:, i:i + 1]).astype(F32).astype(BF16)
        base_ref[i] = pair_ref[i].astype(F32) + dot(one_hot, table)
    wscr[...] = w_ref[...].astype(F32)
    half = int(round(w_ref.shape[0] ** 0.5))
    per = LANES // half
    block_ref[...] = jnp.zeros_like(block_ref)
    for d in range(half):
        value = wscr[pl.ds(d, half, stride=half), :].astype(BF16)
        for k in range(per):
            block_ref[pl.ds(d * LANES + k * half, half), k * channels:(k + 1) * channels] = value


def turn_kernel(count, *refs):
    pairs = count // 2
    rights, (turned_ref, live_ref, rall, tscr) = refs[:pairs], refs[pairs:]
    z = lax.axis_index("resi")
    width, total_seqs = turned_ref.shape
    cols = live_ref.shape[0]
    half = width // cols
    for step in range(pairs):
        for n in range(2):
            rall[z ^ (step + n * pairs)] = rights[step][n]
    right = rall[...].reshape(total_seqs, -1)
    for at in range(0, width, LANES):
        for s in range(0, total_seqs, LANES):
            tscr[s // LANES, at:at + LANES, :] = right[s:s + LANES, at:at + LANES].astype(F32).T
    for d in range(half):
        for s in range(0, total_seqs, LANES):
            turned = tscr[s // LANES, pl.ds(d, cols, stride=half), :]
            turned_ref[d * cols:(d + 1) * cols, s:s + LANES] = turned.astype(BF16)
    live_ref[...] = right[:, width:].astype(F32).T[0:cols].astype(BF16)


def edges_kernel(turned_ref, live_ref, own_ref, swapped_ref, base_ref, block_ref, res_ref,
                 gain_ref, shift_ref, w_ref, bias_ref,
                 updated_ref, left_ref, right_ref, nscr, lall, oscr, escr):
    rows, cols, channels = base_ref.shape
    chips, seqs = own_ref.shape[:2]
    half = block_ref.shape[0] // LANES
    per = LANES // half
    width = rows * half
    q = lax.axis_index(PLANE)
    row_start, col_start = lax.axis_index("resi") * rows, q * cols
    for step in range(chips):
        lall[q ^ step] = own_ref[step]
        lall[q ^ (chips + step)] = swapped_ref[step]
    left = lall[...].reshape(2 * chips * seqs, -1)
    counts = dot(live_ref[...], left[:, width:])
    inverse = 1.0 / jnp.maximum(counts, 1.0)
    wide = 2 * LANES
    tall = 8
    for first in range(0, width, wide):
        for d0 in range(0, half, tall):
            product = dot(turned_ref[d0 * cols:(d0 + tall) * cols, :], left[:, first:first + wide])
            product = product.astype(BF16)
            for dd in range(tall):
                for t in range(wide // LANES):
                    g = first // LANES + t
                    oscr[g * cols:(g + 1) * cols, (d0 + dd) * LANES:(d0 + dd + 1) * LANES] = (
                        product[dd * cols:(dd + 1) * cols, t * LANES:(t + 1) * LANES])
    outer = dot(oscr[...], block_ref[...])
    for i in range(rows):
        g, k = i // per, i % per
        part = outer[g * cols:(g + 1) * cols, k * channels:(k + 1) * channels]
        updated = (base_ref[i] + part * inverse[:, i:i + 1]).astype(BF16)
        updated_ref[i] = updated
        normed = layer_norm(updated.astype(F32), gain_ref[...], shift_ref[...])
        nscr[i * cols:(i + 1) * cols, :] = normed.astype(BF16)
    live = pick_columns(res_ref[...], col_start, cols) * pick_rows(res_ref[...], row_start, rows)
    chunk = 8
    for i0 in range(0, rows, chunk):
        mixture = dot(nscr[i0 * cols:(i0 + chunk) * cols, :], w_ref[:, :4 * channels])
        mixture = mixture + bias_ref[:, :4 * channels]
        part = [mixture[:, n * channels:(n + 1) * channels] for n in range(4)]
        left_edge = sigmoid(part[0]) * part[1]
        right_edge = sigmoid(part[2]) * part[3]
        for ii in range(chunk):
            here = live[:, i0 + ii:i0 + ii + 1]
            at = slice(ii * cols, (ii + 1) * cols)
            left_ref[i0 + ii] = (left_edge[at] * here).astype(BF16)
            escr[(i0 + ii) * cols:(i0 + ii + 1) * cols, :] = right_edge[at] * here
    for k in range(cols):
        right_ref[k] = escr[pl.ds(k, rows, stride=cols), :].astype(BF16)


def gate_kernel(normed_ref, w_ref, bias_ref, gate_ref):
    first = w_ref.shape[1] - gate_ref.shape[1]
    gate_ref[...] = sigmoid(dot(normed_ref[...], w_ref[:, first:]) + bias_ref[:, first:])


def panel_kernel(*refs):
    *lefts, _, panel_ref = refs
    x = lax.axis_index("seq")
    for step, left in enumerate(lefts):
        panel_ref[x ^ step] = left[...].astype(F32).reshape(panel_ref.shape[1:])


def source_of(z, core, x, step, chips):
    block = z ^ step ^ ((x + core) % 2 if step >= chips else 0)
    return block // chips, block % chips


def add_block(panel_ref, chip, rscr, cols, first, before, store):
    rows, depth, channels = store.shape[0] // cols, rscr.shape[0] // cols, rscr.shape[1]
    block = 8
    tiles = cols // 8

    def rows_body(at, carry):
        def place(b, t, start=0):
            return pl.ds(pl.multiple_of((start + at * block + b) * cols + t * 8, 8), 8)

        if before is None:
            sums = [[jnp.zeros((8, channels), F32) for _ in range(tiles)] for _ in range(block)]
        else:
            sums = [[before[place(b, t, first), :] for t in range(tiles)] for b in range(block)]
        for k in range(depth):
            column = [rscr[k * cols + t * 8:k * cols + t * 8 + 8, :] for t in range(tiles)]
            for b in range(block):
                row = panel_ref[chip, pl.ds((first + at * block + b) * depth + k, 1), :]
                for t in range(tiles):
                    sums[b][t] = sums[b][t] + row * column[t]
        for b in range(block):
            for t in range(tiles):
                store[place(b, t), :] = sums[b][t].astype(store.dtype)
        return carry

    lax.fori_loop(0, rows // block, rows_body, 0)


def step_kernel(step, chips, first, fresh, right_ref, panel_ref, *refs):
    out_ref, rscr = refs[-2:]
    z, core, x = [lax.axis_index(axis) for axis in GROUP]
    chip = source_of(z, core, x, step, chips)[1]
    rscr[...] = right_ref[...].astype(F32).reshape(rscr.shape)
    add_block(panel_ref, chip, rscr, right_ref.shape[1], first, None if fresh else refs[0], out_ref)


def last_kernel(step, chips, first, right_ref, panel_ref, far_ref, near_ref, own_ref, other_ref,
                rscr, acc):
    step_kernel(step, chips, first, False, right_ref, panel_ref, far_ref, acc, rscr)
    mine = lax.axis_index("resi") // chips == lax.axis_index("resj")
    at = pl.ds(first * right_ref.shape[1], acc.shape[0])

    @pl.when(mine)
    def _():
        own_ref[...] = near_ref[at, :]
        other_ref[...] = acc[...].astype(BF16)

    @pl.when(jnp.logical_not(mine))
    def _():
        own_ref[...] = acc[...]
        other_ref[...] = near_ref[at, :].astype(BF16)


def final_kernel(first, own_ref, other_ref, updated_ref, gate_ref, gain_ref, shift_ref, w_ref, bias_ref,
                 *refs):
    if first:
        before_ref, out_hbm, value_ref, sems = refs
        moves = [pltpu.make_async_copy(before_ref, out_hbm.at[:first], sems.at[0])]
        moves[0].start()
    else:
        value_ref, = refs
    rows, cols, channels = value_ref.shape
    chunk = 8
    for i0 in range(0, rows, chunk):
        at = slice(i0 * cols, (i0 + chunk) * cols)
        here = slice((first + i0) * cols, (first + i0 + chunk) * cols)
        sums = own_ref[at, :] + other_ref[at, :].astype(F32)
        normed = layer_norm(sums, gain_ref[...], shift_ref[...]).astype(BF16)
        result = dot(normed, w_ref[...]) + bias_ref[...]
        updated = updated_ref[first + i0:first + i0 + chunk].reshape(chunk * cols, channels).astype(F32)
        value = updated + gate_ref[here, :] * result
        value_ref[i0:i0 + chunk] = value.astype(BF16).reshape(chunk, cols, channels)
        if first:
            moves.append(pltpu.make_async_copy(
                value_ref.at[i0:i0 + chunk], out_hbm.at[first + i0:first + i0 + chunk],
                sems.at[1 + i0 // chunk]))
            moves[-1].start()
    if first:
        for move in moves:
            move.wait()


def swap_cores(block, count):
    return lax.ppermute(block, PLANE, [(p, p ^ (count // 2)) for p in range(count)])


def send_chips(block, chips):
    return [
        lax.ppermute(block, "seq", [(x, x ^ m) for x in range(chips)]) for m in range(1, chips)
    ]


def send_turned(block, count, steps):
    return [
        lax.ppermute(
            block, GROUP,
            [(z * count + p, (p ^ m) * count + z) for z in range(count) for p in range(count)])
        for m in range(steps)
    ]


def send_same_core(block, count, chips, step):
    pairs = []
    for z in range(count):
        for p in range(count):
            core, x = p // chips, p % chips
            far, chip = source_of(z, core, x, step, chips)
            pairs.append(((far * chips + x) * count + core * chips + chip, z * count + p))
    return lax.ppermute(block, GROUP, pairs)


def pass_on(block, count):
    return lax.ppermute(block, "resi", [(z, z ^ 1) for z in range(count)])


def call(kernel, outs, scratch, args, flops=0, hbm=False, name=None):
    vmem = pl.BlockSpec(memory_space=pltpu.VMEM)
    size = sum(a.size * a.dtype.itemsize for a in args)
    return pl.pallas_call(
        kernel,
        out_shape=outs,
        in_specs=[vmem] * len(args),
        out_specs=[vmem] * len(outs) if isinstance(outs, list) else (
            pl.BlockSpec(memory_space=pl.ANY) if hbm else vmem),
        scratch_shapes=scratch,
        compiler_params=pltpu.CompilerParams(vmem_limit_bytes=40 * MIB),
        cost_estimate=pl.CostEstimate(flops=flops, bytes_accessed=size, transcendentals=0),
        name=name,
    )(*args)


def body(
    homolog_matrix,
    sequence_pad_mask,
    pair_features,
    residue_pad_mask,
    residue_chain_index,
    homolog_standard_factor,
    homolog_standard_offset,
    factor_mapping_matrices,
    outer_side_biases,
    outer_pair_projection,
    relative_position_table,
    pair_norm_gain,
    pair_norm_bias,
    triangle_projection_weights,
    triangle_projection_biases,
    triangle_sum_norm_gain,
    triangle_sum_norm_bias,
    triangle_output_weight,
    outer_pair_bias,
):
    rows, cols, channels = pair_features.shape
    seqs, _, depth = homolog_matrix.shape
    half = factor_mapping_matrices.shape[1] // 2
    per = LANES // half
    count = lax.axis_size(PLANE)
    width = rows * half
    flat = lambda v: v.reshape(1, -1)
    shape = jax.ShapeDtypeStruct
    residue = flat(residue_pad_mask)
    chain = flat(residue_chain_index)
    pack = shape((seqs, width + LANES), BF16)
    chips = lax.axis_size("seq")
    normed = call(norm_kernel, shape((seqs * rows, depth), F32), [], [homolog_matrix],
                  flops=1 << 36, name="norm")
    left, right = call(
        pack_kernel, [pack, pack],
        [pltpu.VMEM((seqs * rows, LANES), F32)] * 2,
        [normed, sequence_pad_mask, residue, flat(homolog_standard_factor),
         flat(homolog_standard_offset), factor_mapping_matrices.T, flat(outer_side_biases)],
        flops=1 << 30, name="pack")
    right_swap = swap_cores(right, count)
    left_blocks = [left] + send_chips(left, chips)
    pair = call(functools.partial(join_kernel, 2), shape((2,) + pack.shape, BF16), [],
                [right, right_swap], name="join")
    base, block = call(
        base_kernel,
        [shape((rows, cols, channels), F32), shape((half * LANES, per * channels), BF16)],
        [pltpu.VMEM((LANES, channels), F32), pltpu.VMEM((half * half, channels), F32)],
        [pair_features, relative_position_table, chain, outer_pair_projection, pair],
        flops=1 << 30, name="base")
    rights = send_turned(pair, count, count // 2)
    own_lefts = call(functools.partial(join_kernel, chips), shape((chips,) + pack.shape, BF16), [],
                     left_blocks, flops=1 << 36, name="join")
    lefts = [own_lefts, swap_cores(own_lefts, count)]
    turned, live = call(
        functools.partial(turn_kernel, count),
        [shape((width, count * seqs), BF16), shape((cols, count * seqs), BF16)],
        [pltpu.VMEM((count,) + pack.shape, BF16),
         pltpu.VMEM((count * seqs // LANES, width, LANES), F32)],
        rights, flops=1 << 36, name="turn")
    updated, left_edge, right_edge, normed_pair = call(
        edges_kernel,
        [shape((rows, cols, channels), BF16), shape((rows, cols, channels), BF16),
         shape((cols, rows, channels), BF16), shape((rows * cols, channels), BF16)],
        [pltpu.VMEM((count,) + pack.shape, BF16),
         pltpu.VMEM((rows // per * cols, half * LANES), BF16),
         pltpu.VMEM((rows * cols, channels), F32)],
        [turned, live] + lefts + [
            base, block, residue, flat(pair_norm_gain), flat(pair_norm_bias),
            triangle_projection_weights, flat(triangle_projection_biases)],
        name="edges")
    right_edges = [send_same_core(right_edge, count, chips, step) for step in range(chips)]
    for step in range(chips, count, 2):
        block_far = send_same_core(right_edge, count, chips, step)
        right_edges += [block_far, pass_on(block_far, count)]
    left_edges = [left_edge] + send_chips(left_edge, chips)
    gate = call(gate_kernel, shape((rows * cols, channels), F32), [],
                [normed_pair, triangle_projection_weights, flat(triangle_projection_biases)],
                flops=1 << 30, name="gate")
    block_sums = shape((rows * cols, channels), F32)
    scratch = pltpu.VMEM((rows * cols, channels), F32)
    panel = call(panel_kernel, shape((chips, rows * cols, channels), F32), [],
                 left_edges + [gate], name="panel")
    near, far = [], []
    for step in range(count - 1):
        sums = near if step < chips else far
        sums[:] = [call(
            functools.partial(step_kernel, step, chips, 0, not sums), block_sums, [scratch],
            [right_edges[step], panel] + sums, name="triangle")]
    parts = ((0, rows * 3 // 4), (rows * 3 // 4, rows // 4))
    own_sums, other_sums, result = [], [], []
    for first, part in parts:
        own, half_sums = call(
            functools.partial(last_kernel, count - 1, chips, first),
            [shape((part * cols, channels), F32), shape((part * cols, channels), BF16)],
            [scratch, pltpu.VMEM((part * cols, channels), F32)],
            [right_edges[-1], panel] + far + near, flops=1 << 28, name="last")
        own_sums.append(own)
        other_sums.append(swap_cores(half_sums, count))
    for n, (first, part) in enumerate(parts):
        args = [own_sums[n], other_sums[n], updated, gate, flat(triangle_sum_norm_gain),
                flat(triangle_sum_norm_bias), triangle_output_weight, flat(outer_pair_bias)]
        part_shape = (part, cols, channels)
        result = [call(
            functools.partial(final_kernel, first),
            shape((rows, cols, channels) if n else part_shape, BF16),
            [pltpu.VMEM(part_shape, BF16), pltpu.SemaphoreType.DMA((1 + part // 8,))] if n else [],
            args + result, flops=1 << 28, hbm=n == 1, name="final")]
    return result[0]


def solution(mesh):
    pair = P(("groups", "resi"), ("resj", "seq"), None)
    placed = (
        P(("groups", "resj", "seq"), "resi", None),
        P(("groups", "resj", "seq"), "resi"),
        pair,
        P("groups"),
        P("groups"),
    ) + (P(),) * 14
    return jax.shard_map(body, mesh=mesh, in_specs=placed, out_specs=pair, check_vma=False)
```

```python
import functools

import jax
import jax.numpy as jnp
from jax import lax
from jax.experimental import pallas as pl
from jax.experimental.pallas import tpu as pltpu
from jax.sharding import PartitionSpec as P

RELMAX = 32
LANES = 128
PLANE = ("resj", "seq")
GROUP = ("resi", "resj", "seq")
F32 = jnp.float32
BF16 = jnp.bfloat16
MIB = 1 << 20


def iota(shape, axis):
    return lax.broadcasted_iota(jnp.int32, shape, axis)


def dot(a, b):
    return jnp.dot(a, b, preferred_element_type=F32)


def sigmoid(v):
    return 0.5 * jnp.tanh(0.5 * v) + 0.5


def layer_norm(values, gain, shift):
    average = jnp.mean(values, axis=-1, keepdims=True)
    centred = values - average
    variance = jnp.mean(centred * centred, axis=-1, keepdims=True)
    return centred * lax.rsqrt(variance + 1e-05) * gain + shift


def norm_kernel(x_ref, out_ref):
    x = x_ref[...].reshape(out_ref.shape).astype(F32)
    out_ref[...] = layer_norm(x, 1.0, 0.0)


def pack_kernel(x_ref, mask_ref, res_ref, gain_ref, shift_ref, w_ref, bias_ref,
                left_ref, right_ref, lscr, rscr):
    seqs, rows = mask_ref.shape
    half = w_ref.shape[0] // 2
    per = LANES // half
    row_start = lax.axis_index("resi") * rows
    normed = (x_ref[...] * gain_ref[...] + shift_ref[...]).astype(BF16)
    lane = iota((2 * half, 2 * LANES), 1)
    spread = lane % half + jnp.where(lane >= LANES, half, 0) == iota((2 * half, 2 * LANES), 0)
    spread = spread.astype(F32)
    wide = lax.dot_general(
        w_ref[...], spread.astype(BF16), (((0,), (0,)), ((), ())), preferred_element_type=F32)
    wide = wide.astype(BF16)
    bias = jnp.dot(jnp.broadcast_to(bias_ref[...], (8, 2 * half)), spread,
                   precision=lax.Precision.HIGHEST, preferred_element_type=F32)[0:1]
    mapped = dot(normed, wide)
    lscr[...] = mapped[:, :LANES]
    rscr[...] = mapped[:, LANES:]
    row_live = pick_rows(res_ref[...], row_start, rows)
    live = (mask_ref[...].astype(F32) * row_live).astype(BF16)
    width = rows * half
    spread_live = (iota((rows, width), 1) // half == iota((rows, width), 0)).astype(BF16)
    live_wide = dot(live, spread_live)
    sub = iota((seqs, LANES), 1) // half
    for tile in range(width // LANES):
        at = slice(tile * LANES, (tile + 1) * LANES)
        for ref, scr, first in ((left_ref, lscr, 0), (right_ref, rscr, LANES)):
            value = scr[pl.ds(tile * per, seqs, stride=rows), :]
            for k in range(1, per):
                value = jnp.where(sub == k, scr[pl.ds(tile * per + k, seqs, stride=rows), :], value)
            value = (value + bias[:, first:first + LANES]) * live_wide[:, at]
            ref[:, at] = value.astype(BF16)
    live_tile = dot(live, (iota((rows, LANES), 0) == iota((rows, LANES), 1)).astype(BF16))
    for ref in (left_ref, right_ref):
        ref[:, width:] = live_tile.astype(BF16)


def join_kernel(count, *refs):
    for n in range(count):
        refs[-1][n] = refs[n][...]


def pick_columns(values, start, size):
    total = values.shape[1]
    own = iota((size, total), 1) == iota((size, total), 0) + start
    spread = jnp.broadcast_to(values, (size, total)).astype(F32)
    return jnp.sum(jnp.where(own, spread, 0.0), axis=1, keepdims=True)


def pick_rows(values, start, size):
    total = values.shape[1]
    pick = (iota((total, size), 0) == iota((total, size), 1) + start).astype(BF16)
    return dot(jnp.broadcast_to(values.astype(F32), (8, total)).astype(BF16), pick)[0:1]


def base_kernel(pair_ref, table_ref, chain_ref, w_ref, _, base_ref, block_ref, tscr, wscr):
    rows, cols, channels = pair_ref.shape
    row_start = lax.axis_index("resi") * rows
    col_start = lax.axis_index(PLANE) * cols
    tscr[...] = jnp.zeros_like(tscr)
    tscr[0:table_ref.shape[0], :] = table_ref[...].astype(F32)
    table = tscr[...].astype(BF16)
    chain = chain_ref[...]
    same = pick_columns(chain, col_start, cols) == pick_rows(chain, row_start, rows)
    offset = iota((cols, rows), 0) + col_start - iota((cols, rows), 1) - row_start + RELMAX
    bins = jnp.where(same, jnp.clip(offset, 0, 2 * RELMAX), 2 * RELMAX + 1)
    lane = iota((cols, LANES), 1)
    for i in range(rows):
        one_hot = (lane == bins[:, i:i + 1]).astype(F32).astype(BF16)
        base_ref[i] = pair_ref[i].astype(F32) + dot(one_hot, table)
    wscr[...] = w_ref[...].astype(F32)
    half = int(round(w_ref.shape[0] ** 0.5))
    per = LANES // half
    block_ref[...] = jnp.zeros_like(block_ref)
    for d in range(half):
        value = wscr[pl.ds(d, half, stride=half), :].astype(BF16)
        for k in range(per):
            block_ref[pl.ds(d * LANES + k * half, half), k * channels:(k + 1) * channels] = value


def turn_kernel(count, *refs):
    pairs = count // 2
    rights, (turned_ref, live_ref, rall, tscr) = refs[:pairs], refs[pairs:]
    z = lax.axis_index("resi")
    width, total_seqs = turned_ref.shape
    cols = live_ref.shape[0]
    half = width // cols
    for step in range(pairs):
        for n in range(2):
            rall[z ^ (step + n * pairs)] = rights[step][n]
    right = rall[...].reshape(total_seqs, -1)
    for at in range(0, width, LANES):
        for s in range(0, total_seqs, LANES):
            tscr[s // LANES, at:at + LANES, :] = right[s:s + LANES, at:at + LANES].astype(F32).T
    for d in range(half):
        for s in range(0, total_seqs, LANES):
            turned = tscr[s // LANES, pl.ds(d, cols, stride=half), :]
            turned_ref[d * cols:(d + 1) * cols, s:s + LANES] = turned.astype(BF16)
    live_ref[...] = right[:, width:].astype(F32).T[0:cols].astype(BF16)


def edges_kernel(turned_ref, live_ref, own_ref, swapped_ref, base_ref, block_ref, res_ref,
                 gain_ref, shift_ref, w_ref, bias_ref,
                 updated_ref, left_ref, right_ref, nscr, lall, oscr, escr):
    rows, cols, channels = base_ref.shape
    chips, seqs = own_ref.shape[:2]
    half = block_ref.shape[0] // LANES
    per = LANES // half
    width = rows * half
    q = lax.axis_index(PLANE)
    row_start, col_start = lax.axis_index("resi") * rows, q * cols
    for step in range(chips):
        lall[q ^ step] = own_ref[step]
        lall[q ^ (chips + step)] = swapped_ref[step]
    left = lall[...].reshape(2 * chips * seqs, -1)
    counts = dot(live_ref[...], left[:, width:])
    inverse = 1.0 / jnp.maximum(counts, 1.0)
    wide = 2 * LANES
    tall = 8
    for first in range(0, width, wide):
        for d0 in range(0, half, tall):
            product = dot(turned_ref[d0 * cols:(d0 + tall) * cols, :], left[:, first:first + wide])
            product = product.astype(BF16)
            for dd in range(tall):
                for t in range(wide // LANES):
                    g = first // LANES + t
                    oscr[g * cols:(g + 1) * cols, (d0 + dd) * LANES:(d0 + dd + 1) * LANES] = (
                        product[dd * cols:(dd + 1) * cols, t * LANES:(t + 1) * LANES])
    outer = dot(oscr[...], block_ref[...])
    for i in range(rows):
        g, k = i // per, i % per
        part = outer[g * cols:(g + 1) * cols, k * channels:(k + 1) * channels]
        updated = (base_ref[i] + part * inverse[:, i:i + 1]).astype(BF16)
        updated_ref[i] = updated
        normed = layer_norm(updated.astype(F32), gain_ref[...], shift_ref[...])
        nscr[i * cols:(i + 1) * cols, :] = normed.astype(BF16)
    live = pick_columns(res_ref[...], col_start, cols) * pick_rows(res_ref[...], row_start, rows)
    chunk = 8
    for i0 in range(0, rows, chunk):
        mixture = dot(nscr[i0 * cols:(i0 + chunk) * cols, :], w_ref[:, :4 * channels])
        mixture = mixture + bias_ref[:, :4 * channels]
        part = [mixture[:, n * channels:(n + 1) * channels] for n in range(4)]
        left_edge = sigmoid(part[0]) * part[1]
        right_edge = sigmoid(part[2]) * part[3]
        for ii in range(chunk):
            here = live[:, i0 + ii:i0 + ii + 1]
            at = slice(ii * cols, (ii + 1) * cols)
            left_ref[i0 + ii] = (left_edge[at] * here).astype(BF16)
            escr[(i0 + ii) * cols:(i0 + ii + 1) * cols, :] = right_edge[at] * here
    for k in range(cols):
        right_ref[k] = escr[pl.ds(k, rows, stride=cols), :].astype(BF16)


def gate_kernel(normed_ref, w_ref, bias_ref, gate_ref):
    first = w_ref.shape[1] - gate_ref.shape[1]
    gate_ref[...] = sigmoid(dot(normed_ref[...], w_ref[:, first:]) + bias_ref[:, first:])


def panel_kernel(*refs):
    *lefts, _, panel_ref = refs
    x = lax.axis_index("seq")
    for step, left in enumerate(lefts):
        panel_ref[x ^ step] = left[...].astype(F32).reshape(panel_ref.shape[1:])


def source_of(z, x, step, chips):
    block = z ^ step ^ ((x + z // chips) % 2 if step >= chips else 0)
    return block // chips, block % chips


def add_block(panel_ref, chip, rscr, cols, first, before, store):
    rows, depth, channels = store.shape[0] // cols, rscr.shape[0] // cols, rscr.shape[1]
    block = 8
    tiles = cols // 8

    def rows_body(at, carry):
        def place(b, t, start=0):
            return pl.ds(pl.multiple_of((start + at * block + b) * cols + t * 8, 8), 8)

        if before is None:
            sums = [[jnp.zeros((8, channels), F32) for _ in range(tiles)] for _ in range(block)]
        else:
            sums = [[before[place(b, t, first), :] for t in range(tiles)] for b in range(block)]
        for k in range(depth):
            column = [rscr[k * cols + t * 8:k * cols + t * 8 + 8, :] for t in range(tiles)]
            for b in range(block):
                row = panel_ref[chip, pl.ds((first + at * block + b) * depth + k, 1), :]
                for t in range(tiles):
                    sums[b][t] = sums[b][t] + row * column[t]
        for b in range(block):
            for t in range(tiles):
                store[place(b, t), :] = sums[b][t].astype(store.dtype)
        return carry

    lax.fori_loop(0, rows // block, rows_body, 0)


def step_kernel(step, chips, first, fresh, right_ref, panel_ref, *refs):
    out_ref, rscr = refs[-2:]
    chip = source_of(lax.axis_index("resi"), lax.axis_index("seq"), step, chips)[1]
    rscr[...] = right_ref[...].astype(F32).reshape(rscr.shape)
    add_block(panel_ref, chip, rscr, right_ref.shape[1], first, None if fresh else refs[0], out_ref)


def last_kernel(step, chips, first, right_ref, panel_ref, far_ref, near_ref, own_ref, other_ref,
                rscr, acc):
    step_kernel(step, chips, first, False, right_ref, panel_ref, far_ref, acc, rscr)
    mine = lax.axis_index("resi") // chips == lax.axis_index("resj")
    at = pl.ds(first * right_ref.shape[1], acc.shape[0])

    @pl.when(mine)
    def _():
        own_ref[...] = near_ref[at, :]
        other_ref[...] = acc[...].astype(BF16)

    @pl.when(jnp.logical_not(mine))
    def _():
        own_ref[...] = acc[...]
        other_ref[...] = near_ref[at, :].astype(BF16)


def final_kernel(first, own_ref, other_ref, updated_ref, gate_ref, gain_ref, shift_ref, w_ref, bias_ref,
                 *refs):
    if first:
        before_ref, out_hbm, value_ref, sems = refs
        moves = [pltpu.make_async_copy(before_ref, out_hbm.at[:first], sems.at[0])]
        moves[0].start()
    else:
        value_ref, = refs
    rows, cols, channels = value_ref.shape
    chunk = 8
    for i0 in range(0, rows, chunk):
        at = slice(i0 * cols, (i0 + chunk) * cols)
        here = slice((first + i0) * cols, (first + i0 + chunk) * cols)
        sums = own_ref[at, :] + other_ref[at, :].astype(F32)
        normed = layer_norm(sums, gain_ref[...], shift_ref[...]).astype(BF16)
        result = dot(normed, w_ref[...]) + bias_ref[...]
        updated = updated_ref[first + i0:first + i0 + chunk].reshape(chunk * cols, channels).astype(F32)
        value = updated + gate_ref[here, :] * result
        value_ref[i0:i0 + chunk] = value.astype(BF16).reshape(chunk, cols, channels)
        if first:
            moves.append(pltpu.make_async_copy(
                value_ref.at[i0:i0 + chunk], out_hbm.at[first + i0:first + i0 + chunk],
                sems.at[1 + i0 // chunk]))
            moves[-1].start()
    if first:
        for move in moves:
            move.wait()


def swap_cores(block, count):
    return lax.ppermute(block, PLANE, [(p, p ^ (count // 2)) for p in range(count)])


def send_chips(block, chips):
    return [
        lax.ppermute(block, "seq", [(x, x ^ m) for x in range(chips)]) for m in range(1, chips)
    ]


def send_turned(block, count, steps):
    return [
        lax.ppermute(
            block, GROUP,
            [(z * count + p, (p ^ m) * count + z) for z in range(count) for p in range(count)])
        for m in range(steps)
    ]


def send_same_core(block, count, chips, step):
    pairs = []
    for z in range(count):
        for p in range(count):
            core, x = p // chips, p % chips
            far, chip = source_of(z, x, step, chips)
            pairs.append(((far * chips + x) * count + core * chips + chip, z * count + p))
    return lax.ppermute(block, GROUP, pairs)


def pass_on(block, count):
    return lax.ppermute(block, "resi", [(z, z ^ 1) for z in range(count)])


def call(kernel, outs, scratch, args, flops=0, hbm=False, name=None):
    vmem = pl.BlockSpec(memory_space=pltpu.VMEM)
    size = sum(a.size * a.dtype.itemsize for a in args)
    return pl.pallas_call(
        kernel,
        out_shape=outs,
        in_specs=[vmem] * len(args),
        out_specs=[vmem] * len(outs) if isinstance(outs, list) else (
            pl.BlockSpec(memory_space=pl.ANY) if hbm else vmem),
        scratch_shapes=scratch,
        compiler_params=pltpu.CompilerParams(vmem_limit_bytes=40 * MIB),
        cost_estimate=pl.CostEstimate(flops=flops, bytes_accessed=size, transcendentals=0),
        name=name,
    )(*args)


def body(
    homolog_matrix,
    sequence_pad_mask,
    pair_features,
    residue_pad_mask,
    residue_chain_index,
    homolog_standard_factor,
    homolog_standard_offset,
    factor_mapping_matrices,
    outer_side_biases,
    outer_pair_projection,
    relative_position_table,
    pair_norm_gain,
    pair_norm_bias,
    triangle_projection_weights,
    triangle_projection_biases,
    triangle_sum_norm_gain,
    triangle_sum_norm_bias,
    triangle_output_weight,
    outer_pair_bias,
):
    rows, cols, channels = pair_features.shape
    seqs, _, depth = homolog_matrix.shape
    half = factor_mapping_matrices.shape[1] // 2
    per = LANES // half
    count = lax.axis_size(PLANE)
    width = rows * half
    flat = lambda v: v.reshape(1, -1)
    shape = jax.ShapeDtypeStruct
    residue = flat(residue_pad_mask)
    chain = flat(residue_chain_index)
    pack = shape((seqs, width + LANES), BF16)
    chips = lax.axis_size("seq")
    normed = call(norm_kernel, shape((seqs * rows, depth), F32), [], [homolog_matrix],
                  flops=1 << 36, name="norm")
    left, right = call(
        pack_kernel, [pack, pack],
        [pltpu.VMEM((seqs * rows, LANES), F32)] * 2,
        [normed, sequence_pad_mask, residue, flat(homolog_standard_factor),
         flat(homolog_standard_offset), factor_mapping_matrices.T, flat(outer_side_biases)],
        flops=1 << 30, name="pack")
    right_swap = swap_cores(right, count)
    left_blocks = [left] + send_chips(left, chips)
    pair = call(functools.partial(join_kernel, 2), shape((2,) + pack.shape, BF16), [],
                [right, right_swap], name="join")
    base, block = call(
        base_kernel,
        [shape((rows, cols, channels), F32), shape((half * LANES, per * channels), BF16)],
        [pltpu.VMEM((LANES, channels), F32), pltpu.VMEM((half * half, channels), F32)],
        [pair_features, relative_position_table, chain, outer_pair_projection, pair],
        flops=1 << 30, name="base")
    rights = send_turned(pair, count, count // 2)
    own_lefts = call(functools.partial(join_kernel, chips), shape((chips,) + pack.shape, BF16), [],
                     left_blocks, flops=1 << 36, name="join")
    lefts = [own_lefts, swap_cores(own_lefts, count)]
    turned, live = call(
        functools.partial(turn_kernel, count),
        [shape((width, count * seqs), BF16), shape((cols, count * seqs), BF16)],
        [pltpu.VMEM((count,) + pack.shape, BF16),
         pltpu.VMEM((count * seqs // LANES, width, LANES), F32)],
        rights, flops=1 << 36, name="turn")
    updated, left_edge, right_edge, normed_pair = call(
        edges_kernel,
        [shape((rows, cols, channels), BF16), shape((rows, cols, channels), BF16),
         shape((cols, rows, channels), BF16), shape((rows * cols, channels), BF16)],
        [pltpu.VMEM((count,) + pack.shape, BF16),
         pltpu.VMEM((rows // per * cols, half * LANES), BF16),
         pltpu.VMEM((rows * cols, channels), F32)],
        [turned, live] + lefts + [
            base, block, residue, flat(pair_norm_gain), flat(pair_norm_bias),
            triangle_projection_weights, flat(triangle_projection_biases)],
        name="edges")
    right_edges = [send_same_core(right_edge, count, chips, step) for step in range(chips)]
    for step in range(chips, count, 2):
        block_far = send_same_core(right_edge, count, chips, step)
        right_edges += [block_far, pass_on(block_far, count)]
    left_edges = [left_edge] + send_chips(left_edge, chips)
    gate = call(gate_kernel, shape((rows * cols, channels), F32), [],
                [normed_pair, triangle_projection_weights, flat(triangle_projection_biases)],
                flops=1 << 30, name="gate")
    block_sums = shape((rows * cols, channels), F32)
    scratch = pltpu.VMEM((rows * cols, channels), F32)
    panel = call(panel_kernel, shape((chips, rows * cols, channels), F32), [],
                 left_edges + [gate], name="panel")
    near, far = [], []
    for step in range(count - 1):
        sums = near if step < chips else far
        sums[:] = [call(
            functools.partial(step_kernel, step, chips, 0, not sums), block_sums, [scratch],
            [right_edges[step], panel] + sums, name="triangle")]
    parts = ((0, rows * 3 // 4), (rows * 3 // 4, rows // 4))
    own_sums, other_sums, result = [], [], []
    for first, part in parts:
        own, half_sums = call(
            functools.partial(last_kernel, count - 1, chips, first),
            [shape((part * cols, channels), F32), shape((part * cols, channels), BF16)],
            [scratch, pltpu.VMEM((part * cols, channels), F32)],
            [right_edges[-1], panel] + far + near, flops=1 << 28, name="last")
        own_sums.append(own)
        other_sums.append(swap_cores(half_sums, count))
    for n, (first, part) in enumerate(parts):
        args = [own_sums[n], other_sums[n], updated, gate, flat(triangle_sum_norm_gain),
                flat(triangle_sum_norm_bias), triangle_output_weight, flat(outer_pair_bias)]
        part_shape = (part, cols, channels)
        result = [call(
            functools.partial(final_kernel, first),
            shape((rows, cols, channels) if n else part_shape, BF16),
            [pltpu.VMEM(part_shape, BF16), pltpu.SemaphoreType.DMA((1 + part // 8,))] if n else [],
            args + result, flops=1 << 28, hbm=n == 1, name="final")]
    return result[0]


def solution(mesh):
    pair = P(("groups", "resi"), ("resj", "seq"), None)
    placed = (
        P(("groups", "resj", "seq"), "resi", None),
        P(("groups", "resj", "seq"), "resi"),
        pair,
        P("groups"),
        P("groups"),
    ) + (P(),) * 14
    return jax.shard_map(body, mesh=mesh, in_specs=placed, out_specs=pair, check_vma=False)
```

```python
import functools

import jax
import jax.numpy as jnp
from jax import lax
from jax.experimental import pallas as pl
from jax.experimental.pallas import tpu as pltpu
from jax.sharding import PartitionSpec as P

RELMAX = 32
LANES = 128
PLANE = ("resj", "seq")
GROUP = ("resi", "resj", "seq")
F32 = jnp.float32
BF16 = jnp.bfloat16
MIB = 1 << 20


def iota(shape, axis):
    return lax.broadcasted_iota(jnp.int32, shape, axis)


def dot(a, b):
    return jnp.dot(a, b, preferred_element_type=F32)


def sigmoid(v):
    return 0.5 * jnp.tanh(0.5 * v) + 0.5


def layer_norm(values, gain, shift):
    average = jnp.mean(values, axis=-1, keepdims=True)
    centred = values - average
    variance = jnp.mean(centred * centred, axis=-1, keepdims=True)
    return centred * lax.rsqrt(variance + 1e-05) * gain + shift


def norm_kernel(x_ref, out_ref):
    x = x_ref[...].reshape(out_ref.shape).astype(F32)
    out_ref[...] = layer_norm(x, 1.0, 0.0)


def pack_kernel(x_ref, mask_ref, res_ref, gain_ref, shift_ref, w_ref, bias_ref,
                left_ref, right_ref, lscr, rscr):
    seqs, rows = mask_ref.shape
    half = w_ref.shape[0] // 2
    per = LANES // half
    row_start = lax.axis_index("resi") * rows
    normed = (x_ref[...] * gain_ref[...] + shift_ref[...]).astype(BF16)
    lane = iota((2 * half, 2 * LANES), 1)
    spread = lane % half + jnp.where(lane >= LANES, half, 0) == iota((2 * half, 2 * LANES), 0)
    spread = spread.astype(F32)
    wide = lax.dot_general(
        w_ref[...], spread.astype(BF16), (((0,), (0,)), ((), ())), preferred_element_type=F32)
    wide = wide.astype(BF16)
    bias = jnp.dot(jnp.broadcast_to(bias_ref[...], (8, 2 * half)), spread,
                   precision=lax.Precision.HIGHEST, preferred_element_type=F32)[0:1]
    mapped = dot(normed, wide)
    lscr[...] = mapped[:, :LANES]
    rscr[...] = mapped[:, LANES:]
    row_live = pick_rows(res_ref[...], row_start, rows)
    live = (mask_ref[...].astype(F32) * row_live).astype(BF16)
    width = rows * half
    spread_live = (iota((rows, width), 1) // half == iota((rows, width), 0)).astype(BF16)
    live_wide = dot(live, spread_live)
    sub = iota((seqs, LANES), 1) // half
    for tile in range(width // LANES):
        at = slice(tile * LANES, (tile + 1) * LANES)
        for ref, scr, first in ((left_ref, lscr, 0), (right_ref, rscr, LANES)):
            value = scr[pl.ds(tile * per, seqs, stride=rows), :]
            for k in range(1, per):
                value = jnp.where(sub == k, scr[pl.ds(tile * per + k, seqs, stride=rows), :], value)
            value = (value + bias[:, first:first + LANES]) * live_wide[:, at]
            ref[:, at] = value.astype(BF16)
    live_tile = dot(live, (iota((rows, LANES), 0) == iota((rows, LANES), 1)).astype(BF16))
    for ref in (left_ref, right_ref):
        ref[:, width:] = live_tile.astype(BF16)


def join_kernel(count, *refs):
    for n in range(count):
        refs[-1][n] = refs[n][...]


def pick_columns(values, start, size):
    total = values.shape[1]
    own = iota((size, total), 1) == iota((size, total), 0) + start
    spread = jnp.broadcast_to(values, (size, total)).astype(F32)
    return jnp.sum(jnp.where(own, spread, 0.0), axis=1, keepdims=True)


def pick_rows(values, start, size):
    total = values.shape[1]
    pick = (iota((total, size), 0) == iota((total, size), 1) + start).astype(BF16)
    return dot(jnp.broadcast_to(values.astype(F32), (8, total)).astype(BF16), pick)[0:1]


def base_kernel(pair_ref, table_ref, chain_ref, w_ref, _, base_ref, block_ref, tscr, wscr):
    rows, cols, channels = pair_ref.shape
    row_start = lax.axis_index("resi") * rows
    col_start = lax.axis_index(PLANE) * cols
    tscr[...] = jnp.zeros_like(tscr)
    tscr[0:table_ref.shape[0], :] = table_ref[...].astype(F32)
    table = tscr[...].astype(BF16)
    chain = chain_ref[...]
    same = pick_columns(chain, col_start, cols) == pick_rows(chain, row_start, rows)
    offset = iota((cols, rows), 0) + col_start - iota((cols, rows), 1) - row_start + RELMAX
    bins = jnp.where(same, jnp.clip(offset, 0, 2 * RELMAX), 2 * RELMAX + 1)
    lane = iota((cols, LANES), 1)
    for i in range(rows):
        one_hot = (lane == bins[:, i:i + 1]).astype(F32).astype(BF16)
        base_ref[i] = pair_ref[i].astype(F32) + dot(one_hot, table)
    wscr[...] = w_ref[...].astype(F32)
    half = int(round(w_ref.shape[0] ** 0.5))
    per = LANES // half
    block_ref[...] = jnp.zeros_like(block_ref)
    for d in range(half):
        value = wscr[pl.ds(d, half, stride=half), :].astype(BF16)
        for k in range(per):
            block_ref[pl.ds(d * LANES + k * half, half), k * channels:(k + 1) * channels] = value


def turn_kernel(count, *refs):
    pairs = count // 2
    rights, (turned_ref, live_ref, rall, tscr) = refs[:pairs], refs[pairs:]
    z = lax.axis_index("resi")
    width, total_seqs = turned_ref.shape
    cols = live_ref.shape[0]
    half = width // cols
    for step in range(pairs):
        for n in range(2):
            rall[z ^ (step + n * pairs)] = rights[step][n]
    right = rall[...].reshape(total_seqs, -1)
    for at in range(0, width, LANES):
        for s in range(0, total_seqs, LANES):
            tscr[s // LANES, at:at + LANES, :] = right[s:s + LANES, at:at + LANES].astype(F32).T
    for d in range(half):
        for s in range(0, total_seqs, LANES):
            turned = tscr[s // LANES, pl.ds(d, cols, stride=half), :]
            turned_ref[d * cols:(d + 1) * cols, s:s + LANES] = turned.astype(BF16)
    live_ref[...] = right[:, width:].astype(F32).T[0:cols].astype(BF16)


def edges_kernel(turned_ref, live_ref, own_ref, swapped_ref, base_ref, block_ref, res_ref,
                 gain_ref, shift_ref, w_ref, bias_ref,
                 updated_ref, right_ref, nscr, lall, oscr, escr):
    rows, cols, channels = base_ref.shape
    chips, seqs = own_ref.shape[:2]
    half = block_ref.shape[0] // LANES
    per = LANES // half
    width = rows * half
    q = lax.axis_index(PLANE)
    row_start, col_start = lax.axis_index("resi") * rows, q * cols
    for step in range(chips):
        lall[q ^ step] = own_ref[step]
        lall[q ^ (chips + step)] = swapped_ref[step]
    left = lall[...].reshape(2 * chips * seqs, -1)
    counts = dot(live_ref[...], left[:, width:])
    inverse = 1.0 / jnp.maximum(counts, 1.0)
    wide = 2 * LANES
    tall = 8
    for first in range(0, width, wide):
        for d0 in range(0, half, tall):
            product = dot(turned_ref[d0 * cols:(d0 + tall) * cols, :], left[:, first:first + wide])
            product = product.astype(BF16)
            for dd in range(tall):
                for t in range(wide // LANES):
                    g = first // LANES + t
                    oscr[g * cols:(g + 1) * cols, (d0 + dd) * LANES:(d0 + dd + 1) * LANES] = (
                        product[dd * cols:(dd + 1) * cols, t * LANES:(t + 1) * LANES])
    outer = dot(oscr[...], block_ref[...])
    for i in range(rows):
        g, k = i // per, i % per
        part = outer[g * cols:(g + 1) * cols, k * channels:(k + 1) * channels]
        updated = (base_ref[i] + part * inverse[:, i:i + 1]).astype(BF16)
        updated_ref[i] = updated
        normed = layer_norm(updated.astype(F32), gain_ref[...], shift_ref[...])
        nscr[i * cols:(i + 1) * cols, :] = normed.astype(BF16)
    live = pick_columns(res_ref[...], col_start, cols) * pick_rows(res_ref[...], row_start, rows)
    chunk = 8
    for i0 in range(0, rows, chunk):
        mixture = dot(nscr[i0 * cols:(i0 + chunk) * cols, :], w_ref[:, 2 * channels:4 * channels])
        mixture = mixture + bias_ref[:, 2 * channels:4 * channels]
        right_edge = sigmoid(mixture[:, :channels]) * mixture[:, channels:]
        for ii in range(chunk):
            at = slice(ii * cols, (ii + 1) * cols)
            escr[(i0 + ii) * cols:(i0 + ii + 1) * cols, :] = right_edge[at] * live[:, i0 + ii:i0 + ii + 1]
    for k in range(cols):
        right_ref[k] = escr[pl.ds(k, rows, stride=cols), :].astype(BF16)


def left_kernel(normed_ref, res_ref, w_ref, bias_ref, left_ref):
    rows, cols, channels = left_ref.shape
    row_start, col_start = lax.axis_index("resi") * rows, lax.axis_index(PLANE) * cols
    live = pick_columns(res_ref[...], col_start, cols) * pick_rows(res_ref[...], row_start, rows)
    chunk = 8
    for i0 in range(0, rows, chunk):
        mixture = dot(normed_ref[i0 * cols:(i0 + chunk) * cols, :], w_ref[:, :2 * channels])
        mixture = mixture + bias_ref[:, :2 * channels]
        left_edge = sigmoid(mixture[:, :channels]) * mixture[:, channels:]
        for ii in range(chunk):
            here = left_edge[ii * cols:(ii + 1) * cols] * live[:, i0 + ii:i0 + ii + 1]
            left_ref[i0 + ii] = here.astype(BF16)


def gate_kernel(normed_ref, w_ref, bias_ref, gate_ref):
    first = w_ref.shape[1] - gate_ref.shape[1]
    gate_ref[...] = sigmoid(dot(normed_ref[...], w_ref[:, first:]) + bias_ref[:, first:])


def panel_kernel(*refs):
    *lefts, _, panel_ref = refs
    x = lax.axis_index("seq")
    for step, left in enumerate(lefts):
        panel_ref[x ^ step] = left[...].astype(F32).reshape(panel_ref.shape[1:])


def source_of(z, core, x, step, chips):
    block = z ^ step ^ ((x + core) % 2 if step >= chips else 0)
    return block // chips, block % chips


def add_block(panel_ref, chip, rscr, cols, first, before, store):
    rows, depth, channels = store.shape[0] // cols, rscr.shape[0] // cols, rscr.shape[1]
    block = 8
    tiles = cols // 8

    def rows_body(at, carry):
        def place(b, t, start=0):
            return pl.ds(pl.multiple_of((start + at * block + b) * cols + t * 8, 8), 8)

        if before is None:
            sums = [[jnp.zeros((8, channels), F32) for _ in range(tiles)] for _ in range(block)]
        else:
            sums = [[before[place(b, t, first), :] for t in range(tiles)] for b in range(block)]
        for k in range(depth):
            column = [rscr[k * cols + t * 8:k * cols + t * 8 + 8, :] for t in range(tiles)]
            for b in range(block):
                row = panel_ref[chip, pl.ds((first + at * block + b) * depth + k, 1), :]
                for t in range(tiles):
                    sums[b][t] = sums[b][t] + row * column[t]
        for b in range(block):
            for t in range(tiles):
                store[place(b, t), :] = sums[b][t].astype(store.dtype)
        return carry

    lax.fori_loop(0, rows // block, rows_body, 0)


def step_kernel(step, chips, first, fresh, right_ref, panel_ref, *refs):
    out_ref, rscr = refs[-2:]
    z, core, x = [lax.axis_index(axis) for axis in GROUP]
    chip = source_of(z, core, x, step, chips)[1]
    rscr[...] = right_ref[...].astype(F32).reshape(rscr.shape)
    add_block(panel_ref, chip, rscr, right_ref.shape[1], first, None if fresh else refs[0], out_ref)


def last_kernel(step, chips, first, right_ref, panel_ref, far_ref, near_ref, own_ref, other_ref,
                rscr, acc):
    step_kernel(step, chips, first, False, right_ref, panel_ref, far_ref, acc, rscr)
    mine = lax.axis_index("resi") // chips == lax.axis_index("resj")
    at = pl.ds(first * right_ref.shape[1], acc.shape[0])

    @pl.when(mine)
    def _():
        own_ref[...] = near_ref[at, :]
        other_ref[...] = acc[...].astype(BF16)

    @pl.when(jnp.logical_not(mine))
    def _():
        own_ref[...] = acc[...]
        other_ref[...] = near_ref[at, :].astype(BF16)


def final_kernel(first, own_ref, other_ref, updated_ref, gate_ref, gain_ref, shift_ref, w_ref, bias_ref,
                 *refs):
    if first:
        before_ref, out_hbm, value_ref, sems = refs
        moves = [pltpu.make_async_copy(before_ref, out_hbm.at[:first], sems.at[0])]
        moves[0].start()
    else:
        value_ref, = refs
    rows, cols, channels = value_ref.shape
    chunk = 8
    for i0 in range(0, rows, chunk):
        at = slice(i0 * cols, (i0 + chunk) * cols)
        here = slice((first + i0) * cols, (first + i0 + chunk) * cols)
        sums = own_ref[at, :] + other_ref[at, :].astype(F32)
        normed = layer_norm(sums, gain_ref[...], shift_ref[...]).astype(BF16)
        result = dot(normed, w_ref[...]) + bias_ref[...]
        updated = updated_ref[first + i0:first + i0 + chunk].reshape(chunk * cols, channels).astype(F32)
        value = updated + gate_ref[here, :] * result
        value_ref[i0:i0 + chunk] = value.astype(BF16).reshape(chunk, cols, channels)
        if first:
            moves.append(pltpu.make_async_copy(
                value_ref.at[i0:i0 + chunk], out_hbm.at[first + i0:first + i0 + chunk],
                sems.at[1 + i0 // chunk]))
            moves[-1].start()
    if first:
        for move in moves:
            move.wait()


def swap_cores(block, count):
    return lax.ppermute(block, PLANE, [(p, p ^ (count // 2)) for p in range(count)])


def send_chips(block, chips):
    return [
        lax.ppermute(block, "seq", [(x, x ^ m) for x in range(chips)]) for m in range(1, chips)
    ]


def send_turned(block, count, steps):
    return [
        lax.ppermute(
            block, GROUP,
            [(z * count + p, (p ^ m) * count + z) for z in range(count) for p in range(count)])
        for m in range(steps)
    ]


def send_same_core(block, count, chips, step):
    pairs = []
    for z in range(count):
        for p in range(count):
            core, x = p // chips, p % chips
            far, chip = source_of(z, core, x, step, chips)
            pairs.append(((far * chips + x) * count + core * chips + chip, z * count + p))
    return lax.ppermute(block, GROUP, pairs)


def pass_on(block, count):
    return lax.ppermute(block, "resi", [(z, z ^ 1) for z in range(count)])


def call(kernel, outs, scratch, args, flops=0, hbm=False, name=None):
    vmem = pl.BlockSpec(memory_space=pltpu.VMEM)
    size = sum(a.size * a.dtype.itemsize for a in args)
    return pl.pallas_call(
        kernel,
        out_shape=outs,
        in_specs=[vmem] * len(args),
        out_specs=[vmem] * len(outs) if isinstance(outs, list) else (
            pl.BlockSpec(memory_space=pl.ANY) if hbm else vmem),
        scratch_shapes=scratch,
        compiler_params=pltpu.CompilerParams(vmem_limit_bytes=40 * MIB),
        cost_estimate=pl.CostEstimate(flops=flops, bytes_accessed=size, transcendentals=0),
        name=name,
    )(*args)


def body(
    homolog_matrix,
    sequence_pad_mask,
    pair_features,
    residue_pad_mask,
    residue_chain_index,
    homolog_standard_factor,
    homolog_standard_offset,
    factor_mapping_matrices,
    outer_side_biases,
    outer_pair_projection,
    relative_position_table,
    pair_norm_gain,
    pair_norm_bias,
    triangle_projection_weights,
    triangle_projection_biases,
    triangle_sum_norm_gain,
    triangle_sum_norm_bias,
    triangle_output_weight,
    outer_pair_bias,
):
    rows, cols, channels = pair_features.shape
    seqs, _, depth = homolog_matrix.shape
    half = factor_mapping_matrices.shape[1] // 2
    per = LANES // half
    count = lax.axis_size(PLANE)
    width = rows * half
    flat = lambda v: v.reshape(1, -1)
    shape = jax.ShapeDtypeStruct
    residue = flat(residue_pad_mask)
    chain = flat(residue_chain_index)
    pack = shape((seqs, width + LANES), BF16)
    chips = lax.axis_size("seq")
    normed = call(norm_kernel, shape((seqs * rows, depth), F32), [], [homolog_matrix],
                  flops=1 << 36, name="norm")
    left, right = call(
        pack_kernel, [pack, pack],
        [pltpu.VMEM((seqs * rows, LANES), F32)] * 2,
        [normed, sequence_pad_mask, residue, flat(homolog_standard_factor),
         flat(homolog_standard_offset), factor_mapping_matrices.T, flat(outer_side_biases)],
        flops=1 << 30, name="pack")
    right_swap = swap_cores(right, count)
    left_blocks = [left] + send_chips(left, chips)
    pair = call(functools.partial(join_kernel, 2), shape((2,) + pack.shape, BF16), [],
                [right, right_swap], name="join")
    base, block = call(
        base_kernel,
        [shape((rows, cols, channels), F32), shape((half * LANES, per * channels), BF16)],
        [pltpu.VMEM((LANES, channels), F32), pltpu.VMEM((half * half, channels), F32)],
        [pair_features, relative_position_table, chain, outer_pair_projection, pair],
        flops=1 << 30, name="base")
    rights = send_turned(pair, count, count // 2)
    own_lefts = call(functools.partial(join_kernel, chips), shape((chips,) + pack.shape, BF16), [],
                     left_blocks, flops=1 << 36, name="join")
    lefts = [own_lefts, swap_cores(own_lefts, count)]
    turned, live = call(
        functools.partial(turn_kernel, count),
        [shape((width, count * seqs), BF16), shape((cols, count * seqs), BF16)],
        [pltpu.VMEM((count,) + pack.shape, BF16),
         pltpu.VMEM((count * seqs // LANES, width, LANES), F32)],
        rights, flops=1 << 36, name="turn")
    updated, right_edge, normed_pair = call(
        edges_kernel,
        [shape((rows, cols, channels), BF16), shape((cols, rows, channels), BF16),
         shape((rows * cols, channels), BF16)],
        [pltpu.VMEM((count,) + pack.shape, BF16),
         pltpu.VMEM((rows // per * cols, half * LANES), BF16),
         pltpu.VMEM((rows * cols, channels), F32)],
        [turned, live] + lefts + [
            base, block, residue, flat(pair_norm_gain), flat(pair_norm_bias),
            triangle_projection_weights, flat(triangle_projection_biases)],
        name="edges")
    right_edges = [send_same_core(right_edge, count, chips, step) for step in range(chips)]
    for step in range(chips, count, 2):
        block_far = send_same_core(right_edge, count, chips, step)
        right_edges += [block_far, pass_on(block_far, count)]
    left_edge = call(left_kernel, shape((rows, cols, channels), BF16), [],
                     [normed_pair, residue, triangle_projection_weights,
                      flat(triangle_projection_biases)], name="left")
    left_edges = [left_edge] + send_chips(left_edge, chips)
    gate = call(gate_kernel, shape((rows * cols, channels), F32), [],
                [normed_pair, triangle_projection_weights, flat(triangle_projection_biases)],
                flops=1 << 30, name="gate")
    block_sums = shape((rows * cols, channels), F32)
    scratch = pltpu.VMEM((rows * cols, channels), F32)
    panel = call(panel_kernel, shape((chips, rows * cols, channels), F32), [],
                 left_edges + [gate], name="panel")
    near, far = [], []
    for step in range(count - 1):
        sums = near if step < chips else far
        sums[:] = [call(
            functools.partial(step_kernel, step, chips, 0, not sums), block_sums, [scratch],
            [right_edges[step], panel] + sums, name="triangle")]
    parts = ((0, rows * 3 // 4), (rows * 3 // 4, rows // 4))
    own_sums, other_sums, result = [], [], []
    for first, part in parts:
        own, half_sums = call(
            functools.partial(last_kernel, count - 1, chips, first),
            [shape((part * cols, channels), F32), shape((part * cols, channels), BF16)],
            [scratch, pltpu.VMEM((part * cols, channels), F32)],
            [right_edges[-1], panel] + far + near, flops=1 << 28, name="last")
        own_sums.append(own)
        other_sums.append(swap_cores(half_sums, count))
    for n, (first, part) in enumerate(parts):
        args = [own_sums[n], other_sums[n], updated, gate, flat(triangle_sum_norm_gain),
                flat(triangle_sum_norm_bias), triangle_output_weight, flat(outer_pair_bias)]
        part_shape = (part, cols, channels)
        result = [call(
            functools.partial(final_kernel, first),
            shape((rows, cols, channels) if n else part_shape, BF16),
            [pltpu.VMEM(part_shape, BF16), pltpu.SemaphoreType.DMA((1 + part // 8,))] if n else [],
            args + result, flops=1 << 28, hbm=n == 1, name="final")]
    return result[0]


def solution(mesh):
    pair = P(("groups", "resi"), ("resj", "seq"), None)
    placed = (
        P(("groups", "resj", "seq"), "resi", None),
        P(("groups", "resj", "seq"), "resi"),
        pair,
        P("groups"),
        P("groups"),
    ) + (P(),) * 14
    return jax.shard_map(body, mesh=mesh, in_specs=placed, out_specs=pair, check_vma=False)
```

```python
import functools

import jax
import jax.numpy as jnp
from jax import lax
from jax.experimental import pallas as pl
from jax.experimental.pallas import tpu as pltpu
from jax.sharding import PartitionSpec as P

RELMAX = 32
LANES = 128
PLANE = ("resj", "seq")
GROUP = ("resi", "resj", "seq")
F32 = jnp.float32
BF16 = jnp.bfloat16
MIB = 1 << 20


def iota(shape, axis):
    return lax.broadcasted_iota(jnp.int32, shape, axis)


def dot(a, b):
    return jnp.dot(a, b, preferred_element_type=F32)


def sigmoid(v):
    return 0.5 * jnp.tanh(0.5 * v) + 0.5


def layer_norm(values, gain, shift):
    average = jnp.mean(values, axis=-1, keepdims=True)
    centred = values - average
    variance = jnp.mean(centred * centred, axis=-1, keepdims=True)
    return centred * lax.rsqrt(variance + 1e-05) * gain + shift


def norm_kernel(x_ref, out_ref):
    x = x_ref[...].reshape(out_ref.shape).astype(F32)
    out_ref[...] = layer_norm(x, 1.0, 0.0)


def pack_kernel(x_ref, mask_ref, res_ref, gain_ref, shift_ref, w_ref, bias_ref,
                left_ref, right_ref, lscr, rscr):
    seqs, rows = mask_ref.shape
    half = w_ref.shape[0] // 2
    per = LANES // half
    row_start = lax.axis_index("resi") * rows
    normed = (x_ref[...] * gain_ref[...] + shift_ref[...]).astype(BF16)
    lane = iota((2 * half, 2 * LANES), 1)
    spread = lane % half + jnp.where(lane >= LANES, half, 0) == iota((2 * half, 2 * LANES), 0)
    spread = spread.astype(F32)
    wide = lax.dot_general(
        w_ref[...], spread.astype(BF16), (((0,), (0,)), ((), ())), preferred_element_type=F32)
    wide = wide.astype(BF16)
    bias = jnp.dot(jnp.broadcast_to(bias_ref[...], (8, 2 * half)), spread,
                   precision=lax.Precision.HIGHEST, preferred_element_type=F32)[0:1]
    mapped = dot(normed, wide)
    lscr[...] = mapped[:, :LANES]
    rscr[...] = mapped[:, LANES:]
    row_live = pick_rows(res_ref[...], row_start, rows)
    live = (mask_ref[...].astype(F32) * row_live).astype(BF16)
    width = rows * half
    spread_live = (iota((rows, width), 1) // half == iota((rows, width), 0)).astype(BF16)
    live_wide = dot(live, spread_live)
    sub = iota((seqs, LANES), 1) // half
    for tile in range(width // LANES):
        at = slice(tile * LANES, (tile + 1) * LANES)
        for ref, scr, first in ((left_ref, lscr, 0), (right_ref, rscr, LANES)):
            value = scr[pl.ds(tile * per, seqs, stride=rows), :]
            for k in range(1, per):
                value = jnp.where(sub == k, scr[pl.ds(tile * per + k, seqs, stride=rows), :], value)
            value = (value + bias[:, first:first + LANES]) * live_wide[:, at]
            ref[:, at] = value.astype(BF16)
    live_tile = dot(live, (iota((rows, LANES), 0) == iota((rows, LANES), 1)).astype(BF16))
    for ref in (left_ref, right_ref):
        ref[:, width:] = live_tile.astype(BF16)


def join_kernel(count, *refs):
    for n in range(count):
        refs[-1][n] = refs[n][...]


def pick_columns(values, start, size):
    total = values.shape[1]
    own = iota((size, total), 1) == iota((size, total), 0) + start
    spread = jnp.broadcast_to(values, (size, total)).astype(F32)
    return jnp.sum(jnp.where(own, spread, 0.0), axis=1, keepdims=True)


def pick_rows(values, start, size):
    total = values.shape[1]
    pick = (iota((total, size), 0) == iota((total, size), 1) + start).astype(BF16)
    return dot(jnp.broadcast_to(values.astype(F32), (8, total)).astype(BF16), pick)[0:1]


def base_kernel(pair_ref, table_ref, chain_ref, w_ref, _, base_ref, block_ref, tscr, wscr):
    rows, cols, channels = pair_ref.shape
    row_start = lax.axis_index("resi") * rows
    col_start = lax.axis_index(PLANE) * cols
    tscr[...] = jnp.zeros_like(tscr)
    tscr[0:table_ref.shape[0], :] = table_ref[...].astype(F32)
    table = tscr[...].astype(BF16)
    chain = chain_ref[...]
    same = pick_columns(chain, col_start, cols) == pick_rows(chain, row_start, rows)
    offset = iota((cols, rows), 0) + col_start - iota((cols, rows), 1) - row_start + RELMAX
    bins = jnp.where(same, jnp.clip(offset, 0, 2 * RELMAX), 2 * RELMAX + 1)
    lane = iota((cols, LANES), 1)
    for i in range(rows):
        one_hot = (lane == bins[:, i:i + 1]).astype(F32).astype(BF16)
        base_ref[i] = pair_ref[i].astype(F32) + dot(one_hot, table)
    wscr[...] = w_ref[...].astype(F32)
    half = int(round(w_ref.shape[0] ** 0.5))
    per = LANES // half
    block_ref[...] = jnp.zeros_like(block_ref)
    for d in range(half):
        value = wscr[pl.ds(d, half, stride=half), :].astype(BF16)
        for k in range(per):
            block_ref[pl.ds(d * LANES + k * half, half), k * channels:(k + 1) * channels] = value


def turn_kernel(count, *refs):
    pairs = count // 2
    rights, (turned_ref, live_ref, rall, tscr) = refs[:pairs], refs[pairs:]
    z = lax.axis_index("resi")
    width, total_seqs = turned_ref.shape
    cols = live_ref.shape[0]
    half = width // cols
    for step in range(pairs):
        for n in range(2):
            rall[z ^ (step + n * pairs)] = rights[step][n]
    right = rall[...].reshape(total_seqs, -1)
    for at in range(0, width, LANES):
        for s in range(0, total_seqs, LANES):
            tscr[s // LANES, at:at + LANES, :] = right[s:s + LANES, at:at + LANES].astype(F32).T
    for d in range(half):
        for s in range(0, total_seqs, LANES):
            turned = tscr[s // LANES, pl.ds(d, cols, stride=half), :]
            turned_ref[d * cols:(d + 1) * cols, s:s + LANES] = turned.astype(BF16)
    live_ref[...] = right[:, width:].astype(F32).T[0:cols].astype(BF16)


def edges_kernel(turned_ref, live_ref, own_ref, swapped_ref, base_ref, block_ref, res_ref,
                 gain_ref, shift_ref, w_ref, bias_ref,
                 updated_ref, right_ref, nscr, lall, oscr, escr):
    rows, cols, channels = base_ref.shape
    chips, seqs = own_ref.shape[:2]
    half = block_ref.shape[0] // LANES
    per = LANES // half
    width = rows * half
    q = lax.axis_index(PLANE)
    row_start, col_start = lax.axis_index("resi") * rows, q * cols
    for step in range(chips):
        lall[q ^ step] = own_ref[step]
        lall[q ^ (chips + step)] = swapped_ref[step]
    left = lall[...].reshape(2 * chips * seqs, -1)
    counts = dot(live_ref[...], left[:, width:])
    inverse = 1.0 / jnp.maximum(counts, 1.0)
    wide = 2 * LANES
    tall = half
    for first in range(0, width, wide):
        for d0 in range(0, half, tall):
            product = dot(turned_ref[d0 * cols:(d0 + tall) * cols, :], left[:, first:first + wide])
            product = product.astype(BF16)
            for dd in range(tall):
                for t in range(wide // LANES):
                    g = first // LANES + t
                    oscr[g * cols:(g + 1) * cols, (d0 + dd) * LANES:(d0 + dd + 1) * LANES] = (
                        product[dd * cols:(dd + 1) * cols, t * LANES:(t + 1) * LANES])
    outer = dot(oscr[...], block_ref[...])
    for i in range(rows):
        g, k = i // per, i % per
        part = outer[g * cols:(g + 1) * cols, k * channels:(k + 1) * channels]
        updated = (base_ref[i] + part * inverse[:, i:i + 1]).astype(BF16)
        updated_ref[i] = updated
        normed = layer_norm(updated.astype(F32), gain_ref[...], shift_ref[...])
        nscr[i * cols:(i + 1) * cols, :] = normed.astype(BF16)
    live = pick_columns(res_ref[...], col_start, cols) * pick_rows(res_ref[...], row_start, rows)
    chunk = 8
    for i0 in range(0, rows, chunk):
        mixture = dot(nscr[i0 * cols:(i0 + chunk) * cols, :], w_ref[:, 2 * channels:4 * channels])
        mixture = mixture + bias_ref[:, 2 * channels:4 * channels]
        right_edge = sigmoid(mixture[:, :channels]) * mixture[:, channels:]
        for ii in range(chunk):
            at = slice(ii * cols, (ii + 1) * cols)
            escr[(i0 + ii) * cols:(i0 + ii + 1) * cols, :] = right_edge[at] * live[:, i0 + ii:i0 + ii + 1]
    for k in range(cols):
        right_ref[k] = escr[pl.ds(k, rows, stride=cols), :].astype(BF16)


def left_kernel(normed_ref, res_ref, w_ref, bias_ref, left_ref):
    rows, cols, channels = left_ref.shape
    row_start, col_start = lax.axis_index("resi") * rows, lax.axis_index(PLANE) * cols
    live = pick_columns(res_ref[...], col_start, cols) * pick_rows(res_ref[...], row_start, rows)
    chunk = 8
    for i0 in range(0, rows, chunk):
        mixture = dot(normed_ref[i0 * cols:(i0 + chunk) * cols, :], w_ref[:, :2 * channels])
        mixture = mixture + bias_ref[:, :2 * channels]
        left_edge = sigmoid(mixture[:, :channels]) * mixture[:, channels:]
        for ii in range(chunk):
            here = left_edge[ii * cols:(ii + 1) * cols] * live[:, i0 + ii:i0 + ii + 1]
            left_ref[i0 + ii] = here.astype(BF16)


def gate_kernel(normed_ref, w_ref, bias_ref, gate_ref):
    first = w_ref.shape[1] - gate_ref.shape[1]
    gate_ref[...] = sigmoid(dot(normed_ref[...], w_ref[:, first:]) + bias_ref[:, first:])


def panel_kernel(*refs):
    *lefts, _, panel_ref = refs
    x = lax.axis_index("seq")
    for step, left in enumerate(lefts):
        panel_ref[x ^ step] = left[...].astype(F32).reshape(panel_ref.shape[1:])


def source_of(z, core, x, step, chips):
    block = z ^ step ^ ((x + core) % 2 if step >= chips else 0)
    return block // chips, block % chips


def add_block(panel_ref, chip, rscr, cols, first, before, store):
    rows, depth, channels = store.shape[0] // cols, rscr.shape[0] // cols, rscr.shape[1]
    block = 8
    tiles = cols // 8

    def rows_body(at, carry):
        def place(b, t, start=0):
            return pl.ds(pl.multiple_of((start + at * block + b) * cols + t * 8, 8), 8)

        if before is None:
            sums = [[jnp.zeros((8, channels), F32) for _ in range(tiles)] for _ in range(block)]
        else:
            sums = [[before[place(b, t, first), :] for t in range(tiles)] for b in range(block)]
        for k in range(depth):
            column = [rscr[k * cols + t * 8:k * cols + t * 8 + 8, :] for t in range(tiles)]
            for b in range(block):
                row = panel_ref[chip, pl.ds((first + at * block + b) * depth + k, 1), :]
                for t in range(tiles):
                    sums[b][t] = sums[b][t] + row * column[t]
        for b in range(block):
            for t in range(tiles):
                store[place(b, t), :] = sums[b][t].astype(store.dtype)
        return carry

    lax.fori_loop(0, rows // block, rows_body, 0)


def step_kernel(step, chips, first, fresh, right_ref, panel_ref, *refs):
    out_ref, rscr = refs[-2:]
    z, core, x = [lax.axis_index(axis) for axis in GROUP]
    chip = source_of(z, core, x, step, chips)[1]
    rscr[...] = right_ref[...].astype(F32).reshape(rscr.shape)
    add_block(panel_ref, chip, rscr, right_ref.shape[1], first, None if fresh else refs[0], out_ref)


def last_kernel(step, chips, first, right_ref, panel_ref, far_ref, near_ref, own_ref, other_ref,
                rscr, acc):
    step_kernel(step, chips, first, False, right_ref, panel_ref, far_ref, acc, rscr)
    mine = lax.axis_index("resi") // chips == lax.axis_index("resj")
    at = pl.ds(first * right_ref.shape[1], acc.shape[0])

    @pl.when(mine)
    def _():
        own_ref[...] = near_ref[at, :]
        other_ref[...] = acc[...].astype(BF16)

    @pl.when(jnp.logical_not(mine))
    def _():
        own_ref[...] = acc[...]
        other_ref[...] = near_ref[at, :].astype(BF16)


def final_kernel(first, own_ref, other_ref, updated_ref, gate_ref, gain_ref, shift_ref, w_ref, bias_ref,
                 *refs):
    if first:
        before_ref, out_hbm, value_ref, sems = refs
        moves = [pltpu.make_async_copy(before_ref, out_hbm.at[:first], sems.at[0])]
        moves[0].start()
    else:
        value_ref, = refs
    rows, cols, channels = value_ref.shape
    chunk = 8
    for i0 in range(0, rows, chunk):
        at = slice(i0 * cols, (i0 + chunk) * cols)
        here = slice((first + i0) * cols, (first + i0 + chunk) * cols)
        sums = own_ref[at, :] + other_ref[at, :].astype(F32)
        normed = layer_norm(sums, gain_ref[...], shift_ref[...]).astype(BF16)
        result = dot(normed, w_ref[...]) + bias_ref[...]
        updated = updated_ref[first + i0:first + i0 + chunk].reshape(chunk * cols, channels).astype(F32)
        value = updated + gate_ref[here, :] * result
        value_ref[i0:i0 + chunk] = value.astype(BF16).reshape(chunk, cols, channels)
        if first:
            moves.append(pltpu.make_async_copy(
                value_ref.at[i0:i0 + chunk], out_hbm.at[first + i0:first + i0 + chunk],
                sems.at[1 + i0 // chunk]))
            moves[-1].start()
    if first:
        for move in moves:
            move.wait()


def swap_cores(block, count):
    return lax.ppermute(block, PLANE, [(p, p ^ (count // 2)) for p in range(count)])


def send_chips(block, chips):
    return [
        lax.ppermute(block, "seq", [(x, x ^ m) for x in range(chips)]) for m in range(1, chips)
    ]


def send_turned(block, count, steps):
    return [
        lax.ppermute(
            block, GROUP,
            [(z * count + p, (p ^ m) * count + z) for z in range(count) for p in range(count)])
        for m in range(steps)
    ]


def send_same_core(block, count, chips, step):
    pairs = []
    for z in range(count):
        for p in range(count):
            core, x = p // chips, p % chips
            far, chip = source_of(z, core, x, step, chips)
            pairs.append(((far * chips + x) * count + core * chips + chip, z * count + p))
    return lax.ppermute(block, GROUP, pairs)


def pass_on(block, count):
    return lax.ppermute(block, "resi", [(z, z ^ 1) for z in range(count)])


def call(kernel, outs, scratch, args, flops=0, hbm=False, name=None):
    vmem = pl.BlockSpec(memory_space=pltpu.VMEM)
    size = sum(a.size * a.dtype.itemsize for a in args)
    return pl.pallas_call(
        kernel,
        out_shape=outs,
        in_specs=[vmem] * len(args),
        out_specs=[vmem] * len(outs) if isinstance(outs, list) else (
            pl.BlockSpec(memory_space=pl.ANY) if hbm else vmem),
        scratch_shapes=scratch,
        compiler_params=pltpu.CompilerParams(vmem_limit_bytes=40 * MIB),
        cost_estimate=pl.CostEstimate(flops=flops, bytes_accessed=size, transcendentals=0),
        name=name,
    )(*args)


def body(
    homolog_matrix,
    sequence_pad_mask,
    pair_features,
    residue_pad_mask,
    residue_chain_index,
    homolog_standard_factor,
    homolog_standard_offset,
    factor_mapping_matrices,
    outer_side_biases,
    outer_pair_projection,
    relative_position_table,
    pair_norm_gain,
    pair_norm_bias,
    triangle_projection_weights,
    triangle_projection_biases,
    triangle_sum_norm_gain,
    triangle_sum_norm_bias,
    triangle_output_weight,
    outer_pair_bias,
):
    rows, cols, channels = pair_features.shape
    seqs, _, depth = homolog_matrix.shape
    half = factor_mapping_matrices.shape[1] // 2
    per = LANES // half
    count = lax.axis_size(PLANE)
    width = rows * half
    flat = lambda v: v.reshape(1, -1)
    shape = jax.ShapeDtypeStruct
    residue = flat(residue_pad_mask)
    chain = flat(residue_chain_index)
    pack = shape((seqs, width + LANES), BF16)
    chips = lax.axis_size("seq")
    normed = call(norm_kernel, shape((seqs * rows, depth), F32), [], [homolog_matrix],
                  flops=1 << 36, name="norm")
    left, right = call(
        pack_kernel, [pack, pack],
        [pltpu.VMEM((seqs * rows, LANES), F32)] * 2,
        [normed, sequence_pad_mask, residue, flat(homolog_standard_factor),
         flat(homolog_standard_offset), factor_mapping_matrices.T, flat(outer_side_biases)],
        flops=1 << 30, name="pack")
    right_swap = swap_cores(right, count)
    left_blocks = [left] + send_chips(left, chips)
    pair = call(functools.partial(join_kernel, 2), shape((2,) + pack.shape, BF16), [],
                [right, right_swap], name="join")
    base, block = call(
        base_kernel,
        [shape((rows, cols, channels), F32), shape((half * LANES, per * channels), BF16)],
        [pltpu.VMEM((LANES, channels), F32), pltpu.VMEM((half * half, channels), F32)],
        [pair_features, relative_position_table, chain, outer_pair_projection, pair],
        flops=1 << 30, name="base")
    rights = send_turned(pair, count, count // 2)
    own_lefts = call(functools.partial(join_kernel, chips), shape((chips,) + pack.shape, BF16), [],
                     left_blocks, flops=1 << 36, name="join")
    lefts = [own_lefts, swap_cores(own_lefts, count)]
    turned, live = call(
        functools.partial(turn_kernel, count),
        [shape((width, count * seqs), BF16), shape((cols, count * seqs), BF16)],
        [pltpu.VMEM((count,) + pack.shape, BF16),
         pltpu.VMEM((count * seqs // LANES, width, LANES), F32)],
        rights, flops=1 << 36, name="turn")
    updated, right_edge, normed_pair = call(
        edges_kernel,
        [shape((rows, cols, channels), BF16), shape((cols, rows, channels), BF16),
         shape((rows * cols, channels), BF16)],
        [pltpu.VMEM((count,) + pack.shape, BF16),
         pltpu.VMEM((rows // per * cols, half * LANES), BF16),
         pltpu.VMEM((rows * cols, channels), F32)],
        [turned, live] + lefts + [
            base, block, residue, flat(pair_norm_gain), flat(pair_norm_bias),
            triangle_projection_weights, flat(triangle_projection_biases)],
        name="edges")
    right_edges = [send_same_core(right_edge, count, chips, step) for step in range(chips)]
    for step in range(chips, count, 2):
        block_far = send_same_core(right_edge, count, chips, step)
        right_edges += [block_far, pass_on(block_far, count)]
    left_edge = call(left_kernel, shape((rows, cols, channels), BF16), [],
                     [normed_pair, residue, triangle_projection_weights,
                      flat(triangle_projection_biases)], name="left")
    left_edges = [left_edge] + send_chips(left_edge, chips)
    gate = call(gate_kernel, shape((rows * cols, channels), F32), [],
                [normed_pair, triangle_projection_weights, flat(triangle_projection_biases)],
                flops=1 << 30, name="gate")
    block_sums = shape((rows * cols, channels), F32)
    scratch = pltpu.VMEM((rows * cols, channels), F32)
    panel = call(panel_kernel, shape((chips, rows * cols, channels), F32), [],
                 left_edges + [gate], name="panel")
    near, far = [], []
    for step in range(count - 1):
        sums = near if step < chips else far
        sums[:] = [call(
            functools.partial(step_kernel, step, chips, 0, not sums), block_sums, [scratch],
            [right_edges[step], panel] + sums, name="triangle")]
    parts = ((0, rows * 3 // 4), (rows * 3 // 4, rows // 4))
    own_sums, other_sums, result = [], [], []
    for first, part in parts:
        own, half_sums = call(
            functools.partial(last_kernel, count - 1, chips, first),
            [shape((part * cols, channels), F32), shape((part * cols, channels), BF16)],
            [scratch, pltpu.VMEM((part * cols, channels), F32)],
            [right_edges[-1], panel] + far + near, flops=1 << 28, name="last")
        own_sums.append(own)
        other_sums.append(swap_cores(half_sums, count))
    for n, (first, part) in enumerate(parts):
        args = [own_sums[n], other_sums[n], updated, gate, flat(triangle_sum_norm_gain),
                flat(triangle_sum_norm_bias), triangle_output_weight, flat(outer_pair_bias)]
        part_shape = (part, cols, channels)
        result = [call(
            functools.partial(final_kernel, first),
            shape((rows, cols, channels) if n else part_shape, BF16),
            [pltpu.VMEM(part_shape, BF16), pltpu.SemaphoreType.DMA((1 + part // 8,))] if n else [],
            args + result, flops=1 << 28, hbm=n == 1, name="final")]
    return result[0]


def solution(mesh):
    pair = P(("groups", "resi"), ("resj", "seq"), None)
    placed = (
        P(("groups", "resj", "seq"), "resi", None),
        P(("groups", "resj", "seq"), "resi"),
        pair,
        P("groups"),
        P("groups"),
    ) + (P(),) * 14
    return jax.shard_map(body, mesh=mesh, in_specs=placed, out_specs=pair, check_vma=False)
```

```python
import functools

import jax
import jax.numpy as jnp
from jax import lax
from jax.experimental import pallas as pl
from jax.experimental.pallas import tpu as pltpu
from jax.sharding import PartitionSpec as P

RELMAX = 32
LANES = 128
PLANE = ("resj", "seq")
GROUP = ("resi", "resj", "seq")
F32 = jnp.float32
BF16 = jnp.bfloat16
MIB = 1 << 20


def iota(shape, axis):
    return lax.broadcasted_iota(jnp.int32, shape, axis)


def dot(a, b):
    return jnp.dot(a, b, preferred_element_type=F32)


def sigmoid(v):
    return 0.5 * jnp.tanh(0.5 * v) + 0.5


def layer_norm(values, gain, shift):
    average = jnp.mean(values, axis=-1, keepdims=True)
    centred = values - average
    variance = jnp.mean(centred * centred, axis=-1, keepdims=True)
    return centred * lax.rsqrt(variance + 1e-05) * gain + shift


def norm_kernel(x_ref, out_ref):
    x = x_ref[...].reshape(out_ref.shape).astype(F32)
    out_ref[...] = layer_norm(x, 1.0, 0.0)


def pack_kernel(x_ref, mask_ref, res_ref, gain_ref, shift_ref, w_ref, bias_ref,
                left_ref, right_ref, lscr, rscr):
    seqs, rows = mask_ref.shape
    half = w_ref.shape[0] // 2
    per = LANES // half
    row_start = lax.axis_index("resi") * rows
    normed = (x_ref[...] * gain_ref[...] + shift_ref[...]).astype(BF16)
    lane = iota((2 * half, 2 * LANES), 1)
    spread = lane % half + jnp.where(lane >= LANES, half, 0) == iota((2 * half, 2 * LANES), 0)
    spread = spread.astype(F32)
    wide = lax.dot_general(
        w_ref[...], spread.astype(BF16), (((0,), (0,)), ((), ())), preferred_element_type=F32)
    wide = wide.astype(BF16)
    bias = jnp.dot(jnp.broadcast_to(bias_ref[...], (8, 2 * half)), spread,
                   precision=lax.Precision.HIGHEST, preferred_element_type=F32)[0:1]
    mapped = dot(normed, wide)
    lscr[...] = mapped[:, :LANES]
    rscr[...] = mapped[:, LANES:]
    row_live = pick_rows(res_ref[...], row_start, rows)
    live = (mask_ref[...].astype(F32) * row_live).astype(BF16)
    width = rows * half
    spread_live = (iota((rows, width), 1) // half == iota((rows, width), 0)).astype(BF16)
    live_wide = dot(live, spread_live)
    sub = iota((seqs, LANES), 1) // half
    for tile in range(width // LANES):
        at = slice(tile * LANES, (tile + 1) * LANES)
        for ref, scr, first in ((left_ref, lscr, 0), (right_ref, rscr, LANES)):
            value = scr[pl.ds(tile * per, seqs, stride=rows), :]
            for k in range(1, per):
                value = jnp.where(sub == k, scr[pl.ds(tile * per + k, seqs, stride=rows), :], value)
            value = (value + bias[:, first:first + LANES]) * live_wide[:, at]
            ref[:, at] = value.astype(BF16)
    live_tile = dot(live, (iota((rows, LANES), 0) == iota((rows, LANES), 1)).astype(BF16))
    for ref in (left_ref, right_ref):
        ref[:, width:] = live_tile.astype(BF16)


def join_kernel(count, *refs):
    for n in range(count):
        refs[-1][n] = refs[n][...]


def pick_columns(values, start, size):
    total = values.shape[1]
    own = iota((size, total), 1) == iota((size, total), 0) + start
    spread = jnp.broadcast_to(values, (size, total)).astype(F32)
    return jnp.sum(jnp.where(own, spread, 0.0), axis=1, keepdims=True)


def pick_rows(values, start, size):
    total = values.shape[1]
    pick = (iota((total, size), 0) == iota((total, size), 1) + start).astype(BF16)
    return dot(jnp.broadcast_to(values.astype(F32), (8, total)).astype(BF16), pick)[0:1]


def base_kernel(pair_ref, table_ref, chain_ref, w_ref, _, base_ref, block_ref, tscr, wscr):
    rows, cols, channels = pair_ref.shape
    row_start = lax.axis_index("resi") * rows
    col_start = lax.axis_index(PLANE) * cols
    tscr[...] = jnp.zeros_like(tscr)
    tscr[0:table_ref.shape[0], :] = table_ref[...].astype(F32)
    table = tscr[...].astype(BF16)
    chain = chain_ref[...]
    same = pick_columns(chain, col_start, cols) == pick_rows(chain, row_start, rows)
    offset = iota((cols, rows), 0) + col_start - iota((cols, rows), 1) - row_start + RELMAX
    bins = jnp.where(same, jnp.clip(offset, 0, 2 * RELMAX), 2 * RELMAX + 1)
    lane = iota((cols, LANES), 1)
    for i in range(rows):
        one_hot = (lane == bins[:, i:i + 1]).astype(F32).astype(BF16)
        base_ref[i] = pair_ref[i].astype(F32) + dot(one_hot, table)
    wscr[...] = w_ref[...].astype(F32)
    half = int(round(w_ref.shape[0] ** 0.5))
    per = LANES // half
    block_ref[...] = jnp.zeros_like(block_ref)
    for d in range(half):
        value = wscr[pl.ds(d, half, stride=half), :].astype(BF16)
        for k in range(per):
            block_ref[pl.ds(d * LANES + k * half, half), k * channels:(k + 1) * channels] = value


def turn_kernel(count, *refs):
    pairs = count // 2
    rights, (turned_ref, live_ref, rall, tscr) = refs[:pairs], refs[pairs:]
    z = lax.axis_index("resi")
    width, total_seqs = turned_ref.shape
    cols = live_ref.shape[0]
    half = width // cols
    for step in range(pairs):
        for n in range(2):
            rall[z ^ 1 ^ (step + n * pairs)] = rights[step][n]
    right = rall[...].reshape(total_seqs, -1)
    for at in range(0, width, LANES):
        for s in range(0, total_seqs, LANES):
            tscr[s // LANES, at:at + LANES, :] = right[s:s + LANES, at:at + LANES].astype(F32).T
    for d in range(half):
        for s in range(0, total_seqs, LANES):
            turned = tscr[s // LANES, pl.ds(d, cols, stride=half), :]
            turned_ref[d * cols:(d + 1) * cols, s:s + LANES] = turned.astype(BF16)
    live_ref[...] = right[:, width:].astype(F32).T[0:cols].astype(BF16)


def edges_kernel(turned_ref, live_ref, own_ref, swapped_ref, base_ref, block_ref, res_ref,
                 gain_ref, shift_ref, w_ref, bias_ref,
                 updated_ref, right_ref, nscr, lall, oscr, escr):
    rows, cols, channels = base_ref.shape
    chips, seqs = own_ref.shape[:2]
    half = block_ref.shape[0] // LANES
    per = LANES // half
    width = rows * half
    q = lax.axis_index(PLANE)
    row_start, col_start = lax.axis_index("resi") * rows, q * cols
    for step in range(chips):
        lall[q ^ step] = own_ref[step]
        lall[q ^ (chips + step)] = swapped_ref[step]
    left = lall[...].reshape(2 * chips * seqs, -1)
    counts = dot(live_ref[...], left[:, width:])
    inverse = 1.0 / jnp.maximum(counts, 1.0)
    wide = 2 * LANES
    tall = 8
    for first in range(0, width, wide):
        for d0 in range(0, half, tall):
            product = dot(turned_ref[d0 * cols:(d0 + tall) * cols, :], left[:, first:first + wide])
            product = product.astype(BF16)
            for dd in range(tall):
                for t in range(wide // LANES):
                    g = first // LANES + t
                    oscr[g * cols:(g + 1) * cols, (d0 + dd) * LANES:(d0 + dd + 1) * LANES] = (
                        product[dd * cols:(dd + 1) * cols, t * LANES:(t + 1) * LANES])
    outer = dot(oscr[...], block_ref[...])
    for i in range(rows):
        g, k = i // per, i % per
        part = outer[g * cols:(g + 1) * cols, k * channels:(k + 1) * channels]
        updated = (base_ref[i] + part * inverse[:, i:i + 1]).astype(BF16)
        updated_ref[i] = updated
        normed = layer_norm(updated.astype(F32), gain_ref[...], shift_ref[...])
        nscr[i * cols:(i + 1) * cols, :] = normed.astype(BF16)
    live = pick_columns(res_ref[...], col_start, cols) * pick_rows(res_ref[...], row_start, rows)
    chunk = 8
    for i0 in range(0, rows, chunk):
        mixture = dot(nscr[i0 * cols:(i0 + chunk) * cols, :], w_ref[:, 2 * channels:4 * channels])
        mixture = mixture + bias_ref[:, 2 * channels:4 * channels]
        right_edge = sigmoid(mixture[:, :channels]) * mixture[:, channels:]
        for ii in range(chunk):
            at = slice(ii * cols, (ii + 1) * cols)
            escr[(i0 + ii) * cols:(i0 + ii + 1) * cols, :] = right_edge[at] * live[:, i0 + ii:i0 + ii + 1]
    for k in range(cols):
        right_ref[k] = escr[pl.ds(k, rows, stride=cols), :].astype(BF16)


def left_kernel(normed_ref, res_ref, w_ref, bias_ref, left_ref):
    rows, cols, channels = left_ref.shape
    row_start, col_start = lax.axis_index("resi") * rows, lax.axis_index(PLANE) * cols
    live = pick_columns(res_ref[...], col_start, cols) * pick_rows(res_ref[...], row_start, rows)
    chunk = 8
    for i0 in range(0, rows, chunk):
        mixture = dot(normed_ref[i0 * cols:(i0 + chunk) * cols, :], w_ref[:, :2 * channels])
        mixture = mixture + bias_ref[:, :2 * channels]
        left_edge = sigmoid(mixture[:, :channels]) * mixture[:, channels:]
        for ii in range(chunk):
            here = left_edge[ii * cols:(ii + 1) * cols] * live[:, i0 + ii:i0 + ii + 1]
            left_ref[i0 + ii] = here.astype(BF16)


def gate_kernel(normed_ref, w_ref, bias_ref, gate_ref):
    first = w_ref.shape[1] - gate_ref.shape[1]
    gate_ref[...] = sigmoid(dot(normed_ref[...], w_ref[:, first:]) + bias_ref[:, first:])


def panel_kernel(*refs):
    *lefts, _, panel_ref = refs
    x = lax.axis_index("seq")
    for step, left in enumerate(lefts):
        panel_ref[x ^ step] = left[...].astype(F32).reshape(panel_ref.shape[1:])


def source_of(z, core, x, step, chips):
    block = z ^ step ^ ((x + core) % 2 if step >= chips else 0)
    return block // chips, block % chips


def add_block(panel_ref, chip, rscr, cols, first, before, store):
    rows, depth, channels = store.shape[0] // cols, rscr.shape[0] // cols, rscr.shape[1]
    block = 8
    tiles = cols // 8

    def rows_body(at, carry):
        def place(b, t, start=0):
            return pl.ds(pl.multiple_of((start + at * block + b) * cols + t * 8, 8), 8)

        if before is None:
            sums = [[jnp.zeros((8, channels), F32) for _ in range(tiles)] for _ in range(block)]
        else:
            sums = [[before[place(b, t, first), :] for t in range(tiles)] for b in range(block)]
        for k in range(depth):
            column = [rscr[k * cols + t * 8:k * cols + t * 8 + 8, :] for t in range(tiles)]
            for b in range(block):
                row = panel_ref[chip, pl.ds((first + at * block + b) * depth + k, 1), :]
                for t in range(tiles):
                    sums[b][t] = sums[b][t] + row * column[t]
        for b in range(block):
            for t in range(tiles):
                store[place(b, t), :] = sums[b][t].astype(store.dtype)
        return carry

    lax.fori_loop(0, rows // block, rows_body, 0)


def step_kernel(step, chips, first, fresh, right_ref, panel_ref, *refs):
    out_ref, rscr = refs[-2:]
    z, core, x = [lax.axis_index(axis) for axis in GROUP]
    chip = source_of(z, core, x, step, chips)[1]
    rscr[...] = right_ref[...].astype(F32).reshape(rscr.shape)
    add_block(panel_ref, chip, rscr, right_ref.shape[1], first, None if fresh else refs[0], out_ref)


def last_kernel(step, chips, first, right_ref, panel_ref, far_ref, near_ref, own_ref, other_ref,
                rscr, acc):
    step_kernel(step, chips, first, False, right_ref, panel_ref, far_ref, acc, rscr)
    mine = lax.axis_index("resi") // chips == lax.axis_index("resj")
    at = pl.ds(first * right_ref.shape[1], acc.shape[0])

    @pl.when(mine)
    def _():
        own_ref[...] = near_ref[at, :]
        other_ref[...] = acc[...].astype(BF16)

    @pl.when(jnp.logical_not(mine))
    def _():
        own_ref[...] = acc[...]
        other_ref[...] = near_ref[at, :].astype(BF16)


def final_kernel(first, own_ref, other_ref, updated_ref, gate_ref, gain_ref, shift_ref, w_ref, bias_ref,
                 *refs):
    if first:
        before_ref, out_hbm, value_ref, sems = refs
        moves = [pltpu.make_async_copy(before_ref, out_hbm.at[:first], sems.at[0])]
        moves[0].start()
    else:
        value_ref, = refs
    rows, cols, channels = value_ref.shape
    chunk = 8
    for i0 in range(0, rows, chunk):
        at = slice(i0 * cols, (i0 + chunk) * cols)
        here = slice((first + i0) * cols, (first + i0 + chunk) * cols)
        sums = own_ref[at, :] + other_ref[at, :].astype(F32)
        normed = layer_norm(sums, gain_ref[...], shift_ref[...]).astype(BF16)
        result = dot(normed, w_ref[...]) + bias_ref[...]
        updated = updated_ref[first + i0:first + i0 + chunk].reshape(chunk * cols, channels).astype(F32)
        value = updated + gate_ref[here, :] * result
        value_ref[i0:i0 + chunk] = value.astype(BF16).reshape(chunk, cols, channels)
        if first:
            moves.append(pltpu.make_async_copy(
                value_ref.at[i0:i0 + chunk], out_hbm.at[first + i0:first + i0 + chunk],
                sems.at[1 + i0 // chunk]))
            moves[-1].start()
    if first:
        for move in moves:
            move.wait()


def swap_cores(block, count):
    return lax.ppermute(block, PLANE, [(p, p ^ (count // 2)) for p in range(count)])


def send_chips(block, chips):
    return [
        lax.ppermute(block, "seq", [(x, x ^ m) for x in range(chips)]) for m in range(1, chips)
    ]


def send_turned(block, count, steps):
    return [
        lax.ppermute(
            block, GROUP,
            [(z * count + p, (p ^ m ^ 1) * count + z) for z in range(count) for p in range(count)])
        for m in range(steps)
    ]


def send_same_core(block, count, chips, step):
    pairs = []
    for z in range(count):
        for p in range(count):
            core, x = p // chips, p % chips
            far, chip = source_of(z, core, x, step, chips)
            pairs.append(((far * chips + x) * count + core * chips + chip, z * count + p))
    return lax.ppermute(block, GROUP, pairs)


def pass_on(block, count):
    return lax.ppermute(block, "resi", [(z, z ^ 1) for z in range(count)])


def call(kernel, outs, scratch, args, flops=0, hbm=False, name=None):
    vmem = pl.BlockSpec(memory_space=pltpu.VMEM)
    size = sum(a.size * a.dtype.itemsize for a in args)
    return pl.pallas_call(
        kernel,
        out_shape=outs,
        in_specs=[vmem] * len(args),
        out_specs=[vmem] * len(outs) if isinstance(outs, list) else (
            pl.BlockSpec(memory_space=pl.ANY) if hbm else vmem),
        scratch_shapes=scratch,
        compiler_params=pltpu.CompilerParams(vmem_limit_bytes=40 * MIB),
        cost_estimate=pl.CostEstimate(flops=flops, bytes_accessed=size, transcendentals=0),
        name=name,
    )(*args)


def body(
    homolog_matrix,
    sequence_pad_mask,
    pair_features,
    residue_pad_mask,
    residue_chain_index,
    homolog_standard_factor,
    homolog_standard_offset,
    factor_mapping_matrices,
    outer_side_biases,
    outer_pair_projection,
    relative_position_table,
    pair_norm_gain,
    pair_norm_bias,
    triangle_projection_weights,
    triangle_projection_biases,
    triangle_sum_norm_gain,
    triangle_sum_norm_bias,
    triangle_output_weight,
    outer_pair_bias,
):
    rows, cols, channels = pair_features.shape
    seqs, _, depth = homolog_matrix.shape
    half = factor_mapping_matrices.shape[1] // 2
    per = LANES // half
    count = lax.axis_size(PLANE)
    width = rows * half
    flat = lambda v: v.reshape(1, -1)
    shape = jax.ShapeDtypeStruct
    residue = flat(residue_pad_mask)
    chain = flat(residue_chain_index)
    pack = shape((seqs, width + LANES), BF16)
    chips = lax.axis_size("seq")
    normed = call(norm_kernel, shape((seqs * rows, depth), F32), [], [homolog_matrix],
                  flops=1 << 36, name="norm")
    left, right = call(
        pack_kernel, [pack, pack],
        [pltpu.VMEM((seqs * rows, LANES), F32)] * 2,
        [normed, sequence_pad_mask, residue, flat(homolog_standard_factor),
         flat(homolog_standard_offset), factor_mapping_matrices.T, flat(outer_side_biases)],
        flops=1 << 30, name="pack")
    right_swap = swap_cores(right, count)
    left_blocks = [left] + send_chips(left, chips)
    pair = call(functools.partial(join_kernel, 2), shape((2,) + pack.shape, BF16), [],
                [right, right_swap], name="join")
    base, block = call(
        base_kernel,
        [shape((rows, cols, channels), F32), shape((half * LANES, per * channels), BF16)],
        [pltpu.VMEM((LANES, channels), F32), pltpu.VMEM((half * half, channels), F32)],
        [pair_features, relative_position_table, chain, outer_pair_projection, pair],
        flops=1 << 30, name="base")
    rights = send_turned(pair, count, count // 2)
    own_lefts = call(functools.partial(join_kernel, chips), shape((chips,) + pack.shape, BF16), [],
                     left_blocks, flops=1 << 36, name="join")
    lefts = [own_lefts, swap_cores(own_lefts, count)]
    turned, live = call(
        functools.partial(turn_kernel, count),
        [shape((width, count * seqs), BF16), shape((cols, count * seqs), BF16)],
        [pltpu.VMEM((count,) + pack.shape, BF16),
         pltpu.VMEM((count * seqs // LANES, width, LANES), F32)],
        rights, flops=1 << 36, name="turn")
    updated, right_edge, normed_pair = call(
        edges_kernel,
        [shape((rows, cols, channels), BF16), shape((cols, rows, channels), BF16),
         shape((rows * cols, channels), BF16)],
        [pltpu.VMEM((count,) + pack.shape, BF16),
         pltpu.VMEM((rows // per * cols, half * LANES), BF16),
         pltpu.VMEM((rows * cols, channels), F32)],
        [turned, live] + lefts + [
            base, block, residue, flat(pair_norm_gain), flat(pair_norm_bias),
            triangle_projection_weights, flat(triangle_projection_biases)],
        name="edges")
    right_edges = [send_same_core(right_edge, count, chips, step) for step in range(chips)]
    for step in range(chips, count, 2):
        block_far = send_same_core(right_edge, count, chips, step)
        right_edges += [block_far, pass_on(block_far, count)]
    left_edge = call(left_kernel, shape((rows, cols, channels), BF16), [],
                     [normed_pair, residue, triangle_projection_weights,
                      flat(triangle_projection_biases)], name="left")
    left_edges = [left_edge] + send_chips(left_edge, chips)
    gate = call(gate_kernel, shape((rows * cols, channels), F32), [],
                [normed_pair, triangle_projection_weights, flat(triangle_projection_biases)],
                flops=1 << 30, name="gate")
    block_sums = shape((rows * cols, channels), F32)
    scratch = pltpu.VMEM((rows * cols, channels), F32)
    panel = call(panel_kernel, shape((chips, rows * cols, channels), F32), [],
                 left_edges + [gate], name="panel")
    near, far = [], []
    for step in range(count - 1):
        sums = near if step < chips else far
        sums[:] = [call(
            functools.partial(step_kernel, step, chips, 0, not sums), block_sums, [scratch],
            [right_edges[step], panel] + sums, name="triangle")]
    parts = ((0, rows * 3 // 4), (rows * 3 // 4, rows // 4))
    own_sums, other_sums, result = [], [], []
    for first, part in parts:
        own, half_sums = call(
            functools.partial(last_kernel, count - 1, chips, first),
            [shape((part * cols, channels), F32), shape((part * cols, channels), BF16)],
            [scratch, pltpu.VMEM((part * cols, channels), F32)],
            [right_edges[-1], panel] + far + near, flops=1 << 28, name="last")
        own_sums.append(own)
        other_sums.append(swap_cores(half_sums, count))
    for n, (first, part) in enumerate(parts):
        args = [own_sums[n], other_sums[n], updated, gate, flat(triangle_sum_norm_gain),
                flat(triangle_sum_norm_bias), triangle_output_weight, flat(outer_pair_bias)]
        part_shape = (part, cols, channels)
        result = [call(
            functools.partial(final_kernel, first),
            shape((rows, cols, channels) if n else part_shape, BF16),
            [pltpu.VMEM(part_shape, BF16), pltpu.SemaphoreType.DMA((1 + part // 8,))] if n else [],
            args + result, flops=1 << 28, hbm=n == 1, name="final")]
    return result[0]


def solution(mesh):
    pair = P(("groups", "resi"), ("resj", "seq"), None)
    placed = (
        P(("groups", "resj", "seq"), "resi", None),
        P(("groups", "resj", "seq"), "resi"),
        pair,
        P("groups"),
        P("groups"),
    ) + (P(),) * 14
    return jax.shard_map(body, mesh=mesh, in_specs=placed, out_specs=pair, check_vma=False)
```

```python
import functools

import jax
import jax.numpy as jnp
from jax import lax
from jax.experimental import pallas as pl
from jax.experimental.pallas import tpu as pltpu
from jax.sharding import PartitionSpec as P

RELMAX = 32
LANES = 128
PLANE = ("resj", "seq")
GROUP = ("resi", "resj", "seq")
F32 = jnp.float32
BF16 = jnp.bfloat16
MIB = 1 << 20


def iota(shape, axis):
    return lax.broadcasted_iota(jnp.int32, shape, axis)


def dot(a, b):
    return jnp.dot(a, b, preferred_element_type=F32)


def sigmoid(v):
    return 0.5 * jnp.tanh(0.5 * v) + 0.5


def layer_norm(values, gain, shift):
    average = jnp.mean(values, axis=-1, keepdims=True)
    centred = values - average
    variance = jnp.mean(centred * centred, axis=-1, keepdims=True)
    return centred * lax.rsqrt(variance + 1e-05) * gain + shift


def norm_kernel(x_ref, out_ref):
    x = x_ref[...].reshape(out_ref.shape).astype(F32)
    out_ref[...] = layer_norm(x, 1.0, 0.0)


def pack_kernel(x_ref, mask_ref, res_ref, gain_ref, shift_ref, w_ref, bias_ref,
                left_ref, right_ref, lscr, rscr):
    seqs, rows = mask_ref.shape
    half = w_ref.shape[0] // 2
    per = LANES // half
    row_start = lax.axis_index("resi") * rows
    normed = (x_ref[...] * gain_ref[...] + shift_ref[...]).astype(BF16)
    lane = iota((2 * half, 2 * LANES), 1)
    spread = lane % half + jnp.where(lane >= LANES, half, 0) == iota((2 * half, 2 * LANES), 0)
    spread = spread.astype(F32)
    wide = lax.dot_general(
        w_ref[...], spread.astype(BF16), (((0,), (0,)), ((), ())), preferred_element_type=F32)
    wide = wide.astype(BF16)
    bias = jnp.dot(jnp.broadcast_to(bias_ref[...], (8, 2 * half)), spread,
                   precision=lax.Precision.HIGHEST, preferred_element_type=F32)[0:1]
    mapped = dot(normed, wide)
    pitch = rows + 1
    for n in range(seqs):
        lscr[n * pitch:n * pitch + rows, :] = mapped[n * rows:(n + 1) * rows, :LANES]
        rscr[n * pitch:n * pitch + rows, :] = mapped[n * rows:(n + 1) * rows, LANES:]
    row_live = pick_rows(res_ref[...], row_start, rows)
    live = (mask_ref[...].astype(F32) * row_live).astype(BF16)
    width = rows * half
    spread_live = (iota((rows, width), 1) // half == iota((rows, width), 0)).astype(BF16)
    live_wide = dot(live, spread_live)
    sub = iota((seqs, LANES), 1) // half
    for tile in range(width // LANES):
        at = slice(tile * LANES, (tile + 1) * LANES)
        for ref, scr, first in ((left_ref, lscr, 0), (right_ref, rscr, LANES)):
            value = scr[pl.ds(tile * per, seqs, stride=pitch), :]
            for k in range(1, per):
                value = jnp.where(sub == k, scr[pl.ds(tile * per + k, seqs, stride=pitch), :], value)
            value = (value + bias[:, first:first + LANES]) * live_wide[:, at]
            ref[:, at] = value.astype(BF16)
    live_tile = dot(live, (iota((rows, LANES), 0) == iota((rows, LANES), 1)).astype(BF16))
    for ref in (left_ref, right_ref):
        ref[:, width:] = live_tile.astype(BF16)


def join_kernel(count, *refs):
    for n in range(count):
        refs[-1][n] = refs[n][...]


def pick_columns(values, start, size):
    total = values.shape[1]
    own = iota((size, total), 1) == iota((size, total), 0) + start
    spread = jnp.broadcast_to(values, (size, total)).astype(F32)
    return jnp.sum(jnp.where(own, spread, 0.0), axis=1, keepdims=True)


def pick_rows(values, start, size):
    total = values.shape[1]
    pick = (iota((total, size), 0) == iota((total, size), 1) + start).astype(BF16)
    return dot(jnp.broadcast_to(values.astype(F32), (8, total)).astype(BF16), pick)[0:1]


def base_kernel(pair_ref, table_ref, chain_ref, w_ref, _, base_ref, block_ref, tscr, wscr):
    rows, cols, channels = pair_ref.shape
    row_start = lax.axis_index("resi") * rows
    col_start = lax.axis_index(PLANE) * cols
    tscr[...] = jnp.zeros_like(tscr)
    tscr[0:table_ref.shape[0], :] = table_ref[...].astype(F32)
    table = tscr[...].astype(BF16)
    chain = chain_ref[...]
    same = pick_columns(chain, col_start, cols) == pick_rows(chain, row_start, rows)
    offset = iota((cols, rows), 0) + col_start - iota((cols, rows), 1) - row_start + RELMAX
    bins = jnp.where(same, jnp.clip(offset, 0, 2 * RELMAX), 2 * RELMAX + 1)
    lane = iota((cols, LANES), 1)
    for i in range(rows):
        one_hot = (lane == bins[:, i:i + 1]).astype(F32).astype(BF16)
        base_ref[i] = pair_ref[i].astype(F32) + dot(one_hot, table)
    wscr[...] = w_ref[...].astype(F32)
    half = int(round(w_ref.shape[0] ** 0.5))
    per = LANES // half
    block_ref[...] = jnp.zeros_like(block_ref)
    for d in range(half):
        value = wscr[pl.ds(d, half, stride=half), :].astype(BF16)
        for k in range(per):
            block_ref[pl.ds(d * LANES + k * half, half), k * channels:(k + 1) * channels] = value


def turn_kernel(count, *refs):
    pairs = count // 2
    rights, (turned_ref, live_ref, rall, tscr) = refs[:pairs], refs[pairs:]
    z = lax.axis_index("resi")
    width, total_seqs = turned_ref.shape
    cols = live_ref.shape[0]
    half = width // cols
    pitch = half + 1
    for step in range(pairs):
        for n in range(2):
            rall[z ^ (step + n * pairs)] = rights[step][n]
    right = rall[...].reshape(total_seqs, -1)
    for at in range(0, width, LANES):
        for s in range(0, total_seqs, LANES):
            block = right[s:s + LANES, at:at + LANES].astype(F32).T
            for n in range(0, LANES, half):
                first = (at + n) // half * pitch
                tscr[s // LANES, first:first + half, :] = block[n:n + half]
    for d in range(half):
        for s in range(0, total_seqs, LANES):
            turned = tscr[s // LANES, pl.ds(d, cols, stride=pitch), :]
            turned_ref[d * cols:(d + 1) * cols, s:s + LANES] = turned.astype(BF16)
    live_ref[...] = right[:, width:].astype(F32).T[0:cols].astype(BF16)


def edges_kernel(turned_ref, live_ref, own_ref, swapped_ref, base_ref, block_ref, res_ref,
                 gain_ref, shift_ref, w_ref, bias_ref,
                 updated_ref, right_ref, nscr, lall, oscr, escr):
    rows, cols, channels = base_ref.shape
    chips, seqs = own_ref.shape[:2]
    half = block_ref.shape[0] // LANES
    per = LANES // half
    width = rows * half
    q = lax.axis_index(PLANE)
    row_start, col_start = lax.axis_index("resi") * rows, q * cols
    for step in range(chips):
        lall[q ^ step] = own_ref[step]
        lall[q ^ (chips + step)] = swapped_ref[step]
    left = lall[...].reshape(2 * chips * seqs, -1)
    counts = dot(live_ref[...], left[:, width:])
    inverse = 1.0 / jnp.maximum(counts, 1.0)
    wide = 2 * LANES
    tall = 8
    for first in range(0, width, wide):
        for d0 in range(0, half, tall):
            product = dot(turned_ref[d0 * cols:(d0 + tall) * cols, :], left[:, first:first + wide])
            product = product.astype(BF16)
            for dd in range(tall):
                for t in range(wide // LANES):
                    g = first // LANES + t
                    oscr[g * cols:(g + 1) * cols, (d0 + dd) * LANES:(d0 + dd + 1) * LANES] = (
                        product[dd * cols:(dd + 1) * cols, t * LANES:(t + 1) * LANES])
    outer = dot(oscr[...], block_ref[...])
    for i in range(rows):
        g, k = i // per, i % per
        part = outer[g * cols:(g + 1) * cols, k * channels:(k + 1) * channels]
        updated = (base_ref[i] + part * inverse[:, i:i + 1]).astype(BF16)
        updated_ref[i] = updated
        normed = layer_norm(updated.astype(F32), gain_ref[...], shift_ref[...])
        nscr[i * cols:(i + 1) * cols, :] = normed.astype(BF16)
    live = pick_columns(res_ref[...], col_start, cols) * pick_rows(res_ref[...], row_start, rows)
    chunk = 8
    for i0 in range(0, rows, chunk):
        mixture = dot(nscr[i0 * cols:(i0 + chunk) * cols, :], w_ref[:, 2 * channels:4 * channels])
        mixture = mixture + bias_ref[:, 2 * channels:4 * channels]
        right_edge = sigmoid(mixture[:, :channels]) * mixture[:, channels:]
        for ii in range(chunk):
            at = slice(ii * cols, (ii + 1) * cols)
            first = (i0 + ii) * (cols + 1)
            escr[first:first + cols, :] = right_edge[at] * live[:, i0 + ii:i0 + ii + 1]
    for k in range(cols):
        right_ref[k] = escr[pl.ds(k, rows, stride=cols + 1), :].astype(BF16)


def left_kernel(normed_ref, res_ref, w_ref, bias_ref, left_ref):
    rows, cols, channels = left_ref.shape
    row_start, col_start = lax.axis_index("resi") * rows, lax.axis_index(PLANE) * cols
    live = pick_columns(res_ref[...], col_start, cols) * pick_rows(res_ref[...], row_start, rows)
    chunk = 8
    for i0 in range(0, rows, chunk):
        mixture = dot(normed_ref[i0 * cols:(i0 + chunk) * cols, :], w_ref[:, :2 * channels])
        mixture = mixture + bias_ref[:, :2 * channels]
        left_edge = sigmoid(mixture[:, :channels]) * mixture[:, channels:]
        for ii in range(chunk):
            here = left_edge[ii * cols:(ii + 1) * cols] * live[:, i0 + ii:i0 + ii + 1]
            left_ref[i0 + ii] = here.astype(BF16)


def gate_kernel(normed_ref, w_ref, bias_ref, gate_ref):
    first = w_ref.shape[1] - gate_ref.shape[1]
    gate_ref[...] = sigmoid(dot(normed_ref[...], w_ref[:, first:]) + bias_ref[:, first:])


def panel_kernel(*refs):
    *lefts, _, panel_ref = refs
    x = lax.axis_index("seq")
    for step, left in enumerate(lefts):
        panel_ref[x ^ step] = left[...].astype(F32).reshape(panel_ref.shape[1:])


def source_of(z, core, x, step, chips):
    block = z ^ step ^ ((x + core) % 2 if step >= chips else 0)
    return block // chips, block % chips


def add_block(panel_ref, chip, rscr, cols, first, before, store):
    rows, depth, channels = store.shape[0] // cols, rscr.shape[0] // cols, rscr.shape[1]
    block = 8
    tiles = cols // 8

    def rows_body(at, carry):
        def place(b, t, start=0):
            return pl.ds(pl.multiple_of((start + at * block + b) * cols + t * 8, 8), 8)

        if before is None:
            sums = [[jnp.zeros((8, channels), F32) for _ in range(tiles)] for _ in range(block)]
        else:
            sums = [[before[place(b, t, first), :] for t in range(tiles)] for b in range(block)]
        for k in range(depth):
            column = [rscr[k * cols + t * 8:k * cols + t * 8 + 8, :] for t in range(tiles)]
            for b in range(block):
                row = panel_ref[chip, pl.ds((first + at * block + b) * depth + k, 1), :]
                for t in range(tiles):
                    sums[b][t] = sums[b][t] + row * column[t]
        for b in range(block):
            for t in range(tiles):
                store[place(b, t), :] = sums[b][t].astype(store.dtype)
        return carry

    lax.fori_loop(0, rows // block, rows_body, 0)


def step_kernel(step, chips, first, fresh, right_ref, panel_ref, *refs):
    out_ref, rscr = refs[-2:]
    z, core, x = [lax.axis_index(axis) for axis in GROUP]
    chip = source_of(z, core, x, step, chips)[1]
    rscr[...] = right_ref[...].astype(F32).reshape(rscr.shape)
    add_block(panel_ref, chip, rscr, right_ref.shape[1], first, None if fresh else refs[0], out_ref)


def last_kernel(step, chips, first, right_ref, panel_ref, far_ref, near_ref, own_ref, other_ref,
                rscr, acc):
    step_kernel(step, chips, first, False, right_ref, panel_ref, far_ref, acc, rscr)
    mine = lax.axis_index("resi") // chips == lax.axis_index("resj")
    at = pl.ds(first * right_ref.shape[1], acc.shape[0])

    @pl.when(mine)
    def _():
        own_ref[...] = near_ref[at, :]
        other_ref[...] = acc[...].astype(BF16)

    @pl.when(jnp.logical_not(mine))
    def _():
        own_ref[...] = acc[...]
        other_ref[...] = near_ref[at, :].astype(BF16)


def final_kernel(first, own_ref, other_ref, updated_ref, gate_ref, gain_ref, shift_ref, w_ref, bias_ref,
                 *refs):
    if first:
        before_ref, out_hbm, value_ref, sems = refs
        moves = [pltpu.make_async_copy(before_ref, out_hbm.at[:first], sems.at[0])]
        moves[0].start()
    else:
        value_ref, = refs
    rows, cols, channels = value_ref.shape
    chunk = 8
    for i0 in range(0, rows, chunk):
        at = slice(i0 * cols, (i0 + chunk) * cols)
        here = slice((first + i0) * cols, (first + i0 + chunk) * cols)
        sums = own_ref[at, :] + other_ref[at, :].astype(F32)
        normed = layer_norm(sums, gain_ref[...], shift_ref[...]).astype(BF16)
        result = dot(normed, w_ref[...]) + bias_ref[...]
        updated = updated_ref[first + i0:first + i0 + chunk].reshape(chunk * cols, channels).astype(F32)
        value = updated + gate_ref[here, :] * result
        value_ref[i0:i0 + chunk] = value.astype(BF16).reshape(chunk, cols, channels)
        if first:
            moves.append(pltpu.make_async_copy(
                value_ref.at[i0:i0 + chunk], out_hbm.at[first + i0:first + i0 + chunk],
                sems.at[1 + i0 // chunk]))
            moves[-1].start()
    if first:
        for move in moves:
            move.wait()


def swap_cores(block, count):
    return lax.ppermute(block, PLANE, [(p, p ^ (count // 2)) for p in range(count)])


def send_chips(block, chips):
    return [
        lax.ppermute(block, "seq", [(x, x ^ m) for x in range(chips)]) for m in range(1, chips)
    ]


def send_turned(block, count, steps):
    return [
        lax.ppermute(
            block, GROUP,
            [(z * count + p, (p ^ m) * count + z) for z in range(count) for p in range(count)])
        for m in range(steps)
    ]


def send_same_core(block, count, chips, step):
    pairs = []
    for z in range(count):
        for p in range(count):
            core, x = p // chips, p % chips
            far, chip = source_of(z, core, x, step, chips)
            pairs.append(((far * chips + x) * count + core * chips + chip, z * count + p))
    return lax.ppermute(block, GROUP, pairs)


def pass_on(block, count):
    return lax.ppermute(block, "resi", [(z, z ^ 1) for z in range(count)])


def call(kernel, outs, scratch, args, flops=0, hbm=False, name=None):
    vmem = pl.BlockSpec(memory_space=pltpu.VMEM)
    size = sum(a.size * a.dtype.itemsize for a in args)
    return pl.pallas_call(
        kernel,
        out_shape=outs,
        in_specs=[vmem] * len(args),
        out_specs=[vmem] * len(outs) if isinstance(outs, list) else (
            pl.BlockSpec(memory_space=pl.ANY) if hbm else vmem),
        scratch_shapes=scratch,
        compiler_params=pltpu.CompilerParams(vmem_limit_bytes=40 * MIB),
        cost_estimate=pl.CostEstimate(flops=flops, bytes_accessed=size, transcendentals=0),
        name=name,
    )(*args)


def body(
    homolog_matrix,
    sequence_pad_mask,
    pair_features,
    residue_pad_mask,
    residue_chain_index,
    homolog_standard_factor,
    homolog_standard_offset,
    factor_mapping_matrices,
    outer_side_biases,
    outer_pair_projection,
    relative_position_table,
    pair_norm_gain,
    pair_norm_bias,
    triangle_projection_weights,
    triangle_projection_biases,
    triangle_sum_norm_gain,
    triangle_sum_norm_bias,
    triangle_output_weight,
    outer_pair_bias,
):
    rows, cols, channels = pair_features.shape
    seqs, _, depth = homolog_matrix.shape
    half = factor_mapping_matrices.shape[1] // 2
    per = LANES // half
    count = lax.axis_size(PLANE)
    width = rows * half
    flat = lambda v: v.reshape(1, -1)
    shape = jax.ShapeDtypeStruct
    residue = flat(residue_pad_mask)
    chain = flat(residue_chain_index)
    pack = shape((seqs, width + LANES), BF16)
    chips = lax.axis_size("seq")
    normed = call(norm_kernel, shape((seqs * rows, depth), F32), [], [homolog_matrix],
                  flops=1 << 36, name="norm")
    left, right = call(
        pack_kernel, [pack, pack],
        [pltpu.VMEM((seqs * (rows + 1), LANES), F32)] * 2,
        [normed, sequence_pad_mask, residue, flat(homolog_standard_factor),
         flat(homolog_standard_offset), factor_mapping_matrices.T, flat(outer_side_biases)],
        flops=1 << 30, name="pack")
    right_swap = swap_cores(right, count)
    left_blocks = [left] + send_chips(left, chips)
    pair = call(functools.partial(join_kernel, 2), shape((2,) + pack.shape, BF16), [],
                [right, right_swap], name="join")
    base, block = call(
        base_kernel,
        [shape((rows, cols, channels), F32), shape((half * LANES, per * channels), BF16)],
        [pltpu.VMEM((LANES, channels), F32), pltpu.VMEM((half * half, channels), F32)],
        [pair_features, relative_position_table, chain, outer_pair_projection, pair],
        flops=1 << 30, name="base")
    rights = send_turned(pair, count, count // 2)
    own_lefts = call(functools.partial(join_kernel, chips), shape((chips,) + pack.shape, BF16), [],
                     left_blocks, flops=1 << 36, name="join")
    lefts = [own_lefts, swap_cores(own_lefts, count)]
    turned, live = call(
        functools.partial(turn_kernel, count),
        [shape((width, count * seqs), BF16), shape((cols, count * seqs), BF16)],
        [pltpu.VMEM((count,) + pack.shape, BF16),
         pltpu.VMEM((count * seqs // LANES, rows * (half + 1), LANES), F32)],
        rights, flops=1 << 36, name="turn")
    updated, right_edge, normed_pair = call(
        edges_kernel,
        [shape((rows, cols, channels), BF16), shape((cols, rows, channels), BF16),
         shape((rows * cols, channels), BF16)],
        [pltpu.VMEM((count,) + pack.shape, BF16),
         pltpu.VMEM((rows // per * cols, half * LANES), BF16),
         pltpu.VMEM((rows * (cols + 1), channels), F32)],
        [turned, live] + lefts + [
            base, block, residue, flat(pair_norm_gain), flat(pair_norm_bias),
            triangle_projection_weights, flat(triangle_projection_biases)],
        name="edges")
    right_edges = [send_same_core(right_edge, count, chips, step) for step in range(chips)]
    for step in range(chips, count, 2):
        block_far = send_same_core(right_edge, count, chips, step)
        right_edges += [block_far, pass_on(block_far, count)]
    left_edge = call(left_kernel, shape((rows, cols, channels), BF16), [],
                     [normed_pair, residue, triangle_projection_weights,
                      flat(triangle_projection_biases)], name="left")
    left_edges = [left_edge] + send_chips(left_edge, chips)
    gate = call(gate_kernel, shape((rows * cols, channels), F32), [],
                [normed_pair, triangle_projection_weights, flat(triangle_projection_biases)],
                flops=1 << 30, name="gate")
    block_sums = shape((rows * cols, channels), F32)
    scratch = pltpu.VMEM((rows * cols, channels), F32)
    panel = call(panel_kernel, shape((chips, rows * cols, channels), F32), [],
                 left_edges + [gate], name="panel")
    near, far = [], []
    for step in range(count - 1):
        sums = near if step < chips else far
        sums[:] = [call(
            functools.partial(step_kernel, step, chips, 0, not sums), block_sums, [scratch],
            [right_edges[step], panel] + sums, name="triangle")]
    parts = ((0, rows * 3 // 4), (rows * 3 // 4, rows // 4))
    own_sums, other_sums, result = [], [], []
    for first, part in parts:
        own, half_sums = call(
            functools.partial(last_kernel, count - 1, chips, first),
            [shape((part * cols, channels), F32), shape((part * cols, channels), BF16)],
            [scratch, pltpu.VMEM((part * cols, channels), F32)],
            [right_edges[-1], panel] + far + near, flops=1 << 28, name="last")
        own_sums.append(own)
        other_sums.append(swap_cores(half_sums, count))
    for n, (first, part) in enumerate(parts):
        args = [own_sums[n], other_sums[n], updated, gate, flat(triangle_sum_norm_gain),
                flat(triangle_sum_norm_bias), triangle_output_weight, flat(outer_pair_bias)]
        part_shape = (part, cols, channels)
        result = [call(
            functools.partial(final_kernel, first),
            shape((rows, cols, channels) if n else part_shape, BF16),
            [pltpu.VMEM(part_shape, BF16), pltpu.SemaphoreType.DMA((1 + part // 8,))] if n else [],
            args + result, flops=1 << 28, hbm=n == 1, name="final")]
    return result[0]


def solution(mesh):
    pair = P(("groups", "resi"), ("resj", "seq"), None)
    placed = (
        P(("groups", "resj", "seq"), "resi", None),
        P(("groups", "resj", "seq"), "resi"),
        pair,
        P("groups"),
        P("groups"),
    ) + (P(),) * 14
    return jax.shard_map(body, mesh=mesh, in_specs=placed, out_specs=pair, check_vma=False)
```

```python
import functools

import jax
import jax.numpy as jnp
from jax import lax
from jax.experimental import pallas as pl
from jax.experimental.pallas import tpu as pltpu
from jax.sharding import PartitionSpec as P

RELMAX = 32
LANES = 128
PLANE = ("resj", "seq")
GROUP = ("resi", "resj", "seq")
F32 = jnp.float32
BF16 = jnp.bfloat16
MIB = 1 << 20


def iota(shape, axis):
    return lax.broadcasted_iota(jnp.int32, shape, axis)


def dot(a, b):
    return jnp.dot(a, b, preferred_element_type=F32)


def sigmoid(v):
    return 0.5 * jnp.tanh(0.5 * v) + 0.5


def layer_norm(values, gain, shift):
    average = jnp.mean(values, axis=-1, keepdims=True)
    centred = values - average
    variance = jnp.mean(centred * centred, axis=-1, keepdims=True)
    return centred * lax.rsqrt(variance + 1e-05) * gain + shift


def norm_kernel(x_ref, out_ref):
    x = x_ref[...].reshape(out_ref.shape).astype(F32)
    out_ref[...] = layer_norm(x, 1.0, 0.0)


def pack_kernel(x_ref, mask_ref, res_ref, gain_ref, shift_ref, w_ref, bias_ref,
                left_ref, right_ref, lscr, rscr):
    seqs, rows = mask_ref.shape
    half = w_ref.shape[0] // 2
    per = LANES // half
    row_start = lax.axis_index("resi") * rows
    normed = (x_ref[...] * gain_ref[...] + shift_ref[...]).astype(BF16)
    lane = iota((2 * half, 2 * LANES), 1)
    spread = lane % half + jnp.where(lane >= LANES, half, 0) == iota((2 * half, 2 * LANES), 0)
    spread = spread.astype(F32)
    wide = lax.dot_general(
        w_ref[...], spread.astype(BF16), (((0,), (0,)), ((), ())), preferred_element_type=F32)
    wide = wide.astype(BF16)
    bias = jnp.dot(jnp.broadcast_to(bias_ref[...], (8, 2 * half)), spread,
                   precision=lax.Precision.HIGHEST, preferred_element_type=F32)[0:1]
    mapped = dot(normed, wide)
    pitch = rows + 1
    for n in range(seqs):
        lscr[n * pitch:n * pitch + rows, :] = mapped[n * rows:(n + 1) * rows, :LANES]
        rscr[n * pitch:n * pitch + rows, :] = mapped[n * rows:(n + 1) * rows, LANES:]
    row_live = pick_rows(res_ref[...], row_start, rows)
    live = (mask_ref[...].astype(F32) * row_live).astype(BF16)
    width = rows * half
    spread_live = (iota((rows, width), 1) // half == iota((rows, width), 0)).astype(BF16)
    live_wide = dot(live, spread_live)
    sub = iota((seqs, LANES), 1) // half
    for tile in range(width // LANES):
        at = slice(tile * LANES, (tile + 1) * LANES)
        for ref, scr, first in ((left_ref, lscr, 0), (right_ref, rscr, LANES)):
            value = scr[pl.ds(tile * per, seqs, stride=pitch), :]
            for k in range(1, per):
                value = jnp.where(sub == k, scr[pl.ds(tile * per + k, seqs, stride=pitch), :], value)
            value = (value + bias[:, first:first + LANES]) * live_wide[:, at]
            ref[:, at] = value.astype(BF16)
    live_tile = dot(live, (iota((rows, LANES), 0) == iota((rows, LANES), 1)).astype(BF16))
    for ref in (left_ref, right_ref):
        ref[:, width:] = live_tile.astype(BF16)


def join_kernel(count, *refs):
    for n in range(count):
        refs[-1][n] = refs[n][...]


def pick_columns(values, start, size):
    total = values.shape[1]
    own = iota((size, total), 1) == iota((size, total), 0) + start
    spread = jnp.broadcast_to(values, (size, total)).astype(F32)
    return jnp.sum(jnp.where(own, spread, 0.0), axis=1, keepdims=True)


def pick_rows(values, start, size):
    total = values.shape[1]
    pick = (iota((total, size), 0) == iota((total, size), 1) + start).astype(BF16)
    return dot(jnp.broadcast_to(values.astype(F32), (8, total)).astype(BF16), pick)[0:1]


def base_kernel(pair_ref, table_ref, chain_ref, w_ref, _, base_ref, block_ref, tscr, wscr):
    rows, cols, channels = pair_ref.shape
    row_start = lax.axis_index("resi") * rows
    col_start = lax.axis_index(PLANE) * cols
    tscr[...] = jnp.zeros_like(tscr)
    tscr[0:table_ref.shape[0], :] = table_ref[...].astype(F32)
    table = tscr[...].astype(BF16)
    chain = chain_ref[...]
    same = pick_columns(chain, col_start, cols) == pick_rows(chain, row_start, rows)
    offset = iota((cols, rows), 0) + col_start - iota((cols, rows), 1) - row_start + RELMAX
    bins = jnp.where(same, jnp.clip(offset, 0, 2 * RELMAX), 2 * RELMAX + 1)
    lane = iota((cols, LANES), 1)
    for i in range(rows):
        one_hot = (lane == bins[:, i:i + 1]).astype(F32).astype(BF16)
        base_ref[i] = pair_ref[i].astype(F32) + dot(one_hot, table)
    half = int(round(w_ref.shape[0] ** 0.5))
    per = LANES // half
    for c in range(half):
        first = c * (half + 1)
        wscr[first:first + half, :] = w_ref[c * half:(c + 1) * half, :].astype(F32)
    block_ref[...] = jnp.zeros_like(block_ref)
    for d in range(half):
        value = wscr[pl.ds(d, half, stride=half + 1), :].astype(BF16)
        for k in range(per):
            block_ref[pl.ds(d * LANES + k * half, half), k * channels:(k + 1) * channels] = value


def turn_kernel(count, *refs):
    pairs = count // 2
    rights, (turned_ref, live_ref, rall, tscr) = refs[:pairs], refs[pairs:]
    z = lax.axis_index("resi")
    width, total_seqs = turned_ref.shape
    cols = live_ref.shape[0]
    half = width // cols
    pitch = half + 1
    for step in range(pairs):
        for n in range(2):
            rall[z ^ (step + n * pairs)] = rights[step][n]
    right = rall[...].reshape(total_seqs, -1)
    for at in range(0, width, LANES):
        for s in range(0, total_seqs, LANES):
            block = right[s:s + LANES, at:at + LANES].astype(F32).T
            for n in range(0, LANES, half):
                first = (at + n) // half * pitch
                tscr[s // LANES, first:first + half, :] = block[n:n + half]
    for d in range(half):
        for s in range(0, total_seqs, LANES):
            turned = tscr[s // LANES, pl.ds(d, cols, stride=pitch), :]
            turned_ref[d * cols:(d + 1) * cols, s:s + LANES] = turned.astype(BF16)
    live_ref[...] = right[:, width:].astype(F32).T[0:cols].astype(BF16)


def edges_kernel(turned_ref, live_ref, own_ref, swapped_ref, base_ref, block_ref, res_ref,
                 gain_ref, shift_ref, w_ref, bias_ref,
                 updated_ref, right_ref, nscr, lall, oscr, escr):
    rows, cols, channels = base_ref.shape
    chips, seqs = own_ref.shape[:2]
    half = block_ref.shape[0] // LANES
    per = LANES // half
    width = rows * half
    q = lax.axis_index(PLANE)
    row_start, col_start = lax.axis_index("resi") * rows, q * cols
    for step in range(chips):
        lall[q ^ step] = own_ref[step]
        lall[q ^ (chips + step)] = swapped_ref[step]
    left = lall[...].reshape(2 * chips * seqs, -1)
    counts = dot(live_ref[...], left[:, width:])
    inverse = 1.0 / jnp.maximum(counts, 1.0)
    wide = 2 * LANES
    tall = 8
    for first in range(0, width, wide):
        for d0 in range(0, half, tall):
            product = dot(turned_ref[d0 * cols:(d0 + tall) * cols, :], left[:, first:first + wide])
            product = product.astype(BF16)
            for dd in range(tall):
                for t in range(wide // LANES):
                    g = first // LANES + t
                    oscr[g * cols:(g + 1) * cols, (d0 + dd) * LANES:(d0 + dd + 1) * LANES] = (
                        product[dd * cols:(dd + 1) * cols, t * LANES:(t + 1) * LANES])
    outer = dot(oscr[...], block_ref[...])
    for i in range(rows):
        g, k = i // per, i % per
        part = outer[g * cols:(g + 1) * cols, k * channels:(k + 1) * channels]
        updated = (base_ref[i] + part * inverse[:, i:i + 1]).astype(BF16)
        updated_ref[i] = updated
        normed = layer_norm(updated.astype(F32), gain_ref[...], shift_ref[...])
        nscr[i * cols:(i + 1) * cols, :] = normed.astype(BF16)
    live = pick_columns(res_ref[...], col_start, cols) * pick_rows(res_ref[...], row_start, rows)
    chunk = 8
    for i0 in range(0, rows, chunk):
        mixture = dot(nscr[i0 * cols:(i0 + chunk) * cols, :], w_ref[:, 2 * channels:4 * channels])
        mixture = mixture + bias_ref[:, 2 * channels:4 * channels]
        right_edge = sigmoid(mixture[:, :channels]) * mixture[:, channels:]
        for ii in range(chunk):
            at = slice(ii * cols, (ii + 1) * cols)
            first = (i0 + ii) * (cols + 1)
            escr[first:first + cols, :] = right_edge[at] * live[:, i0 + ii:i0 + ii + 1]
    for k in range(cols):
        right_ref[k] = escr[pl.ds(k, rows, stride=cols + 1), :].astype(BF16)


def left_kernel(normed_ref, res_ref, w_ref, bias_ref, left_ref):
    rows, cols, channels = left_ref.shape
    row_start, col_start = lax.axis_index("resi") * rows, lax.axis_index(PLANE) * cols
    live = pick_columns(res_ref[...], col_start, cols) * pick_rows(res_ref[...], row_start, rows)
    chunk = 8
    for i0 in range(0, rows, chunk):
        mixture = dot(normed_ref[i0 * cols:(i0 + chunk) * cols, :], w_ref[:, :2 * channels])
        mixture = mixture + bias_ref[:, :2 * channels]
        left_edge = sigmoid(mixture[:, :channels]) * mixture[:, channels:]
        for ii in range(chunk):
            here = left_edge[ii * cols:(ii + 1) * cols] * live[:, i0 + ii:i0 + ii + 1]
            left_ref[i0 + ii] = here.astype(BF16)


def gate_kernel(normed_ref, w_ref, bias_ref, gate_ref):
    first = w_ref.shape[1] - gate_ref.shape[1]
    gate_ref[...] = sigmoid(dot(normed_ref[...], w_ref[:, first:]) + bias_ref[:, first:])


def panel_kernel(*refs):
    *lefts, _, panel_ref = refs
    x = lax.axis_index("seq")
    for step, left in enumerate(lefts):
        panel_ref[x ^ step] = left[...].astype(F32).reshape(panel_ref.shape[1:])


def source_of(z, core, x, step, chips):
    block = z ^ step ^ ((x + core) % 2 if step >= chips else 0)
    return block // chips, block % chips


def add_block(panel_ref, chip, rscr, cols, first, before, store):
    rows, depth, channels = store.shape[0] // cols, rscr.shape[0] // cols, rscr.shape[1]
    block = 8
    tiles = cols // 8

    def rows_body(at, carry):
        def place(b, t, start=0):
            return pl.ds(pl.multiple_of((start + at * block + b) * cols + t * 8, 8), 8)

        if before is None:
            sums = [[jnp.zeros((8, channels), F32) for _ in range(tiles)] for _ in range(block)]
        else:
            sums = [[before[place(b, t, first), :] for t in range(tiles)] for b in range(block)]
        for k in range(depth):
            column = [rscr[k * cols + t * 8:k * cols + t * 8 + 8, :] for t in range(tiles)]
            for b in range(block):
                row = panel_ref[chip, pl.ds((first + at * block + b) * depth + k, 1), :]
                for t in range(tiles):
                    sums[b][t] = sums[b][t] + row * column[t]
        for b in range(block):
            for t in range(tiles):
                store[place(b, t), :] = sums[b][t].astype(store.dtype)
        return carry

    lax.fori_loop(0, rows // block, rows_body, 0)


def step_kernel(step, chips, first, fresh, right_ref, panel_ref, *refs):
    out_ref, rscr = refs[-2:]
    z, core, x = [lax.axis_index(axis) for axis in GROUP]
    chip = source_of(z, core, x, step, chips)[1]
    rscr[...] = right_ref[...].astype(F32).reshape(rscr.shape)
    add_block(panel_ref, chip, rscr, right_ref.shape[1], first, None if fresh else refs[0], out_ref)


def last_kernel(step, chips, first, right_ref, panel_ref, far_ref, near_ref, own_ref, other_ref,
                rscr, acc):
    step_kernel(step, chips, first, False, right_ref, panel_ref, far_ref, acc, rscr)
    mine = lax.axis_index("resi") // chips == lax.axis_index("resj")
    at = pl.ds(first * right_ref.shape[1], acc.shape[0])

    @pl.when(mine)
    def _():
        own_ref[...] = near_ref[at, :]
        other_ref[...] = acc[...].astype(BF16)

    @pl.when(jnp.logical_not(mine))
    def _():
        own_ref[...] = acc[...]
        other_ref[...] = near_ref[at, :].astype(BF16)


def final_kernel(first, own_ref, other_ref, updated_ref, gate_ref, gain_ref, shift_ref, w_ref, bias_ref,
                 *refs):
    if first:
        before_ref, out_hbm, value_ref, sems = refs
        moves = [pltpu.make_async_copy(before_ref, out_hbm.at[:first], sems.at[0])]
        moves[0].start()
    else:
        value_ref, = refs
    rows, cols, channels = value_ref.shape
    chunk = 8
    for i0 in range(0, rows, chunk):
        at = slice(i0 * cols, (i0 + chunk) * cols)
        here = slice((first + i0) * cols, (first + i0 + chunk) * cols)
        sums = own_ref[at, :] + other_ref[at, :].astype(F32)
        normed = layer_norm(sums, gain_ref[...], shift_ref[...]).astype(BF16)
        result = dot(normed, w_ref[...]) + bias_ref[...]
        updated = updated_ref[first + i0:first + i0 + chunk].reshape(chunk * cols, channels).astype(F32)
        value = updated + gate_ref[here, :] * result
        value_ref[i0:i0 + chunk] = value.astype(BF16).reshape(chunk, cols, channels)
        if first:
            moves.append(pltpu.make_async_copy(
                value_ref.at[i0:i0 + chunk], out_hbm.at[first + i0:first + i0 + chunk],
                sems.at[1 + i0 // chunk]))
            moves[-1].start()
    if first:
        for move in moves:
            move.wait()


def swap_cores(block, count):
    return lax.ppermute(block, PLANE, [(p, p ^ (count // 2)) for p in range(count)])


def send_chips(block, chips):
    return [
        lax.ppermute(block, "seq", [(x, x ^ m) for x in range(chips)]) for m in range(1, chips)
    ]


def send_turned(block, count, steps):
    return [
        lax.ppermute(
            block, GROUP,
            [(z * count + p, (p ^ m) * count + z) for z in range(count) for p in range(count)])
        for m in range(steps)
    ]


def send_same_core(block, count, chips, step):
    pairs = []
    for z in range(count):
        for p in range(count):
            core, x = p // chips, p % chips
            far, chip = source_of(z, core, x, step, chips)
            pairs.append(((far * chips + x) * count + core * chips + chip, z * count + p))
    return lax.ppermute(block, GROUP, pairs)


def pass_on(block, count):
    return lax.ppermute(block, "resi", [(z, z ^ 1) for z in range(count)])


def call(kernel, outs, scratch, args, flops=0, hbm=False, name=None):
    vmem = pl.BlockSpec(memory_space=pltpu.VMEM)
    size = sum(a.size * a.dtype.itemsize for a in args)
    return pl.pallas_call(
        kernel,
        out_shape=outs,
        in_specs=[vmem] * len(args),
        out_specs=[vmem] * len(outs) if isinstance(outs, list) else (
            pl.BlockSpec(memory_space=pl.ANY) if hbm else vmem),
        scratch_shapes=scratch,
        compiler_params=pltpu.CompilerParams(vmem_limit_bytes=40 * MIB),
        cost_estimate=pl.CostEstimate(flops=flops, bytes_accessed=size, transcendentals=0),
        name=name,
    )(*args)


def body(
    homolog_matrix,
    sequence_pad_mask,
    pair_features,
    residue_pad_mask,
    residue_chain_index,
    homolog_standard_factor,
    homolog_standard_offset,
    factor_mapping_matrices,
    outer_side_biases,
    outer_pair_projection,
    relative_position_table,
    pair_norm_gain,
    pair_norm_bias,
    triangle_projection_weights,
    triangle_projection_biases,
    triangle_sum_norm_gain,
    triangle_sum_norm_bias,
    triangle_output_weight,
    outer_pair_bias,
):
    rows, cols, channels = pair_features.shape
    seqs, _, depth = homolog_matrix.shape
    half = factor_mapping_matrices.shape[1] // 2
    per = LANES // half
    count = lax.axis_size(PLANE)
    width = rows * half
    flat = lambda v: v.reshape(1, -1)
    shape = jax.ShapeDtypeStruct
    residue = flat(residue_pad_mask)
    chain = flat(residue_chain_index)
    pack = shape((seqs, width + LANES), BF16)
    chips = lax.axis_size("seq")
    normed = call(norm_kernel, shape((seqs * rows, depth), F32), [], [homolog_matrix],
                  flops=1 << 36, name="norm")
    left, right = call(
        pack_kernel, [pack, pack],
        [pltpu.VMEM((seqs * (rows + 1), LANES), F32)] * 2,
        [normed, sequence_pad_mask, residue, flat(homolog_standard_factor),
         flat(homolog_standard_offset), factor_mapping_matrices.T, flat(outer_side_biases)],
        flops=1 << 30, name="pack")
    right_swap = swap_cores(right, count)
    left_blocks = [left] + send_chips(left, chips)
    pair = call(functools.partial(join_kernel, 2), shape((2,) + pack.shape, BF16), [],
                [right, right_swap], name="join")
    base, block = call(
        base_kernel,
        [shape((rows, cols, channels), F32), shape((half * LANES, per * channels), BF16)],
        [pltpu.VMEM((LANES, channels), F32), pltpu.VMEM((half * (half + 1), channels), F32)],
        [pair_features, relative_position_table, chain, outer_pair_projection, pair],
        flops=1 << 30, name="base")
    rights = send_turned(pair, count, count // 2)
    own_lefts = call(functools.partial(join_kernel, chips), shape((chips,) + pack.shape, BF16), [],
                     left_blocks, flops=1 << 36, name="join")
    lefts = [own_lefts, swap_cores(own_lefts, count)]
    turned, live = call(
        functools.partial(turn_kernel, count),
        [shape((width, count * seqs), BF16), shape((cols, count * seqs), BF16)],
        [pltpu.VMEM((count,) + pack.shape, BF16),
         pltpu.VMEM((count * seqs // LANES, rows * (half + 1), LANES), F32)],
        rights, flops=1 << 36, name="turn")
    updated, right_edge, normed_pair = call(
        edges_kernel,
        [shape((rows, cols, channels), BF16), shape((cols, rows, channels), BF16),
         shape((rows * cols, channels), BF16)],
        [pltpu.VMEM((count,) + pack.shape, BF16),
         pltpu.VMEM((rows // per * cols, half * LANES), BF16),
         pltpu.VMEM((rows * (cols + 1), channels), F32)],
        [turned, live] + lefts + [
            base, block, residue, flat(pair_norm_gain), flat(pair_norm_bias),
            triangle_projection_weights, flat(triangle_projection_biases)],
        name="edges")
    right_edges = [send_same_core(right_edge, count, chips, step) for step in range(chips)]
    for step in range(chips, count, 2):
        block_far = send_same_core(right_edge, count, chips, step)
        right_edges += [block_far, pass_on(block_far, count)]
    left_edge = call(left_kernel, shape((rows, cols, channels), BF16), [],
                     [normed_pair, residue, triangle_projection_weights,
                      flat(triangle_projection_biases)], name="left")
    left_edges = [left_edge] + send_chips(left_edge, chips)
    gate = call(gate_kernel, shape((rows * cols, channels), F32), [],
                [normed_pair, triangle_projection_weights, flat(triangle_projection_biases)],
                flops=1 << 30, name="gate")
    block_sums = shape((rows * cols, channels), F32)
    scratch = pltpu.VMEM((rows * cols, channels), F32)
    panel = call(panel_kernel, shape((chips, rows * cols, channels), F32), [],
                 left_edges + [gate], name="panel")
    near, far = [], []
    for step in range(count - 1):
        sums = near if step < chips else far
        sums[:] = [call(
            functools.partial(step_kernel, step, chips, 0, not sums), block_sums, [scratch],
            [right_edges[step], panel] + sums, name="triangle")]
    parts = ((0, rows * 3 // 4), (rows * 3 // 4, rows // 4))
    own_sums, other_sums, result = [], [], []
    for first, part in parts:
        own, half_sums = call(
            functools.partial(last_kernel, count - 1, chips, first),
            [shape((part * cols, channels), F32), shape((part * cols, channels), BF16)],
            [scratch, pltpu.VMEM((part * cols, channels), F32)],
            [right_edges[-1], panel] + far + near, flops=1 << 28, name="last")
        own_sums.append(own)
        other_sums.append(swap_cores(half_sums, count))
    for n, (first, part) in enumerate(parts):
        args = [own_sums[n], other_sums[n], updated, gate, flat(triangle_sum_norm_gain),
                flat(triangle_sum_norm_bias), triangle_output_weight, flat(outer_pair_bias)]
        part_shape = (part, cols, channels)
        result = [call(
            functools.partial(final_kernel, first),
            shape((rows, cols, channels) if n else part_shape, BF16),
            [pltpu.VMEM(part_shape, BF16), pltpu.SemaphoreType.DMA((1 + part // 8,))] if n else [],
            args + result, flops=1 << 28, hbm=n == 1, name="final")]
    return result[0]


def solution(mesh):
    pair = P(("groups", "resi"), ("resj", "seq"), None)
    placed = (
        P(("groups", "resj", "seq"), "resi", None),
        P(("groups", "resj", "seq"), "resi"),
        pair,
        P("groups"),
        P("groups"),
    ) + (P(),) * 14
    return jax.shard_map(body, mesh=mesh, in_specs=placed, out_specs=pair, check_vma=False)
```
